128 devices in a mesh: prow: 16 (over y, z), pcol: 8 (over x, core).
Axes of the slice: x: 4, y: 4, z: 4, core: 2. Of those that a mesh axis runs over, the one named last changes fastest.
Arguments:
- front: float32 [4, 4096, 8, 2048], P(None, 'prow', None, 'pcol')
- child_update: bfloat16 [8192, 4096], P('prow', 'pcol'), may hold values from -6 to 6
- child_map: int32 [2, 16], replicated, may hold values from 0 to 63, as said below
- pivots: int32 [4, 256], replicated, may hold values from 0 to 255, as said below
Outputs:
- factored: float32 [4, 4096, 8, 2048], P(None, 'prow', None, 'pcol')
The draws below stay inside these ranges and needn't reach their ends.
Inputs may be any that keep to these rules, and one draw needn't show every extreme that they name: `child_map`: each row rises strictly, consecutive entries differing by 1 or 2; row 0 begins at 0 and row 1 ends at 63. `pivots`: each row is a permutation.
All inputs are finite; a program needn't handle non-finite values.
Results may differ from the reference program's by a relative error of at most 0.0003.
Values may be sent and summed in bfloat16 or wider, within the bound.
No kernel may reach another device: no remote copies, remote signals or barrier semaphores. Data moves between devices by JAX's collectives and lax.ppermute only.
A program may use at most 128 MiB of HBM per device.

```python
import math
import jax
import jax.numpy as jnp
from jax import lax

F = 16384
BS = 256
CU = 4096
NPIV = 4
NS = 2
NB = 64
CB = 16
RT = 4
CT = 8


def shared_order(key):
    keys = jax.random.split(key, NPIV)
    return jax.vmap(lambda single: jax.random.permutation(single, BS))(keys).astype(jnp.int32)


def draw_pivots(key, part):
    return shared_order(key)


def draw_front(key, part):
    order = shared_order(key)
    key = jax.random.fold_in(key, 11)
    noise_key, boost_key = jax.random.split(key)
    noise = jax.random.truncated_normal(noise_key, -6.0, 6.0, (F, F), jnp.float32)
    boost = math.sqrt(BS) * jnp.exp(jax.random.uniform(boost_key, (NPIV, BS), jnp.float32, math.log(6.0), math.log(12.0)))
    position = jnp.arange(BS, dtype=jnp.int32)
    onehot = order[:, None, :] == position[None, :, None]
    extra = jnp.where(onehot, boost[:, None, :], 0.0)
    for column_step in range(NPIV):
        low_edge = column_step * BS
        noise = noise.at[low_edge:low_edge + BS, low_edge:low_edge + BS].add(extra[column_step])
    return noise.reshape(RT, F // RT, CT, F // CT)


def draw_child_map(key, part):
    key = jax.random.fold_in(key, 23)
    gaps = jax.random.randint(key, (2, CB - 1), 1, 3).astype(jnp.int32)
    rising = jnp.concatenate([jnp.zeros((2, 1), jnp.int32), jnp.cumsum(gaps, axis=1).astype(jnp.int32)], axis=1)
    first_child = rising[0]
    second_child = (NB - 1 - rising[1])[::-1]
    return jnp.stack([first_child, second_child]).astype(jnp.int32)


def level_of(stream_key, dims, cuts, least, high):
    factor_of = 1.0
    for dim, parts in cuts:
        draws = jax.random.uniform(jax.random.fold_in(jax.random.fold_in(stream_key, 6), dim), (parts,), jnp.float32, least / len(cuts), high / len(cuts))
        factor_of = factor_of * jnp.repeat(jnp.exp(draws), dims[dim] // parts).reshape((-1,) + (1,) * (len(dims) - 1 - dim))
    return factor_of


def bell_draw(rng, shape, scale, reach, shards=(), kind=jnp.bfloat16):
    gain = level_of(rng, shape, shards, -0.22, 0.18) if shards else 1.0
    array = jax.random.normal(rng, shape, jnp.float32) * scale * gain
    return jnp.minimum(jnp.maximum(array, -reach), reach).astype(kind)


def setup_inputs(seed: int = 0) -> dict:
    streams_of = jax.random.split(jax.random.key(seed), 5)
    return {
        "front": draw_front(jax.random.fold_in(streams_of[4], 71), 0),
        "child_update": bell_draw(streams_of[1], (2 * CU, CU), 1.0, 6.0, ((0, 16), (1, 8))),
        "child_map": draw_child_map(jax.random.fold_in(streams_of[4], 71), 0),
        "pivots": draw_pivots(jax.random.fold_in(streams_of[4], 71), 0),
    }


def newton(pivot_block):
    diagonal = jnp.diagonal(pivot_block)
    approx = jnp.diag(diagonal / (diagonal * diagonal + 1.0))
    for sweep_index in range(NS):
        product = jnp.dot(jnp.dot(approx, pivot_block, precision=lax.Precision.HIGHEST), approx, precision=lax.Precision.HIGHEST)
        approx = 2.0 * approx - product
    return approx


def reference(front, child_update, child_map, pivots):
    matrix = front.reshape(F, F)
    offsets = jnp.arange(BS, dtype=jnp.int32)
    for child in range(2):
        row_index = (child_map[child][:, None] * BS + offsets[None, :]).reshape(CU).astype(jnp.int32)
        update_part = child_update[child * CU:(child + 1) * CU].astype(jnp.float32)
        matrix = matrix.at[row_index[:, None], row_index[None, :]].add(update_part)
    for column_step in range(NPIV):
        low_edge = column_step * BS
        high_edge = low_edge + BS
        matrix = matrix.at[low_edge:high_edge].set(matrix[low_edge:high_edge][pivots[column_step]])
        inverse = newton(matrix[low_edge:high_edge, low_edge:high_edge])
        lower_part = jnp.dot(matrix[high_edge:, low_edge:high_edge], inverse, precision=lax.Precision.HIGHEST)
        matrix = matrix.at[high_edge:, low_edge:high_edge].set(lower_part)
        product = jnp.dot(lower_part, matrix[low_edge:high_edge, high_edge:], precision=lax.Precision.HIGHEST)
        matrix = matrix.at[high_edge:, high_edge:].add(-product)
    return matrix.reshape(RT, F // RT, CT, F // CT)
```

```python
import functools

import jax
import jax.numpy as jnp
from jax import lax
from jax.experimental import pallas as pl
from jax.experimental.pallas import tpu as pltpu
from jax.sharding import PartitionSpec as P

NPIV = 4
NS = 2
BS = 256
HALF = 128
REACH = 6.0
TOP = 30000.0
HIGHEST = lax.Precision.HIGHEST
F32 = jnp.float32
BF16 = jnp.bfloat16
F16 = jnp.float16
SMEM = pl.BlockSpec(memory_space=pltpu.SMEM)
VMEM = pl.BlockSpec(memory_space=pltpu.VMEM)
LIMIT = 60 * 1024 * 1024


def call(body, outs, ins, flops=0):
    smem = [a.dtype == jnp.int32 for a in ins]
    moved = sum(a.size * a.dtype.itemsize for a in ins)
    moved += sum(o.size * o.dtype.itemsize for o in outs)
    return pl.pallas_call(
        body,
        out_shape=outs,
        in_specs=[SMEM if flag else VMEM for flag in smem],
        out_specs=[VMEM] * len(outs),
        compiler_params=pltpu.CompilerParams(vmem_limit_bytes=LIMIT),
        cost_estimate=pl.CostEstimate(flops=flops, bytes_accessed=moved, transcendentals=0),
    )(*ins)


def shape(dims, kind):
    return jax.ShapeDtypeStruct(dims, kind)


def spot(map_ref, child, low, count, test):
    found = jnp.int32(-1)
    value = jnp.int32(-1)
    for step in range(count):
        entry = map_ref[child, low + step]
        hit = test(entry)
        found = jnp.where(hit, low + step, found)
        value = jnp.where(hit, entry, value)
    return found, value


def split(value):
    high = value.astype(BF16)
    low = (value - high.astype(F32)).astype(BF16)
    return high, low


def dot(left, right):
    return jnp.dot(left, right, preferred_element_type=F32)


def dot3(left, right):
    (a, b), (c, d) = left, right
    return dot(a, c) + (dot(a, d) + dot(b, c))


def pick_z(map_ref, rc_ref, child_ref, *out_refs):
    row = rc_ref[0]
    z = row % 4
    child = row // 8
    first = 2 * (row % 8)
    second_at = map_ref[child, first + 1] % 4
    for hop in range(4):
        which = jnp.where(second_at == (z + hop) % 4, 1, 0)
        out_refs[hop][...] = child_ref[which]
    out_refs[4][...] = child_ref[jnp.where(row == 0, 1, 0)]
    out_refs[5][...] = child_ref[jnp.where((row == 1) & (map_ref[0, 2] == 3), 0, 1)]


def held_after_z(map_ref, y, z, hop):
    source = (z - hop + 4) % 4
    child = y // 2
    first = 2 * ((4 * y + source) % 8)
    return spot(map_ref, child, first, 2, lambda entry: entry % 4 == z)


def pick_y(map_ref, rc_ref, *refs):
    held, outs = refs[:4], refs[4:]
    row = rc_ref[0]
    y, z = row // 4, row % 4
    stops = [held_after_z(map_ref, y, z, hop) for hop in range(4)]
    for shift in range(4):
        goal = (y + shift) % 4
        for hop in range(4):
            index, value = stops[hop]

            @pl.when((index >= 0) & ((value // 4) % 4 == goal))
            def _(hop=hop, shift=shift):
                outs[shift][...] = held[hop][...]


def row_of(map_ref, row, slot):
    child = slot // 2
    found, value = spot(map_ref, child, 8 * (slot % 2), 8, lambda entry: entry % 16 == row)
    return value


def col_of(map_ref, child, source, col):
    found, value = spot(map_ref, child, 4 * source, 4, lambda entry: entry % 8 == col)
    return found, value


def pick_x(map_ref, rc_ref, *refs):
    mine, other, outs = refs[:4], refs[4:8], refs[8:]
    row, col = rc_ref[0], rc_ref[1]
    y, x, core = row // 4, col // 2, col % 2
    for shift in range(4):
        child = ((y - shift + 4) % 4) // 2
        for hop in range(4):
            goal = 2 * ((x + hop) % 4) + core
            found, value = col_of(map_ref, child, x, goal)
            part = found % 4
            for half in range(2):
                cut = slice(half * BS, half * BS + BS)

                @pl.when((found >= 0) & (part == 2 * core + half))
                def _(shift=shift, hop=hop, cut=cut):
                    outs[hop][shift] = mine[shift][:, cut]

                @pl.when((found >= 0) & (part == 2 * (1 - core) + half))
                def _(shift=shift, hop=hop, cut=cut):
                    outs[hop][shift] = other[shift][:, cut]


def pick_top(map_ref, rc_ref, child_ref, a1, a2, b0, b1, b2, *outs):
    row, col = rc_ref[0], rc_ref[1]
    x, core = col // 2, col % 2
    second_first = map_ref[0, 2] == 2
    for hop in range(4):
        goal = 2 * ((x + hop) % 4) + core
        found, value = col_of(map_ref, 0, x, goal)
        part = found % 4
        for half in range(2):
            cut = slice(half * BS, half * BS + BS)
            near = (found >= 0) & (part == 2 * core + half)
            far = (found >= 0) & (part == 2 * (1 - core) + half)
            use_one = (row == 1) | ((row == 2) & second_first)
            use_two = (row == 3) | ((row == 2) & jnp.logical_not(second_first))
            for cond, here, one, two in ((near, None, a1, a2), (far, b0, b1, b2)):

                @pl.when(cond & (row == 0))
                def _(here=here, hop=hop, cut=cut):
                    source = child_ref[0] if here is None else here[...]
                    outs[hop][...] = source[:, cut]

                @pl.when(cond & use_one)
                def _(one=one, hop=hop, cut=cut):
                    outs[hop][...] = one[:, cut]

                @pl.when(cond & use_two)
                def _(two=two, hop=hop, cut=cut):
                    outs[hop][...] = two[:, cut]


def prepare_top(map_ref, rc_ref, front_ref, pivot_ref, *refs):
    parts, out_ref, work = refs[:4], refs[4], refs[5]
    row, col = rc_ref[0], rc_ref[1]
    x = col // 2

    def load(tile, carry):
        for half in range(2):
            rows = pl.ds(half * 8 + tile, BS, stride=16)
            work[tile, :, half * HALF : half * HALF + HALF] = front_ref[rows, :]
        return carry

    lax.fori_loop(0, 8, load, 0)
    has_row, value = spot(map_ref, 0, 0, 4, lambda entry: entry == row)
    for hop in range(4):
        source = (x - hop + 4) % 4
        found, value = col_of(map_ref, 0, source, col)

        @pl.when((has_row >= 0) & (found >= 0))
        def _(hop=hop, value=value):
            work[value // 8] = work[value // 8] + parts[hop][...].astype(F32)

    order = pivot_ref[...]
    spread = lax.broadcasted_iota(jnp.int32, (BS, BS), 1).astype(F32)
    select = jnp.where(order[:, :1] == spread, 1.0, 0.0).astype(BF16)

    def store(tile, carry):
        value = work[tile]
        high = value.astype(BF16)
        rest = value - high.astype(F32)
        middle = rest.astype(BF16)
        last = (rest - middle.astype(F32)).astype(BF16)
        turned = (dot(select, high) + dot(select, middle)) + dot(select, last)
        for piece in range(4):
            out_ref[piece, tile] = turned[piece * 64 : piece * 64 + 64]
        return carry

    lax.fori_loop(0, 8, store, 0)


def pick_left(map_ref, rc_ref, *refs):
    held, one, two = refs[:4], refs[4], refs[5]
    row, col = rc_ref[0], rc_ref[1]
    y = row // 4
    at_one = jnp.where(col == 0, 1, 0)
    at_two = jnp.where((col == 1) & (map_ref[0, 2] == 3), 0, 1)
    for shift in range(4):
        slot = (y - shift + 4) % 4
        for out, at in ((one, at_one), (two, at_two)):
            for half in range(2):

                @pl.when((slot < 2) & (at == half))
                def _(shift=shift, out=out, half=half, slot=slot):
                    out[slot] = held[shift][:, half * BS : half * BS + BS]


def prepare_left(map_ref, rc_ref, left_ref, top_ref, *refs):
    held, one, two, out_ref = refs[:4], refs[4], refs[5], refs[6]
    row, col = rc_ref[0], rc_ref[1]
    y = row // 4
    out_ref[...] = left_ref[...]
    found, value = spot(map_ref, 0, 0, 4, lambda entry: entry == col)
    second_first = map_ref[0, 2] == 2
    use_one = (found >= 0) & ((col == 1) | ((col == 2) & second_first))
    use_two = (found >= 0) & ((col == 3) | ((col == 2) & jnp.logical_not(second_first)))
    for shift in range(4):
        slot = (y - shift + 4) % 4
        parent = row_of(map_ref, row, slot)
        tile = parent // 16
        good = (slot < 2) & (parent >= 0)

        @pl.when(good & (col == 0))
        def _(shift=shift, tile=tile):
            out_ref[tile] = out_ref[tile] + held[shift][:, :BS].astype(F32)

        for use, part in ((use_one, one), (use_two, two)):

            @pl.when(good & use)
            def _(part=part, slot=slot, tile=tile):
                out_ref[tile] = out_ref[tile] + part[slot].astype(F32)

    @pl.when(row < NPIV)
    def _():
        for piece in range(4):
            out_ref[0, piece * 64 : piece * 64 + 64] = top_ref[piece, 0]


def high_dot(left, right):
    return jnp.dot(left, right, precision=HIGHEST, preferred_element_type=F32)


def block(step):
    return slice(step * BS, step * BS + BS)


def factor_corner(gathered_ref, out_ref, inverse_ref):
    for y in range(4):
        for z in range(4):
            for h in range(2):
                for k in range(4):
                    low = z * BS + h * HALF + y * 32
                    index = ((y * 4 + z) * 2 + h) * 4 + k
                    out_ref[low : low + 32, block(k)] = gathered_ref[index]
    diagonal = lax.broadcasted_iota(jnp.int32, (BS, BS), 0) == lax.broadcasted_iota(
        jnp.int32, (BS, BS), 1
    )
    for k in range(NPIV):
        pivot = out_ref[block(k), block(k)]
        on_line = jnp.where(diagonal, pivot, 0.0)
        approx = on_line / (on_line * on_line + 1.0)
        for sweep_index in range(NS):
            approx = 2.0 * approx - high_dot(high_dot(approx, pivot), approx)
        inverse_ref[k] = approx
        for i in range(k + 1, NPIV):
            lower = high_dot(out_ref[block(i), block(k)], approx)
            out_ref[block(i), block(k)] = lower
            for j in range(k + 1, NPIV):
                out_ref[block(i), block(j)] = out_ref[block(i), block(j)] - high_dot(
                    lower, out_ref[block(k), block(j)]
                )


def finish(
    map_ref, rc_ref, front_ref, top_ref, own_ref, left_ref, corner_ref, inverse_ref,
    p0, p1, p2, p3, out_ref, upper_hi, upper_lo, row_out, lower_hi, lower_lo, col_out,
):
    parts = (p0, p1, p2, p3)
    tile = pl.program_id(0)
    row, col = rc_ref[0], rc_ref[1]
    y, x = row // 4, col // 2

    @pl.when(tile == 0)
    def _():
        def one(s, carry):
            uppers = []
            mine = jnp.zeros((BS, BS), F32)
            for k in range(NPIV):
                raw = jnp.concatenate([top_ref[4 * piece + k, s] for piece in range(4)], axis=0)
                taken = jnp.zeros((BS, BS), F32)
                for m in range(k):
                    taken = taken + dot3(split(corner_ref[block(k), block(m)]), uppers[m])
                mine = jnp.where(row == k, taken, mine)
                high, low = split(raw - taken)
                uppers.append((high, low))
                dead = (s == 0) & (col < NPIV)
                upper_hi[s, block(k)] = jnp.where(dead, jnp.zeros_like(high), high)
                upper_lo[s, block(k)] = jnp.where(dead, jnp.zeros_like(low), low)
            own = jnp.concatenate([own_ref[piece, s] for piece in range(4)], axis=0)
            row_out[s] = own - mine
            return carry

        lax.fori_loop(0, 8, one, 0)

    def lower_step():
        lowers = []
        kept = jnp.zeros((BS, BS), F32)
        for k in range(NPIV):
            value = left_ref[k, 0]
            for m in range(k):
                value = value - dot3(lowers[m], split(corner_ref[block(m), block(k)]))
            lower = dot3(split(value), split(inverse_ref[k]))
            kept = jnp.where(col == k, lower, kept)
            lowers.append(split(lower))
            lower_hi[:, block(k)] = lowers[k][0]
            lower_lo[:, block(k)] = lowers[k][1]
        col_out[...] = kept

    lower_step()

    def at(s, half):
        return pl.ds(half * 8 + s, BS, stride=16)

    def put(s, value):
        for half in range(2):
            out_ref[0, at(s, half), :] = value[:, half * HALF : half * HALF + HALF]

    top_tile = (tile == 0) & (row < NPIV)

    @pl.when(top_tile)
    def _():
        def one(s, carry):
            put(s, row_out[s])
            return carry

        lax.fori_loop(0, 8, one, 0)

        for r in range(NPIV):
            for c in range(NPIV):

                @pl.when((row == r) & (col == c))
                def _(r=r, c=c):
                    put(0, corner_ref[block(r), block(c)])

    @pl.when(jnp.logical_not(top_tile))
    def _():
        def one(s, carry):
            total = dot(lower_hi[...], upper_hi[s])
            total = total + dot(lower_hi[...], upper_lo[s])
            total = total + dot(lower_lo[...], upper_hi[s])
            for half in range(2):
                out_ref[0, at(s, half), :] = (
                    front_ref[0, at(s, half), :] - total[:, half * HALF : half * HALF + HALF]
                )
            return carry

        lax.fori_loop(0, 8, one, 0)

        for shift in range(4):
            slot = (y - shift + 4) % 4
            parent = row_of(map_ref, row, slot)
            for hop in range(4):
                source = (x - hop + 4) % 4
                found, value = col_of(map_ref, slot // 2, source, col)

                @pl.when((parent >= 0) & (parent // 16 == tile) & (found >= 0))
                def _(shift=shift, hop=hop, s=value // 8):
                    for half in range(2):
                        out_ref[0, at(s, half), :] = out_ref[0, at(s, half), :] + parts[hop][
                            shift, :, half * HALF : half * HALF + HALF
                        ].astype(F32)

        @pl.when(col < NPIV)
        def _():
            put(0, col_out[...])


def run_finish(child_map, rc, view, top, own, left, corner, inverse, parts):
    once = pl.Buffered(1)
    whole = lambda a: pl.BlockSpec(
        a.shape, functools.partial(lambda n, t: (0,) * n, a.ndim), pipeline_mode=once
    )
    rows = pl.BlockSpec((1,) + view.shape[1:], lambda t: (t, 0, 0))
    return pl.pallas_call(
        finish,
        grid=(view.shape[0],),
        out_shape=shape(view.shape, F32),
        in_specs=[
            SMEM, SMEM, rows, whole(top), whole(own),
            pl.BlockSpec((NPIV, 1, BS, BS), lambda t: (0, t, 0, 0)),
            whole(corner), whole(inverse), *[whole(p) for p in parts],
        ],
        out_specs=rows,
        scratch_shapes=[
            pltpu.VMEM((8, 4 * BS, BS), BF16),
            pltpu.VMEM((8, 4 * BS, BS), BF16),
            pltpu.VMEM((8, BS, BS), F32),
            pltpu.VMEM((BS, 4 * BS), BF16),
            pltpu.VMEM((BS, 4 * BS), BF16),
            pltpu.VMEM((BS, BS), F32),
        ],
        compiler_params=pltpu.CompilerParams(vmem_limit_bytes=LIMIT),
        cost_estimate=pl.CostEstimate(
            flops=20 * 2**30, bytes_accessed=32 * 2**20, transcendentals=0
        ),
    )(child_map, rc, view, top, own, left, corner, inverse, *parts)


def shards(front, child_update, child_map, pivots):
    row = lax.axis_index("prow")
    col = lax.axis_index("pcol")
    y = row // 4
    rc = jnp.stack([row, col]).astype(jnp.int32)
    tiles = front.shape[0]

    def along_z(a, hop):
        return lax.ppermute(a, "prow", [(4 * i + j, 4 * i + (j + hop) % 4) for i in range(4) for j in range(4)])

    def along_y(a, hop):
        return lax.ppermute(a, "prow", [(4 * i + j, 4 * ((i + hop) % 4) + j) for i in range(4) for j in range(4)])

    def along_x(a, hop):
        return lax.ppermute(a, "pcol", [(2 * i + j, 2 * ((i + hop) % 4) + j) for i in range(4) for j in range(2)])

    def swap(a):
        return lax.ppermute(a, "pcol", [(i, i ^ 1) for i in range(8)])

    def rows_to(a, pairs, turn):
        full = [(8 * s + c, 8 * d + (c ^ turn)) for s, d in pairs for c in range(8)]
        return lax.ppermute(a, ("prow", "pcol"), full)

    edge = jnp.maximum(
        jnp.where(row < NPIV, jnp.max(jnp.abs(front[0])), 0.0),
        jnp.where(col < NPIV, jnp.max(jnp.abs(front[:, :, 0, :])), 0.0),
    )
    reach = lax.pmax(edge, ("prow", "pcol")) + REACH
    up = TOP / reach
    down = reach / TOP

    child = child_update.reshape(2, BS, 2 * BS)
    strip = shape((BS, 2 * BS), BF16)
    square = shape((BS, BS), BF16)
    z0, z1, z2, z3, t1, t2 = call(pick_z, [strip] * 6, [child_map, rc, child])

    a1 = rows_to(t1, [(0, 1), (1, 2)], 0)
    a2 = rows_to(t2, [(0, 2), (1, 3)], 0)
    b0 = rows_to(child[0], [(0, 0)], 1)
    b1 = rows_to(t1, [(0, 1), (1, 2)], 1)
    b2 = rows_to(t2, [(0, 2), (1, 3)], 1)
    tops = call(pick_top, [square] * 4, [child_map, rc, child, a1, a2, b0, b1, b2])

    def top_x(a, hop):
        full = [
            (8 * r + 2 * i + j, 8 * r + 2 * ((i + hop) % 4) + j)
            for r in range(4) for i in range(4) for j in range(2)
        ]
        return lax.ppermute(a, ("prow", "pcol"), full)

    tops = [tops[0]] + [top_x(tops[hop], hop) for hop in (1, 2, 3)]
    view = (
        front.reshape(tiles, BS, 8, 2, HALF).transpose(0, 1, 3, 2, 4).reshape(tiles, BS * 16, HALF)
    )
    order = jnp.where(
        row < NPIV,
        pivots[jnp.minimum(row, NPIV - 1)],
        jnp.arange(BS, dtype=jnp.int32),
    )
    order = jnp.broadcast_to(order.astype(F32)[:, None], (BS, HALF))
    own = pl.pallas_call(
        prepare_top,
        grid=(1,),
        out_shape=shape((4, 8, 64, BS), F32),
        in_specs=[
            SMEM, SMEM,
            pl.BlockSpec((None, BS * 16, HALF), lambda t: (0, 0, 0)),
            pl.BlockSpec((BS, HALF), lambda t: (0, 0)),
            *[pl.BlockSpec((BS, BS), lambda t: (0, 0))] * 4,
        ],
        out_specs=pl.BlockSpec((4, 8, 64, BS), lambda t: (0, 0, 0, 0)),
        scratch_shapes=[pltpu.VMEM((8, BS, BS), F32)],
        compiler_params=pltpu.CompilerParams(vmem_limit_bytes=LIMIT),
        cost_estimate=pl.CostEstimate(flops=2**30, bytes_accessed=4 * 2**20, transcendentals=0),
    )(child_map, rc, view, order, *tops)

    corner = own[:, 0].reshape(BS, BS)
    far = lax.ppermute(
        corner[HALF:], ("prow", "pcol"), [(8 * r + c, 8 * r + c + 4) for r in range(4) for c in range(4)]
    )
    part = jnp.where(col < NPIV, corner[:HALF], far)

    def from_plane(pieces):
        result = pieces[0]
        for hop in (1, 2, 3):
            moved = lax.ppermute(pieces[hop], "prow", [(j, 4 * hop + j) for j in range(4)])
            result = jnp.where(y == hop, moved, result)
        return result

    part = from_plane([part[32 * i : 32 * i + 32] for i in range(4)])
    gathered = lax.all_gather(part, ("prow", "pcol"), axis=0, tiled=False)
    corner, inverse = call(
        factor_corner,
        [shape((4 * BS, 4 * BS), F32), shape((NPIV, BS, BS), F32)],
        [gathered.reshape(128, 32, BS)],
        flops=2**32,
    )

    coded = (own * up).astype(F16)
    piece = from_plane([coded[i] for i in range(4)])
    top = lax.all_gather(piece, "prow", axis=0, tiled=False).astype(F32) * down

    zs = [z0] + [along_z(a, hop) for a, hop in ((z1, 1), (z2, 2), (z3, 3))]
    ys = call(pick_y, [strip] * 4, [child_map, rc, *zs])
    ys = [ys[0]] + [along_y(ys[hop], hop) for hop in (1, 2, 3)]

    pair = shape((2, BS, BS), BF16)
    l1, l2 = call(pick_left, [pair] * 2, [child_map, rc, *ys])

    def cols_to(a, pairs):
        return lax.ppermute(a, "pcol", pairs)

    l1 = cols_to(l1, [(0, 1), (1, 2)])
    l2 = cols_to(l2, [(0, 2), (1, 3)])
    (left,) = call(
        prepare_left,
        [shape((tiles, BS, BS), F32)],
        [child_map, rc, front[:, :, 0, :], own, *ys, l1, l2],
    )
    coded = (left * up).astype(F16)
    half = cols_to(coded[2:], [(c, c + 4) for c in range(4)])
    half = jnp.where(col < NPIV, coded[:2], half)
    left = lax.all_gather(half, "pcol", axis=0, tiled=False).astype(F32) * down
    left = left.reshape(2, 4, 2, BS, BS).transpose(1, 0, 2, 3, 4).reshape(4, 4, BS, BS)

    others = [swap(a) for a in ys]
    xs = call(pick_x, [shape((4, BS, BS), BF16)] * 4, [child_map, rc, *ys, *others])
    xs = [xs[0]] + [along_x(xs[hop], hop) for hop in (1, 2, 3)]

    done = run_finish(child_map, rc, view, top, own, left, corner, inverse, xs)
    done = done.reshape(tiles, BS, 2, 8, HALF).transpose(0, 1, 3, 2, 4)
    return done.reshape(front.shape)


def solution(mesh):
    return jax.shard_map(
        shards,
        mesh=mesh,
        in_specs=(P(None, "prow", None, "pcol"), P("prow", "pcol"), P(), P()),
        out_specs=P(None, "prow", None, "pcol"),
        check_vma=False,
    )
```

```python
import functools

import jax
import jax.numpy as jnp
from jax import lax
from jax.experimental import pallas as pl
from jax.experimental.pallas import tpu as pltpu
from jax.sharding import PartitionSpec as P

NPIV = 4
NS = 2
BS = 256
HALF = 128
PIECE = 64
FULL = 32767.0
HIGHEST = lax.Precision.HIGHEST
F32 = jnp.float32
BF16 = jnp.bfloat16
I16 = jnp.int16
I32 = jnp.int32
SMEM = pl.BlockSpec(memory_space=pltpu.SMEM)
VMEM = pl.BlockSpec(memory_space=pltpu.VMEM)
LIMIT = 56 * 1024 * 1024


def shape(dims, kind):
    return jax.ShapeDtypeStruct(dims, kind)


def call(body, outs, ins, smem=2, flops=0, scratch=()):
    moved = sum(a.size * a.dtype.itemsize for a in ins)
    moved += sum(o.size * o.dtype.itemsize for o in outs)
    return pl.pallas_call(
        body,
        out_shape=outs,
        in_specs=[SMEM] * smem + [VMEM] * (len(ins) - smem),
        out_specs=[VMEM] * len(outs),
        scratch_shapes=list(scratch),
        compiler_params=pltpu.CompilerParams(vmem_limit_bytes=LIMIT),
        cost_estimate=pl.CostEstimate(flops=flops, bytes_accessed=moved, transcendentals=0),
    )(*ins)


def spot(map_ref, child, low, count, test):
    found = jnp.int32(-1)
    value = jnp.int32(-1)
    for step in range(count):
        entry = map_ref[child, low + step]
        hit = test(entry)
        found = jnp.where(hit, low + step, found)
        value = jnp.where(hit, entry, value)
    return found, value


def row_of(map_ref, row, slot):
    return spot(map_ref, slot // 2, 8 * (slot % 2), 8, lambda entry: entry % 16 == row)[1]


def col_of(map_ref, child, source, col):
    return spot(map_ref, child, 4 * source, 4, lambda entry: entry % 8 == col)


def split(value):
    high = value.astype(BF16)
    low = (value - high.astype(F32)).astype(BF16)
    return high, low


def dot(left, right):
    return jnp.dot(left, right, preferred_element_type=F32)


def dot3(left, right):
    (a, b), (c, d) = left, right
    return dot(a, c) + (dot(a, d) + dot(b, c))


def high_dot(left, right):
    return jnp.dot(left, right, precision=HIGHEST, preferred_element_type=F32)


def block(step):
    return slice(step * BS, step * BS + BS)


def one_hot(order):
    spread = lax.broadcasted_iota(I32, (BS, BS), 1).astype(F32)
    return jnp.where(order[:, :1] == spread, 1.0, 0.0).astype(BF16)


def reorder(select, value):
    high = value.astype(BF16)
    rest = value - high.astype(F32)
    middle = rest.astype(BF16)
    last = (rest - middle.astype(F32)).astype(BF16)
    return (dot(select, high) + dot(select, middle)) + dot(select, last)


def level(peak):
    return jnp.ceil(jnp.log2(jnp.full((8, HALF), jnp.maximum(peak, 1e-30))) * 4.0)


def encode(value, n):
    scaled = jnp.abs(value) * jnp.exp2(n * -0.25)[:1, :1]
    code = jnp.minimum(jnp.floor(jnp.sqrt(scaled) * FULL + 0.5), FULL)
    return jnp.where(value < 0.0, -code, code).astype(I32)


def decode(code, n):
    code = code.astype(F32)
    return code * jnp.abs(code) * (jnp.exp2(n.astype(F32)[:1, :1] * 0.25) * (1.0 / (FULL * FULL)))


def cut_front(front_ref, order_ref, *outs):
    select = one_hot(order_ref[...])

    def one(tile, carry):
        halves = [front_ref[pl.ds(half * 8 + tile, BS, stride=16), :] for half in range(2)]
        turned = reorder(select, jnp.concatenate(halves, axis=1))
        for piece in range(4):
            outs[piece][tile] = turned[piece * PIECE : piece * PIECE + PIECE]
        return carry

    lax.fori_loop(0, 8, one, 0)


def pick_rows(map_ref, rc_ref, order_ref, held, *outs):
    pieces, hops = outs[:4], outs[4:]
    row = rc_ref[0]
    y, z = row // 4, row % 4
    found, value = spot(map_ref, 0, 0, 4, lambda entry: entry == row)
    live = (found >= 0) & (row < NPIV)
    at = jnp.maximum(found, 0)

    @pl.when(live)
    def _():
        turned = dot(one_hot(order_ref[...]), held[at // 2, at % 2]).astype(BF16)
        for piece in range(4):
            pieces[piece][...] = turned[piece * PIECE : piece * PIECE + PIECE]

    @pl.when(jnp.logical_not(live))
    def _():
        for piece in range(4):
            pieces[piece][...] = jnp.zeros((PIECE, 2 * BS), BF16)

    low = 8 * (y % 2)
    for shift in range(4):
        goal = 4 * ((y + shift) % 4) + z
        index, value = spot(map_ref, y // 2, low, 8, lambda entry: entry % 16 == goal)
        index = jnp.maximum(index - low, 0)
        hops[shift][...] = held[index // 2, index % 2]


def assemble(map_ref, rc_ref, f0, f1, f2, f3, strip, code_ref, corner_ref, work):
    row, col = rc_ref[0], rc_ref[1]
    y = row // 4
    for piece, source in enumerate((f0, f1, f2, f3)):

        @pl.when(y == piece)
        def _(source=source):
            work[...] = source[...]

    for index in range(16):
        parent = map_ref[0, index]
        cut = slice((index % 2) * BS, (index % 2) * BS + BS)

        @pl.when(parent % 8 == col)
        def _(index=index, cut=cut, tile=parent // 8):
            work[tile] = work[tile] + strip[index // 2, :, cut].astype(F32)

    corner_ref[...] = work[0]

    @pl.when(col < NPIV)
    def _():
        work[0] = jnp.zeros((PIECE, BS), F32)

    n = level(jnp.max(jnp.abs(work[...])))
    for tile in range(8):
        code_ref[tile * PIECE : tile * PIECE + PIECE] = encode(work[tile], n).astype(I16)
    code_ref[8 * PIECE :] = jnp.broadcast_to(n[:1, :1].astype(I32), (16, BS)).astype(I16)


def pick_left(map_ref, rc_ref, *refs):
    held, one, two = refs[:4], refs[4], refs[5]
    row, col = rc_ref[0], rc_ref[1]
    y = row // 4
    at_one = jnp.where(col == 0, 1, 0)
    at_two = jnp.where((col == 1) & (map_ref[0, 2] == 3), 0, 1)
    for shift in range(4):
        slot = (y - shift + 4) % 4
        for out, at in ((one, at_one), (two, at_two)):
            for half in range(2):

                @pl.when((slot < 2) & (at == half))
                def _(shift=shift, out=out, half=half, slot=slot):
                    out[slot] = held[shift][:, half * BS : half * BS + BS]


def prepare_left(map_ref, rc_ref, left_ref, *refs):
    held, one, two, near, far, work = refs[:4], refs[4], refs[5], refs[6], refs[7], refs[8]
    row, col = rc_ref[0], rc_ref[1]
    y = row // 4
    work[...] = left_ref[...]
    found, value = spot(map_ref, 0, 0, 4, lambda entry: entry == col)
    second_first = map_ref[0, 2] == 2
    use_one = (found >= 0) & ((col == 1) | ((col == 2) & second_first))
    use_two = (found >= 0) & ((col == 3) | ((col == 2) & jnp.logical_not(second_first)))
    for shift in range(4):
        slot = (y - shift + 4) % 4
        parent = row_of(map_ref, row, slot)
        tile = parent // 16
        good = (slot < 2) & (parent >= 0)

        @pl.when(good & (col == 0))
        def _(shift=shift, tile=tile):
            work[tile] = work[tile] + held[shift][:, :BS].astype(F32)

        for use, part in ((use_one, one), (use_two, two)):

            @pl.when(good & use)
            def _(part=part, slot=slot, tile=tile):
                work[tile] = work[tile] + part[slot].astype(F32)

    @pl.when(row < NPIV)
    def _():
        work[0] = jnp.zeros((BS, BS), F32)

    n = level(jnp.max(jnp.abs(work[...])))
    for out, first in ((near, 0), (far, 1)):
        out[:BS] = encode(work[first], n) * 65536 + (encode(work[first + 2], n) & 65535)
        out[BS:] = jnp.broadcast_to(n[:1, :1].astype(I32), (8, BS))


def pick_x(map_ref, rc_ref, *refs):
    mine, other, outs = refs[:4], refs[4:8], refs[8:]
    row, col = rc_ref[0], rc_ref[1]
    y, x, core = row // 4, col // 2, col % 2
    for shift in range(4):
        child = ((y - shift + 4) % 4) // 2
        for hop in range(4):
            goal = 2 * ((x + hop) % 4) + core
            found, value = col_of(map_ref, child, x, goal)
            part = found % 4
            for half in range(2):
                cut = slice(half * BS, half * BS + BS)

                @pl.when((found >= 0) & (part == 2 * core + half))
                def _(shift=shift, hop=hop, cut=cut):
                    outs[hop][shift] = mine[shift][:, cut]

                @pl.when((found >= 0) & (part == 2 * (1 - core) + half))
                def _(shift=shift, hop=hop, cut=cut):
                    outs[hop][shift] = other[shift][:, cut]


def factor_corner(gathered, out_ref, inverse_ref):
    for h in range(2):
        for k in range(4):
            for y in range(4):
                for z in range(4):
                    low = z * BS + y * PIECE + h * 32
                    out_ref[low : low + 32, block(k)] = gathered[4 * h + k, 4 * y + z]
    diagonal = lax.broadcasted_iota(I32, (BS, BS), 0) == lax.broadcasted_iota(I32, (BS, BS), 1)
    for k in range(NPIV):
        pivot = out_ref[block(k), block(k)]
        on_line = jnp.where(diagonal, pivot, 0.0)
        across = jnp.sum(on_line, axis=0, keepdims=True)
        down = jnp.sum(on_line, axis=1, keepdims=True)
        across = across / (across * across + 1.0)
        down = down / (down * down + 1.0)
        approx = 2.0 * jnp.where(diagonal, across, 0.0) - (down * pivot) * across
        for sweep_index in range(NS - 1):
            approx = 2.0 * approx - high_dot(high_dot(approx, pivot), approx)
        inverse_ref[k] = approx
        if k + 1 < NPIV:
            below = slice((k + 1) * BS, NPIV * BS)
            lower = dot3(split(out_ref[below, block(k)]), split(approx))
            out_ref[below, block(k)] = lower
            out_ref[below, below] = out_ref[below, below] - dot3(
                split(lower), split(out_ref[block(k), below])
            )


def upper_rows(rc_ref, corner_ref, code_ref, high_ref, low_ref, taken_ref):
    row, col = rc_ref[0], rc_ref[1]
    high_parts = {}

    def one(tile, carry):
        uppers = []
        mine = jnp.zeros((BS, BS), F32)
        low = pl.multiple_of(tile * PIECE, PIECE)
        for k in range(NPIV):
            raw = jnp.concatenate(
                [
                    decode(
                        code_ref[4 * piece + k, pl.ds(low, PIECE), :].astype(I32),
                        code_ref[4 * piece + k, 8 * PIECE :, :].astype(I32),
                    )
                    for piece in range(4)
                ],
                axis=0,
            )
            taken = jnp.zeros((BS, BS), F32)
            for m in range(k):
                taken = taken + dot3(split(corner_ref[block(k), block(m)]), uppers[m])
            mine = jnp.where(row == k, taken, mine)
            uppers.append(split(raw - taken))
            high_ref[tile, block(k)] = uppers[k][0]
            low_ref[tile, block(k)] = uppers[k][1]
        taken_ref[tile] = mine
        return carry

    lax.fori_loop(0, 8, one, 0)


def lower_cols(rc_ref, corner_ref, inverse_ref, code_ref, high_ref, low_ref, own_ref):
    row, col = rc_ref[0], rc_ref[1]
    lowers = []
    kept = jnp.zeros((4 * BS, BS), F32)
    for k in range(NPIV):
        tiles = []
        for tile in range(4):
            word = code_ref[4 * (tile % 2) + k, :BS]
            if tile >= 2:
                word = lax.shift_left(word, 16)
            tiles.append(
                decode(lax.shift_right_arithmetic(word, 16), code_ref[4 * (tile % 2) + k, BS:])
            )
        value = jnp.concatenate(tiles, axis=0)
        for m in range(k):
            value = value - dot3(lowers[m], split(corner_ref[block(m), block(k)]))
        lower = dot3(split(value), split(inverse_ref[k]))
        kept = jnp.where(col == k, lower, kept)
        lowers.append(split(lower))
        high_ref[:, block(k)] = lowers[k][0]
        low_ref[:, block(k)] = lowers[k][1]
    own_ref[...] = kept


SPAN = 2


def finish(
    map_ref, rc_ref, front_ref, high_ref, low_ref, left_high, left_low, own_ref, taken_ref,
    corner_ref, order_ref, p0, p1, p2, p3, out_ref,
):
    parts = (p0, p1, p2, p3)
    step = pl.program_id(0)
    row, col = rc_ref[0], rc_ref[1]
    y, x = row // 4, col // 2

    def at(s, half, tile=0, count=1):
        return pl.ds(tile * BS * 16 + half * 8 + s, count * BS, stride=16)

    def put(s, tile, value):
        for half in range(2):
            out_ref[at(s, half, tile), :] = value[:, half * HALF : half * HALF + HALF]

    def one(s, carry):
        total = dot(left_high[...], high_ref[s])
        total = total + dot(left_high[...], low_ref[s])
        total = total + dot(left_low[...], high_ref[s])
        for half in range(2):
            rows = at(s, half, 0, SPAN)
            out_ref[rows, :] = front_ref[rows, :] - total[:, half * HALF : half * HALF + HALF]
        return carry

    lax.fori_loop(0, 8, one, 0)

    for shift in range(4):
        slot = (y - shift + 4) % 4
        parent = row_of(map_ref, row, slot)
        for hop in range(4):
            source = (x - hop + 4) % 4
            found, value = col_of(map_ref, slot // 2, source, col)
            for tile in range(SPAN):

                @pl.when((parent >= 0) & (parent // 16 == SPAN * step + tile) & (found >= 0))
                def _(shift=shift, hop=hop, tile=tile, s=value // 8):
                    for half in range(2):
                        rows = at(s, half, tile)
                        lanes = slice(half * HALF, half * HALF + HALF)
                        out_ref[rows, :] = out_ref[rows, :] + parts[hop][shift, :, lanes].astype(F32)

    @pl.when(col < NPIV)
    def _():
        for tile in range(SPAN):
            put(0, tile, own_ref[tile * BS : tile * BS + BS])

    @pl.when((step == 0) & (row < NPIV))
    def _():
        select = one_hot(order_ref[...])

        def turn(s, carry):
            value = jnp.concatenate([out_ref[at(s, half), :] for half in range(2)], axis=1)
            put(s, 0, reorder(select, value) - taken_ref[s])
            return carry

        lax.fori_loop(0, 8, turn, 0)

        for r in range(NPIV):
            for c in range(NPIV):

                @pl.when((row == r) & (col == c))
                def _(r=r, c=c):
                    put(0, 0, corner_ref[block(r), block(c)])


def run_finish(child_map, rc, view, upper, lower, own, taken, corner, order, parts):
    once = pl.Buffered(1)
    whole = lambda a: pl.BlockSpec(
        a.shape, functools.partial(lambda n, t: (0,) * n, a.ndim), pipeline_mode=once
    )
    rows = pl.BlockSpec((SPAN * BS * 16, HALF), lambda t: (t, 0))
    lefts = pl.BlockSpec((SPAN * BS, 4 * BS), lambda t: (t, 0))
    return pl.pallas_call(
        finish,
        grid=(4 // SPAN,),
        out_shape=shape(view.shape, F32),
        in_specs=[
            SMEM, SMEM, rows, whole(upper[0]), whole(upper[1]), lefts, lefts,
            pl.BlockSpec((SPAN * BS, BS), lambda t: (t, 0)),
            whole(taken), whole(corner), whole(order), *[whole(p) for p in parts],
        ],
        out_specs=rows,
        compiler_params=pltpu.CompilerParams(vmem_limit_bytes=LIMIT),
        cost_estimate=pl.CostEstimate(
            flops=13 * 2**30, bytes_accessed=32 * 2**20, transcendentals=0
        ),
    )(child_map, rc, view, *upper, *lower, own, taken, corner, order, *parts)


def shards(front, child_update, child_map, pivots):
    row = lax.axis_index("prow")
    col = lax.axis_index("pcol")
    y = row // 4
    rc = jnp.stack([row, col]).astype(I32)
    tiles = front.shape[0]
    planes = [[4 * i + j for j in range(4)] for i in range(4)]

    def along_y(a, hop):
        return lax.ppermute(
            a, "prow", [(4 * i + j, 4 * ((i + hop) % 4) + j) for i in range(4) for j in range(4)]
        )

    def along_x(a, hop):
        return lax.ppermute(
            a, "pcol", [(2 * i + j, 2 * ((i + hop) % 4) + j) for i in range(4) for j in range(2)]
        )

    def from_plane(a, hop):
        return lax.ppermute(a, "prow", [(j, 4 * hop + j) for j in range(4)])

    def cols_to(a, pairs):
        return lax.ppermute(a, "pcol", pairs)

    held = lax.all_gather(child_update, "prow", axis=0, tiled=False, axis_index_groups=planes)
    held = held.reshape(4, 2, BS, 2 * BS)

    order = jnp.where(
        row < NPIV, pivots[jnp.minimum(row, NPIV - 1)], jnp.arange(BS, dtype=I32)
    )
    order = jnp.broadcast_to(order.astype(F32)[:, None], (BS, HALF))
    view = front.reshape(tiles, BS, 8, 2, HALF).transpose(0, 1, 3, 2, 4)
    view = view.reshape(tiles * BS * 16, HALF)

    cuts = pl.pallas_call(
        cut_front,
        grid=(1,),
        out_shape=[shape((8, PIECE, BS), F32)] * 4,
        in_specs=[
            pl.BlockSpec((BS * 16, HALF), lambda t: (0, 0)),
            pl.BlockSpec((BS, HALF), lambda t: (0, 0)),
        ],
        out_specs=[pl.BlockSpec((8, PIECE, BS), lambda t: (0, 0, 0))] * 4,
        compiler_params=pltpu.CompilerParams(vmem_limit_bytes=LIMIT),
        cost_estimate=pl.CostEstimate(flops=2**30, bytes_accessed=4 * 2**20, transcendentals=0),
    )(view, order)
    cuts = [cuts[0]] + [from_plane(cuts[hop], hop) for hop in (1, 2, 3)]

    strip = shape((BS, 2 * BS), BF16)
    thin = shape((PIECE, 2 * BS), BF16)
    picked = call(pick_rows, [thin] * 4 + [strip] * 4, [child_map, rc, order, held])
    thin = picked[0]
    for hop in (1, 2, 3):
        thin = jnp.where(y == hop, from_plane(picked[hop], hop), thin)
    thin = lax.all_gather(thin, "pcol", axis=0, tiled=False)
    ys = [picked[4]] + [along_y(picked[4 + hop], hop) for hop in (1, 2, 3)]

    code, piece = call(
        assemble,
        [shape((8 * PIECE + 16, BS), I16), shape((PIECE, BS), F32)],
        [child_map, rc, *cuts, thin],
        scratch=[pltpu.VMEM((8, PIECE, BS), F32)],
    )

    far = lax.ppermute(
        piece[32:], "pcol", [(c, c + 4) for c in range(4)]
    )
    piece = jnp.where(col < NPIV, piece[:32], far)
    corner = lax.all_gather(piece, "prow", axis=0, tiled=False)
    corner = lax.all_gather(corner, "pcol", axis=0, tiled=False)

    pair = shape((2, BS, BS), BF16)
    l1, l2 = call(pick_left, [pair] * 2, [child_map, rc, *ys])
    l1 = cols_to(l1, [(0, 1), (1, 2)])
    l2 = cols_to(l2, [(0, 2), (1, 3)])
    near, far = call(
        prepare_left,
        [shape((BS + 8, BS), I32)] * 2,
        [child_map, rc, front[:, :, 0, :], *ys, l1, l2],
        scratch=[pltpu.VMEM((tiles, BS, BS), F32)],
    )
    far = cols_to(far, [(c, c + 4) for c in range(4)])
    left = lax.all_gather(jnp.where(col < NPIV, near, far), "pcol", axis=0, tiled=False)

    others = cols_to(jnp.stack(ys), [(i, i ^ 1) for i in range(8)])
    xs = call(
        pick_x, [shape((4, BS, BS), BF16)] * 4, [child_map, rc, *ys, *[others[i] for i in range(4)]]
    )
    xs = [xs[0]] + [along_x(xs[hop], hop) for hop in (1, 2, 3)]

    top = lax.all_gather(code, "prow", axis=0, tiled=False)

    corner, inverse = call(
        factor_corner,
        [shape((4 * BS, 4 * BS), F32), shape((NPIV, BS, BS), F32)],
        [corner],
        smem=0,
        flops=2**32,
    )
    *upper, taken = call(
        upper_rows,
        [shape((8, 4 * BS, BS), BF16)] * 2 + [shape((8, BS, BS), F32)],
        [rc, corner, top],
        smem=1,
        flops=5 * 2**30,
    )
    *lower, own = call(
        lower_cols,
        [shape((4 * BS, 4 * BS), BF16)] * 2 + [shape((4 * BS, BS), F32)],
        [rc, corner, inverse, left],
        smem=1,
        flops=4 * 2**30,
    )
    done = run_finish(child_map, rc, view, upper, lower, own, taken, corner, order, xs)
    done = done.reshape(tiles, BS, 2, 8, HALF).transpose(0, 1, 3, 2, 4)
    return done.reshape(front.shape)


def solution(mesh):
    return jax.shard_map(
        shards,
        mesh=mesh,
        in_specs=(P(None, "prow", None, "pcol"), P("prow", "pcol"), P(), P()),
        out_specs=P(None, "prow", None, "pcol"),
        check_vma=False,
    )
```

```python
import functools

import jax
import jax.numpy as jnp
from jax import lax
from jax.experimental import pallas as pl
from jax.experimental.pallas import tpu as pltpu
from jax.sharding import PartitionSpec as P

NPIV = 4
NS = 2
BS = 256
HALF = 128
PIECE = 64
FULL = 32767.0
HIGHEST = lax.Precision.HIGHEST
F32 = jnp.float32
BF16 = jnp.bfloat16
I16 = jnp.int16
I32 = jnp.int32
SMEM = pl.BlockSpec(memory_space=pltpu.SMEM)
VMEM = pl.BlockSpec(memory_space=pltpu.VMEM)
LIMIT = 56 * 1024 * 1024


def shape(dims, kind):
    return jax.ShapeDtypeStruct(dims, kind)


def call(body, outs, ins, smem=2, flops=0, scratch=()):
    moved = sum(a.size * a.dtype.itemsize for a in ins)
    moved += sum(o.size * o.dtype.itemsize for o in outs)
    return pl.pallas_call(
        body,
        out_shape=outs,
        in_specs=[SMEM] * smem + [VMEM] * (len(ins) - smem),
        out_specs=[VMEM] * len(outs),
        scratch_shapes=list(scratch),
        compiler_params=pltpu.CompilerParams(vmem_limit_bytes=LIMIT),
        cost_estimate=pl.CostEstimate(flops=flops, bytes_accessed=moved, transcendentals=0),
    )(*ins)


def spot(map_ref, child, low, count, test):
    found = jnp.int32(-1)
    value = jnp.int32(-1)
    for step in range(count):
        entry = map_ref[child, low + step]
        hit = test(entry)
        found = jnp.where(hit, low + step, found)
        value = jnp.where(hit, entry, value)
    return found, value


def row_of(map_ref, row, slot):
    return spot(map_ref, slot // 2, 8 * (slot % 2), 8, lambda entry: entry % 16 == row)[1]


def col_of(map_ref, child, source, col):
    return spot(map_ref, child, 4 * source, 4, lambda entry: entry % 8 == col)


def split(value):
    high = value.astype(BF16)
    low = (value - high.astype(F32)).astype(BF16)
    return high, low


def dot(left, right):
    return jnp.dot(left, right, preferred_element_type=F32)


def dot3(left, right):
    (a, b), (c, d) = left, right
    return dot(a, c) + (dot(a, d) + dot(b, c))


def high_dot(left, right):
    return jnp.dot(left, right, precision=HIGHEST, preferred_element_type=F32)


def block(step):
    return slice(step * BS, step * BS + BS)


def one_hot(order):
    spread = lax.broadcasted_iota(I32, (BS, BS), 1).astype(F32)
    return jnp.where(order[:, :1] == spread, 1.0, 0.0).astype(BF16)


def reorder(select, value):
    high = value.astype(BF16)
    rest = value - high.astype(F32)
    middle = rest.astype(BF16)
    last = (rest - middle.astype(F32)).astype(BF16)
    return (dot(select, high) + dot(select, middle)) + dot(select, last)


def level(peak):
    return jnp.ceil(jnp.log2(jnp.full((8, HALF), jnp.maximum(peak, 1e-30))) * 4.0)


def encode(value, n):
    scaled = jnp.abs(value) * jnp.exp2(n * -0.25)[:1, :1]
    code = jnp.minimum(jnp.floor(jnp.sqrt(scaled) * FULL + 0.5), FULL)
    return jnp.where(value < 0.0, -code, code).astype(I32)


def decode(code, n):
    code = code.astype(F32)
    return code * jnp.abs(code) * (jnp.exp2(n.astype(F32)[:1, :1] * 0.25) * (1.0 / (FULL * FULL)))


def cut_front(front_ref, order_ref, *outs):
    select = one_hot(order_ref[...])

    def one(tile, carry):
        halves = [front_ref[pl.ds(half * 8 + tile, BS, stride=16), :] for half in range(2)]
        turned = reorder(select, jnp.concatenate(halves, axis=1))
        for piece in range(4):
            outs[piece][tile] = turned[piece * PIECE : piece * PIECE + PIECE]
        return carry

    lax.fori_loop(0, 8, one, 0)


def pick_z(map_ref, rc_ref, child_ref, *outs):
    row = rc_ref[0]
    z = row % 4
    second_at = map_ref[row // 8, 2 * (row % 8) + 1] % 4
    for hop in range(4):
        outs[hop][...] = child_ref[jnp.where(second_at == (z + hop) % 4, 1, 0)]


def pick_rows(map_ref, rc_ref, order_ref, *refs):
    held, pieces, hops = refs[:4], refs[4:8], refs[8:]
    row = rc_ref[0]
    y, z = row // 4, row % 4
    found, value = spot(map_ref, 0, 0, 4, lambda entry: entry == row)
    live = (found >= 0) & (row < NPIV)
    for hop in range(4):

        @pl.when(live & (found // 2 == (z - hop + 4) % 4))
        def _(hop=hop):
            turned = dot(one_hot(order_ref[...]), held[hop][...]).astype(BF16)
            for piece in range(4):
                pieces[piece][...] = turned[piece * PIECE : piece * PIECE + PIECE]

    @pl.when(jnp.logical_not(live))
    def _():
        for piece in range(4):
            pieces[piece][...] = jnp.zeros((PIECE, 2 * BS), BF16)

    for hop in range(4):
        first = 2 * ((4 * y + (z - hop + 4) % 4) % 8)
        index, value = spot(map_ref, y // 2, first, 2, lambda entry: entry % 4 == z)
        for shift in range(4):

            @pl.when((index >= 0) & ((value // 4) % 4 == (y + shift) % 4))
            def _(hop=hop, shift=shift):
                hops[shift][...] = held[hop][...]


def assemble(map_ref, rc_ref, f0, f1, f2, f3, far_ref, strip, code_ref, corner_ref, work):
    row, col = rc_ref[0], rc_ref[1]
    y = row // 4
    for piece, source in enumerate((f0, f1, f2, f3)):

        @pl.when(y == piece)
        def _(source=source):
            work[...] = source[...]

    for index in range(16):
        parent = map_ref[0, index]
        cut = slice((index % 2) * BS, (index % 2) * BS + BS)

        @pl.when(parent % 8 == col)
        def _(index=index, cut=cut, tile=parent // 8):
            work[tile] = work[tile] + strip[index // 2, :, cut].astype(F32)

    @pl.when(col < NPIV)
    def _():
        corner_ref[...] = work[0, :32]
        work[0] = jnp.zeros((PIECE, BS), F32)

    @pl.when(col >= NPIV)
    def _():
        corner_ref[...] = far_ref[...]

    for index in range(4):
        cut = slice((index % 2) * BS, (index % 2) * BS + BS)

        @pl.when((col >= NPIV) & (map_ref[0, index] == col - NPIV))
        def _(index=index, cut=cut):
            corner_ref[...] = corner_ref[...] + strip[index // 2, 32:, cut].astype(F32)

    n = level(jnp.max(jnp.abs(work[...])))
    for tile in range(8):
        code_ref[tile * PIECE : tile * PIECE + PIECE] = encode(work[tile], n).astype(I16)
    code_ref[8 * PIECE :] = jnp.broadcast_to(n[:1, :1].astype(I32), (16, BS)).astype(I16)


def pick_left(map_ref, rc_ref, h0, h1, h2, h3, out_ref):
    y = rc_ref[0] // 4
    for shift, source in enumerate((h0, h1, h2, h3)):
        slot = (y - shift + 4) % 4

        @pl.when(slot < 2)
        def _(source=source, slot=slot):
            out_ref[slot] = source[...]


def pick_x(map_ref, rc_ref, *refs):
    mine, other, outs = refs[:4], refs[4:8], refs[8:]
    row, col = rc_ref[0], rc_ref[1]
    y, x, core = row // 4, col // 2, col % 2
    for shift in range(4):
        child = ((y - shift + 4) % 4) // 2
        for hop in range(4):
            goal = 2 * ((x + hop) % 4) + core
            found, value = col_of(map_ref, child, x, goal)
            part = found % 4
            for half in range(2):
                cut = slice(half * BS, half * BS + BS)

                @pl.when((found >= 0) & (part == 2 * core + half))
                def _(shift=shift, hop=hop, cut=cut):
                    outs[hop][shift] = mine[shift][:, cut]

                @pl.when((found >= 0) & (part == 2 * (1 - core) + half))
                def _(shift=shift, hop=hop, cut=cut):
                    outs[hop][shift] = other[shift][:, cut]


def factor_corner(gathered, work, inverse_ref):
    for h in range(2):
        for k in range(4):
            for y in range(4):
                for z in range(4):
                    low = z * BS + y * PIECE + h * 32
                    work[low : low + 32, block(k)] = gathered[4 * h + k, y, z]
    diagonal = lax.broadcasted_iota(I32, (BS, BS), 0) == lax.broadcasted_iota(I32, (BS, BS), 1)
    for k in range(NPIV):
        pivot = work[block(k), block(k)]
        on_line = jnp.where(diagonal, pivot, 0.0)
        across = jnp.sum(on_line, axis=0, keepdims=True)
        down = jnp.sum(on_line, axis=1, keepdims=True)
        across = across / (across * across + 1.0)
        down = down / (down * down + 1.0)
        approx = 2.0 * jnp.where(diagonal, across, 0.0) - (down * pivot) * across
        for sweep_index in range(NS - 1):
            approx = 2.0 * approx - high_dot(high_dot(approx, pivot), approx)
        inverse_ref[k] = approx
        if k + 1 < NPIV:
            below = slice((k + 1) * BS, NPIV * BS)
            lower = dot3(split(work[below, block(k)]), split(approx))
            work[below, block(k)] = lower
            work[below, below] = work[below, below] - dot3(
                split(lower), split(work[block(k), below])
            )


def panels(
    map_ref, rc_ref, gathered, code_ref, level_ref, front_ref, near_ref, far_ref,
    high_ref, low_ref, taken_ref, left_high, left_low, own_ref, block_ref,
    work, inverse, chi, clo, xhi, xlo, left,
):
    step = pl.program_id(0)
    row, col = rc_ref[0], rc_ref[1]
    core = col % 2

    @pl.when(step == 0)
    def _():
        factor_corner(gathered, work, inverse)
        for k in range(NPIV):
            chi[block(k)], clo[block(k)] = split(work[block(k)])
            xhi[k], xlo[k] = split(inverse[k])
        for r in range(NPIV):
            for c in range(NPIV):

                @pl.when((row == r) & (col == c))
                def _(r=r, c=c):
                    block_ref[...] = work[block(r), block(c)]

    mine = jnp.zeros((BS, BS), F32)
    for k in range(NPIV):
        raw = jnp.concatenate(
            [
                decode(code_ref[4 * piece + k].astype(I32), level_ref[4 * piece + k].astype(I32))
                for piece in range(4)
            ],
            axis=0,
        )
        if k:
            done = slice(0, k * BS)
            taken = dot3(
                (chi[block(k), done], clo[block(k), done]), (high_ref[0, done], low_ref[0, done])
            )
            mine = jnp.where(row == k, taken, mine)
            raw = raw - taken
        high_ref[0, block(k)], low_ref[0, block(k)] = split(raw)
    taken_ref[0] = mine

    @pl.when(step % 2 == 1)
    def _():
        tile = step // 2
        left[...] = front_ref[...]
        for slot in range(2):
            parent = row_of(map_ref, row, slot)
            for index in range(4):
                target = map_ref[0, index]
                good = (parent >= 0) & (parent // 16 == tile) & (target < NPIV)
                cut = slice((index % 2) * BS, (index % 2) * BS + BS)

                @pl.when(good & (core == index // 2))
                def _(slot=slot, cut=cut, target=target):
                    left[target] = left[target] + near_ref[slot, :, cut].astype(F32)

                @pl.when(good & (core != index // 2))
                def _(slot=slot, cut=cut, target=target):
                    left[target] = left[target] + far_ref[slot, :, cut].astype(F32)

        @pl.when((tile == 0) & (row < NPIV))
        def _():
            left[...] = jnp.zeros((NPIV, BS, BS), F32)

        kept = jnp.zeros((BS, BS), F32)
        for k in range(NPIV):
            value = left[k]
            if k:
                done = slice(0, k * BS)
                value = value - dot3(
                    (left_high[:, done], left_low[:, done]), (chi[done, block(k)], clo[done, block(k)])
                )
            lower = dot3(split(value), (xhi[k], xlo[k]))
            kept = jnp.where(col == k, lower, kept)
            left_high[:, block(k)], left_low[:, block(k)] = split(lower)
        own_ref[...] = kept


def run_panels(child_map, rc, gathered, top, front_left, near, far):
    once = pl.Buffered(1)
    whole = lambda a: pl.BlockSpec(
        a.shape, functools.partial(lambda n, s: (0,) * n, a.ndim), pipeline_mode=once
    )
    upper = pl.BlockSpec((1, 4 * BS, BS), lambda s: (s, 0, 0))
    lower = pl.BlockSpec((BS, 4 * BS), lambda s: (s // 2, 0))
    return pl.pallas_call(
        panels,
        grid=(8,),
        out_shape=[
            shape((8, 4 * BS, BS), BF16), shape((8, 4 * BS, BS), BF16), shape((8, BS, BS), F32),
            shape((4 * BS, 4 * BS), BF16), shape((4 * BS, 4 * BS), BF16), shape((4 * BS, BS), F32),
            shape((BS, BS), F32),
        ],
        in_specs=[
            SMEM, SMEM, whole(gathered),
            pl.BlockSpec((16, PIECE, BS), lambda s: (0, s, 0)),
            pl.BlockSpec((16, 16, BS), lambda s: (0, 32, 0), pipeline_mode=once),
            pl.BlockSpec((4, BS, BS), lambda s: (0, s // 2, 0)),
            whole(near), whole(far),
        ],
        out_specs=[
            upper, upper, pl.BlockSpec((1, BS, BS), lambda s: (s, 0, 0)), lower, lower,
            pl.BlockSpec((BS, BS), lambda s: (s // 2, 0)),
            pl.BlockSpec((BS, BS), lambda s: (0, 0)),
        ],
        scratch_shapes=[
            pltpu.VMEM((4 * BS, 4 * BS), F32), pltpu.VMEM((NPIV, BS, BS), F32),
            pltpu.VMEM((4 * BS, 4 * BS), BF16), pltpu.VMEM((4 * BS, 4 * BS), BF16),
            pltpu.VMEM((NPIV, BS, BS), BF16), pltpu.VMEM((NPIV, BS, BS), BF16),
            pltpu.VMEM((NPIV, BS, BS), F32),
        ],
        compiler_params=pltpu.CompilerParams(vmem_limit_bytes=LIMIT),
        cost_estimate=pl.CostEstimate(
            flops=10 * 2**30, bytes_accessed=32 * 2**20, transcendentals=0
        ),
    )(child_map, rc, gathered, top, top, front_left, near, far)


SPAN = 2


def finish(
    map_ref, rc_ref, front_ref, high_ref, low_ref, left_high, left_low, own_ref, taken_ref,
    block_ref, order_ref, p0, p1, p2, p3, out_ref,
):
    parts = (p0, p1, p2, p3)
    step, s = pl.program_id(0), pl.program_id(1)
    row, col = rc_ref[0], rc_ref[1]
    y, x = row // 4, col // 2

    def at(s, half, tile=0, count=1):
        return pl.ds(tile * BS * 16 + half * 8 + s, count * BS, stride=16)

    def put(s, tile, value):
        for half in range(2):
            out_ref[at(s, half, tile), :] = value[:, half * HALF : half * HALF + HALF]

    total = dot(left_high[...], high_ref[0])
    total = total + dot(left_high[...], low_ref[0])
    total = total + dot(left_low[...], high_ref[0])
    for half in range(2):
        rows = at(s, half, 0, SPAN)
        out_ref[rows, :] = front_ref[rows, :] - total[:, half * HALF : half * HALF + HALF]

    @pl.when(s == 7)
    def _():
        for shift in range(4):
            slot = (y - shift + 4) % 4
            parent = row_of(map_ref, row, slot)
            for hop in range(4):
                source = (x - hop + 4) % 4
                found, value = col_of(map_ref, slot // 2, source, col)
                for tile in range(SPAN):

                    @pl.when((parent >= 0) & (parent // 16 == SPAN * step + tile) & (found >= 0))
                    def _(shift=shift, hop=hop, tile=tile, s=value // 8):
                        for half in range(2):
                            rows = at(s, half, tile)
                            lanes = slice(half * HALF, half * HALF + HALF)
                            out_ref[rows, :] = out_ref[rows, :] + parts[hop][
                                shift, :, lanes
                            ].astype(F32)

        @pl.when(col < NPIV)
        def _():
            for tile in range(SPAN):
                put(0, tile, own_ref[tile * BS : tile * BS + BS])

        @pl.when((step == 0) & (row < NPIV))
        def _():
            select = one_hot(order_ref[...])

            def turn(s, carry):
                value = jnp.concatenate([out_ref[at(s, half), :] for half in range(2)], axis=1)
                put(s, 0, reorder(select, value) - taken_ref[s])
                return carry

            lax.fori_loop(0, 8, turn, 0)

            @pl.when(col < NPIV)
            def _():
                put(0, 0, block_ref[...])


def run_finish(child_map, rc, view, upper, lower, own, taken, corner, order, parts):
    once = pl.Buffered(1)
    whole = lambda a: pl.BlockSpec(
        a.shape, functools.partial(lambda n, t, s: (0,) * n, a.ndim), pipeline_mode=once
    )
    rows = pl.BlockSpec((SPAN * BS * 16, HALF), lambda t, s: (t, 0))
    lefts = pl.BlockSpec((SPAN * BS, 4 * BS), lambda t, s: (t, 0))
    uppers = pl.BlockSpec((1, 4 * BS, BS), lambda t, s: (s, 0, 0))
    return pl.pallas_call(
        finish,
        grid=(4 // SPAN, 8),
        out_shape=shape(view.shape, F32),
        in_specs=[
            SMEM, SMEM, rows, uppers, uppers, lefts, lefts,
            pl.BlockSpec((SPAN * BS, BS), lambda t, s: (t, 0)),
            whole(taken), whole(corner), whole(order), *[whole(p) for p in parts],
        ],
        out_specs=rows,
        compiler_params=pltpu.CompilerParams(vmem_limit_bytes=LIMIT),
        cost_estimate=pl.CostEstimate(
            flops=13 * 2**30, bytes_accessed=32 * 2**20, transcendentals=0
        ),
    )(child_map, rc, view, *upper, *lower, own, taken, corner, order, *parts)


def shards(front, child_update, child_map, pivots):
    row = lax.axis_index("prow")
    col = lax.axis_index("pcol")
    y = row // 4
    x = col // 2
    rc = jnp.stack([row, col]).astype(I32)
    tiles = front.shape[0]
    planes = [[4 * i + j for j in range(4)] for i in range(4)]
    lines = [[4 * j + i for j in range(4)] for i in range(4)]

    def along_z(a, hop):
        return lax.ppermute(
            a, "prow", [(4 * i + j, 4 * i + (j + hop) % 4) for i in range(4) for j in range(4)]
        )

    def along_y(a, hop):
        return lax.ppermute(
            a, "prow", [(4 * i + j, 4 * ((i + hop) % 4) + j) for i in range(4) for j in range(4)]
        )

    def along_x(a, hop):
        return lax.ppermute(
            a, "pcol", [(2 * i + j, 2 * ((i + hop) % 4) + j) for i in range(4) for j in range(2)]
        )

    def from_plane(a, hop):
        return lax.ppermute(a, "prow", [(j, 4 * hop + j) for j in range(4)])

    def cols_to(a, pairs):
        return lax.ppermute(a, "pcol", pairs)

    def chosen(index, options):
        result = options[0]
        for at, option in enumerate(options[1:], 1):
            result = jnp.where(index == at, option, result)
        return result

    cores = [(i, i ^ 1) for i in range(8)]
    second = [(c, c + 4) for c in range(4)]

    strip = shape((BS, 2 * BS), BF16)
    thin = shape((PIECE, 2 * BS), BF16)
    zs = call(pick_z, [strip] * 4, [child_map, rc, child_update.reshape(2, BS, 2 * BS)])
    zs = [zs[0]] + [along_z(zs[hop], hop) for hop in (1, 2, 3)]

    order = jnp.where(
        row < NPIV, pivots[jnp.minimum(row, NPIV - 1)], jnp.arange(BS, dtype=I32)
    )
    order = jnp.broadcast_to(order.astype(F32)[:, None], (BS, HALF))
    view = front.reshape(tiles, BS, 8, 2, HALF).transpose(0, 1, 3, 2, 4)
    view = view.reshape(tiles * BS * 16, HALF)

    cuts = pl.pallas_call(
        cut_front,
        grid=(1,),
        out_shape=[shape((8, PIECE, BS), F32)] * 4,
        in_specs=[
            pl.BlockSpec((BS * 16, HALF), lambda t: (0, 0)),
            pl.BlockSpec((BS, HALF), lambda t: (0, 0)),
        ],
        out_specs=[pl.BlockSpec((8, PIECE, BS), lambda t: (0, 0, 0))] * 4,
        compiler_params=pltpu.CompilerParams(vmem_limit_bytes=LIMIT),
        cost_estimate=pl.CostEstimate(flops=2**30, bytes_accessed=4 * 2**20, transcendentals=0),
    )(view, order)
    cuts = [cuts[0]] + [from_plane(cuts[hop], hop) for hop in (1, 2, 3)]
    far_front = cols_to(chosen(y, [cut[0, 32:] for cut in cuts]), second)

    first = front[:, :, 0, :].reshape(tiles * BS, BS)
    front_left = lax.all_gather(first, "pcol", axis=0, tiled=False)

    zs, cuts = lax.optimization_barrier((zs, cuts))
    picked = call(pick_rows, [thin] * 4 + [strip] * 4, [child_map, rc, order, *zs])
    thin = [picked[0]] + [from_plane(picked[hop], hop) for hop in (1, 2, 3)]
    thin = lax.all_gather(chosen(y, thin), "pcol", axis=0, tiled=False)
    ys = [picked[4]] + [along_y(picked[4 + hop], hop) for hop in (1, 2, 3)]

    thin, ys, front_left = lax.optimization_barrier((thin, ys, front_left))
    code, piece = call(
        assemble,
        [shape((8 * PIECE + 16, BS), I16), shape((32, BS), F32)],
        [child_map, rc, *cuts, far_front, thin],
        scratch=[pltpu.VMEM((8, PIECE, BS), F32)],
    )

    corner = lax.all_gather(piece, "prow", axis=0, tiled=False, axis_index_groups=planes)
    corner = lax.all_gather(corner, "prow", axis=0, tiled=False, axis_index_groups=lines)
    corner = lax.all_gather(corner, "pcol", axis=0, tiled=False)

    (near,) = call(pick_left, [shape((2, BS, 2 * BS), BF16)], [child_map, rc, *ys])
    near = chosen(
        x, [near] + [cols_to(near, [(j, 2 * hop + j) for j in range(2)]) for hop in (1, 2, 3)]
    )
    far = cols_to(near, cores)

    others = cols_to(jnp.stack(ys), cores)
    xs = call(
        pick_x, [shape((4, BS, BS), BF16)] * 4, [child_map, rc, *ys, *[others[i] for i in range(4)]]
    )
    code, *xs = lax.optimization_barrier((code, *xs))
    xs = [xs[0]] + [along_x(xs[hop], hop) for hop in (1, 2, 3)]

    top = lax.all_gather(code, "prow", axis=0, tiled=False)

    *upper, taken, low_a, low_b, own, block_own = run_panels(
        child_map, rc, corner, top, front_left, near, far
    )
    done = run_finish(
        child_map, rc, view, upper, (low_a, low_b), own, taken, block_own, order, xs
    )
    done = done.reshape(tiles, BS, 2, 8, HALF).transpose(0, 1, 3, 2, 4)
    return done.reshape(front.shape)


def solution(mesh):
    return jax.shard_map(
        shards,
        mesh=mesh,
        in_specs=(P(None, "prow", None, "pcol"), P("prow", "pcol"), P(), P()),
        out_specs=P(None, "prow", None, "pcol"),
        check_vma=False,
    )
```

```python
import functools

import jax
import jax.numpy as jnp
from jax import lax
from jax.experimental import pallas as pl
from jax.experimental.pallas import tpu as pltpu
from jax.sharding import PartitionSpec as P

NPIV = 4
NS = 2
BS = 256
HALF = 128
PIECE = 64
FULL = 32767.0
F32 = jnp.float32
BF16 = jnp.bfloat16
I16 = jnp.int16
I32 = jnp.int32
SMEM = pl.BlockSpec(memory_space=pltpu.SMEM)
VMEM = pl.BlockSpec(memory_space=pltpu.VMEM)
LIMIT = 56 * 1024 * 1024


def shape(dims, kind):
    return jax.ShapeDtypeStruct(dims, kind)


def call(body, outs, ins, smem=2, flops=0, scratch=()):
    moved = sum(a.size * a.dtype.itemsize for a in ins)
    moved += sum(o.size * o.dtype.itemsize for o in outs)
    return pl.pallas_call(
        body,
        out_shape=outs,
        in_specs=[SMEM] * smem + [VMEM] * (len(ins) - smem),
        out_specs=[VMEM] * len(outs),
        scratch_shapes=list(scratch),
        compiler_params=pltpu.CompilerParams(vmem_limit_bytes=LIMIT),
        cost_estimate=pl.CostEstimate(flops=flops, bytes_accessed=moved, transcendentals=0),
    )(*ins)


def spot(map_ref, child, low, count, test):
    found = jnp.int32(-1)
    value = jnp.int32(-1)
    for step in range(count):
        entry = map_ref[child, low + step]
        hit = test(entry)
        found = jnp.where(hit, low + step, found)
        value = jnp.where(hit, entry, value)
    return found, value


def row_of(map_ref, row, slot):
    return spot(map_ref, slot // 2, 8 * (slot % 2), 8, lambda entry: entry % 16 == row)[1]


def col_of(map_ref, child, source, col):
    return spot(map_ref, child, 4 * source, 4, lambda entry: entry % 8 == col)


def split(value):
    high = value.astype(BF16)
    low = (value - high.astype(F32)).astype(BF16)
    return high, low


def dot(left, right):
    return jnp.dot(left, right, preferred_element_type=F32)


def dot3(left, right):
    (a, b), (c, d) = left, right
    return dot(a, c) + (dot(a, d) + dot(b, c))


def block(step):
    return slice(step * BS, step * BS + BS)


def one_hot(order):
    spread = lax.broadcasted_iota(I32, (BS, BS), 1).astype(F32)
    return jnp.where(order[:, :1] == spread, 1.0, 0.0).astype(BF16)


def reorder(select, value):
    high = value.astype(BF16)
    rest = value - high.astype(F32)
    middle = rest.astype(BF16)
    last = (rest - middle.astype(F32)).astype(BF16)
    return (dot(select, high) + dot(select, middle)) + dot(select, last)


def level(peak):
    return jnp.ceil(jnp.log2(jnp.full((8, HALF), jnp.maximum(peak, 1e-30))) * 4.0)


def encode(value, n):
    scaled = jnp.abs(value) * jnp.exp2(n * -0.25)[:1, :1]
    code = jnp.minimum(jnp.floor(jnp.sqrt(scaled) * FULL + 0.5), FULL)
    return jnp.where(value < 0.0, -code, code).astype(I32)


def decode(code, n):
    code = code.astype(F32)
    return code * jnp.abs(code) * (jnp.exp2(n.astype(F32)[:1, :1] * 0.25) * (1.0 / (FULL * FULL)))


def cut_front(front_ref, order_ref, *outs):
    firsts, wholes = outs[:4], outs[4:]
    select = one_hot(order_ref[...])

    def one(tile, carry):
        halves = [front_ref[pl.ds(half * 8 + tile, BS, stride=16), :] for half in range(2)]
        turned = reorder(select, jnp.concatenate(halves, axis=1))
        for piece in range(4):
            wholes[piece][tile] = turned[piece * PIECE : piece * PIECE + PIECE]
        return carry

    lax.fori_loop(0, 8, one, 0)
    for piece in range(4):
        firsts[piece][...] = wholes[piece][0]


def pick_z(map_ref, rc_ref, child_ref, *outs):
    row = rc_ref[0]
    z = row % 4
    second_at = map_ref[row // 8, 2 * (row % 8) + 1] % 4
    for hop in range(4):
        outs[hop][...] = child_ref[jnp.where(second_at == (z + hop) % 4, 1, 0)]


def pick_rows(map_ref, rc_ref, order_ref, *refs):
    held, pieces, hops = refs[:4], refs[4:8], refs[8:]
    row = rc_ref[0]
    y, z = row // 4, row % 4
    found, value = spot(map_ref, 0, 0, 4, lambda entry: entry == row)
    live = (found >= 0) & (row < NPIV)
    for hop in range(4):

        @pl.when(live & (found // 2 == (z - hop + 4) % 4))
        def _(hop=hop):
            turned = dot(one_hot(order_ref[...]), held[hop][...]).astype(BF16)
            for piece in range(4):
                pieces[piece][...] = turned[piece * PIECE : piece * PIECE + PIECE]

    @pl.when(jnp.logical_not(live))
    def _():
        for piece in range(4):
            pieces[piece][...] = jnp.zeros((PIECE, 2 * BS), BF16)

    for hop in range(4):
        first = 2 * ((4 * y + (z - hop + 4) % 4) % 8)
        index, value = spot(map_ref, y // 2, first, 2, lambda entry: entry % 4 == z)
        for shift in range(4):

            @pl.when((index >= 0) & ((value // 4) % 4 == (y + shift) % 4))
            def _(hop=hop, shift=shift):
                hops[shift][...] = held[hop][...]


def assemble(map_ref, rc_ref, f0, f1, f2, f3, first_ref, strip, code_ref, work, corner):
    row, col = rc_ref[0], rc_ref[1]
    y = row // 4
    for piece, source in enumerate((f0, f1, f2, f3)):

        @pl.when(y == piece)
        def _(source=source):
            work[...] = source[...]

    corner[...] = first_ref[:NPIV]
    for index in range(16):
        parent = map_ref[0, index]
        cut = slice((index % 2) * BS, (index % 2) * BS + BS)

        @pl.when(parent % 8 == col)
        def _(index=index, cut=cut, tile=parent // 8):
            work[tile] = work[tile] + strip[index // 2, :, cut].astype(F32)

        if index < NPIV:

            @pl.when(parent < NPIV)
            def _(index=index, cut=cut, parent=parent):
                corner[parent] = corner[parent] + strip[index // 2, :, cut].astype(F32)

    @pl.when(col < NPIV)
    def _():
        work[0] = jnp.zeros((PIECE, BS), F32)

    n = level(jnp.max(jnp.abs(work[...])))
    for tile in range(8):
        code_ref[tile * PIECE : tile * PIECE + PIECE] = encode(work[tile], n).astype(I16)
    first = level(jnp.max(jnp.abs(corner[...])))
    low = 8 * PIECE
    for k in range(NPIV):
        code = encode(corner[k], first)
        code_ref[low + k * PIECE : low + k * PIECE + PIECE] = code.astype(I16)
        corner[k] = corner[k] - decode(code, first)
    second = level(jnp.max(jnp.abs(corner[...])))
    low = 12 * PIECE
    for k in range(NPIV):
        code_ref[low + k * PIECE : low + k * PIECE + PIECE] = encode(corner[k], second).astype(I16)
    line = lax.broadcasted_iota(I32, (16, BS), 0)
    scales = jnp.where(line == 0, n[:1, :1], jnp.where(line == 1, first[:1, :1], second[:1, :1]))
    code_ref[16 * PIECE :] = scales.astype(I32).astype(I16)


def pack(rc_ref, h0, h1, h2, h3, out_ref):
    y = rc_ref[0] // 4
    for shift, source in enumerate((h0, h1, h2, h3)):
        out_ref[(y - shift + 4) % 4] = source[...]


def factor_corner(code_ref, level_ref, work, xhi, xlo):
    for y in range(4):
        for z in range(4):
            low = z * BS + y * PIECE
            scale = level_ref[4 * y + z].astype(I32)
            for k in range(4):
                rows = slice(k * PIECE, k * PIECE + PIECE)
                rest = slice((4 + k) * PIECE, (4 + k) * PIECE + PIECE)
                work[low : low + PIECE, block(k)] = decode(
                    code_ref[4 * y + z, rows].astype(I32), scale[1:2]
                ) + decode(code_ref[4 * y + z, rest].astype(I32), scale[2:3])
    diagonal = lax.broadcasted_iota(I32, (BS, BS), 0) == lax.broadcasted_iota(I32, (BS, BS), 1)
    for k in range(NPIV):
        pivot = work[block(k), block(k)]
        parts = split(pivot)
        on_line = jnp.where(diagonal, pivot, 0.0)
        across = jnp.sum(on_line, axis=0, keepdims=True)
        down = jnp.sum(on_line, axis=1, keepdims=True)
        across = across / (across * across + 1.0)
        down = down / (down * down + 1.0)
        approx = 2.0 * jnp.where(diagonal, across, 0.0) - (down * pivot) * across
        for sweep_index in range(NS - 1):
            pair = split(approx)
            approx = 2.0 * approx - dot3(split(dot3(pair, parts)), pair)
        xhi[k], xlo[k] = split(approx)
        if k + 1 < NPIV:
            below = slice((k + 1) * BS, NPIV * BS)
            lower = dot3(split(work[below, block(k)]), (xhi[k], xlo[k]))
            work[below, block(k)] = lower
            work[below, below] = work[below, below] - dot3(
                split(lower), split(work[block(k), below])
            )


SPAN = 2
WIDE = 4


def panels(
    map_ref, rc_ref, corner_ref, code_ref, level_ref, front_ref, child_ref,
    high_ref, low_ref, taken_ref, left_high, left_low, own_ref, block_ref,
    work, chi, clo, xhi, xlo, raw, left,
):
    step = pl.program_id(0)
    row, col = rc_ref[0], rc_ref[1]

    @pl.when(step == 0)
    def _():
        factor_corner(corner_ref, level_ref, work, xhi, xlo)
        for k in range(NPIV):
            chi[block(k)], clo[block(k)] = split(work[block(k)])
        for r in range(NPIV):
            for c in range(NPIV):

                @pl.when((row == r) & (col == c))
                def _(r=r, c=c):
                    block_ref[...] = work[block(r), block(c)]

    taken_ref[0] = jnp.zeros((BS, WIDE * BS), F32)
    for k in range(NPIV):
        for piece in range(4):
            scale = level_ref[4 * piece + k].astype(I32)
            for q in range(WIDE):
                raw[piece * PIECE : piece * PIECE + PIECE, block(q)] = decode(
                    code_ref[4 * piece + k, q * PIECE : q * PIECE + PIECE].astype(I32), scale
                )
        if k:
            done = slice(0, k * BS)
            taken = dot3(
                (chi[block(k), done], clo[block(k), done]), (high_ref[0, done], low_ref[0, done])
            )
            raw[...] = raw[...] - taken

            @pl.when(row == k)
            def _(taken=taken):
                taken_ref[0] = taken

        high_ref[0, block(k)], low_ref[0, block(k)] = split(raw[...])

    for k in range(NPIV):
        left[:, block(k)] = front_ref[k]
    for slot in range(2):
        parent = row_of(map_ref, row, slot)
        for index in range(4):
            target = map_ref[0, index]
            cut = slice((index % 2) * BS, (index % 2) * BS + BS)
            for tile in range(SPAN):
                for k in range(index, NPIV):

                    @pl.when((parent >= 0) & (parent // 16 == SPAN * step + tile) & (target == k))
                    def _(slot=slot, index=index, cut=cut, tile=tile, k=k):
                        left[block(tile), block(k)] = left[block(tile), block(k)] + child_ref[
                            index // 2, slot, :, cut
                        ].astype(F32)

    @pl.when((step == 0) & (row < NPIV))
    def _():
        left[:BS] = jnp.zeros((BS, NPIV * BS), F32)

    for k in range(NPIV):
        lower = dot3(split(left[:, block(k)]), (xhi[k], xlo[k]))
        pair = split(lower)
        left_high[:, block(k)], left_low[:, block(k)] = pair

        @pl.when(col == k)
        def _(lower=lower):
            own_ref[...] = lower

        if k + 1 < NPIV:
            rest = slice((k + 1) * BS, NPIV * BS)
            left[:, rest] = left[:, rest] - dot3(pair, (chi[block(k), rest], clo[block(k), rest]))


def run_panels(child_map, rc, top, front_left, child):
    once = pl.Buffered(1)
    upper = pl.BlockSpec((1, 4 * BS, WIDE * BS), lambda s: (s, 0, 0))
    lower = pl.BlockSpec((SPAN * BS, 4 * BS), lambda s: (s, 0))
    return pl.pallas_call(
        panels,
        grid=(2,),
        out_shape=[
            shape((2, 4 * BS, WIDE * BS), BF16), shape((2, 4 * BS, WIDE * BS), BF16),
            shape((2, BS, WIDE * BS), F32),
            shape((4 * BS, 4 * BS), BF16), shape((4 * BS, 4 * BS), BF16), shape((4 * BS, BS), F32),
            shape((BS, BS), F32),
        ],
        in_specs=[
            SMEM, SMEM,
            pl.BlockSpec((16, 8 * PIECE, BS), lambda s: (0, 1, 0), pipeline_mode=once),
            pl.BlockSpec((16, WIDE * PIECE, BS), lambda s: (0, s, 0)),
            pl.BlockSpec((16, 16, BS), lambda s: (0, PIECE, 0), pipeline_mode=once),
            pl.BlockSpec((4, SPAN * BS, BS), lambda s: (0, s, 0)),
            pl.BlockSpec((2, 2, BS, 2 * BS), lambda s: (0, 0, 0, 0), pipeline_mode=once),
        ],
        out_specs=[
            upper, upper, pl.BlockSpec((1, BS, WIDE * BS), lambda s: (s, 0, 0)), lower, lower,
            pl.BlockSpec((SPAN * BS, BS), lambda s: (s, 0)),
            pl.BlockSpec((BS, BS), lambda s: (0, 0)),
        ],
        scratch_shapes=[
            pltpu.VMEM((4 * BS, 4 * BS), F32),
            pltpu.VMEM((4 * BS, 4 * BS), BF16), pltpu.VMEM((4 * BS, 4 * BS), BF16),
            pltpu.VMEM((NPIV, BS, BS), BF16), pltpu.VMEM((NPIV, BS, BS), BF16),
            pltpu.VMEM((BS, WIDE * BS), F32), pltpu.VMEM((SPAN * BS, 4 * BS), F32),
        ],
        compiler_params=pltpu.CompilerParams(vmem_limit_bytes=LIMIT),
        cost_estimate=pl.CostEstimate(
            flops=10 * 2**30, bytes_accessed=32 * 2**20, transcendentals=0
        ),
    )(child_map, rc, top, top, top, front_left, child)


def finish(
    map_ref, rc_ref, front_ref, high_ref, low_ref, left_high, left_low, own_ref, taken_ref,
    block_ref, order_ref, child_ref, out_ref, total, parts, arrived,
):
    step, group = pl.program_id(0), pl.program_id(1)
    row, col = rc_ref[0], rc_ref[1]

    def at(s, half, tile=0, count=1):
        return pl.ds(tile * BS * 16 + half * 8 + s, count * BS, stride=16)

    def put(s, tile, value):
        for half in range(2):
            out_ref[at(s, half, tile), :] = value[:, half * HALF : half * HALF + HALF]

    def each_child(act):
        for slot in range(4):
            parent = row_of(map_ref, row, slot)
            here = (parent >= 0) & (parent // 16 // SPAN == step)
            for source in range(4):
                found, value = col_of(map_ref, slot // 2, source, col)
                where = jnp.maximum(found, 0)
                start = pl.multiple_of((where % 2) * BS, BS)
                index = 4 * slot + source
                copy = pltpu.make_async_copy(
                    child_ref.at[where // 2, slot, :, pl.ds(start, BS)],
                    parts.at[index],
                    arrived.at[index],
                )

                @pl.when(here & (found >= 0))
                def _(copy=copy, index=index, tile=(parent // 16) % SPAN, s=value // 8):
                    act(copy, index, tile, s)

    @pl.when(group == 0)
    def _():
        each_child(lambda copy, index, tile, s: copy.start())

    total[...] = dot(left_high[...], high_ref[0])
    total[...] += dot(left_high[...], low_ref[0])
    total[...] += dot(left_low[...], high_ref[0])
    for q in range(WIDE):
        for half in range(2):
            rows = at(WIDE * group + q, half, 0, SPAN)
            low = q * BS + half * HALF
            out_ref[rows, :] = front_ref[rows, :] - total[:, low : low + HALF]

    @pl.when(group == 1)
    def _():
        def add(copy, index, tile, s):
            copy.wait()
            for half in range(2):
                rows = at(s, half, tile)
                lanes = slice(half * HALF, half * HALF + HALF)
                out_ref[rows, :] = out_ref[rows, :] + parts[index, :, lanes].astype(F32)

        each_child(add)

        @pl.when(col < NPIV)
        def _():
            for tile in range(SPAN):
                put(0, tile, own_ref[tile * BS : tile * BS + BS])

        @pl.when((step == 0) & (row < NPIV))
        def _():
            select = one_hot(order_ref[...])
            for s in range(2 * WIDE):
                value = jnp.concatenate([out_ref[at(s, half), :] for half in range(2)], axis=1)
                put(s, 0, reorder(select, value) - taken_ref[s // WIDE, :, block(s % WIDE)])

            @pl.when(col < NPIV)
            def _():
                put(0, 0, block_ref[...])


def run_finish(child_map, rc, view, upper, lower, own, taken, corner, order, child):
    once = pl.Buffered(1)
    whole = lambda a: pl.BlockSpec(
        a.shape, functools.partial(lambda n, t, s: (0,) * n, a.ndim), pipeline_mode=once
    )
    rows = pl.BlockSpec((SPAN * BS * 16, HALF), lambda t, s: (t, 0))
    lefts = pl.BlockSpec((SPAN * BS, 4 * BS), lambda t, s: (t, 0))
    uppers = pl.BlockSpec((1, 4 * BS, WIDE * BS), lambda t, s: (s, 0, 0))
    return pl.pallas_call(
        finish,
        grid=(4 // SPAN, 2),
        out_shape=shape(view.shape, F32),
        in_specs=[
            SMEM, SMEM, rows, uppers, uppers, lefts, lefts,
            pl.BlockSpec((SPAN * BS, BS), lambda t, s: (t, 0)),
            whole(taken), whole(corner), whole(order), pl.BlockSpec(memory_space=pl.ANY),
        ],
        out_specs=rows,
        scratch_shapes=[
            pltpu.VMEM((SPAN * BS, WIDE * BS), F32),
            pltpu.VMEM((16, BS, BS), BF16),
            pltpu.SemaphoreType.DMA((16,)),
        ],
        compiler_params=pltpu.CompilerParams(vmem_limit_bytes=LIMIT),
        cost_estimate=pl.CostEstimate(
            flops=13 * 2**30, bytes_accessed=32 * 2**20, transcendentals=0
        ),
    )(child_map, rc, view, *upper, *lower, own, taken, corner, order, child)


def shards(front, child_update, child_map, pivots):
    row = lax.axis_index("prow")
    col = lax.axis_index("pcol")
    y = row // 4
    rc = jnp.stack([row, col]).astype(I32)
    tiles = front.shape[0]

    def along_z(a, hop):
        return lax.ppermute(
            a, "prow", [(4 * i + j, 4 * i + (j + hop) % 4) for i in range(4) for j in range(4)]
        )

    def along_y(a, hop):
        return lax.ppermute(
            a, "prow", [(4 * i + j, 4 * ((i + hop) % 4) + j) for i in range(4) for j in range(4)]
        )

    def from_plane(a, hop):
        return lax.ppermute(a, "prow", [(j, 4 * hop + j) for j in range(4)])

    def spread(pieces):
        return [pieces[0]] + [from_plane(pieces[hop], hop) for hop in (1, 2, 3)]

    def chosen(index, options):
        result = options[0]
        for at, option in enumerate(options[1:], 1):
            result = jnp.where(index == at, option, result)
        return result

    strip = shape((BS, 2 * BS), BF16)
    zs = call(pick_z, [strip] * 4, [child_map, rc, child_update.reshape(2, BS, 2 * BS)])
    zs = [zs[0]] + [along_z(zs[hop], hop) for hop in (1, 2, 3)]

    order = jnp.where(
        row < NPIV, pivots[jnp.minimum(row, NPIV - 1)], jnp.arange(BS, dtype=I32)
    )
    order = jnp.broadcast_to(order.astype(F32)[:, None], (BS, HALF))
    view = front.reshape(tiles, BS, 8, 2, HALF).transpose(0, 1, 3, 2, 4)
    view = view.reshape(tiles * BS * 16, HALF)

    cuts = pl.pallas_call(
        cut_front,
        grid=(1,),
        out_shape=[shape((PIECE, BS), F32)] * 4 + [shape((8, PIECE, BS), F32)] * 4,
        in_specs=[
            pl.BlockSpec((BS * 16, HALF), lambda t: (0, 0)),
            pl.BlockSpec((BS, HALF), lambda t: (0, 0)),
        ],
        out_specs=[pl.BlockSpec((PIECE, BS), lambda t: (0, 0))] * 4
        + [pl.BlockSpec((8, PIECE, BS), lambda t: (0, 0, 0))] * 4,
        compiler_params=pltpu.CompilerParams(vmem_limit_bytes=LIMIT),
        cost_estimate=pl.CostEstimate(flops=2**30, bytes_accessed=4 * 2**20, transcendentals=0),
    )(view, order)
    firsts = lax.all_gather(chosen(y, spread(cuts[:4])), "pcol", axis=0, tiled=False)
    cuts = spread(cuts[4:])

    front_left = front[:, :, 0, :].reshape(tiles * BS, BS)
    zs, firsts, front_left = lax.optimization_barrier((zs, firsts, front_left))
    front_left = lax.all_gather(front_left, "pcol", axis=0, tiled=False)

    thin = shape((PIECE, 2 * BS), BF16)
    picked = call(pick_rows, [thin] * 4 + [strip] * 4, [child_map, rc, order, *zs])
    thin = lax.all_gather(chosen(y, spread(picked[:4])), "pcol", axis=0, tiled=False)
    ys = [picked[4]] + [along_y(picked[4 + hop], hop) for hop in (1, 2, 3)]

    thin, ys, front_left = lax.optimization_barrier((thin, ys, front_left))
    (code,) = call(
        assemble,
        [shape((16 * PIECE + 16, BS), I16)],
        [child_map, rc, *cuts, firsts, thin],
        scratch=[pltpu.VMEM((8, PIECE, BS), F32), pltpu.VMEM((NPIV, PIECE, BS), F32)],
    )

    (child,) = call(pack, [shape((4, BS, 2 * BS), BF16)], [rc, *ys], smem=1)
    code, child = lax.optimization_barrier((code, child))
    child = lax.all_gather(child, "pcol", axis=0, tiled=False)
    top = lax.all_gather(code, "prow", axis=0, tiled=False)

    *upper, taken, low_a, low_b, own, block_own = run_panels(
        child_map, rc, top, front_left, child
    )
    done = run_finish(
        child_map, rc, view, upper, (low_a, low_b), own, taken, block_own, order, child
    )
    done = done.reshape(tiles, BS, 2, 8, HALF).transpose(0, 1, 3, 2, 4)
    return done.reshape(front.shape)


def solution(mesh):
    return jax.shard_map(
        shards,
        mesh=mesh,
        in_specs=(P(None, "prow", None, "pcol"), P("prow", "pcol"), P(), P()),
        out_specs=P(None, "prow", None, "pcol"),
        check_vma=False,
    )
```

```python
import functools

import jax
import jax.numpy as jnp
from jax import lax
from jax.experimental import pallas as pl
from jax.experimental.pallas import tpu as pltpu
from jax.sharding import PartitionSpec as P

NPIV = 4
NS = 2
BS = 256
HALF = 128
PIECE = 64
FULL = 32767.0
F32 = jnp.float32
BF16 = jnp.bfloat16
I16 = jnp.int16
I32 = jnp.int32
SMEM = pl.BlockSpec(memory_space=pltpu.SMEM)
VMEM = pl.BlockSpec(memory_space=pltpu.VMEM)
LIMIT = 56 * 1024 * 1024


def shape(dims, kind):
    return jax.ShapeDtypeStruct(dims, kind)


def call(body, outs, ins, smem=2, flops=0, scratch=()):
    moved = sum(a.size * a.dtype.itemsize for a in ins)
    moved += sum(o.size * o.dtype.itemsize for o in outs)
    return pl.pallas_call(
        body,
        out_shape=outs,
        in_specs=[SMEM] * smem + [VMEM] * (len(ins) - smem),
        out_specs=[VMEM] * len(outs),
        scratch_shapes=list(scratch),
        compiler_params=pltpu.CompilerParams(vmem_limit_bytes=LIMIT),
        cost_estimate=pl.CostEstimate(flops=flops, bytes_accessed=moved, transcendentals=0),
    )(*ins)


def spot(map_ref, child, low, count, test):
    found = jnp.int32(-1)
    value = jnp.int32(-1)
    for step in range(count):
        entry = map_ref[child, low + step]
        hit = test(entry)
        found = jnp.where(hit, low + step, found)
        value = jnp.where(hit, entry, value)
    return found, value


def row_of(map_ref, row, slot):
    return spot(map_ref, slot // 2, 8 * (slot % 2), 8, lambda entry: entry % 16 == row)[1]


def col_of(map_ref, child, source, col):
    return spot(map_ref, child, 4 * source, 4, lambda entry: entry % 8 == col)


def split(value):
    high = value.astype(BF16)
    low = (value - high.astype(F32)).astype(BF16)
    return high, low


def dot(left, right):
    return jnp.dot(left, right, preferred_element_type=F32)


def dot3(left, right):
    (a, b), (c, d) = left, right
    return dot(a, c) + (dot(a, d) + dot(b, c))


def block(step):
    return slice(step * BS, step * BS + BS)


def one_hot(order):
    spread = lax.broadcasted_iota(I32, (BS, BS), 1).astype(F32)
    return jnp.where(order[:, :1] == spread, 1.0, 0.0).astype(BF16)


def reorder(select, value):
    high = value.astype(BF16)
    rest = value - high.astype(F32)
    middle = rest.astype(BF16)
    last = (rest - middle.astype(F32)).astype(BF16)
    return (dot(select, high) + dot(select, middle)) + dot(select, last)


def level(peak):
    return jnp.ceil(jnp.log2(jnp.full((8, HALF), jnp.maximum(peak, 1e-30))) * 4.0)


def encode(value, n):
    scaled = jnp.abs(value) * jnp.exp2(n * -0.25)[:1, :1]
    code = jnp.minimum(jnp.floor(jnp.sqrt(scaled) * FULL + 0.5), FULL)
    return jnp.where(value < 0.0, -code, code).astype(I32)


def decode(code, n):
    code = code.astype(F32)
    return code * jnp.abs(code) * (jnp.exp2(n.astype(F32)[:1, :1] * 0.25) * (1.0 / (FULL * FULL)))


def cut_front(front_ref, order_ref, *outs):
    firsts, wholes = outs[:4], outs[4:]
    select = one_hot(order_ref[...])

    def one(tile, carry):
        halves = [front_ref[pl.ds(half * 8 + tile, BS, stride=16), :] for half in range(2)]
        turned = reorder(select, jnp.concatenate(halves, axis=1))
        for piece in range(4):
            wholes[piece][tile] = turned[piece * PIECE : piece * PIECE + PIECE]
        return carry

    lax.fori_loop(0, 8, one, 0)
    for piece in range(4):
        firsts[piece][...] = wholes[piece][0]


def pick_z(map_ref, rc_ref, child_ref, *outs):
    row = rc_ref[0]
    z = row % 4
    second_at = map_ref[row // 8, 2 * (row % 8) + 1] % 4
    for hop in range(4):
        outs[hop][...] = child_ref[jnp.where(second_at == (z + hop) % 4, 1, 0)]


def pick_rows(map_ref, rc_ref, order_ref, *refs):
    held, pieces, hops = refs[:4], refs[4:8], refs[8:]
    row = rc_ref[0]
    y, z = row // 4, row % 4
    found, value = spot(map_ref, 0, 0, 4, lambda entry: entry == row)
    live = (found >= 0) & (row < NPIV)
    for hop in range(4):

        @pl.when(live & (found // 2 == (z - hop + 4) % 4))
        def _(hop=hop):
            turned = dot(one_hot(order_ref[...]), held[hop][...]).astype(BF16)
            for piece in range(4):
                pieces[piece][...] = turned[piece * PIECE : piece * PIECE + PIECE]

    @pl.when(jnp.logical_not(live))
    def _():
        for piece in range(4):
            pieces[piece][...] = jnp.zeros((PIECE, 2 * BS), BF16)

    for hop in range(4):
        first = 2 * ((4 * y + (z - hop + 4) % 4) % 8)
        index, value = spot(map_ref, y // 2, first, 2, lambda entry: entry % 4 == z)
        for shift in range(4):

            @pl.when((index >= 0) & ((value // 4) % 4 == (y + shift) % 4))
            def _(hop=hop, shift=shift):
                hops[shift][...] = held[hop][...]


def assemble(map_ref, rc_ref, f0, f1, f2, f3, first_ref, strip, code_ref, work, corner):
    row, col = rc_ref[0], rc_ref[1]
    y = row // 4
    for piece, source in enumerate((f0, f1, f2, f3)):

        @pl.when(y == piece)
        def _(source=source):
            work[...] = source[...]

    corner[...] = first_ref[:NPIV]
    for index in range(16):
        parent = map_ref[0, index]
        cut = slice((index % 2) * BS, (index % 2) * BS + BS)

        @pl.when(parent % 8 == col)
        def _(index=index, cut=cut, tile=parent // 8):
            work[tile] = work[tile] + strip[index // 2, :, cut].astype(F32)

        if index < NPIV:

            @pl.when(parent < NPIV)
            def _(index=index, cut=cut, parent=parent):
                corner[parent] = corner[parent] + strip[index // 2, :, cut].astype(F32)

    @pl.when(col < NPIV)
    def _():
        work[0] = jnp.zeros((PIECE, BS), F32)

    n = level(jnp.max(jnp.abs(work[...])))
    for tile in range(8):
        code_ref[tile * PIECE : tile * PIECE + PIECE] = encode(work[tile], n).astype(I16)
    z = row % 4
    square = corner[z]
    corner[z] = jnp.zeros((PIECE, BS), F32)
    first = level(jnp.max(jnp.abs(corner[...])))
    low = 8 * PIECE
    for k in range(NPIV):
        code_ref[low + k * PIECE : low + k * PIECE + PIECE] = encode(corner[k], first).astype(I16)
    second = level(jnp.max(jnp.abs(square)))
    code = encode(square, second)
    code_ref[pl.ds(pl.multiple_of(low + z * PIECE, PIECE), PIECE), :] = code.astype(I16)
    square = square - decode(code, second)
    third = level(jnp.max(jnp.abs(square)))
    code_ref[12 * PIECE : 13 * PIECE] = encode(square, third).astype(I16)
    line = lax.broadcasted_iota(I32, (16, BS), 0)
    scales = third[:1, :1]
    for at, n in enumerate((n, first, second)):
        scales = jnp.where(line == at, n[:1, :1], scales)
    code_ref[13 * PIECE :] = scales.astype(I32).astype(I16)


def pack(rc_ref, h0, h1, h2, h3, out_ref):
    y = rc_ref[0] // 4
    for shift, source in enumerate((h0, h1, h2, h3)):
        out_ref[(y - shift + 4) % 4] = source[...]


def factor_corner(code_ref, rest_ref, level_ref, work, xhi, xlo):
    for y in range(4):
        for z in range(4):
            low = z * BS + y * PIECE
            scale = level_ref[4 * y + z].astype(I32)
            for k in range(4):
                code = code_ref[4 * y + z, k * PIECE : k * PIECE + PIECE].astype(I32)
                if k == z:
                    value = decode(code, scale[2:3])
                    value = value + decode(rest_ref[4 * y + z].astype(I32), scale[3:4])
                else:
                    value = decode(code, scale[1:2])
                work[low : low + PIECE, block(k)] = value
    diagonal = lax.broadcasted_iota(I32, (BS, BS), 0) == lax.broadcasted_iota(I32, (BS, BS), 1)
    for k in range(NPIV):
        pivot = work[block(k), block(k)]
        parts = split(pivot)
        on_line = jnp.where(diagonal, pivot, 0.0)
        across = jnp.sum(on_line, axis=0, keepdims=True)
        down = jnp.sum(on_line, axis=1, keepdims=True)
        across = across / (across * across + 1.0)
        down = down / (down * down + 1.0)
        approx = 2.0 * jnp.where(diagonal, across, 0.0) - (down * pivot) * across
        for sweep_index in range(NS - 1):
            pair = split(approx)
            approx = 2.0 * approx - dot3(split(dot3(pair, parts)), pair)
        xhi[k], xlo[k] = split(approx)
        if k + 1 < NPIV:
            below = slice((k + 1) * BS, NPIV * BS)
            lower = dot3(split(work[below, block(k)]), (xhi[k], xlo[k]))
            work[below, block(k)] = lower
            work[below, below] = work[below, below] - dot3(
                split(lower), split(work[block(k), below])
            )


SPAN = 2
WIDE = 4


def panels(
    map_ref, rc_ref, corner_ref, rest_ref, code_ref, level_ref, front_ref, child_ref,
    upper_ref, taken_ref, lower_ref, own_ref, block_ref,
    work, chi, clo, xhi, xlo, raw, left,
):
    step = pl.program_id(0)
    row, col = rc_ref[0], rc_ref[1]

    @pl.when(step == 0)
    def _():
        factor_corner(corner_ref, rest_ref, level_ref, work, xhi, xlo)
        for k in range(NPIV):
            chi[block(k)], clo[block(k)] = split(work[block(k)])
        for r in range(NPIV):
            for c in range(NPIV):

                @pl.when((row == r) & (col == c))
                def _(r=r, c=c):
                    block_ref[...] = work[block(r), block(c)]

    taken_ref[0] = jnp.zeros((BS, WIDE * BS), F32)
    for k in range(NPIV):
        for piece in range(4):
            scale = level_ref[4 * piece + k].astype(I32)
            for q in range(WIDE):
                raw[piece * PIECE : piece * PIECE + PIECE, block(q)] = decode(
                    code_ref[4 * piece + k, q * PIECE : q * PIECE + PIECE].astype(I32), scale
                )
        if k:
            done = slice(0, k * BS)
            taken = dot3(
                (chi[block(k), done], clo[block(k), done]),
                (upper_ref[0, done], upper_ref[0, 4 * BS : (4 + k) * BS]),
            )
            raw[...] = raw[...] - taken

            @pl.when(row == k)
            def _(taken=taken):
                taken_ref[0] = taken

        high, low = split(raw[...])
        upper_ref[0, block(k)] = high
        upper_ref[0, block(4 + k)] = low
        upper_ref[0, block(8 + k)] = high

    for k in range(NPIV):
        left[:, block(k)] = front_ref[k]
    for slot in range(2):
        parent = row_of(map_ref, row, slot)
        for index in range(4):
            target = map_ref[0, index]
            cut = slice((index % 2) * BS, (index % 2) * BS + BS)
            for tile in range(SPAN):
                for k in range(index, NPIV):

                    @pl.when((parent >= 0) & (parent // 16 == SPAN * step + tile) & (target == k))
                    def _(slot=slot, index=index, cut=cut, tile=tile, k=k):
                        left[block(tile), block(k)] = left[block(tile), block(k)] + child_ref[
                            index // 2, slot, :, cut
                        ].astype(F32)

    @pl.when((step == 0) & (row < NPIV))
    def _():
        left[:BS] = jnp.zeros((BS, NPIV * BS), F32)

    for k in range(NPIV):
        lower = dot3(split(left[:, block(k)]), (xhi[k], xlo[k]))
        pair = split(lower)
        lower_ref[:, block(k)] = pair[0]
        lower_ref[:, block(4 + k)] = pair[0]
        lower_ref[:, block(8 + k)] = pair[1]

        @pl.when(col == k)
        def _(lower=lower):
            own_ref[...] = lower

        if k + 1 < NPIV:
            rest = slice((k + 1) * BS, NPIV * BS)
            left[:, rest] = left[:, rest] - dot3(pair, (chi[block(k), rest], clo[block(k), rest]))


def run_panels(child_map, rc, top, front_left, child):
    once = pl.Buffered(1)
    upper = pl.BlockSpec((1, 12 * BS, WIDE * BS), lambda s: (s, 0, 0))
    lower = pl.BlockSpec((SPAN * BS, 12 * BS), lambda s: (s, 0))
    return pl.pallas_call(
        panels,
        grid=(2,),
        out_shape=[
            shape((2, 12 * BS, WIDE * BS), BF16), shape((2, BS, WIDE * BS), F32),
            shape((4 * BS, 12 * BS), BF16), shape((4 * BS, BS), F32),
            shape((BS, BS), F32),
        ],
        in_specs=[
            SMEM, SMEM,
            pl.BlockSpec((16, 4 * PIECE, BS), lambda s: (0, 2, 0), pipeline_mode=once),
            pl.BlockSpec((16, PIECE, BS), lambda s: (0, 12, 0), pipeline_mode=once),
            pl.BlockSpec((16, WIDE * PIECE, BS), lambda s: (0, s, 0)),
            pl.BlockSpec((16, 16, BS), lambda s: (0, 13 * PIECE // 16, 0), pipeline_mode=once),
            pl.BlockSpec((4, SPAN * BS, BS), lambda s: (0, s, 0)),
            pl.BlockSpec((2, 2, BS, 2 * BS), lambda s: (0, 0, 0, 0), pipeline_mode=once),
        ],
        out_specs=[
            upper, pl.BlockSpec((1, BS, WIDE * BS), lambda s: (s, 0, 0)), lower,
            pl.BlockSpec((SPAN * BS, BS), lambda s: (s, 0)),
            pl.BlockSpec((BS, BS), lambda s: (0, 0)),
        ],
        scratch_shapes=[
            pltpu.VMEM((4 * BS, 4 * BS), F32),
            pltpu.VMEM((4 * BS, 4 * BS), BF16), pltpu.VMEM((4 * BS, 4 * BS), BF16),
            pltpu.VMEM((NPIV, BS, BS), BF16), pltpu.VMEM((NPIV, BS, BS), BF16),
            pltpu.VMEM((BS, WIDE * BS), F32), pltpu.VMEM((SPAN * BS, 4 * BS), F32),
        ],
        compiler_params=pltpu.CompilerParams(vmem_limit_bytes=LIMIT),
        cost_estimate=pl.CostEstimate(
            flops=10 * 2**30, bytes_accessed=32 * 2**20, transcendentals=0
        ),
    )(child_map, rc, top, top, top, top, front_left, child)


def finish(
    map_ref, rc_ref, front_ref, upper_ref, lower_ref, own_ref, taken_ref,
    block_ref, order_ref, child_ref, out_ref, total, parts, arrived,
):
    step, group = pl.program_id(0), pl.program_id(1)
    row, col = rc_ref[0], rc_ref[1]

    def at(s, half, tile=0, count=1):
        return pl.ds(tile * BS * 16 + half * 8 + s, count * BS, stride=16)

    def put(s, tile, value):
        for half in range(2):
            out_ref[at(s, half, tile), :] = value[:, half * HALF : half * HALF + HALF]

    def each_child(act):
        for slot in range(4):
            parent = row_of(map_ref, row, slot)
            here = (parent >= 0) & (parent // 16 // SPAN == step)
            for source in range(4):
                found, value = col_of(map_ref, slot // 2, source, col)
                where = jnp.maximum(found, 0)
                start = pl.multiple_of((where % 2) * BS, BS)
                index = 4 * slot + source
                copy = pltpu.make_async_copy(
                    child_ref.at[where // 2, slot, :, pl.ds(start, BS)],
                    parts.at[index],
                    arrived.at[index],
                )

                @pl.when(here & (found >= 0))
                def _(copy=copy, index=index, tile=(parent // 16) % SPAN, s=value // 8):
                    act(copy, index, tile, s)

    @pl.when(group == 0)
    def _():
        each_child(lambda copy, index, tile, s: copy.start())

    total[...] = dot(lower_ref[...], upper_ref[0])
    for q in range(WIDE):
        for half in range(2):
            rows = at(WIDE * group + q, half, 0, SPAN)
            low = q * BS + half * HALF
            out_ref[rows, :] = front_ref[rows, :] - total[:, low : low + HALF]

    @pl.when(group == 1)
    def _():
        def add(copy, index, tile, s):
            copy.wait()
            for half in range(2):
                rows = at(s, half, tile)
                lanes = slice(half * HALF, half * HALF + HALF)
                out_ref[rows, :] = out_ref[rows, :] + parts[index, :, lanes].astype(F32)

        each_child(add)

        @pl.when(col < NPIV)
        def _():
            for tile in range(SPAN):
                put(0, tile, own_ref[tile * BS : tile * BS + BS])

        @pl.when((step == 0) & (row < NPIV))
        def _():
            select = one_hot(order_ref[...])
            for s in range(2 * WIDE):
                value = jnp.concatenate([out_ref[at(s, half), :] for half in range(2)], axis=1)
                put(s, 0, reorder(select, value) - taken_ref[s // WIDE, :, block(s % WIDE)])

            @pl.when(col < NPIV)
            def _():
                put(0, 0, block_ref[...])


def run_finish(child_map, rc, view, upper, lower, own, taken, corner, order, child):
    once = pl.Buffered(1)
    whole = lambda a: pl.BlockSpec(
        a.shape, functools.partial(lambda n, t, s: (0,) * n, a.ndim), pipeline_mode=once
    )
    rows = pl.BlockSpec((SPAN * BS * 16, HALF), lambda t, s: (t, 0))
    lefts = pl.BlockSpec((SPAN * BS, 12 * BS), lambda t, s: (t, 0))
    uppers = pl.BlockSpec((1, 12 * BS, WIDE * BS), lambda t, s: (s, 0, 0))
    return pl.pallas_call(
        finish,
        grid=(4 // SPAN, 2),
        out_shape=shape(view.shape, F32),
        in_specs=[
            SMEM, SMEM, rows, uppers, lefts,
            pl.BlockSpec((SPAN * BS, BS), lambda t, s: (t, 0)),
            whole(taken), whole(corner), whole(order), pl.BlockSpec(memory_space=pl.ANY),
        ],
        out_specs=rows,
        scratch_shapes=[
            pltpu.VMEM((SPAN * BS, WIDE * BS), F32),
            pltpu.VMEM((16, BS, BS), BF16),
            pltpu.SemaphoreType.DMA((16,)),
        ],
        compiler_params=pltpu.CompilerParams(vmem_limit_bytes=LIMIT),
        cost_estimate=pl.CostEstimate(
            flops=13 * 2**30, bytes_accessed=32 * 2**20, transcendentals=0
        ),
    )(child_map, rc, view, upper, lower, own, taken, corner, order, child)


def shards(front, child_update, child_map, pivots):
    row = lax.axis_index("prow")
    col = lax.axis_index("pcol")
    y = row // 4
    rc = jnp.stack([row, col]).astype(I32)
    tiles = front.shape[0]

    def along_z(a, hop):
        return lax.ppermute(
            a, "prow", [(4 * i + j, 4 * i + (j + hop) % 4) for i in range(4) for j in range(4)]
        )

    def along_y(a, hop):
        return lax.ppermute(
            a, "prow", [(4 * i + j, 4 * ((i + hop) % 4) + j) for i in range(4) for j in range(4)]
        )

    def from_plane(a, hop):
        return lax.ppermute(a, "prow", [(j, 4 * hop + j) for j in range(4)])

    def spread(pieces):
        return [pieces[0]] + [from_plane(pieces[hop], hop) for hop in (1, 2, 3)]

    def chosen(index, options):
        result = options[0]
        for at, option in enumerate(options[1:], 1):
            result = jnp.where(index == at, option, result)
        return result

    strip = shape((BS, 2 * BS), BF16)
    zs = call(pick_z, [strip] * 4, [child_map, rc, child_update.reshape(2, BS, 2 * BS)])
    order = jnp.where(
        row < NPIV, pivots[jnp.minimum(row, NPIV - 1)], jnp.arange(BS, dtype=I32)
    )
    order = jnp.broadcast_to(order.astype(F32)[:, None], (BS, HALF))
    order, *zs = lax.optimization_barrier((order, *zs))
    zs = [zs[0]] + [along_z(zs[hop], hop) for hop in (1, 2, 3)]
    view = front.reshape(tiles, BS, 8, 2, HALF).transpose(0, 1, 3, 2, 4)
    view = view.reshape(tiles * BS * 16, HALF)

    cuts = pl.pallas_call(
        cut_front,
        grid=(1,),
        out_shape=[shape((PIECE, BS), F32)] * 4 + [shape((8, PIECE, BS), F32)] * 4,
        in_specs=[
            pl.BlockSpec((BS * 16, HALF), lambda t: (0, 0)),
            pl.BlockSpec((BS, HALF), lambda t: (0, 0)),
        ],
        out_specs=[pl.BlockSpec((PIECE, BS), lambda t: (0, 0))] * 4
        + [pl.BlockSpec((8, PIECE, BS), lambda t: (0, 0, 0))] * 4,
        compiler_params=pltpu.CompilerParams(vmem_limit_bytes=LIMIT),
        cost_estimate=pl.CostEstimate(flops=2**30, bytes_accessed=4 * 2**20, transcendentals=0),
    )(view, order)
    firsts = lax.all_gather(chosen(y, spread(cuts[:4])), "pcol", axis=0, tiled=False)
    cuts = spread(cuts[4:])

    front_left = front[:, :, 0, :].reshape(tiles * BS, BS)
    zs, cuts, firsts, unused = lax.optimization_barrier((zs, cuts, firsts, front_left))
    front_left = lax.all_gather(front_left, "pcol", axis=0, tiled=False)

    thin = shape((PIECE, 2 * BS), BF16)
    picked = call(pick_rows, [thin] * 4 + [strip] * 4, [child_map, rc, order, *zs])
    thin = lax.all_gather(chosen(y, spread(picked[:4])), "pcol", axis=0, tiled=False)
    ys = [picked[4]] + [along_y(picked[4 + hop], hop) for hop in (1, 2, 3)]

    (code,) = call(
        assemble,
        [shape((13 * PIECE + 16, BS), I16)],
        [child_map, rc, *cuts, firsts, thin],
        scratch=[pltpu.VMEM((8, PIECE, BS), F32), pltpu.VMEM((NPIV, PIECE, BS), F32)],
    )

    (child,) = call(pack, [shape((4, BS, 2 * BS), BF16)], [rc, *ys], smem=1)
    code, child = lax.optimization_barrier((code, child))
    child = lax.all_gather(child, "pcol", axis=0, tiled=False)
    top = lax.all_gather(code, "prow", axis=0, tiled=False)

    upper, taken, lower, own, block_own = run_panels(
        child_map, rc, top, front_left, child
    )
    done = run_finish(
        child_map, rc, view, upper, lower, own, taken, block_own, order, child
    )
    done = done.reshape(tiles, BS, 2, 8, HALF).transpose(0, 1, 3, 2, 4)
    return done.reshape(front.shape)


def solution(mesh):
    return jax.shard_map(
        shards,
        mesh=mesh,
        in_specs=(P(None, "prow", None, "pcol"), P("prow", "pcol"), P(), P()),
        out_specs=P(None, "prow", None, "pcol"),
        check_vma=False,
    )
```

```python
import functools

import jax
import jax.numpy as jnp
from jax import lax
from jax.experimental import pallas as pl
from jax.experimental.pallas import tpu as pltpu
from jax.sharding import PartitionSpec as P

NPIV = 4
NS = 2
BS = 256
HALF = 128
PIECE = 64
FULL = 32767.0
CHILD_LEVEL = 11.0
F32 = jnp.float32
BF16 = jnp.bfloat16
I16 = jnp.int16
I32 = jnp.int32
SMEM = pl.BlockSpec(memory_space=pltpu.SMEM)
VMEM = pl.BlockSpec(memory_space=pltpu.VMEM)
LIMIT = 60 * 1024 * 1024


def shape(dims, kind):
    return jax.ShapeDtypeStruct(dims, kind)


def call(body, outs, ins, smem=2, flops=0, scratch=()):
    moved = sum(a.size * a.dtype.itemsize for a in ins)
    moved += sum(o.size * o.dtype.itemsize for o in outs)
    return pl.pallas_call(
        body,
        out_shape=outs,
        in_specs=[SMEM] * smem + [VMEM] * (len(ins) - smem),
        out_specs=[VMEM] * len(outs),
        scratch_shapes=list(scratch),
        compiler_params=pltpu.CompilerParams(vmem_limit_bytes=LIMIT),
        cost_estimate=pl.CostEstimate(flops=flops, bytes_accessed=moved, transcendentals=0),
    )(*ins)


def spot(map_ref, child, low, count, test):
    found = jnp.int32(-1)
    value = jnp.int32(-1)
    for step in range(count):
        entry = map_ref[child, low + step]
        hit = test(entry)
        found = jnp.where(hit, low + step, found)
        value = jnp.where(hit, entry, value)
    return found, value


def row_of(map_ref, row, slot):
    return spot(map_ref, slot // 2, 8 * (slot % 2), 8, lambda entry: entry % 16 == row)[1]


def col_of(map_ref, child, source, col):
    return spot(map_ref, child, 4 * source, 4, lambda entry: entry % 8 == col)


def split(value):
    high = value.astype(BF16)
    low = (value - high.astype(F32)).astype(BF16)
    return high, low


def dot(left, right):
    return jnp.dot(left, right, preferred_element_type=F32)


def dot3(left, right):
    (a, b), (c, d) = left, right
    return dot(a, c) + (dot(a, d) + dot(b, c))


def block(step):
    return slice(step * BS, step * BS + BS)


def one_hot(order):
    spread = lax.broadcasted_iota(I32, (BS, BS), 1).astype(F32)
    return jnp.where(order[:, :1] == spread, 1.0, 0.0).astype(BF16)


def reorder(select, value):
    high = value.astype(BF16)
    rest = value - high.astype(F32)
    middle = rest.astype(BF16)
    last = (rest - middle.astype(F32)).astype(BF16)
    return (dot(select, high) + dot(select, middle)) + dot(select, last)


def level(peak):
    return jnp.ceil(jnp.log2(jnp.full((8, HALF), jnp.maximum(peak, 1e-30))) * 4.0)


def encode(value, n):
    scaled = jnp.abs(value) * jnp.exp2(n * -0.25)[:1, :1]
    code = jnp.minimum(jnp.floor(jnp.sqrt(scaled) * FULL + 0.5), FULL)
    return jnp.where(value < 0.0, -code, code).astype(I32)


def decode(code, n):
    code = code.astype(F32)
    return code * jnp.abs(code) * (jnp.exp2(n.astype(F32)[:1, :1] * 0.25) * (1.0 / (FULL * FULL)))


def cut_front(front_ref, order_ref, *outs):
    select = one_hot(order_ref[...])

    def one(tile, carry):
        halves = [front_ref[pl.ds(half * 8 + tile, BS, stride=16), :] for half in range(2)]
        turned = reorder(select, jnp.concatenate(halves, axis=1))
        for piece in range(4):
            outs[piece][tile] = turned[piece * PIECE : piece * PIECE + PIECE]
        return carry

    lax.fori_loop(0, 8, one, 0)


def pick_z(map_ref, rc_ref, child_ref, *outs):
    row = rc_ref[0]
    z = row % 4
    second_at = map_ref[row // 8, 2 * (row % 8) + 1] % 4
    for hop in range(4):
        outs[hop][...] = child_ref[jnp.where(second_at == (z + hop) % 4, 1, 0)]


def pick_rows(map_ref, rc_ref, order_ref, *refs):
    held, pieces, hops = refs[:4], refs[4:8], refs[8:]
    row = rc_ref[0]
    y, z = row // 4, row % 4
    found, value = spot(map_ref, 0, 0, 4, lambda entry: entry == row)
    live = (found >= 0) & (row < NPIV)
    for hop in range(4):

        @pl.when(live & (found // 2 == (z - hop + 4) % 4))
        def _(hop=hop):
            turned = dot(one_hot(order_ref[...]), held[hop][...]).astype(BF16)
            for piece in range(4):
                pieces[piece][...] = turned[piece * PIECE : piece * PIECE + PIECE]

    @pl.when(jnp.logical_not(live))
    def _():
        for piece in range(4):
            pieces[piece][...] = jnp.zeros((PIECE, 2 * BS), BF16)

    for hop in range(4):
        first = 2 * ((4 * y + (z - hop + 4) % 4) % 8)
        index, value = spot(map_ref, y // 2, first, 2, lambda entry: entry % 4 == z)
        for shift in range(4):

            @pl.when((index >= 0) & ((value // 4) % 4 == (y + shift) % 4))
            def _(hop=hop, shift=shift):
                hops[shift][...] = held[hop][...]


def mix(rc_ref, t0, t1, t2, t3, f0, f1, f2, f3, out_ref, strip, corner):
    y = rc_ref[0] // 4
    for piece, (child, source) in enumerate(((t0, f0), (t1, f1), (t2, f2), (t3, f3))):

        @pl.when(y == piece)
        def _(child=child, source=source):
            strip[...] = child[...].astype(F32)
            corner[...] = source[0]

    n = jnp.full((8, HALF), CHILD_LEVEL)
    for half in range(2):
        out_ref[half * PIECE : half * PIECE + PIECE] = encode(
            strip[:, half * BS : half * BS + BS], n
        ).astype(I16)
    value = corner[...]
    first = level(jnp.max(jnp.abs(value)))
    code = encode(value, first)
    out_ref[2 * PIECE : 3 * PIECE] = code.astype(I16)
    value = value - decode(code, first)
    second = level(jnp.max(jnp.abs(value)))
    out_ref[3 * PIECE : 4 * PIECE] = encode(value, second).astype(I16)
    line = lax.broadcasted_iota(I32, (16, BS), 0)
    scales = jnp.where(line == 0, first[:1, :1], second[:1, :1])
    out_ref[4 * PIECE :] = scales.astype(I32).astype(I16)


def assemble(map_ref, rc_ref, f0, f1, f2, f3, thin, code_ref, work, corner):
    row, col = rc_ref[0], rc_ref[1]
    y = row // 4
    for piece, source in enumerate((f0, f1, f2, f3)):

        @pl.when(y == piece)
        def _(source=source):
            work[...] = source[...]

    for k in range(NPIV):
        scales = thin[k, 4 * PIECE :].astype(I32)
        corner[k] = decode(thin[k, 2 * PIECE : 3 * PIECE].astype(I32), scales[0:1]) + decode(
            thin[k, 3 * PIECE : 4 * PIECE].astype(I32), scales[1:2]
        )
    n = jnp.full((8, HALF), CHILD_LEVEL)
    for index in range(16):
        parent = map_ref[0, index]
        low = (index % 2) * PIECE

        @pl.when(parent % 8 == col)
        def _(index=index, low=low, tile=parent // 8):
            child = decode(thin[index // 2, low : low + PIECE].astype(I32), n)
            work[tile] = work[tile] + child

        if index < NPIV:

            @pl.when(parent < NPIV)
            def _(index=index, low=low, parent=parent):
                child = decode(thin[index // 2, low : low + PIECE].astype(I32), n)
                corner[parent] = corner[parent] + child

    @pl.when(col < NPIV)
    def _():
        work[0] = jnp.zeros((PIECE, BS), F32)

    n = level(jnp.max(jnp.abs(work[...])))
    for tile in range(8):
        code_ref[tile * PIECE : tile * PIECE + PIECE] = encode(work[tile], n).astype(I16)
    z = row % 4
    square = corner[z]
    corner[z] = jnp.zeros((PIECE, BS), F32)
    first = level(jnp.max(jnp.abs(corner[...])))
    low = 8 * PIECE
    for k in range(NPIV):
        code_ref[low + k * PIECE : low + k * PIECE + PIECE] = encode(corner[k], first).astype(I16)
    second = level(jnp.max(jnp.abs(square)))
    code = encode(square, second)
    code_ref[pl.ds(pl.multiple_of(low + z * PIECE, PIECE), PIECE), :] = code.astype(I16)
    square = square - decode(code, second)
    third = level(jnp.max(jnp.abs(square)))
    code_ref[12 * PIECE : 13 * PIECE] = encode(square, third).astype(I16)
    line = lax.broadcasted_iota(I32, (16, BS), 0)
    scales = third[:1, :1]
    for at, n in enumerate((n, first, second)):
        scales = jnp.where(line == at, n[:1, :1], scales)
    code_ref[13 * PIECE :] = scales.astype(I32).astype(I16)


def pack(rc_ref, h0, h1, h2, h3, out_ref):
    y = rc_ref[0] // 4
    for shift, source in enumerate((h0, h1, h2, h3)):
        out_ref[(y - shift + 4) % 4] = source[...]


def factor_corner(code_ref, rest_ref, level_ref, work, xhi, xlo):
    for y in range(4):
        for z in range(4):
            low = z * BS + y * PIECE
            scale = level_ref[4 * y + z].astype(I32)
            for k in range(4):
                code = code_ref[4 * y + z, k * PIECE : k * PIECE + PIECE].astype(I32)
                if k == z:
                    value = decode(code, scale[2:3])
                    value = value + decode(rest_ref[4 * y + z].astype(I32), scale[3:4])
                else:
                    value = decode(code, scale[1:2])
                work[low : low + PIECE, block(k)] = value
    diagonal = lax.broadcasted_iota(I32, (BS, BS), 0) == lax.broadcasted_iota(I32, (BS, BS), 1)
    for k in range(NPIV):
        pivot = work[block(k), block(k)]
        parts = split(pivot)
        on_line = jnp.where(diagonal, pivot, 0.0)
        across = jnp.sum(on_line, axis=0, keepdims=True)
        down = jnp.sum(on_line, axis=1, keepdims=True)
        across = across / (across * across + 1.0)
        down = down / (down * down + 1.0)
        approx = 2.0 * jnp.where(diagonal, across, 0.0) - (down * pivot) * across
        for sweep_index in range(NS - 1):
            pair = split(approx)
            approx = 2.0 * approx - dot3(split(dot3(pair, parts)), pair)
        xhi[k], xlo[k] = split(approx)
        if k + 1 < NPIV:
            below = slice((k + 1) * BS, NPIV * BS)
            lower = dot3(split(work[below, block(k)]), (xhi[k], xlo[k]))
            work[below, block(k)] = lower
            work[below, below] = work[below, below] - dot3(
                split(lower), split(work[block(k), below])
            )


SPAN = 2
WIDE = 4


def finish(
    map_ref, rc_ref, corner_ref, rest_ref, level_ref, code_ref, left_ref, near_ref, order_ref,
    front_ref, f0, f1, f2, f3, child_ref, out_ref,
    work, chi, clo, xhi, xlo, uhi, ulo, lhi, llo, own_col, own_block, own_row, parts,
    arrived, own_arrived,
):
    step, group = pl.program_id(0), pl.program_id(1)
    row, col = rc_ref[0], rc_ref[1]
    top_row = row < NPIV
    low_rows = slice(0, SPAN * BS)
    high_rows = slice(SPAN * BS, 2 * SPAN * BS)

    def at(s, half, tile=0, count=1):
        return pl.ds(tile * BS * 16 + half * 8 + s, count * BS, stride=16)

    def put(s, tile, value):
        for half in range(2):
            out_ref[at(s, half, tile), :] = value[:, half * HALF : half * HALF + HALF]

    def each_child(act):
        for slot in range(4):
            parent = row_of(map_ref, row, slot)
            here = (parent >= 0) & (parent // 16 // SPAN == step)
            for source in range(4):
                found, value = col_of(map_ref, slot // 2, source, col)
                where = jnp.maximum(found, 0)
                start = pl.multiple_of((where % 2) * BS, BS)
                index = 4 * slot + source
                copy = pltpu.make_async_copy(
                    child_ref.at[where // 2, slot, :, pl.ds(start, BS)],
                    parts.at[index],
                    arrived.at[index],
                )

                @pl.when(here & (found >= 0))
                def _(copy=copy, index=index, tile=(parent // 16) % SPAN, s=value // 8):
                    act(copy, index, tile, s)

    def own_copies():
        return [
            pltpu.make_async_copy(source, own_row.at[piece], own_arrived.at[piece])
            for piece, source in enumerate((f0, f1, f2, f3))
        ]

    @pl.when(group == 0)
    def _():
        each_child(lambda copy, index, tile, s: copy.start())

    @pl.when((step == 0) & (group == 0))
    def _():
        @pl.when(top_row)
        def _():
            for copy in own_copies():
                copy.start()

        factor_corner(corner_ref, rest_ref, level_ref, work, xhi, xlo)
        for k in range(NPIV):
            chi[block(k)], clo[block(k)] = split(work[block(k)])
        for r in range(NPIV):
            for c in range(NPIV):

                @pl.when((row == r) & (col == c))
                def _(r=r, c=c):
                    own_block[...] = work[block(r), block(c)]

        @pl.when(top_row)
        def _():
            for copy in own_copies():
                copy.wait()

    @pl.when(step == 0)
    def _():
        for k in range(NPIV):
            raw = slice(0, BS)
            for piece in range(4):
                scale = level_ref[4 * piece + k].astype(I32)
                for q in range(WIDE):
                    work[piece * PIECE : piece * PIECE + PIECE, block(q)] = decode(
                        code_ref[4 * piece + k, q * PIECE : q * PIECE + PIECE].astype(I32), scale
                    )
            if k:
                done = slice(0, k * BS)
                taken = dot3(
                    (chi[block(k), done], clo[block(k), done]),
                    (uhi[group, done], ulo[group, done]),
                )
                work[raw] = work[raw] - taken

                @pl.when(row == k)
                def _(taken=taken):
                    for piece in range(4):
                        for q in range(WIDE):
                            tile = WIDE * group + q
                            own_row[piece, tile] = (
                                own_row[piece, tile]
                                - taken[piece * PIECE : piece * PIECE + PIECE, block(q)]
                            )

            uhi[group, block(k)], ulo[group, block(k)] = split(work[raw])

    @pl.when(group == 0)
    def _():
        left = work.at[high_rows]
        for k in range(NPIV):
            left[:, block(k)] = left_ref[k]
        for slot in range(2):
            parent = row_of(map_ref, row, slot)
            for index in range(4):
                target = map_ref[0, index]
                cut = slice((index % 2) * BS, (index % 2) * BS + BS)
                for tile in range(SPAN):
                    for k in range(index, NPIV):

                        @pl.when(
                            (parent >= 0) & (parent // 16 == SPAN * step + tile) & (target == k)
                        )
                        def _(slot=slot, index=index, cut=cut, tile=tile, k=k):
                            left[block(tile), block(k)] = left[block(tile), block(k)] + near_ref[
                                index // 2, slot, :, cut
                            ].astype(F32)

        @pl.when((step == 0) & top_row)
        def _():
            left[:BS] = jnp.zeros((BS, NPIV * BS), F32)

        for k in range(NPIV):
            lower = dot3(split(left[:, block(k)]), (xhi[k], xlo[k]))
            pair = split(lower)
            lhi[:, block(k)], llo[:, block(k)] = pair

            @pl.when(col == k)
            def _(lower=lower):
                own_col[...] = lower

            if k + 1 < NPIV:
                rest = slice((k + 1) * BS, NPIV * BS)
                left[:, rest] = left[:, rest] - dot3(pair, (chi[block(k), rest], clo[block(k), rest]))

    total = work.at[low_rows]
    total[...] = dot(lhi[...], uhi[group])
    total[...] += dot(lhi[...], ulo[group])
    total[...] += dot(llo[...], uhi[group])
    for q in range(WIDE):
        for half in range(2):
            rows = at(WIDE * group + q, half, 0, SPAN)
            low = q * BS + half * HALF
            out_ref[rows, :] = front_ref[rows, :] - total[:, low : low + HALF]

    @pl.when(group == 1)
    def _():
        top_tile = (step == 0) & top_row

        @pl.when(top_tile)
        def _():
            for s in range(2 * WIDE):
                put(s, 0, jnp.concatenate([own_row[piece, s] for piece in range(4)], axis=0))

        def add(copy, index, tile, s):
            copy.wait()
            turn = top_tile & (tile == 0)

            @pl.when(turn)
            def _():
                turned = dot(one_hot(order_ref[...]), parts[index])
                for half in range(2):
                    rows = at(s, half)
                    lanes = slice(half * HALF, half * HALF + HALF)
                    out_ref[rows, :] = out_ref[rows, :] + turned[:, lanes]

            @pl.when(jnp.logical_not(turn))
            def _():
                for half in range(2):
                    rows = at(s, half, tile)
                    lanes = slice(half * HALF, half * HALF + HALF)
                    out_ref[rows, :] = out_ref[rows, :] + parts[index, :, lanes].astype(F32)

        each_child(add)

        @pl.when(col < NPIV)
        def _():
            @pl.when(jnp.logical_not(top_tile))
            def _():
                put(0, 0, own_col[:BS])

            put(0, 1, own_col[BS:])

            @pl.when(top_tile)
            def _():
                put(0, 0, own_block[...])


def run_finish(child_map, rc, top, front_left, order, view, cuts, child):
    once = pl.Buffered(1)
    rows = pl.BlockSpec((SPAN * BS * 16, HALF), lambda t, g: (t, 0))
    away = pl.BlockSpec(memory_space=pl.ANY)
    return pl.pallas_call(
        finish,
        grid=(4 // SPAN, 2),
        out_shape=shape(view.shape, F32),
        in_specs=[
            SMEM, SMEM,
            pl.BlockSpec((16, 4 * PIECE, BS), lambda t, g: (0, 2, 0), pipeline_mode=once),
            pl.BlockSpec((16, PIECE, BS), lambda t, g: (0, 12, 0), pipeline_mode=once),
            pl.BlockSpec((16, 16, BS), lambda t, g: (0, 13 * PIECE // 16, 0), pipeline_mode=once),
            pl.BlockSpec((16, WIDE * PIECE, BS), lambda t, g: (0, jnp.maximum(t, g), 0)),
            pl.BlockSpec((4, SPAN * BS, BS), lambda t, g: (0, t, 0)),
            pl.BlockSpec((2, 2, BS, 2 * BS), lambda t, g: (0, 0, 0, 0), pipeline_mode=once),
            pl.BlockSpec((BS, HALF), lambda t, g: (0, 0), pipeline_mode=once),
            rows, away, away, away, away, away,
        ],
        out_specs=rows,
        scratch_shapes=[
            pltpu.VMEM((4 * BS, 4 * BS), F32),
            pltpu.VMEM((4 * BS, 4 * BS), BF16), pltpu.VMEM((4 * BS, 4 * BS), BF16),
            pltpu.VMEM((NPIV, BS, BS), BF16), pltpu.VMEM((NPIV, BS, BS), BF16),
            pltpu.VMEM((2, 4 * BS, WIDE * BS), BF16), pltpu.VMEM((2, 4 * BS, WIDE * BS), BF16),
            pltpu.VMEM((SPAN * BS, 4 * BS), BF16), pltpu.VMEM((SPAN * BS, 4 * BS), BF16),
            pltpu.VMEM((SPAN * BS, BS), F32), pltpu.VMEM((BS, BS), F32),
            pltpu.VMEM((4, 8, PIECE, BS), F32),
            pltpu.VMEM((16, BS, BS), BF16),
            pltpu.SemaphoreType.DMA((16,)), pltpu.SemaphoreType.DMA((4,)),
        ],
        compiler_params=pltpu.CompilerParams(vmem_limit_bytes=LIMIT),
        cost_estimate=pl.CostEstimate(
            flops=23 * 2**30, bytes_accessed=32 * 2**20, transcendentals=0
        ),
    )(child_map, rc, top, top, top, top, front_left, child, order, view, *cuts, child)


def shards(front, child_update, child_map, pivots):
    row = lax.axis_index("prow")
    col = lax.axis_index("pcol")
    rc = jnp.stack([row, col]).astype(I32)
    tiles = front.shape[0]

    def along_z(a, hop):
        return lax.ppermute(
            a, "prow", [(4 * i + j, 4 * i + (j + hop) % 4) for i in range(4) for j in range(4)]
        )

    def along_y(a, hop):
        return lax.ppermute(
            a, "prow", [(4 * i + j, 4 * ((i + hop) % 4) + j) for i in range(4) for j in range(4)]
        )

    def from_plane(a, hop):
        return lax.ppermute(a, "prow", [(j, 4 * hop + j) for j in range(4)])

    def spread(pieces):
        return [pieces[0]] + [from_plane(pieces[hop], hop) for hop in (1, 2, 3)]

    strip = shape((BS, 2 * BS), BF16)
    zs = call(pick_z, [strip] * 4, [child_map, rc, child_update.reshape(2, BS, 2 * BS)])
    order = jnp.where(
        row < NPIV, pivots[jnp.minimum(row, NPIV - 1)], jnp.arange(BS, dtype=I32)
    )
    order = jnp.broadcast_to(order.astype(F32)[:, None], (BS, HALF))
    order, *zs = lax.optimization_barrier((order, *zs))
    zs = [zs[0]] + [along_z(zs[hop], hop) for hop in (1, 2, 3)]
    view = front.reshape(tiles, BS, 8, 2, HALF).transpose(0, 1, 3, 2, 4)
    view = view.reshape(tiles * BS * 16, HALF)

    cuts = pl.pallas_call(
        cut_front,
        grid=(1,),
        out_shape=[shape((8, PIECE, BS), F32)] * 4,
        in_specs=[
            pl.BlockSpec((BS * 16, HALF), lambda t: (0, 0)),
            pl.BlockSpec((BS, HALF), lambda t: (0, 0)),
        ],
        out_specs=[pl.BlockSpec((8, PIECE, BS), lambda t: (0, 0, 0))] * 4,
        compiler_params=pltpu.CompilerParams(vmem_limit_bytes=LIMIT),
        cost_estimate=pl.CostEstimate(flops=2**30, bytes_accessed=4 * 2**20, transcendentals=0),
    )(view, order)
    moved = spread(cuts)

    front_left = front[:, :, 0, :].reshape(tiles * BS, BS)
    zs, unused, unused = lax.optimization_barrier((zs, front_left, moved[0]))
    front_left = lax.all_gather(front_left, "pcol", axis=0, tiled=False)

    thin = shape((PIECE, 2 * BS), BF16)
    picked = call(pick_rows, [thin] * 4 + [strip] * 4, [child_map, rc, order, *zs])
    thin = spread(picked[:4])
    ys = [picked[4]] + [along_y(picked[4 + hop], hop) for hop in (1, 2, 3)]

    (thin,) = call(
        mix,
        [shape((4 * PIECE + 16, BS), I16)],
        [rc, *thin, *moved],
        smem=1,
        scratch=[pltpu.VMEM((PIECE, 2 * BS), F32), pltpu.VMEM((PIECE, BS), F32)],
    )
    thin = lax.all_gather(thin, "pcol", axis=0, tiled=False)
    (code,) = call(
        assemble,
        [shape((13 * PIECE + 16, BS), I16)],
        [child_map, rc, *moved, thin],
        scratch=[pltpu.VMEM((8, PIECE, BS), F32), pltpu.VMEM((NPIV, PIECE, BS), F32)],
    )

    (child,) = call(pack, [shape((4, BS, 2 * BS), BF16)], [rc, *ys], smem=1)
    code, child = lax.optimization_barrier((code, child))
    child = lax.all_gather(child, "pcol", axis=0, tiled=False)
    top = lax.all_gather(code, "prow", axis=0, tiled=False)

    done = run_finish(child_map, rc, top, front_left, order, view, cuts, child)
    done = done.reshape(tiles, BS, 2, 8, HALF).transpose(0, 1, 3, 2, 4)
    return done.reshape(front.shape)


def solution(mesh):
    return jax.shard_map(
        shards,
        mesh=mesh,
        in_specs=(P(None, "prow", None, "pcol"), P("prow", "pcol"), P(), P()),
        out_specs=P(None, "prow", None, "pcol"),
        check_vma=False,
    )
```

```python
import functools

import jax
import jax.numpy as jnp
from jax import lax
from jax.experimental import pallas as pl
from jax.experimental.pallas import tpu as pltpu
from jax.sharding import PartitionSpec as P

NPIV = 4
NS = 2
BS = 256
HALF = 128
PIECE = 64
FULL = 32767.0
CHILD_LEVEL = 11.0
F32 = jnp.float32
BF16 = jnp.bfloat16
I16 = jnp.int16
I32 = jnp.int32
SMEM = pl.BlockSpec(memory_space=pltpu.SMEM)
VMEM = pl.BlockSpec(memory_space=pltpu.VMEM)
LIMIT = 60 * 1024 * 1024


def shape(dims, kind):
    return jax.ShapeDtypeStruct(dims, kind)


def call(body, outs, ins, smem=2, flops=0, scratch=()):
    moved = sum(a.size * a.dtype.itemsize for a in ins)
    moved += sum(o.size * o.dtype.itemsize for o in outs)
    return pl.pallas_call(
        body,
        out_shape=outs,
        in_specs=[SMEM] * smem + [VMEM] * (len(ins) - smem),
        out_specs=[VMEM] * len(outs),
        scratch_shapes=list(scratch),
        compiler_params=pltpu.CompilerParams(vmem_limit_bytes=LIMIT),
        cost_estimate=pl.CostEstimate(flops=flops, bytes_accessed=moved, transcendentals=0),
    )(*ins)


def spot(map_ref, child, low, count, test):
    found = jnp.int32(-1)
    value = jnp.int32(-1)
    for step in range(count):
        entry = map_ref[child, low + step]
        hit = test(entry)
        found = jnp.where(hit, low + step, found)
        value = jnp.where(hit, entry, value)
    return found, value


def row_of(map_ref, row, slot):
    return spot(map_ref, slot // 2, 8 * (slot % 2), 8, lambda entry: entry % 16 == row)[1]


def col_of(map_ref, child, source, col):
    return spot(map_ref, child, 4 * source, 4, lambda entry: entry % 8 == col)


def split(value):
    high = value.astype(BF16)
    low = (value - high.astype(F32)).astype(BF16)
    return high, low


def dot(left, right):
    return jnp.dot(left, right, preferred_element_type=F32)


def dot3(left, right):
    (a, b), (c, d) = left, right
    return dot(a, c) + (dot(a, d) + dot(b, c))


CHUNK = 128


def chunk(step):
    return pl.ds(pl.multiple_of(step * CHUNK, CHUNK), CHUNK)


def block(step):
    return slice(step * BS, step * BS + BS)


def one_hot(order):
    spread = lax.broadcasted_iota(I32, (BS, BS), 1).astype(F32)
    return jnp.where(order[:, :1] == spread, 1.0, 0.0).astype(BF16)


def reorder(select, value):
    high = value.astype(BF16)
    rest = value - high.astype(F32)
    middle = rest.astype(BF16)
    last = (rest - middle.astype(F32)).astype(BF16)
    return (dot(select, high) + dot(select, middle)) + dot(select, last)


def level(peak):
    return jnp.ceil(jnp.log2(jnp.full((8, HALF), jnp.maximum(peak, 1e-30))) * 4.0)


def encode(value, n):
    scaled = jnp.abs(value) * jnp.exp2(n * -0.25)[:1, :1]
    code = jnp.minimum(jnp.floor(jnp.sqrt(scaled) * FULL + 0.5), FULL)
    return jnp.where(value < 0.0, -code, code).astype(I32)


def decode(code, n):
    code = code.astype(F32)
    return code * jnp.abs(code) * (jnp.exp2(n.astype(F32)[:1, :1] * 0.25) * (1.0 / (FULL * FULL)))


def cut_front(front_ref, order_ref, *outs):
    select = one_hot(order_ref[...])

    def one(tile, carry):
        halves = [front_ref[pl.ds(half * 8 + tile, BS, stride=16), :] for half in range(2)]
        turned = reorder(select, jnp.concatenate(halves, axis=1))
        for piece in range(4):
            outs[piece][tile] = turned[piece * PIECE : piece * PIECE + PIECE]
        return carry

    lax.fori_loop(0, 8, one, 0)


def begin(map_ref, rc_ref, child_ref, view_ref, o0, o1, o2, o3, left_ref, arrived):
    copies = [
        pltpu.make_async_copy(
            view_ref.at[:, half, 0, :],
            left_ref.at[:, half * HALF : half * HALF + HALF],
            arrived.at[half],
        )
        for half in range(2)
    ]
    for copy in copies:
        copy.start()
    row = rc_ref[0]
    z = row % 4
    second_at = map_ref[row // 8, 2 * (row % 8) + 1] % 4
    for hop, out in enumerate((o0, o1, o2, o3)):
        out[...] = child_ref[jnp.where(second_at == (z + hop) % 4, 1, 0)]
    for copy in copies:
        copy.wait()


def pick_rows(map_ref, rc_ref, order_ref, *refs):
    held, pieces, hops = refs[:4], refs[4:8], refs[8:]
    row = rc_ref[0]
    y, z = row // 4, row % 4
    found, value = spot(map_ref, 0, 0, 4, lambda entry: entry == row)
    live = (found >= 0) & (row < NPIV)
    for hop in range(4):

        @pl.when(live & (found // 2 == (z - hop + 4) % 4))
        def _(hop=hop):
            turned = dot(one_hot(order_ref[...]), held[hop][...]).astype(BF16)
            for piece in range(4):
                pieces[piece][...] = turned[piece * PIECE : piece * PIECE + PIECE]

    @pl.when(jnp.logical_not(live))
    def _():
        for piece in range(4):
            pieces[piece][...] = jnp.zeros((PIECE, 2 * BS), BF16)

    for hop in range(4):
        first = 2 * ((4 * y + (z - hop + 4) % 4) % 8)
        index, value = spot(map_ref, y // 2, first, 2, lambda entry: entry % 4 == z)
        for shift in range(4):

            @pl.when((index >= 0) & ((value // 4) % 4 == (y + shift) % 4))
            def _(hop=hop, shift=shift):
                hops[shift][...] = held[hop][...]


def mix(rc_ref, t0, t1, t2, t3, f0, f1, f2, f3, out_ref, strip, corner):
    y = rc_ref[0] // 4
    for piece, (child, source) in enumerate(((t0, f0), (t1, f1), (t2, f2), (t3, f3))):

        @pl.when(y == piece)
        def _(child=child, source=source):
            strip[...] = child[...].astype(F32)
            corner[...] = source[0]

    n = jnp.full((8, HALF), CHILD_LEVEL)
    for half in range(2):
        out_ref[half * PIECE : half * PIECE + PIECE] = encode(
            strip[:, half * BS : half * BS + BS], n
        ).astype(I16)
    value = corner[...]
    first = level(jnp.max(jnp.abs(value)))
    code = encode(value, first)
    out_ref[2 * PIECE : 3 * PIECE] = code.astype(I16)
    value = value - decode(code, first)
    second = level(jnp.max(jnp.abs(value)))
    out_ref[3 * PIECE : 4 * PIECE] = encode(value, second).astype(I16)
    line = lax.broadcasted_iota(I32, (16, BS), 0)
    scales = jnp.where(line == 0, first[:1, :1], second[:1, :1])
    out_ref[4 * PIECE :] = scales.astype(I32).astype(I16)


def assemble(map_ref, rc_ref, f0, f1, f2, f3, thin, code_ref, work, corner):
    row, col = rc_ref[0], rc_ref[1]
    y = row // 4
    for piece, source in enumerate((f0, f1, f2, f3)):

        @pl.when(y == piece)
        def _(source=source):
            work[...] = source[...]

    for k in range(NPIV):
        scales = thin[k, 4 * PIECE :].astype(I32)
        corner[k] = decode(thin[k, 2 * PIECE : 3 * PIECE].astype(I32), scales[0:1]) + decode(
            thin[k, 3 * PIECE : 4 * PIECE].astype(I32), scales[1:2]
        )
    n = jnp.full((8, HALF), CHILD_LEVEL)
    for index in range(16):
        parent = map_ref[0, index]
        low = (index % 2) * PIECE

        @pl.when(parent % 8 == col)
        def _(index=index, low=low, tile=parent // 8):
            child = decode(thin[index // 2, low : low + PIECE].astype(I32), n)
            work[tile] = work[tile] + child

        if index < NPIV:

            @pl.when(parent < NPIV)
            def _(index=index, low=low, parent=parent):
                child = decode(thin[index // 2, low : low + PIECE].astype(I32), n)
                corner[parent] = corner[parent] + child

    @pl.when(col < NPIV)
    def _():
        work[0] = jnp.zeros((PIECE, BS), F32)

    n = level(jnp.max(jnp.abs(work[...])))
    for tile in range(8):
        code_ref[tile * PIECE : tile * PIECE + PIECE] = encode(work[tile], n).astype(I16)
    z = row % 4
    square = corner[z]
    corner[z] = jnp.zeros((PIECE, BS), F32)
    first = level(jnp.max(jnp.abs(corner[...])))
    low = 8 * PIECE
    for k in range(NPIV):
        code_ref[low + k * PIECE : low + k * PIECE + PIECE] = encode(corner[k], first).astype(I16)
    second = level(jnp.max(jnp.abs(square)))
    code = encode(square, second)
    code_ref[pl.ds(pl.multiple_of(low + z * PIECE, PIECE), PIECE), :] = code.astype(I16)
    square = square - decode(code, second)
    third = level(jnp.max(jnp.abs(square)))
    code_ref[12 * PIECE : 13 * PIECE] = encode(square, third).astype(I16)
    line = lax.broadcasted_iota(I32, (16, BS), 0)
    scales = third[:1, :1]
    for at, n in enumerate((n, first, second)):
        scales = jnp.where(line == at, n[:1, :1], scales)
    code_ref[13 * PIECE :] = scales.astype(I32).astype(I16)


def pack(rc_ref, h0, h1, h2, h3, out_ref):
    y = rc_ref[0] // 4
    for shift, source in enumerate((h0, h1, h2, h3)):
        out_ref[(y - shift + 4) % 4] = source[...]


def factor_corner(code_ref, rest_ref, level_ref, work, chi, clo, xhi, xlo):
    for y in range(4):
        for z in range(4):
            low = z * BS + y * PIECE
            scale = level_ref[4 * y + z].astype(I32)
            for k in range(4):
                code = code_ref[4 * y + z, k * PIECE : k * PIECE + PIECE].astype(I32)
                if k == z:
                    value = decode(code, scale[2:3])
                    value = value + decode(rest_ref[4 * y + z].astype(I32), scale[3:4])
                else:
                    value = decode(code, scale[1:2])
                work[low : low + PIECE, block(k)] = value
    diagonal = lax.broadcasted_iota(I32, (BS, BS), 0) == lax.broadcasted_iota(I32, (BS, BS), 1)
    for k in range(NPIV):
        pivot = work[block(k), block(k)]
        parts = split(pivot)
        on_line = jnp.where(diagonal, pivot, 0.0)
        across = jnp.sum(on_line, axis=0, keepdims=True)
        down = jnp.sum(on_line, axis=1, keepdims=True)
        across = across / (across * across + 1.0)
        down = down / (down * down + 1.0)
        approx = 2.0 * jnp.where(diagonal, across, 0.0) - (down * pivot) * across
        for sweep_index in range(NS - 1):
            pair = split(approx)
            halves = []
            for half in range(2):
                rows = slice(half * CHUNK, half * CHUNK + CHUNK)
                left = split(dot3((pair[0][rows], pair[1][rows]), parts))
                halves.append(2.0 * approx[rows] - dot3(left, pair))
            approx = jnp.concatenate(halves, axis=0)
        xhi[k], xlo[k] = split(approx)
        chi[block(k)], clo[block(k)] = split(work[block(k)])

        def below(step, carry, k=k):
            rows = chunk(step)
            pair = split(dot3(split(work[rows, block(k)]), (xhi[k], xlo[k])))
            work[rows, block(k)] = pair[0].astype(F32) + pair[1].astype(F32)
            for j in range(k + 1, NPIV):
                work[rows, block(j)] = work[rows, block(j)] - dot3(
                    pair, (chi[block(k), block(j)], clo[block(k), block(j)])
                )
            return carry

        lax.fori_loop(2 * (k + 1), 2 * NPIV, below, 0)


SPAN = 2
WIDE = 4


def finish(
    map_ref, rc_ref, corner_ref, rest_ref, level_ref, code_ref, left_ref, near_ref, order_ref,
    front_ref, f0, f1, f2, f3, child_ref, out_ref,
    work, chi, clo, xhi, xlo, uhi, ulo, lhi, llo, own_col, own_block, own_row, parts,
    arrived, own_arrived,
):
    step, group = pl.program_id(0), pl.program_id(1)
    row, col = rc_ref[0], rc_ref[1]
    top_row = row < NPIV
    high_rows = slice(SPAN * BS, 2 * SPAN * BS)

    def at(s, half, tile=0, count=1):
        return pl.ds(tile * BS * 16 + half * 8 + s, count * BS, stride=16)

    def put(s, tile, value):
        for half in range(2):
            out_ref[at(s, half, tile), :] = value[:, half * HALF : half * HALF + HALF]

    def each_child(act):
        for slot in range(4):
            parent = row_of(map_ref, row, slot)
            here = (parent >= 0) & (parent // 16 // SPAN == step)
            for source in range(4):
                found, value = col_of(map_ref, slot // 2, source, col)
                where = jnp.maximum(found, 0)
                start = pl.multiple_of((where % 2) * BS, BS)
                index = 4 * slot + source
                copy = pltpu.make_async_copy(
                    child_ref.at[where // 2, slot, :, pl.ds(start, BS)],
                    parts.at[index],
                    arrived.at[index],
                )

                @pl.when(here & (found >= 0))
                def _(copy=copy, index=index, tile=(parent // 16) % SPAN, s=value // 8):
                    act(copy, index, tile, s)

    def own_copies():
        return [
            pltpu.make_async_copy(source, own_row.at[piece], own_arrived.at[piece])
            for piece, source in enumerate((f0, f1, f2, f3))
        ]

    @pl.when(group == 0)
    def _():
        each_child(lambda copy, index, tile, s: copy.start())

    @pl.when((step == 0) & (group == 0))
    def _():
        @pl.when(top_row)
        def _():
            for copy in own_copies():
                copy.start()

        factor_corner(corner_ref, rest_ref, level_ref, work, chi, clo, xhi, xlo)
        for r in range(NPIV):
            for c in range(NPIV):

                @pl.when((row == r) & (col == c))
                def _(r=r, c=c):
                    own_block[...] = work[block(r), block(c)]

        @pl.when(top_row)
        def _():
            for copy in own_copies():
                copy.wait()

    @pl.when(step == 0)
    def _():
        for k in range(NPIV):
            for piece in range(4):
                scale = level_ref[4 * piece + k].astype(I32)
                for q in range(WIDE):
                    work[piece * PIECE : piece * PIECE + PIECE, block(q)] = decode(
                        code_ref[4 * piece + k, q * PIECE : q * PIECE + PIECE].astype(I32), scale
                    )

            def upper(half, carry, k=k):
                rows = chunk(half)
                put_rows = chunk(2 * k + half)
                for q in range(WIDE):
                    value = work[rows, block(q)]
                    if k:
                        done = slice(0, k * BS)
                        taken = dot3(
                            (chi[put_rows, done], clo[put_rows, done]),
                            (uhi[group, done, block(q)], ulo[group, done, block(q)]),
                        )
                        value = value - taken

                        @pl.when(row == k)
                        def _(taken=taken, q=q):
                            tile = WIDE * group + q
                            for part in range(2):
                                low = part * PIECE
                                own_row[2 * half + part, tile] = (
                                    own_row[2 * half + part, tile] - taken[low : low + PIECE]
                                )

                    high, low = split(value)
                    uhi[group, put_rows, block(q)] = high
                    ulo[group, put_rows, block(q)] = low
                return carry

            lax.fori_loop(0, 2, upper, 0)

    @pl.when(group == 0)
    def _():
        left = work.at[high_rows]
        for k in range(NPIV):
            left[:, block(k)] = left_ref[k]
        for slot in range(2):
            parent = row_of(map_ref, row, slot)
            for index in range(4):
                target = map_ref[0, index]
                cut = slice((index % 2) * BS, (index % 2) * BS + BS)
                for tile in range(SPAN):
                    for k in range(index, NPIV):

                        @pl.when(
                            (parent >= 0) & (parent // 16 == SPAN * step + tile) & (target == k)
                        )
                        def _(slot=slot, index=index, cut=cut, tile=tile, k=k):
                            left[block(tile), block(k)] = left[block(tile), block(k)] + near_ref[
                                index // 2, slot, :, cut
                            ].astype(F32)

        @pl.when((step == 0) & top_row)
        def _():
            left[:BS] = jnp.zeros((BS, NPIV * BS), F32)

        def lower(step, carry):
            lines = [chunk(2 * step + half) for half in range(2)]
            for k in range(NPIV):
                for rows in lines:
                    value = dot3(split(left[rows, block(k)]), (xhi[k], xlo[k]))
                    pair = split(value)
                    lhi[rows, block(k)], llo[rows, block(k)] = pair

                    @pl.when(col == k)
                    def _(value=value, rows=rows):
                        own_col[rows, :] = value

                    for j in range(k + 1, NPIV):
                        left[rows, block(j)] = left[rows, block(j)] - dot3(
                            pair, (chi[block(k), block(j)], clo[block(k), block(j)])
                        )
            return carry

        lax.fori_loop(0, SPAN * BS // (2 * CHUNK), lower, 0)

    def update(step, carry):
        rows = chunk(step)
        for q in range(WIDE):
            upper = (uhi[group, :, block(q)], ulo[group, :, block(q)])
            total = dot3((lhi[rows, :], llo[rows, :]), upper)
            for half in range(2):
                first = step * (CHUNK * 16) + half * 8 + WIDE * group + q
                lines = pl.ds(first, CHUNK, stride=16)
                out_ref[lines, :] = (
                    front_ref[lines, :] - total[:, half * HALF : half * HALF + HALF]
                )
        return carry

    lax.fori_loop(0, SPAN * BS // CHUNK, update, 0)

    @pl.when(group == 1)
    def _():
        top_tile = (step == 0) & top_row

        @pl.when(top_tile)
        def _():
            for s in range(2 * WIDE):
                put(s, 0, jnp.concatenate([own_row[piece, s] for piece in range(4)], axis=0))

        def add(copy, index, tile, s):
            copy.wait()
            turn = top_tile & (tile == 0)

            @pl.when(turn)
            def _():
                turned = dot(one_hot(order_ref[...]), parts[index])
                for half in range(2):
                    rows = at(s, half)
                    lanes = slice(half * HALF, half * HALF + HALF)
                    out_ref[rows, :] = out_ref[rows, :] + turned[:, lanes]

            @pl.when(jnp.logical_not(turn))
            def _():
                for half in range(2):
                    rows = at(s, half, tile)
                    lanes = slice(half * HALF, half * HALF + HALF)
                    out_ref[rows, :] = out_ref[rows, :] + parts[index, :, lanes].astype(F32)

        each_child(add)

        @pl.when(col < NPIV)
        def _():
            @pl.when(jnp.logical_not(top_tile))
            def _():
                put(0, 0, own_col[:BS])

            put(0, 1, own_col[BS:])

            @pl.when(top_tile)
            def _():
                put(0, 0, own_block[...])


def run_finish(child_map, rc, top, front_left, order, view, cuts, child):
    once = pl.Buffered(1)
    rows = pl.BlockSpec((SPAN * BS * 16, HALF), lambda t, g: (t, 0))
    away = pl.BlockSpec(memory_space=pl.ANY)
    return pl.pallas_call(
        finish,
        grid=(4 // SPAN, 2),
        out_shape=shape(view.shape, F32),
        in_specs=[
            SMEM, SMEM,
            pl.BlockSpec((16, 4 * PIECE, BS), lambda t, g: (0, 2, 0), pipeline_mode=once),
            pl.BlockSpec((16, PIECE, BS), lambda t, g: (0, 12, 0), pipeline_mode=once),
            pl.BlockSpec((16, 16, BS), lambda t, g: (0, 13 * PIECE // 16, 0), pipeline_mode=once),
            pl.BlockSpec((16, WIDE * PIECE, BS), lambda t, g: (0, jnp.maximum(t, g), 0)),
            pl.BlockSpec((4, SPAN * BS, BS), lambda t, g: (0, t, 0)),
            pl.BlockSpec((2, 2, BS, 2 * BS), lambda t, g: (0, 0, 0, 0), pipeline_mode=once),
            pl.BlockSpec((BS, HALF), lambda t, g: (0, 0), pipeline_mode=once),
            rows, away, away, away, away, away,
        ],
        out_specs=rows,
        scratch_shapes=[
            pltpu.VMEM((4 * BS, 4 * BS), F32),
            pltpu.VMEM((4 * BS, 4 * BS), BF16), pltpu.VMEM((4 * BS, 4 * BS), BF16),
            pltpu.VMEM((NPIV, BS, BS), BF16), pltpu.VMEM((NPIV, BS, BS), BF16),
            pltpu.VMEM((2, 4 * BS, WIDE * BS), BF16), pltpu.VMEM((2, 4 * BS, WIDE * BS), BF16),
            pltpu.VMEM((SPAN * BS, 4 * BS), BF16), pltpu.VMEM((SPAN * BS, 4 * BS), BF16),
            pltpu.VMEM((SPAN * BS, BS), F32), pltpu.VMEM((BS, BS), F32),
            pltpu.VMEM((4, 8, PIECE, BS), F32),
            pltpu.VMEM((16, BS, BS), BF16),
            pltpu.SemaphoreType.DMA((16,)), pltpu.SemaphoreType.DMA((4,)),
        ],
        compiler_params=pltpu.CompilerParams(vmem_limit_bytes=LIMIT),
        cost_estimate=pl.CostEstimate(
            flops=23 * 2**30, bytes_accessed=32 * 2**20, transcendentals=0
        ),
    )(child_map, rc, top, top, top, top, front_left, child, order, view, *cuts, child)


def shards(front, child_update, child_map, pivots):
    row = lax.axis_index("prow")
    col = lax.axis_index("pcol")
    rc = jnp.stack([row, col]).astype(I32)
    tiles = front.shape[0]

    def along_z(a, hop):
        return lax.ppermute(
            a, "prow", [(4 * i + j, 4 * i + (j + hop) % 4) for i in range(4) for j in range(4)]
        )

    def along_y(a, hop):
        return lax.ppermute(
            a, "prow", [(4 * i + j, 4 * ((i + hop) % 4) + j) for i in range(4) for j in range(4)]
        )

    def from_plane(a, hop):
        return lax.ppermute(a, "prow", [(j, 4 * hop + j) for j in range(4)])

    def spread(pieces):
        return [pieces[0]] + [from_plane(pieces[hop], hop) for hop in (1, 2, 3)]

    strip = shape((BS, 2 * BS), BF16)
    view = front.reshape(tiles, BS, 8, 2, HALF).transpose(0, 1, 3, 2, 4)
    *zs, front_left = pl.pallas_call(
        begin,
        out_shape=[strip] * 4 + [shape((tiles * BS, BS), F32)],
        in_specs=[SMEM, SMEM, VMEM, pl.BlockSpec(memory_space=pl.ANY)],
        out_specs=[VMEM] * 5,
        scratch_shapes=[pltpu.SemaphoreType.DMA((2,))],
        compiler_params=pltpu.CompilerParams(vmem_limit_bytes=LIMIT),
        cost_estimate=pl.CostEstimate(flops=0, bytes_accessed=4 * 2**20, transcendentals=0),
    )(child_map, rc, child_update.reshape(2, BS, 2 * BS), view.reshape(tiles * BS, 2, 8, HALF))
    view = view.reshape(tiles * BS * 16, HALF)
    order = jnp.where(
        row < NPIV, pivots[jnp.minimum(row, NPIV - 1)], jnp.arange(BS, dtype=I32)
    )
    order = jnp.broadcast_to(order.astype(F32)[:, None], (BS, HALF))
    order, *zs = lax.optimization_barrier((order, *zs))
    zs = [zs[0]] + [along_z(zs[hop], hop) for hop in (1, 2, 3)]
    cuts = pl.pallas_call(
        cut_front,
        grid=(1,),
        out_shape=[shape((8, PIECE, BS), F32)] * 4,
        in_specs=[
            pl.BlockSpec((BS * 16, HALF), lambda t: (0, 0)),
            pl.BlockSpec((BS, HALF), lambda t: (0, 0)),
        ],
        out_specs=[pl.BlockSpec((8, PIECE, BS), lambda t: (0, 0, 0))] * 4,
        compiler_params=pltpu.CompilerParams(vmem_limit_bytes=LIMIT),
        cost_estimate=pl.CostEstimate(flops=2**30, bytes_accessed=4 * 2**20, transcendentals=0),
    )(view, order)
    moved = spread(cuts)

    front_left = lax.all_gather(front_left, "pcol", axis=0, tiled=False)

    thin = shape((PIECE, 2 * BS), BF16)
    zs, unused = lax.optimization_barrier((zs, moved[1]))
    picked = call(
        pick_rows, [thin] * 4 + [strip] * 4, [child_map, rc, order, *zs], flops=20 * 2**30
    )
    thin = spread(picked[:4])
    ys = [picked[4]] + [along_y(picked[4 + hop], hop) for hop in (1, 2, 3)]

    (thin,) = call(
        mix,
        [shape((4 * PIECE + 16, BS), I16)],
        [rc, *thin, *moved],
        smem=1,
        scratch=[pltpu.VMEM((PIECE, 2 * BS), F32), pltpu.VMEM((PIECE, BS), F32)],
    )
    thin = lax.all_gather(thin, "pcol", axis=0, tiled=False)
    (child,) = call(pack, [shape((4, BS, 2 * BS), BF16)], [rc, *ys], smem=1)
    thin, child = lax.optimization_barrier((thin, child))
    (code,) = call(
        assemble,
        [shape((13 * PIECE + 16, BS), I16)],
        [child_map, rc, *moved, thin],
        scratch=[pltpu.VMEM((8, PIECE, BS), F32), pltpu.VMEM((NPIV, PIECE, BS), F32)],
    )

    child = lax.all_gather(child, "pcol", axis=0, tiled=False)
    top = lax.all_gather(code, "prow", axis=0, tiled=False)

    done = run_finish(child_map, rc, top, front_left, order, view, cuts, child)
    done = done.reshape(tiles, BS, 2, 8, HALF).transpose(0, 1, 3, 2, 4)
    return done.reshape(front.shape)


def solution(mesh):
    return jax.shard_map(
        shards,
        mesh=mesh,
        in_specs=(P(None, "prow", None, "pcol"), P("prow", "pcol"), P(), P()),
        out_specs=P(None, "prow", None, "pcol"),
        check_vma=False,
    )
```

```python
import functools

import jax
import jax.numpy as jnp
from jax import lax
from jax.experimental import pallas as pl
from jax.experimental.pallas import tpu as pltpu
from jax.sharding import PartitionSpec as P

NPIV = 4
NS = 2
BS = 256
HALF = 128
PIECE = 64
FULL = 32767.0
CHILD_LEVEL = 11.0
F32 = jnp.float32
BF16 = jnp.bfloat16
I16 = jnp.int16
I32 = jnp.int32
SMEM = pl.BlockSpec(memory_space=pltpu.SMEM)
VMEM = pl.BlockSpec(memory_space=pltpu.VMEM)
LIMIT = 60 * 1024 * 1024


def shape(dims, kind):
    return jax.ShapeDtypeStruct(dims, kind)


def call(body, outs, ins, smem=2, flops=0, scratch=()):
    moved = sum(a.size * a.dtype.itemsize for a in ins)
    moved += sum(o.size * o.dtype.itemsize for o in outs)
    return pl.pallas_call(
        body,
        out_shape=outs,
        in_specs=[SMEM] * smem + [VMEM] * (len(ins) - smem),
        out_specs=[VMEM] * len(outs),
        scratch_shapes=list(scratch),
        compiler_params=pltpu.CompilerParams(vmem_limit_bytes=LIMIT),
        cost_estimate=pl.CostEstimate(flops=flops, bytes_accessed=moved, transcendentals=0),
    )(*ins)


def spot(map_ref, child, low, count, test):
    found = jnp.int32(-1)
    value = jnp.int32(-1)
    for step in range(count):
        entry = map_ref[child, low + step]
        hit = test(entry)
        found = jnp.where(hit, low + step, found)
        value = jnp.where(hit, entry, value)
    return found, value


def row_of(map_ref, row, slot):
    return spot(map_ref, slot // 2, 8 * (slot % 2), 8, lambda entry: entry % 16 == row)[1]


def col_of(map_ref, child, source, col):
    return spot(map_ref, child, 4 * source, 4, lambda entry: entry % 8 == col)


def split(value):
    high = value.astype(BF16)
    low = (value - high.astype(F32)).astype(BF16)
    return high, low


def dot(left, right):
    return jnp.dot(left, right, preferred_element_type=F32)


def dot3(left, right):
    (a, b), (c, d) = left, right
    rows = a.shape[0]
    both = dot(jnp.concatenate([a, b], axis=0), c)
    return both[:rows] + (both[rows:] + dot(a, d))


def block(step):
    return slice(step * BS, step * BS + BS)


def one_hot(order):
    spread = lax.broadcasted_iota(I32, (BS, BS), 1).astype(F32)
    return jnp.where(order[:, :1] == spread, 1.0, 0.0).astype(BF16)


def reorder(select, value):
    high = value.astype(BF16)
    rest = value - high.astype(F32)
    middle = rest.astype(BF16)
    last = (rest - middle.astype(F32)).astype(BF16)
    return (dot(select, high) + dot(select, middle)) + dot(select, last)


def level(peak):
    return jnp.ceil(jnp.log2(jnp.full((8, HALF), jnp.maximum(peak, 1e-30))) * 4.0)


def encode(value, n):
    scaled = jnp.abs(value) * jnp.exp2(n * -0.25)[:1, :1]
    code = jnp.minimum(jnp.floor(jnp.sqrt(scaled) * FULL + 0.5), FULL)
    return jnp.where(value < 0.0, -code, code).astype(I32)


def decode(code, n):
    code = code.astype(F32)
    return code * jnp.abs(code) * (jnp.exp2(n.astype(F32)[:1, :1] * 0.25) * (1.0 / (FULL * FULL)))


def cut_front(front_ref, order_ref, *outs):
    select = one_hot(order_ref[...])

    def one(tile, carry):
        halves = [front_ref[pl.ds(half * 8 + tile, BS, stride=16), :] for half in range(2)]
        turned = reorder(select, jnp.concatenate(halves, axis=1))
        for piece in range(4):
            outs[piece][tile] = turned[piece * PIECE : piece * PIECE + PIECE]
        return carry

    lax.fori_loop(0, 8, one, 0)


def begin(map_ref, rc_ref, child_ref, view_ref, o0, o1, o2, o3, left_ref, arrived):
    copies = [
        pltpu.make_async_copy(
            view_ref.at[:, half, 0, :],
            left_ref.at[:, half * HALF : half * HALF + HALF],
            arrived.at[half],
        )
        for half in range(2)
    ]
    for copy in copies:
        copy.start()
    row = rc_ref[0]
    z = row % 4
    second_at = map_ref[row // 8, 2 * (row % 8) + 1] % 4
    for hop, out in enumerate((o0, o1, o2, o3)):
        out[...] = child_ref[jnp.where(second_at == (z + hop) % 4, 1, 0)]
    for copy in copies:
        copy.wait()


def pick_rows(map_ref, rc_ref, order_ref, *refs):
    held, pieces, hops = refs[:4], refs[4:8], refs[8:]
    row = rc_ref[0]
    y, z = row // 4, row % 4
    found, value = spot(map_ref, 0, 0, 4, lambda entry: entry == row)
    live = (found >= 0) & (row < NPIV)
    for hop in range(4):

        @pl.when(live & (found // 2 == (z - hop + 4) % 4))
        def _(hop=hop):
            turned = dot(one_hot(order_ref[...]), held[hop][...]).astype(BF16)
            for piece in range(4):
                pieces[piece][...] = turned[piece * PIECE : piece * PIECE + PIECE]

    @pl.when(jnp.logical_not(live))
    def _():
        for piece in range(4):
            pieces[piece][...] = jnp.zeros((PIECE, 2 * BS), BF16)

    for hop in range(4):
        first = 2 * ((4 * y + (z - hop + 4) % 4) % 8)
        index, value = spot(map_ref, y // 2, first, 2, lambda entry: entry % 4 == z)
        for shift in range(4):

            @pl.when((index >= 0) & ((value // 4) % 4 == (y + shift) % 4))
            def _(hop=hop, shift=shift):
                hops[shift][...] = held[hop][...]


def mix(rc_ref, t0, t1, t2, t3, f0, f1, f2, f3, out_ref, strip, corner):
    y = rc_ref[0] // 4
    for piece, (child, source) in enumerate(((t0, f0), (t1, f1), (t2, f2), (t3, f3))):

        @pl.when(y == piece)
        def _(child=child, source=source):
            strip[...] = child[...].astype(F32)
            corner[...] = source[0]

    n = jnp.full((8, HALF), CHILD_LEVEL)
    for half in range(2):
        out_ref[half * PIECE : half * PIECE + PIECE] = encode(
            strip[:, half * BS : half * BS + BS], n
        ).astype(I16)
    value = corner[...]
    first = level(jnp.max(jnp.abs(value)))
    code = encode(value, first)
    out_ref[2 * PIECE : 3 * PIECE] = code.astype(I16)
    value = value - decode(code, first)
    second = level(jnp.max(jnp.abs(value)))
    out_ref[3 * PIECE : 4 * PIECE] = encode(value, second).astype(I16)
    line = lax.broadcasted_iota(I32, (16, BS), 0)
    scales = jnp.where(line == 0, first[:1, :1], second[:1, :1])
    out_ref[4 * PIECE :] = scales.astype(I32).astype(I16)


def assemble(map_ref, rc_ref, f0, f1, f2, f3, thin, code_ref, work, corner):
    row, col = rc_ref[0], rc_ref[1]
    y = row // 4
    for piece, source in enumerate((f0, f1, f2, f3)):

        @pl.when(y == piece)
        def _(source=source):
            work[...] = source[...]

    for k in range(NPIV):
        scales = thin[k, 4 * PIECE :].astype(I32)
        corner[k] = decode(thin[k, 2 * PIECE : 3 * PIECE].astype(I32), scales[0:1]) + decode(
            thin[k, 3 * PIECE : 4 * PIECE].astype(I32), scales[1:2]
        )
    n = jnp.full((8, HALF), CHILD_LEVEL)
    for index in range(16):
        parent = map_ref[0, index]
        low = (index % 2) * PIECE

        @pl.when(parent % 8 == col)
        def _(index=index, low=low, tile=parent // 8):
            child = decode(thin[index // 2, low : low + PIECE].astype(I32), n)
            work[tile] = work[tile] + child

        if index < NPIV:

            @pl.when(parent < NPIV)
            def _(index=index, low=low, parent=parent):
                child = decode(thin[index // 2, low : low + PIECE].astype(I32), n)
                corner[parent] = corner[parent] + child

    @pl.when(col < NPIV)
    def _():
        work[0] = jnp.zeros((PIECE, BS), F32)

    n = level(jnp.max(jnp.abs(work[...])))
    for tile in range(8):
        code_ref[tile * PIECE : tile * PIECE + PIECE] = encode(work[tile], n).astype(I16)
    z = row % 4
    square = corner[z]
    corner[z] = jnp.zeros((PIECE, BS), F32)
    first = level(jnp.max(jnp.abs(corner[...])))
    low = 8 * PIECE
    for k in range(NPIV):
        code_ref[low + k * PIECE : low + k * PIECE + PIECE] = encode(corner[k], first).astype(I16)
    second = level(jnp.max(jnp.abs(square)))
    code = encode(square, second)
    code_ref[pl.ds(pl.multiple_of(low + z * PIECE, PIECE), PIECE), :] = code.astype(I16)
    square = square - decode(code, second)
    third = level(jnp.max(jnp.abs(square)))
    code_ref[12 * PIECE : 13 * PIECE] = encode(square, third).astype(I16)
    line = lax.broadcasted_iota(I32, (16, BS), 0)
    scales = third[:1, :1]
    for at, n in enumerate((n, first, second)):
        scales = jnp.where(line == at, n[:1, :1], scales)
    code_ref[13 * PIECE :] = scales.astype(I32).astype(I16)


def pack(rc_ref, h0, h1, h2, h3, out_ref):
    y = rc_ref[0] // 4
    for shift, source in enumerate((h0, h1, h2, h3)):
        out_ref[(y - shift + 4) % 4] = source[...]


def factor_corner(code_ref, rest_ref, level_ref, work, chi, clo, xhi, xlo):
    for y in range(4):
        for z in range(4):
            low = z * BS + y * PIECE
            scale = level_ref[4 * y + z].astype(I32)
            for k in range(4):
                code = code_ref[4 * y + z, k * PIECE : k * PIECE + PIECE].astype(I32)
                if k == z:
                    value = decode(code, scale[2:3])
                    value = value + decode(rest_ref[4 * y + z].astype(I32), scale[3:4])
                else:
                    value = decode(code, scale[1:2])
                work[low : low + PIECE, block(k)] = value
    diagonal = lax.broadcasted_iota(I32, (BS, BS), 0) == lax.broadcasted_iota(I32, (BS, BS), 1)
    for k in range(NPIV):
        pivot = work[block(k), block(k)]
        parts = split(pivot)
        on_line = jnp.where(diagonal, pivot, 0.0)
        across = jnp.sum(on_line, axis=0, keepdims=True)
        down = jnp.sum(on_line, axis=1, keepdims=True)
        across = across / (across * across + 1.0)
        down = down / (down * down + 1.0)
        approx = 2.0 * jnp.where(diagonal, across, 0.0) - (down * pivot) * across
        for sweep_index in range(NS - 1):
            pair = split(approx)
            approx = 2.0 * approx - dot3(split(dot3(pair, parts)), pair)
        xhi[k], xlo[k] = split(approx)
        chi[block(k)], clo[block(k)] = split(work[block(k)])
        if k + 1 < NPIV:
            below = slice((k + 1) * BS, NPIV * BS)
            pair = split(dot3(split(work[below, block(k)]), (xhi[k], xlo[k])))
            work[below, block(k)] = pair[0].astype(F32) + pair[1].astype(F32)
            work[below, below] = work[below, below] - dot3(
                pair, (chi[block(k), below], clo[block(k), below])
            )


SPAN = 2
WIDE = 4


def finish(
    map_ref, rc_ref, corner_ref, rest_ref, level_ref, code_ref, left_ref, near_ref, order_ref,
    front_ref, f0, f1, f2, f3, child_ref, out_ref,
    work, chi, clo, xhi, xlo, uhi, ulo, lower, own_col, own_block, own_row, parts,
    arrived, own_arrived,
):
    step, group = pl.program_id(0), pl.program_id(1)
    row, col = rc_ref[0], rc_ref[1]
    top_row = row < NPIV
    high_rows = slice(SPAN * BS, 2 * SPAN * BS)

    def at(s, half, tile=0, count=1):
        return pl.ds(tile * BS * 16 + half * 8 + s, count * BS, stride=16)

    def put(s, tile, value):
        for half in range(2):
            out_ref[at(s, half, tile), :] = value[:, half * HALF : half * HALF + HALF]

    def each_child(act):
        for slot in range(4):
            parent = row_of(map_ref, row, slot)
            here = (parent >= 0) & (parent // 16 // SPAN == step)
            for source in range(4):
                found, value = col_of(map_ref, slot // 2, source, col)
                where = jnp.maximum(found, 0)
                start = pl.multiple_of((where % 2) * BS, BS)
                index = 4 * slot + source
                copy = pltpu.make_async_copy(
                    child_ref.at[where // 2, slot, :, pl.ds(start, BS)],
                    parts.at[index],
                    arrived.at[index],
                )

                @pl.when(here & (found >= 0))
                def _(copy=copy, index=index, tile=(parent // 16) % SPAN, s=value // 8):
                    act(copy, index, tile, s)

    def own_copies():
        return [
            pltpu.make_async_copy(source, own_row.at[piece], own_arrived.at[piece])
            for piece, source in enumerate((f0, f1, f2, f3))
        ]

    @pl.when(group == 0)
    def _():
        each_child(lambda copy, index, tile, s: copy.start())

    @pl.when((step == 0) & (group == 0))
    def _():
        @pl.when(top_row)
        def _():
            for copy in own_copies():
                copy.start()

        factor_corner(corner_ref, rest_ref, level_ref, work, chi, clo, xhi, xlo)
        for r in range(NPIV):
            for c in range(NPIV):

                @pl.when((row == r) & (col == c))
                def _(r=r, c=c):
                    own_block[...] = work[block(r), block(c)]

        @pl.when(top_row)
        def _():
            for copy in own_copies():
                copy.wait()

    @pl.when(step == 0)
    def _():
        for k in range(NPIV):
            for piece in range(4):
                low = k * BS + piece * PIECE
                scale = level_ref[4 * piece + k].astype(I32)
                for q in range(WIDE):
                    work[low : low + PIECE, block(q)] = decode(
                        code_ref[4 * piece + k, q * PIECE : q * PIECE + PIECE].astype(I32), scale
                    )
        for k in range(NPIV):
            uhi[group, block(k)], ulo[group, block(k)] = split(work[block(k)])
            if k + 1 == NPIV:
                break
            below = slice((k + 1) * BS, NPIV * BS)
            for pair in range(WIDE // 2):
                wide = slice(2 * pair * BS, 2 * (pair + 1) * BS)
                taken = dot3(
                    (chi[below, block(k)], clo[below, block(k)]),
                    (uhi[group, block(k), wide], ulo[group, block(k), wide]),
                )
                work[below, wide] = work[below, wide] - taken
                for j in range(k + 1, NPIV):

                    @pl.when(row == j)
                    def _(taken=taken, pair=pair, j=j, k=k):
                        for piece in range(4):
                            low = (j - k - 1) * BS + piece * PIECE
                            for q in range(2):
                                tile = WIDE * group + 2 * pair + q
                                own_row[piece, tile] = (
                                    own_row[piece, tile] - taken[low : low + PIECE, block(q)]
                                )

    @pl.when(group == 0)
    def _():
        left = work.at[high_rows]
        for k in range(NPIV):
            left[:, block(k)] = left_ref[k]
        for slot in range(2):
            parent = row_of(map_ref, row, slot)
            for index in range(4):
                target = map_ref[0, index]
                cut = slice((index % 2) * BS, (index % 2) * BS + BS)
                for tile in range(SPAN):
                    for k in range(index, NPIV):

                        @pl.when(
                            (parent >= 0) & (parent // 16 == SPAN * step + tile) & (target == k)
                        )
                        def _(slot=slot, index=index, cut=cut, tile=tile, k=k):
                            left[block(tile), block(k)] = left[block(tile), block(k)] + near_ref[
                                index // 2, slot, :, cut
                            ].astype(F32)

        @pl.when((step == 0) & top_row)
        def _():
            left[:BS] = jnp.zeros((BS, NPIV * BS), F32)

        for k in range(NPIV):
            value = dot3(split(left[:, block(k)]), (xhi[k], xlo[k]))
            lower[: SPAN * BS, block(k)], lower[SPAN * BS :, block(k)] = split(value)

            @pl.when(col == k)
            def _(value=value):
                own_col[...] = value

            if k + 1 < NPIV:
                rest = slice((k + 1) * BS, NPIV * BS)
                both = dot(lower[:, block(k)], chi[block(k), rest])
                both = both[: SPAN * BS] + both[SPAN * BS :]
                both = both + dot(lower[: SPAN * BS, block(k)], clo[block(k), rest])
                left[:, rest] = left[:, rest] - both

    for pair in range(WIDE // 2):
        wide = slice(2 * pair * BS, 2 * (pair + 1) * BS)
        both = dot(lower[...], uhi[group, :, wide])
        total = both[: SPAN * BS] + (
            both[SPAN * BS :] + dot(lower[: SPAN * BS], ulo[group, :, wide])
        )
        for q in range(2):
            for half in range(2):
                rows = at(WIDE * group + 2 * pair + q, half, 0, SPAN)
                low = q * BS + half * HALF
                out_ref[rows, :] = front_ref[rows, :] - total[:, low : low + HALF]

    @pl.when(group == 1)
    def _():
        top_tile = (step == 0) & top_row

        @pl.when(top_tile)
        def _():
            for s in range(2 * WIDE):
                put(s, 0, jnp.concatenate([own_row[piece, s] for piece in range(4)], axis=0))

        def add(copy, index, tile, s):
            copy.wait()
            turn = top_tile & (tile == 0)

            @pl.when(turn)
            def _():
                turned = dot(one_hot(order_ref[...]), parts[index])
                for half in range(2):
                    rows = at(s, half)
                    lanes = slice(half * HALF, half * HALF + HALF)
                    out_ref[rows, :] = out_ref[rows, :] + turned[:, lanes]

            @pl.when(jnp.logical_not(turn))
            def _():
                for half in range(2):
                    rows = at(s, half, tile)
                    lanes = slice(half * HALF, half * HALF + HALF)
                    out_ref[rows, :] = out_ref[rows, :] + parts[index, :, lanes].astype(F32)

        each_child(add)

        @pl.when(col < NPIV)
        def _():
            @pl.when(jnp.logical_not(top_tile))
            def _():
                put(0, 0, own_col[:BS])

            put(0, 1, own_col[BS:])

            @pl.when(top_tile)
            def _():
                put(0, 0, own_block[...])


def run_finish(child_map, rc, top, front_left, order, view, cuts, child):
    once = pl.Buffered(1)
    rows = pl.BlockSpec((SPAN * BS * 16, HALF), lambda t, g: (t, 0))
    away = pl.BlockSpec(memory_space=pl.ANY)
    return pl.pallas_call(
        finish,
        grid=(4 // SPAN, 2),
        out_shape=shape(view.shape, F32),
        in_specs=[
            SMEM, SMEM,
            pl.BlockSpec((16, 4 * PIECE, BS), lambda t, g: (0, 2, 0), pipeline_mode=once),
            pl.BlockSpec((16, PIECE, BS), lambda t, g: (0, 12, 0), pipeline_mode=once),
            pl.BlockSpec((16, 16, BS), lambda t, g: (0, 13 * PIECE // 16, 0), pipeline_mode=once),
            pl.BlockSpec((16, WIDE * PIECE, BS), lambda t, g: (0, jnp.maximum(t, g), 0)),
            pl.BlockSpec((4, SPAN * BS, BS), lambda t, g: (0, t, 0)),
            pl.BlockSpec((2, 2, BS, 2 * BS), lambda t, g: (0, 0, 0, 0), pipeline_mode=once),
            pl.BlockSpec((BS, HALF), lambda t, g: (0, 0), pipeline_mode=once),
            rows, away, away, away, away, away,
        ],
        out_specs=rows,
        scratch_shapes=[
            pltpu.VMEM((4 * BS, 4 * BS), F32),
            pltpu.VMEM((4 * BS, 4 * BS), BF16), pltpu.VMEM((4 * BS, 4 * BS), BF16),
            pltpu.VMEM((NPIV, BS, BS), BF16), pltpu.VMEM((NPIV, BS, BS), BF16),
            pltpu.VMEM((2, 4 * BS, WIDE * BS), BF16), pltpu.VMEM((2, 4 * BS, WIDE * BS), BF16),
            pltpu.VMEM((2 * SPAN * BS, 4 * BS), BF16),
            pltpu.VMEM((SPAN * BS, BS), F32), pltpu.VMEM((BS, BS), F32),
            pltpu.VMEM((4, 8, PIECE, BS), F32),
            pltpu.VMEM((16, BS, BS), BF16),
            pltpu.SemaphoreType.DMA((16,)), pltpu.SemaphoreType.DMA((4,)),
        ],
        compiler_params=pltpu.CompilerParams(vmem_limit_bytes=LIMIT),
        cost_estimate=pl.CostEstimate(
            flops=23 * 2**30, bytes_accessed=32 * 2**20, transcendentals=0
        ),
    )(child_map, rc, top, top, top, top, front_left, child, order, view, *cuts, child)


def shards(front, child_update, child_map, pivots):
    row = lax.axis_index("prow")
    col = lax.axis_index("pcol")
    rc = jnp.stack([row, col]).astype(I32)
    tiles = front.shape[0]

    def along_z(a, hop):
        return lax.ppermute(
            a, "prow", [(4 * i + j, 4 * i + (j + hop) % 4) for i in range(4) for j in range(4)]
        )

    def along_y(a, hop):
        return lax.ppermute(
            a, "prow", [(4 * i + j, 4 * ((i + hop) % 4) + j) for i in range(4) for j in range(4)]
        )

    def from_plane(a, hop):
        return lax.ppermute(a, "prow", [(j, 4 * hop + j) for j in range(4)])

    def spread(pieces):
        return [pieces[0]] + [from_plane(pieces[hop], hop) for hop in (1, 2, 3)]

    strip = shape((BS, 2 * BS), BF16)
    view = front.reshape(tiles, BS, 8, 2, HALF).transpose(0, 1, 3, 2, 4)
    *zs, front_left = pl.pallas_call(
        begin,
        out_shape=[strip] * 4 + [shape((tiles * BS, BS), F32)],
        in_specs=[SMEM, SMEM, VMEM, pl.BlockSpec(memory_space=pl.ANY)],
        out_specs=[VMEM] * 5,
        scratch_shapes=[pltpu.SemaphoreType.DMA((2,))],
        compiler_params=pltpu.CompilerParams(vmem_limit_bytes=LIMIT),
        cost_estimate=pl.CostEstimate(flops=0, bytes_accessed=4 * 2**20, transcendentals=0),
    )(child_map, rc, child_update.reshape(2, BS, 2 * BS), view.reshape(tiles * BS, 2, 8, HALF))
    view = view.reshape(tiles * BS * 16, HALF)
    order = jnp.where(
        row < NPIV, pivots[jnp.minimum(row, NPIV - 1)], jnp.arange(BS, dtype=I32)
    )
    order = jnp.broadcast_to(order.astype(F32)[:, None], (BS, HALF))
    order, *zs = lax.optimization_barrier((order, *zs))
    zs = [zs[0]] + [along_z(zs[hop], hop) for hop in (1, 2, 3)]
    cuts = pl.pallas_call(
        cut_front,
        grid=(1,),
        out_shape=[shape((8, PIECE, BS), F32)] * 4,
        in_specs=[
            pl.BlockSpec((BS * 16, HALF), lambda t: (0, 0)),
            pl.BlockSpec((BS, HALF), lambda t: (0, 0)),
        ],
        out_specs=[pl.BlockSpec((8, PIECE, BS), lambda t: (0, 0, 0))] * 4,
        compiler_params=pltpu.CompilerParams(vmem_limit_bytes=LIMIT),
        cost_estimate=pl.CostEstimate(flops=2**30, bytes_accessed=4 * 2**20, transcendentals=0),
    )(view, order)
    moved = spread(cuts)

    front_left = lax.all_gather(front_left, "pcol", axis=0, tiled=False)

    thin = shape((PIECE, 2 * BS), BF16)
    zs, unused = lax.optimization_barrier((zs, moved[1]))
    picked = call(
        pick_rows, [thin] * 4 + [strip] * 4, [child_map, rc, order, *zs], flops=20 * 2**30
    )
    thin = spread(picked[:4])
    ys = [picked[4]] + [along_y(picked[4 + hop], hop) for hop in (1, 2, 3)]

    (thin,) = call(
        mix,
        [shape((4 * PIECE + 16, BS), I16)],
        [rc, *thin, *moved],
        smem=1,
        scratch=[pltpu.VMEM((PIECE, 2 * BS), F32), pltpu.VMEM((PIECE, BS), F32)],
    )
    thin = lax.all_gather(thin, "pcol", axis=0, tiled=False)
    (child,) = call(pack, [shape((4, BS, 2 * BS), BF16)], [rc, *ys], smem=1)
    thin, child = lax.optimization_barrier((thin, child))
    (code,) = call(
        assemble,
        [shape((13 * PIECE + 16, BS), I16)],
        [child_map, rc, *moved, thin],
        scratch=[pltpu.VMEM((8, PIECE, BS), F32), pltpu.VMEM((NPIV, PIECE, BS), F32)],
    )

    child = lax.all_gather(child, "pcol", axis=0, tiled=False)
    top = lax.all_gather(code, "prow", axis=0, tiled=False)

    done = run_finish(child_map, rc, top, front_left, order, view, cuts, child)
    done = done.reshape(tiles, BS, 2, 8, HALF).transpose(0, 1, 3, 2, 4)
    return done.reshape(front.shape)


def solution(mesh):
    return jax.shard_map(
        shards,
        mesh=mesh,
        in_specs=(P(None, "prow", None, "pcol"), P("prow", "pcol"), P(), P()),
        out_specs=P(None, "prow", None, "pcol"),
        check_vma=False,
    )
```

```python
import functools

import jax
import jax.numpy as jnp
from jax import lax
from jax.experimental import pallas as pl
from jax.experimental.pallas import tpu as pltpu
from jax.sharding import PartitionSpec as P

NPIV = 4
NS = 2
BS = 256
HALF = 128
PIECE = 64
FULL = 32767.0
CHILD_LEVEL = 11.0
F32 = jnp.float32
BF16 = jnp.bfloat16
I16 = jnp.int16
I32 = jnp.int32
SMEM = pl.BlockSpec(memory_space=pltpu.SMEM)
VMEM = pl.BlockSpec(memory_space=pltpu.VMEM)
LIMIT = 60 * 1024 * 1024


def shape(dims, kind):
    return jax.ShapeDtypeStruct(dims, kind)


def call(body, outs, ins, smem=2, flops=0, scratch=()):
    moved = sum(a.size * a.dtype.itemsize for a in ins)
    moved += sum(o.size * o.dtype.itemsize for o in outs)
    return pl.pallas_call(
        body,
        out_shape=outs,
        in_specs=[SMEM] * smem + [VMEM] * (len(ins) - smem),
        out_specs=[VMEM] * len(outs),
        scratch_shapes=list(scratch),
        compiler_params=pltpu.CompilerParams(vmem_limit_bytes=LIMIT),
        cost_estimate=pl.CostEstimate(flops=flops, bytes_accessed=moved, transcendentals=0),
    )(*ins)


def spot(map_ref, child, low, count, test):
    found = jnp.int32(-1)
    value = jnp.int32(-1)
    for step in range(count):
        entry = map_ref[child, low + step]
        hit = test(entry)
        found = jnp.where(hit, low + step, found)
        value = jnp.where(hit, entry, value)
    return found, value


def row_of(map_ref, row, slot):
    return spot(map_ref, slot // 2, 8 * (slot % 2), 8, lambda entry: entry % 16 == row)[1]


def col_of(map_ref, child, source, col):
    return spot(map_ref, child, 4 * source, 4, lambda entry: entry % 8 == col)


def split(value):
    high = value.astype(BF16)
    low = (value - high.astype(F32)).astype(BF16)
    return high, low


def dot(left, right):
    return jnp.dot(left, right, preferred_element_type=F32)


def dot3(left, right):
    (a, b), (c, d) = left, right
    rows = a.shape[0]
    both = dot(jnp.concatenate([a, b], axis=0), c)
    return both[:rows] + (both[rows:] + dot(a, d))


def block(step):
    return slice(step * BS, step * BS + BS)


def one_hot(order):
    spread = lax.broadcasted_iota(I32, (BS, BS), 1).astype(F32)
    return jnp.where(order[:, :1] == spread, 1.0, 0.0).astype(BF16)


def reorder(select, value):
    high = value.astype(BF16)
    rest = value - high.astype(F32)
    middle = rest.astype(BF16)
    last = (rest - middle.astype(F32)).astype(BF16)
    return (dot(select, high) + dot(select, middle)) + dot(select, last)


def level(peak):
    return jnp.ceil(jnp.log2(jnp.full((8, HALF), jnp.maximum(peak, 1e-30))) * 4.0)


def encode(value, n):
    scaled = jnp.abs(value) * jnp.exp2(n * -0.25)[:1, :1]
    code = jnp.minimum(jnp.floor(jnp.sqrt(scaled) * FULL + 0.5), FULL)
    return jnp.where(value < 0.0, -code, code).astype(I32)


def decode(code, n):
    code = code.astype(F32)
    return code * jnp.abs(code) * (jnp.exp2(n.astype(F32)[:1, :1] * 0.25) * (1.0 / (FULL * FULL)))


def cut_front(front_ref, order_ref, *outs):
    select = one_hot(order_ref[...])

    def one(tile, carry):
        halves = [front_ref[pl.ds(half * 8 + tile, BS, stride=16), :] for half in range(2)]
        turned = reorder(select, jnp.concatenate(halves, axis=1))
        for piece in range(4):
            outs[piece][tile] = turned[piece * PIECE : piece * PIECE + PIECE]
        return carry

    lax.fori_loop(0, 8, one, 0)


def begin(map_ref, rc_ref, child_ref, view_ref, o0, o1, o2, o3, left_ref, arrived):
    copies = [
        pltpu.make_async_copy(
            view_ref.at[:, half, 0, :],
            left_ref.at[:, half * HALF : half * HALF + HALF],
            arrived.at[half],
        )
        for half in range(2)
    ]
    for copy in copies:
        copy.start()
    row = rc_ref[0]
    z = row % 4
    second_at = map_ref[row // 8, 2 * (row % 8) + 1] % 4
    for hop, out in enumerate((o0, o1, o2, o3)):
        out[...] = child_ref[jnp.where(second_at == (z + hop) % 4, 1, 0)]
    for copy in copies:
        copy.wait()


def pick_rows(map_ref, rc_ref, order_ref, *refs):
    held, pieces, hops = refs[:4], refs[4:8], refs[8:]
    row = rc_ref[0]
    y, z = row // 4, row % 4
    found, value = spot(map_ref, 0, 0, 4, lambda entry: entry == row)
    live = (found >= 0) & (row < NPIV)
    for hop in range(4):

        @pl.when(live & (found // 2 == (z - hop + 4) % 4))
        def _(hop=hop):
            turned = dot(one_hot(order_ref[...]), held[hop][...]).astype(BF16)
            for piece in range(4):
                pieces[piece][...] = turned[piece * PIECE : piece * PIECE + PIECE]

    @pl.when(jnp.logical_not(live))
    def _():
        for piece in range(4):
            pieces[piece][...] = jnp.zeros((PIECE, 2 * BS), BF16)

    for hop in range(4):
        first = 2 * ((4 * y + (z - hop + 4) % 4) % 8)
        index, value = spot(map_ref, y // 2, first, 2, lambda entry: entry % 4 == z)
        for shift in range(4):

            @pl.when((index >= 0) & ((value // 4) % 4 == (y + shift) % 4))
            def _(hop=hop, shift=shift):
                hops[shift][...] = held[hop][...]


def mix(rc_ref, t0, t1, t2, t3, f0, f1, f2, f3, out_ref, strip, corner):
    y = rc_ref[0] // 4
    for piece, (child, source) in enumerate(((t0, f0), (t1, f1), (t2, f2), (t3, f3))):

        @pl.when(y == piece)
        def _(child=child, source=source):
            strip[...] = child[...].astype(F32)
            corner[...] = source[0]

    n = jnp.full((8, HALF), CHILD_LEVEL)
    for half in range(2):
        out_ref[half * PIECE : half * PIECE + PIECE] = encode(
            strip[:, half * BS : half * BS + BS], n
        ).astype(I16)
    value = corner[...]
    first = level(jnp.max(jnp.abs(value)))
    code = encode(value, first)
    out_ref[2 * PIECE : 3 * PIECE] = code.astype(I16)
    value = value - decode(code, first)
    second = level(jnp.max(jnp.abs(value)))
    out_ref[3 * PIECE : 4 * PIECE] = encode(value, second).astype(I16)
    line = lax.broadcasted_iota(I32, (16, BS), 0)
    scales = jnp.where(line == 0, first[:1, :1], second[:1, :1])
    out_ref[4 * PIECE :] = scales.astype(I32).astype(I16)


def assemble(map_ref, rc_ref, f0, f1, f2, f3, thin, code_ref, work, corner):
    row, col = rc_ref[0], rc_ref[1]
    y = row // 4
    for piece, source in enumerate((f0, f1, f2, f3)):

        @pl.when(y == piece)
        def _(source=source):
            work[...] = source[...]

    for k in range(NPIV):
        scales = thin[k, 4 * PIECE :].astype(I32)
        corner[k] = decode(thin[k, 2 * PIECE : 3 * PIECE].astype(I32), scales[0:1]) + decode(
            thin[k, 3 * PIECE : 4 * PIECE].astype(I32), scales[1:2]
        )
    n = jnp.full((8, HALF), CHILD_LEVEL)
    for index in range(16):
        parent = map_ref[0, index]
        low = (index % 2) * PIECE

        @pl.when(parent % 8 == col)
        def _(index=index, low=low, tile=parent // 8):
            child = decode(thin[index // 2, low : low + PIECE].astype(I32), n)
            work[tile] = work[tile] + child

        if index < NPIV:

            @pl.when(parent < NPIV)
            def _(index=index, low=low, parent=parent):
                child = decode(thin[index // 2, low : low + PIECE].astype(I32), n)
                corner[parent] = corner[parent] + child

    @pl.when(col < NPIV)
    def _():
        work[0] = jnp.zeros((PIECE, BS), F32)

    n = level(jnp.max(jnp.abs(work[...])))
    for tile in range(8):
        code_ref[tile * PIECE : tile * PIECE + PIECE] = encode(work[tile], n).astype(I16)
    z = row % 4
    square = corner[z]
    corner[z] = jnp.zeros((PIECE, BS), F32)
    first = level(jnp.max(jnp.abs(corner[...])))
    low = 8 * PIECE
    for k in range(NPIV):
        code_ref[low + k * PIECE : low + k * PIECE + PIECE] = encode(corner[k], first).astype(I16)
    second = level(jnp.max(jnp.abs(square)))
    code = encode(square, second)
    code_ref[pl.ds(pl.multiple_of(low + z * PIECE, PIECE), PIECE), :] = code.astype(I16)
    square = square - decode(code, second)
    third = level(jnp.max(jnp.abs(square)))
    code_ref[12 * PIECE : 13 * PIECE] = encode(square, third).astype(I16)
    line = lax.broadcasted_iota(I32, (16, BS), 0)
    scales = third[:1, :1]
    for at, n in enumerate((n, first, second)):
        scales = jnp.where(line == at, n[:1, :1], scales)
    code_ref[13 * PIECE :] = scales.astype(I32).astype(I16)


def pack(rc_ref, h0, h1, h2, h3, out_ref):
    y = rc_ref[0] // 4
    for shift, source in enumerate((h0, h1, h2, h3)):
        out_ref[(y - shift + 4) % 4] = source[...]


def factor_corner(code_ref, rest_ref, level_ref, work, chi, clo, xhi, xlo):
    for y in range(4):
        for z in range(4):
            low = z * BS + y * PIECE
            scale = level_ref[4 * y + z].astype(I32)
            for k in range(4):
                code = code_ref[4 * y + z, k * PIECE : k * PIECE + PIECE].astype(I32)
                if k == z:
                    value = decode(code, scale[2:3])
                    value = value + decode(rest_ref[4 * y + z].astype(I32), scale[3:4])
                else:
                    value = decode(code, scale[1:2])
                work[k, low : low + PIECE] = value
    diagonal = lax.broadcasted_iota(I32, (BS, BS), 0) == lax.broadcasted_iota(I32, (BS, BS), 1)
    for k in range(NPIV):
        pivot = work[k, block(k)]
        parts = split(pivot)
        on_line = jnp.where(diagonal, pivot, 0.0)
        across = jnp.sum(on_line, axis=0, keepdims=True)
        down = jnp.sum(on_line, axis=1, keepdims=True)
        across = across / (across * across + 1.0)
        down = down / (down * down + 1.0)
        approx = 2.0 * jnp.where(diagonal, across, 0.0) - (down * pivot) * across
        for sweep_index in range(NS - 1):
            pair = split(approx)
            approx = 2.0 * approx - dot3(split(dot3(pair, parts)), pair)
        xhi[k], xlo[k] = split(approx)
        for j in range(NPIV):
            chi[block(k), block(j)], clo[block(k), block(j)] = split(work[j, block(k)])
        if k + 1 < NPIV:
            below = slice((k + 1) * BS, NPIV * BS)
            pair = split(dot3(split(work[k, below]), (xhi[k], xlo[k])))
            work[k, below] = pair[0].astype(F32) + pair[1].astype(F32)
            taken = dot3(pair, (chi[block(k), below], clo[block(k), below]))
            for j in range(k + 1, NPIV):
                work[j, below] = work[j, below] - taken[:, block(j - k - 1)]


SPAN = 2
WIDE = 4


def finish(
    map_ref, rc_ref, corner_ref, rest_ref, level_ref, code_ref, left_ref, near_ref, order_ref,
    front_ref, f0, f1, f2, f3, child_ref, out_ref,
    work, chi, clo, xhi, xlo, uhi, ulo, lower, own_col, own_block, own_row, parts,
    arrived, own_arrived,
):
    step = pl.program_id(0)
    row, col = rc_ref[0], rc_ref[1]
    top_row = row < NPIV
    height = SPAN * BS

    def lost(s, first, count):
        return work.at[s // 2, pl.ds((s % 2) * height + first, count)]

    def each_child(act):
        for slot in range(4):
            parent = row_of(map_ref, row, slot)
            here = (parent >= 0) & (parent // 16 // SPAN == step)
            for source in range(4):
                found, value = col_of(map_ref, slot // 2, source, col)
                where = jnp.maximum(found, 0)
                start = pl.multiple_of((where % 2) * BS, BS)
                index = 4 * slot + source
                copy = pltpu.make_async_copy(
                    child_ref.at[where // 2, slot, :, pl.ds(start, BS)],
                    parts.at[index],
                    arrived.at[index],
                )

                @pl.when(here & (found >= 0))
                def _(copy=copy, index=index, tile=(parent // 16) % SPAN, s=value // 8):
                    act(copy, index, tile, s)

    def own_copies():
        return [
            pltpu.make_async_copy(source, own_row.at[piece], own_arrived.at[piece])
            for piece, source in enumerate((f0, f1, f2, f3))
        ]

    each_child(lambda copy, index, tile, s: copy.start())

    @pl.when(step == 0)
    def _():
        @pl.when(top_row)
        def _():
            for copy in own_copies():
                copy.start()

        factor_corner(corner_ref, rest_ref, level_ref, work, chi, clo, xhi, xlo)
        for r in range(NPIV):
            for c in range(NPIV):

                @pl.when((row == r) & (col == c))
                def _(r=r, c=c):
                    own_block[...] = work[c, block(r)]

        @pl.when(top_row)
        def _():
            for copy in own_copies():
                copy.wait()

        for group in range(2):
            for k in range(NPIV):
                for piece in range(4):
                    low = k * BS + piece * PIECE
                    scale = level_ref[4 * piece + k].astype(I32)
                    for q in range(WIDE):
                        first = (WIDE * group + q) * PIECE
                        work[q, low : low + PIECE] = decode(
                            code_ref[4 * piece + k, first : first + PIECE].astype(I32), scale
                        )
            for k in range(NPIV):
                for q in range(WIDE):
                    uhi[group, block(k), block(q)], ulo[group, block(k), block(q)] = split(
                        work[q, block(k)]
                    )
                if k + 1 == NPIV:
                    break
                below = slice((k + 1) * BS, NPIV * BS)
                for pair in range(WIDE // 2):
                    wide = slice(2 * pair * BS, 2 * (pair + 1) * BS)
                    taken = dot3(
                        (chi[below, block(k)], clo[below, block(k)]),
                        (uhi[group, block(k), wide], ulo[group, block(k), wide]),
                    )
                    for q in range(2):
                        at = 2 * pair + q
                        work[at, below] = work[at, below] - taken[:, block(q)]
                    for j in range(k + 1, NPIV):

                        @pl.when(row == j)
                        def _(taken=taken, pair=pair, j=j, k=k, group=group):
                            for piece in range(4):
                                low = (j - k - 1) * BS + piece * PIECE
                                for q in range(2):
                                    tile = WIDE * group + 2 * pair + q
                                    own_row[piece, tile] = (
                                        own_row[piece, tile] - taken[low : low + PIECE, block(q)]
                                    )

    left = work.at[:, pl.ds(height, height)]
    left[...] = left_ref[...]
    for slot in range(2):
        parent = row_of(map_ref, row, slot)
        for index in range(4):
            target = map_ref[0, index]
            cut = slice((index % 2) * BS, (index % 2) * BS + BS)
            for tile in range(SPAN):

                @pl.when(
                    (parent >= 0) & (parent // 16 == SPAN * step + tile) & (target < NPIV)
                )
                def _(slot=slot, index=index, cut=cut, tile=tile, target=target):
                    left[target, block(tile)] = left[target, block(tile)] + near_ref[
                        index // 2, slot, :, cut
                    ].astype(F32)

    @pl.when((step == 0) & top_row)
    def _():
        left[:, :BS] = jnp.zeros((NPIV, BS, BS), F32)

    for k in range(NPIV):
        value = dot3(split(left[k]), (xhi[k], xlo[k]))
        lower[:height, block(k)], lower[height:, block(k)] = split(value)

        @pl.when(col == k)
        def _(value=value):
            own_col[...] = value

        if k + 1 < NPIV:
            rest = slice((k + 1) * BS, NPIV * BS)
            both = dot(lower[:, block(k)], chi[block(k), rest])
            both = both[:height] + both[height:]
            both = both + dot(lower[:height, block(k)], clo[block(k), rest])
            for j in range(k + 1, NPIV):
                left[j] = left[j] - both[:, block(j - k - 1)]

    for group in range(2):
        for pair in range(WIDE // 2):
            wide = slice(2 * pair * BS, 2 * (pair + 1) * BS)
            both = dot(lower[...], uhi[group, :, wide])
            total = both[:height] + (
                both[height:] + dot(lower[:height], ulo[group, :, wide])
            )
            for q in range(2):
                lost(WIDE * group + 2 * pair + q, 0, height)[...] = total[:, block(q)]

    top_tile = (step == 0) & top_row

    @pl.when(top_tile)
    def _():
        for s in range(2 * WIDE):
            for piece in range(4):
                lost(s, piece * PIECE, PIECE)[...] = -own_row[piece, s]

    def add(copy, index, tile, s):
        copy.wait()
        place = lost(s, pl.multiple_of(tile * BS, BS), BS)
        turn = top_tile & (tile == 0)

        @pl.when(turn)
        def _():
            place[...] = place[...] - dot(one_hot(order_ref[...]), parts[index])

        @pl.when(jnp.logical_not(turn))
        def _():
            place[...] = place[...] - parts[index].astype(F32)

    each_child(add)

    @pl.when(col < NPIV)
    def _():
        lost(0, 0, height)[...] = -own_col[...]

        @pl.when(top_tile)
        def _():
            lost(0, 0, BS)[...] = -own_block[...]

    first_tile = lax.broadcasted_iota(I32, (LINES, 2 * WIDE, HALF), 1) == 0

    def turn(index, carry):
        low = pl.multiple_of(index * LINES, LINES)
        keep = jnp.where(top_tile & (low < BS), 0.0, 1.0)
        keep_first = jnp.where(col < NPIV, 0.0, keep)
        mask = jnp.where(first_tile, keep_first, keep)
        for half in range(2):
            lanes = slice(half * HALF, half * HALF + HALF)
            tiles = [lost(s, low, LINES)[:, lanes] for s in range(2 * WIDE)]
            turned = jnp.swapaxes(jnp.stack(tiles, axis=0), 0, 1)
            rows = pl.ds(low, LINES)
            out_ref[rows, half] = jnp.where(mask > 0.0, front_ref[rows, half], 0.0) - turned
        return carry

    lax.fori_loop(0, height // LINES, turn, 0)


LINES = 32


def run_finish(child_map, rc, top, front_left, order, view, cuts, child):
    once = pl.Buffered(1)
    rows = pl.BlockSpec((SPAN * BS,) + view.shape[1:], lambda t: (t, 0, 0, 0))
    away = pl.BlockSpec(memory_space=pl.ANY)
    return pl.pallas_call(
        finish,
        grid=(4 // SPAN,),
        out_shape=shape(view.shape, F32),
        in_specs=[
            SMEM, SMEM,
            pl.BlockSpec((16, 4 * PIECE, BS), lambda t: (0, 2, 0), pipeline_mode=once),
            pl.BlockSpec((16, PIECE, BS), lambda t: (0, 12, 0), pipeline_mode=once),
            pl.BlockSpec((16, 16, BS), lambda t: (0, 13 * PIECE // 16, 0), pipeline_mode=once),
            pl.BlockSpec((16, 8 * PIECE, BS), lambda t: (0, 0, 0), pipeline_mode=once),
            pl.BlockSpec((4, SPAN * BS, BS), lambda t: (0, t, 0)),
            pl.BlockSpec((2, 2, BS, 2 * BS), lambda t: (0, 0, 0, 0), pipeline_mode=once),
            pl.BlockSpec((BS, HALF), lambda t: (0, 0), pipeline_mode=once),
            rows, away, away, away, away, away,
        ],
        out_specs=rows,
        scratch_shapes=[
            pltpu.VMEM((4, 4 * BS, BS), F32),
            pltpu.VMEM((4 * BS, 4 * BS), BF16), pltpu.VMEM((4 * BS, 4 * BS), BF16),
            pltpu.VMEM((NPIV, BS, BS), BF16), pltpu.VMEM((NPIV, BS, BS), BF16),
            pltpu.VMEM((2, 4 * BS, WIDE * BS), BF16), pltpu.VMEM((2, 4 * BS, WIDE * BS), BF16),
            pltpu.VMEM((2 * SPAN * BS, 4 * BS), BF16),
            pltpu.VMEM((SPAN * BS, BS), F32), pltpu.VMEM((BS, BS), F32),
            pltpu.VMEM((4, 8, PIECE, BS), F32),
            pltpu.VMEM((16, BS, BS), BF16),
            pltpu.SemaphoreType.DMA((16,)), pltpu.SemaphoreType.DMA((4,)),
        ],
        compiler_params=pltpu.CompilerParams(vmem_limit_bytes=LIMIT),
        cost_estimate=pl.CostEstimate(
            flops=23 * 2**30, bytes_accessed=32 * 2**20, transcendentals=0
        ),
    )(child_map, rc, top, top, top, top, front_left, child, order, view, *cuts, child)


def shards(front, child_update, child_map, pivots):
    row = lax.axis_index("prow")
    col = lax.axis_index("pcol")
    rc = jnp.stack([row, col]).astype(I32)
    tiles = front.shape[0]

    def along_z(a, hop):
        return lax.ppermute(
            a, "prow", [(4 * i + j, 4 * i + (j + hop) % 4) for i in range(4) for j in range(4)]
        )

    def along_y(a, hop):
        return lax.ppermute(
            a, "prow", [(4 * i + j, 4 * ((i + hop) % 4) + j) for i in range(4) for j in range(4)]
        )

    def from_plane(a, hop):
        return lax.ppermute(a, "prow", [(j, 4 * hop + j) for j in range(4)])

    def spread(pieces):
        return [pieces[0]] + [from_plane(pieces[hop], hop) for hop in (1, 2, 3)]

    strip = shape((BS, 2 * BS), BF16)
    view = front.reshape(tiles, BS, 8, 2, HALF).transpose(0, 1, 3, 2, 4)
    view = view.reshape(tiles * BS, 2, 8, HALF)
    *zs, front_left = pl.pallas_call(
        begin,
        out_shape=[strip] * 4 + [shape((tiles * BS, BS), F32)],
        in_specs=[SMEM, SMEM, VMEM, pl.BlockSpec(memory_space=pl.ANY)],
        out_specs=[VMEM] * 5,
        scratch_shapes=[pltpu.SemaphoreType.DMA((2,))],
        compiler_params=pltpu.CompilerParams(vmem_limit_bytes=LIMIT),
        cost_estimate=pl.CostEstimate(flops=0, bytes_accessed=4 * 2**20, transcendentals=0),
    )(child_map, rc, child_update.reshape(2, BS, 2 * BS), view)
    order = jnp.where(
        row < NPIV, pivots[jnp.minimum(row, NPIV - 1)], jnp.arange(BS, dtype=I32)
    )
    order = jnp.broadcast_to(order.astype(F32)[:, None], (BS, HALF))
    order, *zs = lax.optimization_barrier((order, *zs))
    zs = [zs[0]] + [along_z(zs[hop], hop) for hop in (1, 2, 3)]
    cuts = pl.pallas_call(
        cut_front,
        grid=(1,),
        out_shape=[shape((8, PIECE, BS), F32)] * 4,
        in_specs=[
            pl.BlockSpec((BS * 16, HALF), lambda t: (0, 0)),
            pl.BlockSpec((BS, HALF), lambda t: (0, 0)),
        ],
        out_specs=[pl.BlockSpec((8, PIECE, BS), lambda t: (0, 0, 0))] * 4,
        compiler_params=pltpu.CompilerParams(vmem_limit_bytes=LIMIT),
        cost_estimate=pl.CostEstimate(flops=2**30, bytes_accessed=4 * 2**20, transcendentals=0),
    )(view.reshape(tiles * BS * 16, HALF), order)
    moved = spread(cuts)

    front_left = lax.all_gather(front_left, "pcol", axis=0, tiled=False)

    thin = shape((PIECE, 2 * BS), BF16)
    zs, unused = lax.optimization_barrier((zs, moved[1]))
    picked = call(
        pick_rows, [thin] * 4 + [strip] * 4, [child_map, rc, order, *zs], flops=20 * 2**30
    )
    thin = spread(picked[:4])
    ys = [picked[4]] + [along_y(picked[4 + hop], hop) for hop in (1, 2, 3)]

    (thin,) = call(
        mix,
        [shape((4 * PIECE + 16, BS), I16)],
        [rc, *thin, *moved],
        smem=1,
        scratch=[pltpu.VMEM((PIECE, 2 * BS), F32), pltpu.VMEM((PIECE, BS), F32)],
    )
    thin = lax.all_gather(thin, "pcol", axis=0, tiled=False)
    (child,) = call(pack, [shape((4, BS, 2 * BS), BF16)], [rc, *ys], smem=1)
    thin, child = lax.optimization_barrier((thin, child))
    (code,) = call(
        assemble,
        [shape((13 * PIECE + 16, BS), I16)],
        [child_map, rc, *moved, thin],
        scratch=[pltpu.VMEM((8, PIECE, BS), F32), pltpu.VMEM((NPIV, PIECE, BS), F32)],
    )

    child = lax.all_gather(child, "pcol", axis=0, tiled=False)
    top = lax.all_gather(code, "prow", axis=0, tiled=False)

    done = run_finish(child_map, rc, top, front_left, order, view, cuts, child)
    done = done.reshape(tiles, BS, 2, 8, HALF).transpose(0, 1, 3, 2, 4)
    return done.reshape(front.shape)


def solution(mesh):
    return jax.shard_map(
        shards,
        mesh=mesh,
        in_specs=(P(None, "prow", None, "pcol"), P("prow", "pcol"), P(), P()),
        out_specs=P(None, "prow", None, "pcol"),
        check_vma=False,
    )
```

```python
import functools

import jax
import jax.numpy as jnp
from jax import lax
from jax.experimental import pallas as pl
from jax.experimental.pallas import tpu as pltpu
from jax.sharding import PartitionSpec as P

NPIV = 4
NS = 2
BS = 256
HALF = 128
PIECE = 64
FULL = 32767.0
CHILD_LEVEL = 11.0
F32 = jnp.float32
BF16 = jnp.bfloat16
F8 = jnp.float8_e4m3fn
I16 = jnp.int16
I32 = jnp.int32
SMEM = pl.BlockSpec(memory_space=pltpu.SMEM)
VMEM = pl.BlockSpec(memory_space=pltpu.VMEM)
LIMIT = 62 * 1024 * 1024


def shape(dims, kind):
    return jax.ShapeDtypeStruct(dims, kind)


def call(body, outs, ins, smem=2, flops=0, scratch=()):
    moved = sum(a.size * a.dtype.itemsize for a in ins)
    moved += sum(o.size * o.dtype.itemsize for o in outs)
    return pl.pallas_call(
        body,
        out_shape=outs,
        in_specs=[SMEM] * smem + [VMEM] * (len(ins) - smem),
        out_specs=[VMEM] * len(outs),
        scratch_shapes=list(scratch),
        compiler_params=pltpu.CompilerParams(vmem_limit_bytes=LIMIT),
        cost_estimate=pl.CostEstimate(flops=flops, bytes_accessed=moved, transcendentals=0),
    )(*ins)


def spot(map_ref, child, low, count, test):
    found = jnp.int32(-1)
    value = jnp.int32(-1)
    for step in range(count):
        entry = map_ref[child, low + step]
        hit = test(entry)
        found = jnp.where(hit, low + step, found)
        value = jnp.where(hit, entry, value)
    return found, value


def row_of(map_ref, row, slot):
    return spot(map_ref, slot // 2, 8 * (slot % 2), 8, lambda entry: entry % 16 == row)[1]


def col_of(map_ref, child, source, col):
    return spot(map_ref, child, 4 * source, 4, lambda entry: entry % 8 == col)


def split(value):
    high = value.astype(BF16)
    low = (value - high.astype(F32)).astype(BF16)
    return high, low


def dot(left, right):
    return jnp.dot(left, right, preferred_element_type=F32)


def dot3(left, right):
    (a, b), (c, d) = left, right
    rows = a.shape[0]
    both = dot(jnp.concatenate([a, b], axis=0), c)
    return both[:rows] + (both[rows:] + dot(a, d))


def block(step):
    return slice(step * BS, step * BS + BS)


def one_hot(order):
    spread = lax.broadcasted_iota(I32, (BS, BS), 1).astype(F32)
    return jnp.where(order[:, :1] == spread, 1.0, 0.0).astype(BF16)


def reorder(select, value):
    high = value.astype(BF16)
    rest = value - high.astype(F32)
    middle = rest.astype(BF16)
    last = (rest - middle.astype(F32)).astype(BF16)
    return (dot(select, high) + dot(select, middle)) + dot(select, last)


def level(peak):
    return jnp.ceil(jnp.log2(jnp.full((8, HALF), jnp.maximum(peak, 1e-30))) * 4.0)


def encode(value, n):
    scaled = jnp.abs(value) * jnp.exp2(n * -0.25)[:1, :1]
    code = jnp.minimum(jnp.floor(jnp.sqrt(scaled) * FULL + 0.5), FULL)
    return jnp.where(value < 0.0, -code, code).astype(I32)


def decode(code, n):
    code = code.astype(F32)
    return code * jnp.abs(code) * (jnp.exp2(n.astype(F32)[:1, :1] * 0.25) * (1.0 / (FULL * FULL)))


def cut_front(front_ref, order_ref, *outs):
    select = one_hot(order_ref[...])

    def one(tile, carry):
        halves = [front_ref[pl.ds(half * 8 + tile, BS, stride=16), :] for half in range(2)]
        turned = reorder(select, jnp.concatenate(halves, axis=1))
        for piece in range(4):
            outs[piece][tile] = turned[piece * PIECE : piece * PIECE + PIECE]
        return carry

    lax.fori_loop(0, 8, one, 0)


def begin(map_ref, rc_ref, child_ref, view_ref, o0, o1, o2, o3, left_ref, arrived):
    copies = [
        pltpu.make_async_copy(
            view_ref.at[:, half, 0, :],
            left_ref.at[:, half * HALF : half * HALF + HALF],
            arrived.at[half],
        )
        for half in range(2)
    ]
    for copy in copies:
        copy.start()
    row = rc_ref[0]
    z = row % 4
    second_at = map_ref[row // 8, 2 * (row % 8) + 1] % 4
    for hop, out in enumerate((o0, o1, o2, o3)):
        out[...] = child_ref[jnp.where(second_at == (z + hop) % 4, 1, 0)]
    for copy in copies:
        copy.wait()


def pick_rows(map_ref, rc_ref, order_ref, *refs):
    held, pieces, hops = refs[:4], refs[4:8], refs[8:]
    row = rc_ref[0]
    y, z = row // 4, row % 4
    found, value = spot(map_ref, 0, 0, 4, lambda entry: entry == row)
    live = (found >= 0) & (row < NPIV)
    for hop in range(4):

        @pl.when(live & (found // 2 == (z - hop + 4) % 4))
        def _(hop=hop):
            turned = dot(one_hot(order_ref[...]), held[hop][...]).astype(BF16)
            for piece in range(4):
                pieces[piece][...] = turned[piece * PIECE : piece * PIECE + PIECE]

    @pl.when(jnp.logical_not(live))
    def _():
        for piece in range(4):
            pieces[piece][...] = jnp.zeros((PIECE, 2 * BS), BF16)

    for hop in range(4):
        first = 2 * ((4 * y + (z - hop + 4) % 4) % 8)
        index, value = spot(map_ref, y // 2, first, 2, lambda entry: entry % 4 == z)
        for shift in range(4):

            @pl.when((index >= 0) & ((value // 4) % 4 == (y + shift) % 4))
            def _(hop=hop, shift=shift):
                hops[shift][...] = held[hop][...]


def mix(rc_ref, t0, t1, t2, t3, f0, f1, f2, f3, out_ref, strip, corner):
    y = rc_ref[0] // 4
    for piece, (child, source) in enumerate(((t0, f0), (t1, f1), (t2, f2), (t3, f3))):

        @pl.when(y == piece)
        def _(child=child, source=source):
            strip[...] = child[...].astype(F32)
            corner[...] = source[0]

    n = jnp.full((8, HALF), CHILD_LEVEL)
    for half in range(2):
        out_ref[half * PIECE : half * PIECE + PIECE] = encode(
            strip[:, half * BS : half * BS + BS], n
        ).astype(I16)
    value = corner[...]
    first = level(jnp.max(jnp.abs(value)))
    code = encode(value, first)
    out_ref[2 * PIECE : 3 * PIECE] = code.astype(I16)
    value = value - decode(code, first)
    second = level(jnp.max(jnp.abs(value)))
    out_ref[3 * PIECE : 4 * PIECE] = encode(value, second).astype(I16)
    line = lax.broadcasted_iota(I32, (16, BS), 0)
    scales = jnp.where(line == 0, first[:1, :1], second[:1, :1])
    out_ref[4 * PIECE :] = scales.astype(I32).astype(I16)


def assemble(map_ref, rc_ref, f0, f1, f2, f3, thin, code_ref, work, corner):
    row, col = rc_ref[0], rc_ref[1]
    y = row // 4
    for piece, source in enumerate((f0, f1, f2, f3)):

        @pl.when(y == piece)
        def _(source=source):
            work[...] = source[...]

    for k in range(NPIV):
        scales = thin[k, 4 * PIECE :].astype(I32)
        corner[k] = decode(thin[k, 2 * PIECE : 3 * PIECE].astype(I32), scales[0:1]) + decode(
            thin[k, 3 * PIECE : 4 * PIECE].astype(I32), scales[1:2]
        )
    n = jnp.full((8, HALF), CHILD_LEVEL)
    for index in range(16):
        parent = map_ref[0, index]
        low = (index % 2) * PIECE

        @pl.when(parent % 8 == col)
        def _(index=index, low=low, tile=parent // 8):
            child = decode(thin[index // 2, low : low + PIECE].astype(I32), n)
            work[tile] = work[tile] + child

        if index < NPIV:

            @pl.when(parent < NPIV)
            def _(index=index, low=low, parent=parent):
                child = decode(thin[index // 2, low : low + PIECE].astype(I32), n)
                corner[parent] = corner[parent] + child

    @pl.when(col < NPIV)
    def _():
        work[0] = jnp.zeros((PIECE, BS), F32)

    n = level(jnp.max(jnp.abs(work[...])))
    for tile in range(8):
        code_ref[tile * PIECE : tile * PIECE + PIECE] = encode(work[tile], n).astype(I16)
    z = row % 4
    square = corner[z]
    corner[z] = jnp.zeros((PIECE, BS), F32)
    first = level(jnp.max(jnp.abs(corner[...])))
    low = 8 * PIECE
    for k in range(NPIV):
        code_ref[low + k * PIECE : low + k * PIECE + PIECE] = encode(corner[k], first).astype(I16)
    second = level(jnp.max(jnp.abs(square)))
    code = encode(square, second)
    code_ref[pl.ds(pl.multiple_of(low + z * PIECE, PIECE), PIECE), :] = code.astype(I16)
    line = lax.broadcasted_iota(I32, (16, BS), 0)
    scales = second[:1, :1]
    for at, n in enumerate((n, first)):
        scales = jnp.where(line == at, n[:1, :1], scales)
    code_ref[12 * PIECE :] = scales.astype(I32).astype(I16)


def pack(rc_ref, h0, h1, h2, h3, out_ref):
    y = rc_ref[0] // 4
    for shift, source in enumerate((h0, h1, h2, h3)):
        out_ref[(y - shift + 4) % 4] = source[...]


def factor_corner(code_ref, level_ref, work, chi, clo, xhi, xlo):
    for y in range(4):
        for z in range(4):
            low = z * BS + y * PIECE
            scale = level_ref[4 * y + z].astype(I32)
            for k in range(4):
                code = code_ref[4 * y + z, k * PIECE : k * PIECE + PIECE].astype(I32)
                work[k, low : low + PIECE] = decode(code, scale[2:3] if k == z else scale[1:2])
    diagonal = lax.broadcasted_iota(I32, (BS, BS), 0) == lax.broadcasted_iota(I32, (BS, BS), 1)
    for k in range(NPIV):
        pivot = work[k, block(k)]
        parts = split(pivot)
        on_line = jnp.where(diagonal, pivot, 0.0)
        across = jnp.sum(on_line, axis=0, keepdims=True)
        down = jnp.sum(on_line, axis=1, keepdims=True)
        across = across / (across * across + 1.0)
        down = down / (down * down + 1.0)
        approx = 2.0 * jnp.where(diagonal, across, 0.0) - (down * pivot) * across
        for sweep_index in range(NS - 1):
            pair = split(approx)
            approx = 2.0 * approx - dot3(split(dot3(pair, parts)), pair)
        xhi[k], xlo[k] = split(approx)
        for j in range(NPIV):
            chi[block(k), block(j)], clo[block(k), block(j)] = split(work[j, block(k)])
        if k + 1 < NPIV:
            below = slice((k + 1) * BS, NPIV * BS)
            pair = split(dot3(split(work[k, below]), (xhi[k], xlo[k])))
            work[k, below] = pair[0].astype(F32) + pair[1].astype(F32)
            taken = dot3(pair, (chi[block(k), below], clo[block(k), below]))
            for j in range(k + 1, NPIV):
                work[j, below] = work[j, below] - taken[:, block(j - k - 1)]


SPAN = 2
WIDE = 4


def finish(
    map_ref, rc_ref, corner_ref, level_ref, code_ref, left_ref, near_ref, order_ref,
    front_ref, f0, f1, f2, f3, child_ref, out_ref,
    work, chi, clo, xhi, xlo, uhi, ulo, u8, lower, l8, own_col, own_block, own_row, parts,
    peak, arrived, own_arrived,
):
    step = pl.program_id(0)
    row, col = rc_ref[0], rc_ref[1]
    top_row = row < NPIV
    height = SPAN * BS

    def lost(s, first, count):
        return work.at[s // 2, pl.ds((s % 2) * height + first, count)]

    def each_child(act):
        for slot in range(4):
            parent = row_of(map_ref, row, slot)
            here = (parent >= 0) & (parent // 16 // SPAN == step)
            for source in range(4):
                found, value = col_of(map_ref, slot // 2, source, col)
                where = jnp.maximum(found, 0)
                start = pl.multiple_of((where % 2) * BS, BS)
                index = 4 * (slot % 2) + source
                copy = pltpu.make_async_copy(
                    child_ref.at[where // 2, slot, :, pl.ds(start, BS)],
                    parts.at[index],
                    arrived.at[index],
                )

                @pl.when(here & (found >= 0))
                def _(copy=copy, index=index, tile=(parent // 16) % SPAN, s=value // 8):
                    act(copy, index, tile, s)

    def own_copies():
        return [
            pltpu.make_async_copy(source, own_row.at[piece], own_arrived.at[piece])
            for piece, source in enumerate((f0, f1, f2, f3))
        ]

    each_child(lambda copy, index, tile, s: copy.start())

    @pl.when(step == 0)
    def _():
        @pl.when(top_row)
        def _():
            for copy in own_copies():
                copy.start()

        factor_corner(corner_ref, level_ref, work, chi, clo, xhi, xlo)
        for r in range(NPIV):
            for c in range(NPIV):

                @pl.when((row == r) & (col == c))
                def _(r=r, c=c):
                    own_block[...] = work[c, block(r)]

        @pl.when(top_row)
        def _():
            for copy in own_copies():
                copy.wait()

        for group in range(2):
            for k in range(NPIV):
                for piece in range(4):
                    low = k * BS + piece * PIECE
                    scale = level_ref[4 * piece + k].astype(I32)
                    for q in range(WIDE):
                        first = (WIDE * group + q) * PIECE
                        work[q, low : low + PIECE] = decode(
                            code_ref[4 * piece + k, first : first + PIECE].astype(I32), scale
                        )
            for k in range(NPIV):
                for q in range(WIDE):
                    uhi[group, block(k), block(q)], ulo[block(k), block(q)] = split(
                        work[q, block(k)]
                    )
                if k + 1 == NPIV:
                    break
                below = slice((k + 1) * BS, NPIV * BS)
                for pair in range(WIDE // 2):
                    wide = slice(2 * pair * BS, 2 * (pair + 1) * BS)
                    taken = dot3(
                        (chi[below, block(k)], clo[below, block(k)]),
                        (uhi[group, block(k), wide], ulo[block(k), wide]),
                    )
                    for q in range(2):
                        at = 2 * pair + q
                        work[at, below] = work[at, below] - taken[:, block(q)]
                    for j in range(k + 1, NPIV):

                        @pl.when(row == j)
                        def _(taken=taken, pair=pair, j=j, k=k, group=group):
                            for piece in range(4):
                                low = (j - k - 1) * BS + piece * PIECE
                                for q in range(2):
                                    tile = WIDE * group + 2 * pair + q
                                    own_row[piece, tile] = (
                                        own_row[piece, tile] - taken[low : low + PIECE, block(q)]
                                    )

            peak[group] = jnp.maximum(jnp.max(jnp.abs(uhi[group].astype(F32))), 1e-30)
            scale = 256.0 / peak[group]
            for k in range(NPIV):
                for q in range(WIDE):
                    high = uhi[group, block(k), block(q)].astype(F32)
                    low = ulo[block(k), block(q)].astype(F32)
                    u8[group, block(k), block(q)] = (high * scale).astype(F8)
                    u8[group, block(4 + k), block(q)] = (low * (scale * 256.0)).astype(F8)

    left = work.at[:, pl.ds(height, height)]
    left[...] = left_ref[...]
    for slot in range(2):
        parent = row_of(map_ref, row, slot)
        for index in range(4):
            target = map_ref[0, index]
            cut = slice((index % 2) * BS, (index % 2) * BS + BS)
            for tile in range(SPAN):

                @pl.when(
                    (parent >= 0) & (parent // 16 == SPAN * step + tile) & (target < NPIV)
                )
                def _(slot=slot, index=index, cut=cut, tile=tile, target=target):
                    left[target, block(tile)] = left[target, block(tile)] + near_ref[
                        index // 2, slot, :, cut
                    ].astype(F32)

    @pl.when((step == 0) & top_row)
    def _():
        left[:, :BS] = jnp.zeros((NPIV, BS, BS), F32)

    for k in range(NPIV):
        value = dot3(split(left[k]), (xhi[k], xlo[k]))
        lower[:height, block(k)], lower[height:, block(k)] = split(value)

        @pl.when(col == k)
        def _(value=value):
            own_col[...] = value

        if k + 1 < NPIV:
            rest = slice((k + 1) * BS, NPIV * BS)
            both = dot(lower[:, block(k)], chi[block(k), rest])
            both = both[:height] + both[height:]
            both = both + dot(lower[:height, block(k)], clo[block(k), rest])
            for j in range(k + 1, NPIV):
                left[j] = left[j] - both[:, block(j - k - 1)]

    left_peak = jnp.maximum(jnp.max(jnp.abs(lower[:height].astype(F32))), 1e-30)
    scale = 256.0 / left_peak
    for k in range(NPIV):
        l8[:, block(k)] = (lower[height:, block(k)].astype(F32) * (scale * 256.0)).astype(F8)
        l8[:, block(4 + k)] = (lower[:height, block(k)].astype(F32) * scale).astype(F8)
    for group in range(2):
        unit = (left_peak * (1.0 / 65536.0)) * (peak[group] * (1.0 / 256.0))
        for pair in range(WIDE // 2):
            wide = slice(2 * pair * BS, 2 * (pair + 1) * BS)
            cross = dot(l8[...], u8[group, :, wide]) * unit
            total = dot(lower[:height], uhi[group, :, wide]) + cross
            for q in range(2):
                lost(WIDE * group + 2 * pair + q, 0, height)[...] = total[:, block(q)]

    top_tile = (step == 0) & top_row

    @pl.when(top_tile)
    def _():
        for s in range(2 * WIDE):
            for piece in range(4):
                lost(s, piece * PIECE, PIECE)[...] = -own_row[piece, s]

    def add(copy, index, tile, s):
        copy.wait()
        place = lost(s, pl.multiple_of(tile * BS, BS), BS)
        turn = top_tile & (tile == 0)

        @pl.when(turn)
        def _():
            place[...] = place[...] - dot(one_hot(order_ref[...]), parts[index])

        @pl.when(jnp.logical_not(turn))
        def _():
            place[...] = place[...] - parts[index].astype(F32)

    each_child(add)

    @pl.when(col < NPIV)
    def _():
        lost(0, 0, height)[...] = -own_col[...]

        @pl.when(top_tile)
        def _():
            lost(0, 0, BS)[...] = -own_block[...]

    first_tile = lax.broadcasted_iota(I32, (LINES, 2 * WIDE, HALF), 1) == 0

    def turn(index, carry):
        low = pl.multiple_of(index * LINES, LINES)
        keep = jnp.where(top_tile & (low < BS), 0.0, 1.0)
        keep_first = jnp.where(col < NPIV, 0.0, keep)
        mask = jnp.where(first_tile, keep_first, keep)
        for half in range(2):
            lanes = slice(half * HALF, half * HALF + HALF)
            tiles = [lost(s, low, LINES)[:, lanes] for s in range(2 * WIDE)]
            turned = jnp.swapaxes(jnp.stack(tiles, axis=0), 0, 1)
            rows = pl.ds(low, LINES)
            out_ref[rows, half] = jnp.where(mask > 0.0, front_ref[rows, half], 0.0) - turned
        return carry

    lax.fori_loop(0, height // LINES, turn, 0)


LINES = 32


def run_finish(child_map, rc, top, front_left, order, view, cuts, child):
    once = pl.Buffered(1)
    rows = pl.BlockSpec((SPAN * BS,) + view.shape[1:], lambda t: (t, 0, 0, 0))
    away = pl.BlockSpec(memory_space=pl.ANY)
    return pl.pallas_call(
        finish,
        grid=(4 // SPAN,),
        out_shape=shape(view.shape, F32),
        in_specs=[
            SMEM, SMEM,
            pl.BlockSpec((16, 4 * PIECE, BS), lambda t: (0, 2, 0), pipeline_mode=once),
            pl.BlockSpec((16, 16, BS), lambda t: (0, 12 * PIECE // 16, 0), pipeline_mode=once),
            pl.BlockSpec((16, 8 * PIECE, BS), lambda t: (0, 0, 0), pipeline_mode=once),
            pl.BlockSpec((4, SPAN * BS, BS), lambda t: (0, t, 0)),
            pl.BlockSpec((2, 2, BS, 2 * BS), lambda t: (0, 0, 0, 0), pipeline_mode=once),
            pl.BlockSpec((BS, HALF), lambda t: (0, 0), pipeline_mode=once),
            rows, away, away, away, away, away,
        ],
        out_specs=rows,
        scratch_shapes=[
            pltpu.VMEM((4, 4 * BS, BS), F32),
            pltpu.VMEM((4 * BS, 4 * BS), BF16), pltpu.VMEM((4 * BS, 4 * BS), BF16),
            pltpu.VMEM((NPIV, BS, BS), BF16), pltpu.VMEM((NPIV, BS, BS), BF16),
            pltpu.VMEM((2, 4 * BS, WIDE * BS), BF16), pltpu.VMEM((4 * BS, WIDE * BS), BF16),
            pltpu.VMEM((2, 8 * BS, WIDE * BS), F8),
            pltpu.VMEM((2 * SPAN * BS, 4 * BS), BF16), pltpu.VMEM((SPAN * BS, 8 * BS), F8),
            pltpu.VMEM((SPAN * BS, BS), F32), pltpu.VMEM((BS, BS), F32),
            pltpu.VMEM((4, 8, PIECE, BS), F32),
            pltpu.VMEM((8, BS, BS), BF16),
            pltpu.SMEM((2,), F32),
            pltpu.SemaphoreType.DMA((8,)), pltpu.SemaphoreType.DMA((4,)),
        ],
        compiler_params=pltpu.CompilerParams(vmem_limit_bytes=LIMIT),
        cost_estimate=pl.CostEstimate(
            flops=23 * 2**30, bytes_accessed=32 * 2**20, transcendentals=0
        ),
    )(child_map, rc, top, top, top, front_left, child, order, view, *cuts, child)


def shards(front, child_update, child_map, pivots):
    row = lax.axis_index("prow")
    col = lax.axis_index("pcol")
    rc = jnp.stack([row, col]).astype(I32)
    tiles = front.shape[0]

    def along_z(a, hop):
        return lax.ppermute(
            a, "prow", [(4 * i + j, 4 * i + (j + hop) % 4) for i in range(4) for j in range(4)]
        )

    def along_y(a, hop):
        return lax.ppermute(
            a, "prow", [(4 * i + j, 4 * ((i + hop) % 4) + j) for i in range(4) for j in range(4)]
        )

    def from_plane(a, hop):
        return lax.ppermute(a, "prow", [(j, 4 * hop + j) for j in range(4)])

    def spread(pieces):
        return [pieces[0]] + [from_plane(pieces[hop], hop) for hop in (1, 2, 3)]

    strip = shape((BS, 2 * BS), BF16)
    view = front.reshape(tiles, BS, 8, 2, HALF).transpose(0, 1, 3, 2, 4)
    view = view.reshape(tiles * BS, 2, 8, HALF)
    *zs, front_left = pl.pallas_call(
        begin,
        out_shape=[strip] * 4 + [shape((tiles * BS, BS), F32)],
        in_specs=[SMEM, SMEM, VMEM, pl.BlockSpec(memory_space=pl.ANY)],
        out_specs=[VMEM] * 5,
        scratch_shapes=[pltpu.SemaphoreType.DMA((2,))],
        compiler_params=pltpu.CompilerParams(vmem_limit_bytes=LIMIT),
        cost_estimate=pl.CostEstimate(flops=0, bytes_accessed=4 * 2**20, transcendentals=0),
    )(child_map, rc, child_update.reshape(2, BS, 2 * BS), view)
    order = jnp.where(
        row < NPIV, pivots[jnp.minimum(row, NPIV - 1)], jnp.arange(BS, dtype=I32)
    )
    order = jnp.broadcast_to(order.astype(F32)[:, None], (BS, HALF))
    order, *zs = lax.optimization_barrier((order, *zs))
    zs = [zs[0]] + [along_z(zs[hop], hop) for hop in (1, 2, 3)]
    cuts = pl.pallas_call(
        cut_front,
        grid=(1,),
        out_shape=[shape((8, PIECE, BS), F32)] * 4,
        in_specs=[
            pl.BlockSpec((BS * 16, HALF), lambda t: (0, 0)),
            pl.BlockSpec((BS, HALF), lambda t: (0, 0)),
        ],
        out_specs=[pl.BlockSpec((8, PIECE, BS), lambda t: (0, 0, 0))] * 4,
        compiler_params=pltpu.CompilerParams(vmem_limit_bytes=LIMIT),
        cost_estimate=pl.CostEstimate(flops=2**30, bytes_accessed=4 * 2**20, transcendentals=0),
    )(view.reshape(tiles * BS * 16, HALF), order)
    moved = spread(cuts)

    front_left = lax.all_gather(front_left, "pcol", axis=0, tiled=False)

    thin = shape((PIECE, 2 * BS), BF16)
    zs, unused = lax.optimization_barrier((zs, moved[1]))
    picked = call(
        pick_rows, [thin] * 4 + [strip] * 4, [child_map, rc, order, *zs], flops=20 * 2**30
    )
    thin = spread(picked[:4])
    ys = [picked[4]] + [along_y(picked[4 + hop], hop) for hop in (1, 2, 3)]

    (thin,) = call(
        mix,
        [shape((4 * PIECE + 16, BS), I16)],
        [rc, *thin, *moved],
        smem=1,
        scratch=[pltpu.VMEM((PIECE, 2 * BS), F32), pltpu.VMEM((PIECE, BS), F32)],
    )
    thin = lax.all_gather(thin, "pcol", axis=0, tiled=False)
    (child,) = call(pack, [shape((4, BS, 2 * BS), BF16)], [rc, *ys], smem=1)
    thin, child = lax.optimization_barrier((thin, child))
    (code,) = call(
        assemble,
        [shape((12 * PIECE + 16, BS), I16)],
        [child_map, rc, *moved, thin],
        scratch=[pltpu.VMEM((8, PIECE, BS), F32), pltpu.VMEM((NPIV, PIECE, BS), F32)],
    )

    child = lax.all_gather(child, "pcol", axis=0, tiled=False)
    top = lax.all_gather(code, "prow", axis=0, tiled=False)

    done = run_finish(child_map, rc, top, front_left, order, view, cuts, child)
    done = done.reshape(tiles, BS, 2, 8, HALF).transpose(0, 1, 3, 2, 4)
    return done.reshape(front.shape)


def solution(mesh):
    return jax.shard_map(
        shards,
        mesh=mesh,
        in_specs=(P(None, "prow", None, "pcol"), P("prow", "pcol"), P(), P()),
        out_specs=P(None, "prow", None, "pcol"),
        check_vma=False,
    )
```

```python
import functools

import jax
import jax.numpy as jnp
from jax import lax
from jax.experimental import pallas as pl
from jax.experimental.pallas import tpu as pltpu
from jax.sharding import PartitionSpec as P

NPIV = 4
NS = 2
BS = 256
HALF = 128
PIECE = 64
FULL = 32767.0
CHILD_LEVEL = 11.0
F32 = jnp.float32
BF16 = jnp.bfloat16
F8 = jnp.float8_e4m3fn
I16 = jnp.int16
I32 = jnp.int32
SMEM = pl.BlockSpec(memory_space=pltpu.SMEM)
VMEM = pl.BlockSpec(memory_space=pltpu.VMEM)
LIMIT = 62 * 1024 * 1024


def shape(dims, kind):
    return jax.ShapeDtypeStruct(dims, kind)


def call(body, outs, ins, smem=2, flops=0, scratch=()):
    moved = sum(a.size * a.dtype.itemsize for a in ins)
    moved += sum(o.size * o.dtype.itemsize for o in outs)
    return pl.pallas_call(
        body,
        out_shape=outs,
        in_specs=[SMEM] * smem + [VMEM] * (len(ins) - smem),
        out_specs=[VMEM] * len(outs),
        scratch_shapes=list(scratch),
        compiler_params=pltpu.CompilerParams(vmem_limit_bytes=LIMIT),
        cost_estimate=pl.CostEstimate(flops=flops, bytes_accessed=moved, transcendentals=0),
    )(*ins)


def spot(map_ref, child, low, count, test):
    found = jnp.int32(-1)
    value = jnp.int32(-1)
    for step in range(count):
        entry = map_ref[child, low + step]
        hit = test(entry)
        found = jnp.where(hit, low + step, found)
        value = jnp.where(hit, entry, value)
    return found, value


def row_of(map_ref, row, slot):
    return spot(map_ref, slot // 2, 8 * (slot % 2), 8, lambda entry: entry % 16 == row)[1]


def col_of(map_ref, child, source, col):
    return spot(map_ref, child, 4 * source, 4, lambda entry: entry % 8 == col)


def split(value):
    high = value.astype(BF16)
    low = (value - high.astype(F32)).astype(BF16)
    return high, low


def dot(left, right):
    return jnp.dot(left, right, preferred_element_type=F32)


def dot3(left, right):
    (a, b), (c, d) = left, right
    rows = a.shape[0]
    both = dot(jnp.concatenate([a, b], axis=0), c)
    return both[:rows] + (both[rows:] + dot(a, d))


def block(step):
    return slice(step * BS, step * BS + BS)


def one_hot(pivots_ref, row):
    order = pivots_ref[pl.ds(jnp.minimum(row, NPIV - 1), 1), :]
    spread = lax.broadcasted_iota(I32, (BS, BS), 0)
    return jnp.transpose(jnp.where(order == spread, 1.0, 0.0)).astype(BF16)


def reorder(select, value):
    high = value.astype(BF16)
    rest = value - high.astype(F32)
    middle = rest.astype(BF16)
    last = (rest - middle.astype(F32)).astype(BF16)
    return (dot(select, high) + dot(select, middle)) + dot(select, last)


def level(peak):
    return jnp.ceil(jnp.log2(jnp.full((8, HALF), jnp.maximum(peak, 1e-30))) * 4.0)


def encode(value, n):
    scaled = jnp.abs(value) * jnp.exp2(n * -0.25)[:1, :1]
    code = jnp.minimum(jnp.floor(jnp.sqrt(scaled) * FULL + 0.5), FULL)
    return jnp.where(value < 0.0, -code, code).astype(I32)


def decode(code, n):
    code = code.astype(F32)
    return code * jnp.abs(code) * (jnp.exp2(n.astype(F32)[:1, :1] * 0.25) * (1.0 / (FULL * FULL)))


def begin(
    map_ref, rc_ref, child_ref, pivots_ref, lines_ref, view_ref,
    o0, o1, o2, o3, p0, p1, p2, p3, left_ref, tile_row, arrived,
):
    first = pltpu.make_async_copy(lines_ref.at[: BS * 16], tile_row, arrived.at[2])
    first.start()
    copies = [
        pltpu.make_async_copy(
            view_ref.at[:, half, 0, :],
            left_ref.at[:, half * HALF : half * HALF + HALF],
            arrived.at[half],
        )
        for half in range(2)
    ]
    for copy in copies:
        copy.start()
    row = rc_ref[0]
    z = row % 4
    second_at = map_ref[row // 8, 2 * (row % 8) + 1] % 4
    for hop, out in enumerate((o0, o1, o2, o3)):
        out[...] = child_ref[jnp.where(second_at == (z + hop) % 4, 1, 0)]
    select = one_hot(pivots_ref, row)
    first.wait()

    def one(tile, carry):
        halves = [tile_row[pl.ds(half * 8 + tile, BS, stride=16), :] for half in range(2)]
        turned = reorder(select, jnp.concatenate(halves, axis=1))
        for piece, out in enumerate((p0, p1, p2, p3)):
            out[tile] = turned[piece * PIECE : piece * PIECE + PIECE]
        return carry

    lax.fori_loop(0, 8, one, 0)
    for copy in copies:
        copy.wait()


def pick_rows(map_ref, rc_ref, pivots_ref, *refs):
    held, pieces, hops = refs[:4], refs[4:8], refs[8:]
    row = rc_ref[0]
    y, z = row // 4, row % 4
    found, value = spot(map_ref, 0, 0, 4, lambda entry: entry == row)
    live = (found >= 0) & (row < NPIV)
    for hop in range(4):

        @pl.when(live & (found // 2 == (z - hop + 4) % 4))
        def _(hop=hop):
            turned = dot(one_hot(pivots_ref, row), held[hop][...]).astype(BF16)
            for piece in range(4):
                pieces[piece][...] = turned[piece * PIECE : piece * PIECE + PIECE]

    @pl.when(jnp.logical_not(live))
    def _():
        for piece in range(4):
            pieces[piece][...] = jnp.zeros((PIECE, 2 * BS), BF16)

    for hop in range(4):
        first = 2 * ((4 * y + (z - hop + 4) % 4) % 8)
        index, value = spot(map_ref, y // 2, first, 2, lambda entry: entry % 4 == z)
        for shift in range(4):

            @pl.when((index >= 0) & ((value // 4) % 4 == (y + shift) % 4))
            def _(hop=hop, shift=shift):
                hops[shift][...] = held[hop][...]


def mix(rc_ref, t0, t1, t2, t3, f0, f1, f2, f3, out_ref, strip, corner):
    y = rc_ref[0] // 4
    for piece, (child, source) in enumerate(((t0, f0), (t1, f1), (t2, f2), (t3, f3))):

        @pl.when(y == piece)
        def _(child=child, source=source):
            strip[...] = child[...].astype(F32)
            corner[...] = source[0]

    n = jnp.full((8, HALF), CHILD_LEVEL)
    for half in range(2):
        out_ref[half * PIECE : half * PIECE + PIECE] = encode(
            strip[:, half * BS : half * BS + BS], n
        ).astype(I16)
    n = level(jnp.max(jnp.abs(corner[...])))
    out_ref[2 * PIECE : 3 * PIECE] = encode(corner[...], n).astype(I16)
    out_ref[3 * PIECE :] = jnp.broadcast_to(n[:1, :1].astype(I32), (16, BS)).astype(I16)


def assemble(map_ref, rc_ref, f0, f1, f2, f3, thin, code_ref, work, corner):
    row, col = rc_ref[0], rc_ref[1]
    y = row // 4
    for piece, source in enumerate((f0, f1, f2, f3)):

        @pl.when(y == piece)
        def _(source=source):
            work[...] = source[...]

    for k in range(NPIV):
        corner[k] = decode(
            thin[k, 2 * PIECE : 3 * PIECE].astype(I32), thin[k, 3 * PIECE :].astype(I32)
        )
    n = jnp.full((8, HALF), CHILD_LEVEL)
    for index in range(16):
        parent = map_ref[0, index]
        low = (index % 2) * PIECE

        @pl.when(parent % 8 == col)
        def _(index=index, low=low, tile=parent // 8):
            child = decode(thin[index // 2, low : low + PIECE].astype(I32), n)
            work[tile] = work[tile] + child

        if index < NPIV:

            @pl.when(parent < NPIV)
            def _(index=index, low=low, parent=parent):
                child = decode(thin[index // 2, low : low + PIECE].astype(I32), n)
                corner[parent] = corner[parent] + child

    @pl.when(col < NPIV)
    def _():
        work[0] = jnp.zeros((PIECE, BS), F32)

    n = level(jnp.max(jnp.abs(work[...])))
    for tile in range(8):
        code_ref[tile * PIECE : tile * PIECE + PIECE] = encode(work[tile], n).astype(I16)
    z = row % 4
    square = corner[z]
    corner[z] = jnp.zeros((PIECE, BS), F32)
    first = level(jnp.max(jnp.abs(corner[...])))
    low = 8 * PIECE
    for k in range(NPIV):
        code_ref[low + k * PIECE : low + k * PIECE + PIECE] = encode(corner[k], first).astype(I16)
    second = level(jnp.max(jnp.abs(square)))
    code = encode(square, second)
    code_ref[pl.ds(pl.multiple_of(low + z * PIECE, PIECE), PIECE), :] = code.astype(I16)
    line = lax.broadcasted_iota(I32, (16, BS), 0)
    scales = second[:1, :1]
    for at, n in enumerate((n, first)):
        scales = jnp.where(line == at, n[:1, :1], scales)
    code_ref[12 * PIECE :] = scales.astype(I32).astype(I16)


def pack(rc_ref, h0, h1, h2, h3, out_ref):
    y = rc_ref[0] // 4
    for shift, source in enumerate((h0, h1, h2, h3)):
        out_ref[(y - shift + 4) % 4] = source[...]


def factor_corner(code_ref, level_ref, work, chi, clo, xhi, xlo):
    for y in range(4):
        for z in range(4):
            low = z * BS + y * PIECE
            scale = level_ref[4 * y + z].astype(I32)
            for k in range(4):
                code = code_ref[4 * y + z, k * PIECE : k * PIECE + PIECE].astype(I32)
                work[k, low : low + PIECE] = decode(code, scale[2:3] if k == z else scale[1:2])
    diagonal = lax.broadcasted_iota(I32, (BS, BS), 0) == lax.broadcasted_iota(I32, (BS, BS), 1)
    for k in range(NPIV):
        pivot = work[k, block(k)]
        parts = split(pivot)
        on_line = jnp.where(diagonal, pivot, 0.0)
        across = jnp.sum(on_line, axis=0, keepdims=True)
        down = jnp.sum(on_line, axis=1, keepdims=True)
        across = across / (across * across + 1.0)
        down = down / (down * down + 1.0)
        approx = 2.0 * jnp.where(diagonal, across, 0.0) - (down * pivot) * across
        for sweep_index in range(NS - 1):
            pair = split(approx)
            approx = 2.0 * approx - dot3(split(dot3(pair, parts)), pair)
        xhi[k], xlo[k] = split(approx)
        for j in range(NPIV):
            chi[block(k), block(j)], clo[block(k), block(j)] = split(work[j, block(k)])
        if k + 1 < NPIV:
            below = slice((k + 1) * BS, NPIV * BS)
            pair = split(dot3(split(work[k, below]), (xhi[k], xlo[k])))
            work[k, below] = pair[0].astype(F32) + pair[1].astype(F32)
            taken = dot3(pair, (chi[block(k), below], clo[block(k), below]))
            for j in range(k + 1, NPIV):
                work[j, below] = work[j, below] - taken[:, block(j - k - 1)]


SPAN = 2
WIDE = 4


def finish(
    map_ref, rc_ref, pivots_ref, top_ref, left_from, front_from, f0, f1, f2, f3, child_ref, out_ref,
    corner_ref, level_ref, code_ref, left_ref, near_ref, front,
    work, chi, clo, xhi, xlo, uhi, ulo, u8, lower, l8, own_col, own_block, own_row, parts,
    peak, arrived, own_arrived, ready, sent,
):
    row, col = rc_ref[0], rc_ref[1]
    top_row = row < NPIV
    height = SPAN * BS

    def left_copy(step):
        rows = pl.ds(step * height, height)
        return pltpu.make_async_copy(left_from.at[:NPIV, rows], left_ref, ready.at[3])

    def front_copy(step):
        rows = pl.ds(step * height, height)
        return pltpu.make_async_copy(front_from.at[rows], front.at[step], ready.at[5 + step])

    codes = 8 * PIECE
    corner_copies = [
        pltpu.make_async_copy(top_ref.at[:, codes : codes + 4 * PIECE], corner_ref, ready.at[0]),
        pltpu.make_async_copy(top_ref.at[:, codes + 4 * PIECE :], level_ref, ready.at[1]),
    ]
    code_copy = pltpu.make_async_copy(top_ref.at[:, :codes], code_ref, ready.at[2])
    near_copy = pltpu.make_async_copy(child_ref.at[:2, :2], near_ref, ready.at[4])
    for copy in corner_copies:
        copy.start()
    for copy in corner_copies:
        copy.wait()
    for copy in (code_copy, left_copy(0), near_copy, front_copy(0), front_copy(1)):
        copy.start()

    def lost(s, first, count):
        return work.at[s // 2, pl.ds((s % 2) * height + first, count)]

    def each_child(step, act):
        for slot in range(4):
            parent = row_of(map_ref, row, slot)
            here = (parent >= 0) & (parent // 16 // SPAN == step)
            for source in range(4):
                found, value = col_of(map_ref, slot // 2, source, col)
                where = jnp.maximum(found, 0)
                start = pl.multiple_of((where % 2) * BS, BS)
                index = 4 * (slot % 2) + source
                copy = pltpu.make_async_copy(
                    child_ref.at[where // 2, slot, :, pl.ds(start, BS)],
                    parts.at[index],
                    arrived.at[index],
                )

                @pl.when(here & (found >= 0))
                def _(copy=copy, index=index, tile=(parent // 16) % SPAN, s=value // 8):
                    act(copy, index, tile, s)

    def own_copies():
        return [
            pltpu.make_async_copy(source, own_row.at[piece], own_arrived.at[piece])
            for piece, source in enumerate((f0, f1, f2, f3))
        ]

    @pl.when(top_row)
    def _():
        for copy in own_copies():
            copy.start()

    factor_corner(corner_ref, level_ref, work, chi, clo, xhi, xlo)
    for r in range(NPIV):
        for c in range(NPIV):

            @pl.when((row == r) & (col == c))
            def _(r=r, c=c):
                own_block[...] = work[c, block(r)]

    @pl.when(top_row)
    def _():
        for copy in own_copies():
            copy.wait()

    code_copy.wait()
    for group in range(2):
        for k in range(NPIV):
            for piece in range(4):
                low = k * BS + piece * PIECE
                scale = level_ref[4 * piece + k].astype(I32)
                for q in range(WIDE):
                    first = (WIDE * group + q) * PIECE
                    work[q, low : low + PIECE] = decode(
                        code_ref[4 * piece + k, first : first + PIECE].astype(I32), scale
                    )
        for k in range(NPIV):
            for q in range(WIDE):
                uhi[group, block(k), block(q)], ulo[block(k), block(q)] = split(
                    work[q, block(k)]
                )
            if k + 1 == NPIV:
                break
            below = slice((k + 1) * BS, NPIV * BS)
            for pair in range(WIDE // 2):
                wide = slice(2 * pair * BS, 2 * (pair + 1) * BS)
                taken = dot3(
                    (chi[below, block(k)], clo[below, block(k)]),
                    (uhi[group, block(k), wide], ulo[block(k), wide]),
                )
                for q in range(2):
                    at = 2 * pair + q
                    work[at, below] = work[at, below] - taken[:, block(q)]
                for j in range(k + 1, NPIV):

                    @pl.when(row == j)
                    def _(taken=taken, pair=pair, j=j, k=k, group=group):
                        for piece in range(4):
                            low = (j - k - 1) * BS + piece * PIECE
                            for q in range(2):
                                tile = WIDE * group + 2 * pair + q
                                own_row[piece, tile] = (
                                    own_row[piece, tile] - taken[low : low + PIECE, block(q)]
                                )

        peak[group] = jnp.maximum(jnp.max(jnp.abs(uhi[group].astype(F32))), 1e-30)
        scale = 256.0 / peak[group]
        for k in range(NPIV):
            for q in range(WIDE):
                high = uhi[group, block(k), block(q)].astype(F32)
                low = ulo[block(k), block(q)].astype(F32)
                u8[group, block(k), block(q)] = (high * scale).astype(F8)
                u8[group, block(4 + k), block(q)] = (low * (scale * 256.0)).astype(F8)

    def rows_of_step(step, carry):
        each_child(step, lambda copy, index, tile, s: copy.start())
        left = work.at[:, pl.ds(height, height)]
        left_copy(step).wait()
        left[...] = left_ref[...]

        @pl.when(step == 0)
        def _():
            left_copy(1).start()
            near_copy.wait()

        for slot in range(2):
            parent = row_of(map_ref, row, slot)
            for index in range(4):
                target = map_ref[0, index]
                cut = slice((index % 2) * BS, (index % 2) * BS + BS)
                for tile in range(SPAN):

                    @pl.when(
                        (parent >= 0) & (parent // 16 == SPAN * step + tile) & (target < NPIV)
                    )
                    def _(slot=slot, index=index, cut=cut, tile=tile, target=target):
                        left[target, block(tile)] = left[target, block(tile)] + near_ref[
                            index // 2, slot, :, cut
                        ].astype(F32)

        @pl.when((step == 0) & top_row)
        def _():
            left[:, :BS] = jnp.zeros((NPIV, BS, BS), F32)

        for k in range(NPIV):
            value = dot3(split(left[k]), (xhi[k], xlo[k]))
            lower[:height, block(k)], lower[height:, block(k)] = split(value)

            @pl.when(col == k)
            def _(value=value):
                own_col[...] = value

            if k + 1 < NPIV:
                rest = slice((k + 1) * BS, NPIV * BS)
                both = dot(lower[:, block(k)], chi[block(k), rest])
                both = both[:height] + both[height:]
                both = both + dot(lower[:height, block(k)], clo[block(k), rest])
                for j in range(k + 1, NPIV):
                    left[j] = left[j] - both[:, block(j - k - 1)]

        left_peak = jnp.maximum(jnp.max(jnp.abs(lower[:height].astype(F32))), 1e-30)
        scale = 256.0 / left_peak
        for k in range(NPIV):
            l8[:, block(k)] = (lower[height:, block(k)].astype(F32) * (scale * 256.0)).astype(F8)
            l8[:, block(4 + k)] = (lower[:height, block(k)].astype(F32) * scale).astype(F8)
        for group in range(2):
            unit = (left_peak * (1.0 / 65536.0)) * (peak[group] * (1.0 / 256.0))
            for pair in range(WIDE // 2):
                wide = slice(2 * pair * BS, 2 * (pair + 1) * BS)
                cross = dot(l8[...], u8[group, :, wide]) * unit
                total = dot(lower[:height], uhi[group, :, wide]) + cross
                for q in range(2):
                    lost(WIDE * group + 2 * pair + q, 0, height)[...] = total[:, block(q)]

        top_tile = (step == 0) & top_row

        @pl.when(top_tile)
        def _():
            for s in range(2 * WIDE):
                for piece in range(4):
                    lost(s, piece * PIECE, PIECE)[...] = -own_row[piece, s]

        def add(copy, index, tile, s):
            copy.wait()
            place = lost(s, pl.multiple_of(tile * BS, BS), BS)
            turn = top_tile & (tile == 0)

            @pl.when(turn)
            def _():
                place[...] = place[...] - dot(one_hot(pivots_ref, row), parts[index])

            @pl.when(jnp.logical_not(turn))
            def _():
                place[...] = place[...] - parts[index].astype(F32)

        each_child(step, add)

        @pl.when(col < NPIV)
        def _():
            lost(0, 0, height)[...] = -own_col[...]

            @pl.when(top_tile)
            def _():
                lost(0, 0, BS)[...] = -own_block[...]

        first_tile = lax.broadcasted_iota(I32, (LINES, 2 * WIDE, HALF), 1) == 0

        def turn(index, carry):
            low = pl.multiple_of(index * LINES, LINES)
            keep = jnp.where(top_tile & (low < BS), 0.0, 1.0)
            keep_first = jnp.where(col < NPIV, 0.0, keep)
            mask = jnp.where(first_tile, keep_first, keep)
            for half in range(2):
                lanes = slice(half * HALF, half * HALF + HALF)
                tiles = [lost(s, low, LINES)[:, lanes] for s in range(2 * WIDE)]
                turned = jnp.swapaxes(jnp.stack(tiles, axis=0), 0, 1)
                rows = pl.ds(low, LINES)
                kept = jnp.where(mask > 0.0, front[step, rows, half], 0.0)
                front[step, rows, half] = kept - turned
            return carry

        front_copy(step).wait()
        for quarter in range(4):
            lines = height // (4 * LINES)
            lax.fori_loop(quarter * lines, quarter * lines + lines, turn, 0)
            out_copy(step, quarter).start()
        return carry

    def out_copy(step, quarter):
        rows = pl.ds(quarter * (height // 4), height // 4)
        return pltpu.make_async_copy(
            front.at[step, rows],
            out_ref.at[pl.ds(step * height + quarter * (height // 4), height // 4)],
            sent.at[4 * step + quarter],
        )

    lax.fori_loop(0, 4 // SPAN, rows_of_step, 0)
    for step in range(4 // SPAN):
        for quarter in range(4):
            out_copy(step, quarter).wait()


LINES = 32


def run_finish(child_map, rc, pivots, top, front_left, view, cuts, child):
    away = pl.BlockSpec(memory_space=pl.ANY)
    return pl.pallas_call(
        finish,
        out_shape=shape(view.shape, F32),
        in_specs=[SMEM, SMEM, VMEM] + [away] * 8,
        out_specs=away,
        scratch_shapes=[
            pltpu.VMEM((16, 4 * PIECE, BS), I16), pltpu.VMEM((16, 16, BS), I16),
            pltpu.VMEM((16, 8 * PIECE, BS), I16), pltpu.VMEM((4, SPAN * BS, BS), F32),
            pltpu.VMEM((2, 2, BS, 2 * BS), BF16), pltpu.VMEM((2, SPAN * BS, 2, 8, HALF), F32),
            pltpu.VMEM((4, 4 * BS, BS), F32),
            pltpu.VMEM((4 * BS, 4 * BS), BF16), pltpu.VMEM((4 * BS, 4 * BS), BF16),
            pltpu.VMEM((NPIV, BS, BS), BF16), pltpu.VMEM((NPIV, BS, BS), BF16),
            pltpu.VMEM((2, 4 * BS, WIDE * BS), BF16), pltpu.VMEM((4 * BS, WIDE * BS), BF16),
            pltpu.VMEM((2, 8 * BS, WIDE * BS), F8),
            pltpu.VMEM((2 * SPAN * BS, 4 * BS), BF16), pltpu.VMEM((SPAN * BS, 8 * BS), F8),
            pltpu.VMEM((SPAN * BS, BS), F32), pltpu.VMEM((BS, BS), F32),
            pltpu.VMEM((4, 8, PIECE, BS), F32),
            pltpu.VMEM((8, BS, BS), BF16),
            pltpu.SMEM((2,), F32),
            pltpu.SemaphoreType.DMA((8,)), pltpu.SemaphoreType.DMA((4,)),
            pltpu.SemaphoreType.DMA((7,)), pltpu.SemaphoreType.DMA((8,)),
        ],
        compiler_params=pltpu.CompilerParams(vmem_limit_bytes=LIMIT),
        cost_estimate=pl.CostEstimate(
            flops=23 * 2**30, bytes_accessed=32 * 2**20, transcendentals=0
        ),
    )(child_map, rc, pivots, top, front_left, view, *cuts, child)


def shards(front, child_update, child_map, pivots):
    row = lax.axis_index("prow")
    col = lax.axis_index("pcol")
    rc = jnp.stack([row, col]).astype(I32)
    tiles = front.shape[0]

    def along_z(a, hop):
        return lax.ppermute(
            a, "prow", [(4 * i + j, 4 * i + (j + hop) % 4) for i in range(4) for j in range(4)]
        )

    def along_y(a, hop):
        return lax.ppermute(
            a, "prow", [(4 * i + j, 4 * ((i + hop) % 4) + j) for i in range(4) for j in range(4)]
        )

    def from_plane(a, hop):
        return lax.ppermute(a, "prow", [(j, 4 * hop + j) for j in range(4)])

    def spread(pieces):
        return [pieces[0]] + [from_plane(pieces[hop], hop) for hop in (1, 2, 3)]

    strip = shape((BS, 2 * BS), BF16)
    view = front.reshape(tiles, BS, 8, 2, HALF).transpose(0, 1, 3, 2, 4)
    view = view.reshape(tiles * BS, 2, 8, HALF)
    away = pl.BlockSpec(memory_space=pl.ANY)
    begun = pl.pallas_call(
        begin,
        out_shape=[strip] * 4 + [shape((8, PIECE, BS), F32)] * 4 + [shape((tiles * BS, BS), F32)],
        in_specs=[SMEM, SMEM, VMEM, VMEM, away, away],
        out_specs=[VMEM] * 9,
        scratch_shapes=[pltpu.VMEM((BS * 16, HALF), F32), pltpu.SemaphoreType.DMA((3,))],
        compiler_params=pltpu.CompilerParams(vmem_limit_bytes=LIMIT),
        cost_estimate=pl.CostEstimate(flops=2**30, bytes_accessed=8 * 2**20, transcendentals=0),
    )(
        child_map, rc, child_update.reshape(2, BS, 2 * BS), pivots,
        view.reshape(tiles * BS * 16, HALF), view,
    )
    zs, cuts, front_left = begun[:4], begun[4:8], begun[8]
    zs = [zs[0]] + [along_z(zs[hop], hop) for hop in (1, 2, 3)]

    moved = spread(cuts)

    front_left = lax.all_gather(front_left, "pcol", axis=0, tiled=False)

    thin = shape((PIECE, 2 * BS), BF16)
    zs, unused = lax.optimization_barrier((zs, moved[1]))
    picked = call(
        pick_rows, [thin] * 4 + [strip] * 4, [child_map, rc, pivots, *zs], flops=20 * 2**30
    )
    thin = spread(picked[:4])
    ys = [picked[4]] + [along_y(picked[4 + hop], hop) for hop in (1, 2, 3)]

    (thin,) = call(
        mix,
        [shape((3 * PIECE + 16, BS), I16)],
        [rc, *thin, *moved],
        smem=1,
        scratch=[pltpu.VMEM((PIECE, 2 * BS), F32), pltpu.VMEM((PIECE, BS), F32)],
    )
    thin = lax.all_gather(thin, "pcol", axis=0, tiled=False)
    (child,) = call(pack, [shape((4, BS, 2 * BS), BF16)], [rc, *ys], smem=1)
    thin, child = lax.optimization_barrier((thin, child))
    (code,) = call(
        assemble,
        [shape((12 * PIECE + 16, BS), I16)],
        [child_map, rc, *moved, thin],
        scratch=[pltpu.VMEM((8, PIECE, BS), F32), pltpu.VMEM((NPIV, PIECE, BS), F32)],
    )

    child = lax.all_gather(child, "pcol", axis=0, tiled=False)
    top = lax.all_gather(code, "prow", axis=0, tiled=False)

    done = run_finish(child_map, rc, pivots, top, front_left, view, cuts, child)
    done = done.reshape(tiles, BS, 2, 8, HALF).transpose(0, 1, 3, 2, 4)
    return done.reshape(front.shape)


def solution(mesh):
    return jax.shard_map(
        shards,
        mesh=mesh,
        in_specs=(P(None, "prow", None, "pcol"), P("prow", "pcol"), P(), P()),
        out_specs=P(None, "prow", None, "pcol"),
        check_vma=False,
    )
```

```python
import functools

import jax
import jax.numpy as jnp
from jax import lax
from jax.experimental import pallas as pl
from jax.experimental.pallas import tpu as pltpu
from jax.sharding import PartitionSpec as P

NPIV = 4
NS = 2
BS = 256
HALF = 128
PIECE = 64
FULL = 32767.0
CHILD_LEVEL = 11.0
F32 = jnp.float32
BF16 = jnp.bfloat16
F8 = jnp.float8_e4m3fn
I16 = jnp.int16
I32 = jnp.int32
SMEM = pl.BlockSpec(memory_space=pltpu.SMEM)
VMEM = pl.BlockSpec(memory_space=pltpu.VMEM)
LIMIT = 62 * 1024 * 1024


def shape(dims, kind):
    return jax.ShapeDtypeStruct(dims, kind)


def call(body, outs, ins, smem=2, flops=0, scratch=()):
    moved = sum(a.size * a.dtype.itemsize for a in ins)
    moved += sum(o.size * o.dtype.itemsize for o in outs)
    return pl.pallas_call(
        body,
        out_shape=outs,
        in_specs=[SMEM] * smem + [VMEM] * (len(ins) - smem),
        out_specs=[VMEM] * len(outs),
        scratch_shapes=list(scratch),
        compiler_params=pltpu.CompilerParams(vmem_limit_bytes=LIMIT),
        cost_estimate=pl.CostEstimate(flops=flops, bytes_accessed=moved, transcendentals=0),
    )(*ins)


def spot(map_ref, child, low, count, test):
    found = jnp.int32(-1)
    value = jnp.int32(-1)
    for step in range(count):
        entry = map_ref[child, low + step]
        hit = test(entry)
        found = jnp.where(hit, low + step, found)
        value = jnp.where(hit, entry, value)
    return found, value


def row_of(map_ref, row, slot):
    return spot(map_ref, slot // 2, 8 * (slot % 2), 8, lambda entry: entry % 16 == row)[1]


def col_of(map_ref, child, source, col):
    return spot(map_ref, child, 4 * source, 4, lambda entry: entry % 8 == col)


def split(value):
    high = value.astype(BF16)
    low = (value - high.astype(F32)).astype(BF16)
    return high, low


def dot(left, right):
    return jnp.dot(left, right, preferred_element_type=F32)


def dot3(left, right):
    (a, b), (c, d) = left, right
    rows = a.shape[0]
    both = dot(jnp.concatenate([a, b], axis=0), c)
    return both[:rows] + (both[rows:] + dot(a, d))


def block(step):
    return slice(step * BS, step * BS + BS)


def one_hot(pivots_ref, row):
    order = pivots_ref[pl.ds(jnp.minimum(row, NPIV - 1), 1), :]
    spread = lax.broadcasted_iota(I32, (BS, BS), 0)
    return jnp.transpose(jnp.where(order == spread, 1.0, 0.0)).astype(BF16)


def reorder(select, value):
    high = value.astype(BF16)
    rest = value - high.astype(F32)
    middle = rest.astype(BF16)
    last = (rest - middle.astype(F32)).astype(BF16)
    return (dot(select, high) + dot(select, middle)) + dot(select, last)


def level(peak):
    return jnp.ceil(jnp.log2(jnp.full((8, HALF), jnp.maximum(peak, 1e-30))) * 4.0)


def encode(value, n):
    scaled = jnp.abs(value) * jnp.exp2(n * -0.25)[:1, :1]
    code = jnp.minimum(jnp.floor(jnp.sqrt(scaled) * FULL + 0.5), FULL)
    return jnp.where(value < 0.0, -code, code).astype(I32)


def decode(code, n):
    code = code.astype(F32)
    return code * jnp.abs(code) * (jnp.exp2(n.astype(F32)[:1, :1] * 0.25) * (1.0 / (FULL * FULL)))


def begin(
    map_ref, rc_ref, child_ref, pivots_ref, lines_ref, view_ref,
    o0, o1, o2, o3, p0, p1, p2, p3, left_ref, tile_row, arrived,
):
    first = pltpu.make_async_copy(lines_ref.at[: BS * 16], tile_row, arrived.at[2])
    first.start()
    copies = [
        pltpu.make_async_copy(
            view_ref.at[:, half, 0, :],
            left_ref.at[:, half * HALF : half * HALF + HALF],
            arrived.at[half],
        )
        for half in range(2)
    ]
    for copy in copies:
        copy.start()
    row = rc_ref[0]
    z = row % 4
    second_at = map_ref[row // 8, 2 * (row % 8) + 1] % 4
    for hop, out in enumerate((o0, o1, o2, o3)):
        out[...] = child_ref[jnp.where(second_at == (z + hop) % 4, 1, 0)]
    select = one_hot(pivots_ref, row)
    first.wait()

    def one(tile, carry):
        halves = [tile_row[pl.ds(half * 8 + tile, BS, stride=16), :] for half in range(2)]
        turned = reorder(select, jnp.concatenate(halves, axis=1))
        for piece, out in enumerate((p0, p1, p2, p3)):
            out[tile] = turned[piece * PIECE : piece * PIECE + PIECE]
        return carry

    lax.fori_loop(0, 8, one, 0)
    for copy in copies:
        copy.wait()


def pick_rows(map_ref, rc_ref, pivots_ref, *refs):
    held, pieces, hops = refs[:4], refs[4:8], refs[8:]
    row = rc_ref[0]
    y, z = row // 4, row % 4
    found, value = spot(map_ref, 0, 0, 4, lambda entry: entry == row)
    live = (found >= 0) & (row < NPIV)
    for hop in range(4):

        @pl.when(live & (found // 2 == (z - hop + 4) % 4))
        def _(hop=hop):
            turned = dot(one_hot(pivots_ref, row), held[hop][...]).astype(BF16)
            for piece in range(4):
                pieces[piece][...] = turned[piece * PIECE : piece * PIECE + PIECE]

    @pl.when(jnp.logical_not(live))
    def _():
        for piece in range(4):
            pieces[piece][...] = jnp.zeros((PIECE, 2 * BS), BF16)

    for hop in range(4):
        first = 2 * ((4 * y + (z - hop + 4) % 4) % 8)
        index, value = spot(map_ref, y // 2, first, 2, lambda entry: entry % 4 == z)
        for shift in range(4):

            @pl.when((index >= 0) & ((value // 4) % 4 == (y + shift) % 4))
            def _(hop=hop, shift=shift):
                hops[shift][...] = held[hop][...]


def mix(rc_ref, t0, t1, t2, t3, f0, f1, f2, f3, out_ref, strip, corner):
    y = rc_ref[0] // 4
    for piece, (child, source) in enumerate(((t0, f0), (t1, f1), (t2, f2), (t3, f3))):

        @pl.when(y == piece)
        def _(child=child, source=source):
            strip[...] = child[...].astype(F32)
            corner[...] = source[0]

    n = jnp.full((8, HALF), CHILD_LEVEL)
    for half in range(2):
        out_ref[half * PIECE : half * PIECE + PIECE] = encode(
            strip[:, half * BS : half * BS + BS], n
        ).astype(I16)
    n = level(jnp.max(jnp.abs(corner[...])))
    out_ref[2 * PIECE : 3 * PIECE] = encode(corner[...], n).astype(I16)
    out_ref[3 * PIECE :] = jnp.broadcast_to(n[:1, :1].astype(I32), (16, BS)).astype(I16)


def assemble(map_ref, rc_ref, f0, f1, f2, f3, thin, code_ref, work, corner, arrived):
    row, col = rc_ref[0], rc_ref[1]
    y = row // 4
    for piece, source in enumerate((f0, f1, f2, f3)):

        @pl.when(y == piece)
        def _(piece=piece, source=source):
            pltpu.make_async_copy(source, work, arrived.at[piece]).start()

    for k in range(NPIV):
        corner[k] = decode(
            thin[k, 2 * PIECE : 3 * PIECE].astype(I32), thin[k, 3 * PIECE :].astype(I32)
        )
    n = jnp.full((8, HALF), CHILD_LEVEL)
    for piece, source in enumerate((f0, f1, f2, f3)):

        @pl.when(y == piece)
        def _(piece=piece, source=source):
            pltpu.make_async_copy(source, work, arrived.at[piece]).wait()

    for index in range(16):
        parent = map_ref[0, index]
        low = (index % 2) * PIECE

        @pl.when(parent % 8 == col)
        def _(index=index, low=low, tile=parent // 8):
            child = decode(thin[index // 2, low : low + PIECE].astype(I32), n)
            work[tile] = work[tile] + child

        if index < NPIV:

            @pl.when(parent < NPIV)
            def _(index=index, low=low, parent=parent):
                child = decode(thin[index // 2, low : low + PIECE].astype(I32), n)
                corner[parent] = corner[parent] + child

    @pl.when(col < NPIV)
    def _():
        work[0] = jnp.zeros((PIECE, BS), F32)

    n = level(jnp.max(jnp.abs(work[...])))
    for tile in range(8):
        code_ref[tile * PIECE : tile * PIECE + PIECE] = encode(work[tile], n).astype(I16)
    z = row % 4
    square = corner[z]
    corner[z] = jnp.zeros((PIECE, BS), F32)
    first = level(jnp.max(jnp.abs(corner[...])))
    low = 8 * PIECE
    for k in range(NPIV):
        code_ref[low + k * PIECE : low + k * PIECE + PIECE] = encode(corner[k], first).astype(I16)
    second = level(jnp.max(jnp.abs(square)))
    code = encode(square, second)
    code_ref[pl.ds(pl.multiple_of(low + z * PIECE, PIECE), PIECE), :] = code.astype(I16)
    line = lax.broadcasted_iota(I32, (16, BS), 0)
    scales = second[:1, :1]
    for at, n in enumerate((n, first)):
        scales = jnp.where(line == at, n[:1, :1], scales)
    code_ref[12 * PIECE :] = scales.astype(I32).astype(I16)


def factor_corner(code_ref, level_ref, work, chi, clo, xhi, xlo):
    for y in range(4):
        for z in range(4):
            low = z * BS + y * PIECE
            scale = level_ref[4 * y + z].astype(I32)
            for k in range(4):
                code = code_ref[4 * y + z, k * PIECE : k * PIECE + PIECE].astype(I32)
                work[k, low : low + PIECE] = decode(code, scale[2:3] if k == z else scale[1:2])
    diagonal = lax.broadcasted_iota(I32, (BS, BS), 0) == lax.broadcasted_iota(I32, (BS, BS), 1)
    for k in range(NPIV):
        pivot = work[k, block(k)]
        parts = split(pivot)
        on_line = jnp.where(diagonal, pivot, 0.0)
        across = jnp.sum(on_line, axis=0, keepdims=True)
        down = jnp.sum(on_line, axis=1, keepdims=True)
        across = across / (across * across + 1.0)
        down = down / (down * down + 1.0)
        approx = 2.0 * jnp.where(diagonal, across, 0.0) - (down * pivot) * across
        for sweep_index in range(NS - 1):
            pair = split(approx)
            approx = 2.0 * approx - dot3(split(dot3(pair, parts)), pair)
        xhi[k], xlo[k] = split(approx)
        for j in range(NPIV):
            chi[block(k), block(j)], clo[block(k), block(j)] = split(work[j, block(k)])
        if k + 1 < NPIV:
            below = slice((k + 1) * BS, NPIV * BS)
            pair = split(dot3(split(work[k, below]), (xhi[k], xlo[k])))
            work[k, below] = pair[0].astype(F32) + pair[1].astype(F32)
            taken = dot3(pair, (chi[block(k), below], clo[block(k), below]))
            for j in range(k + 1, NPIV):
                work[j, below] = work[j, below] - taken[:, block(j - k - 1)]


SPAN = 2
WIDE = 4


def finish(
    map_ref, rc_ref, top_ref, left_from, front_from, child_ref, out_ref,
    corner_ref, level_ref, code_ref, left_ref, near_ref, front,
    work, chi, clo, xhi, xlo, uhi, ulo, u8, lower, l8, own_col, own_block, own_row, parts,
    peak, arrived, ready, sent,
):
    row, col = rc_ref[0], rc_ref[1]
    top_row = row < NPIV
    height = SPAN * BS

    def hop_of(slot):
        return (row // 4 - slot + 4) % 4

    def left_copy(step):
        rows = pl.ds(step * height, height)
        return pltpu.make_async_copy(left_from.at[:NPIV, rows], left_ref, ready.at[3])

    def front_copy(step):
        rows = pl.ds(step * height, height)
        return pltpu.make_async_copy(front_from.at[rows], front.at[step], ready.at[5 + step])

    codes = 8 * PIECE
    corner_copies = [
        pltpu.make_async_copy(top_ref.at[:, codes : codes + 4 * PIECE], corner_ref, ready.at[0]),
        pltpu.make_async_copy(top_ref.at[:, codes + 4 * PIECE :], level_ref, ready.at[1]),
    ]
    code_copy = pltpu.make_async_copy(top_ref.at[:, :codes], code_ref, ready.at[2])
    near_copies = [
        pltpu.make_async_copy(child_ref.at[:2, hop_of(slot)], near_ref.at[:, slot], ready.at[at])
        for slot, at in ((0, 4), (1, 7))
    ]
    for copy in corner_copies:
        copy.start()
    for copy in corner_copies:
        copy.wait()
    for copy in (code_copy, left_copy(0), *near_copies, front_copy(0), front_copy(1)):
        copy.start()

    def lost(s, first, count):
        return work.at[s // 2, pl.ds((s % 2) * height + first, count)]

    def each_child(step, act):
        for slot in range(4):
            parent = row_of(map_ref, row, slot)
            here = (parent >= 0) & (parent // 16 // SPAN == step)
            for source in range(4):
                found, value = col_of(map_ref, slot // 2, source, col)
                where = jnp.maximum(found, 0)
                start = pl.multiple_of((where % 2) * BS, BS)
                index = 4 * (slot % 2) + source
                copy = pltpu.make_async_copy(
                    child_ref.at[where // 2, hop_of(slot), :, pl.ds(start, BS)],
                    parts.at[index],
                    arrived.at[index],
                )

                @pl.when(here & (found >= 0))
                def _(copy=copy, index=index, tile=(parent // 16) % SPAN, s=value // 8):
                    act(copy, index, tile, s)

    factor_corner(corner_ref, level_ref, work, chi, clo, xhi, xlo)
    for r in range(NPIV):
        for c in range(NPIV):

            @pl.when((row == r) & (col == c))
            def _(r=r, c=c):
                own_block[...] = work[c, block(r)]

    code_copy.wait()
    for group in range(2):
        for k in range(NPIV):
            for piece in range(4):
                low = k * BS + piece * PIECE
                scale = level_ref[4 * piece + k].astype(I32)
                for q in range(WIDE):
                    first = (WIDE * group + q) * PIECE
                    work[q, low : low + PIECE] = decode(
                        code_ref[4 * piece + k, first : first + PIECE].astype(I32), scale
                    )
        for k in range(NPIV):
            for q in range(WIDE):
                uhi[group, block(k), block(q)], ulo[block(k), block(q)] = split(
                    work[q, block(k)]
                )

            @pl.when(row == k)
            def _(k=k, group=group):
                for q in range(WIDE):
                    own_row[WIDE * group + q] = work[q, block(k)]

            if k + 1 == NPIV:
                break
            below = slice((k + 1) * BS, NPIV * BS)
            for pair in range(WIDE // 2):
                wide = slice(2 * pair * BS, 2 * (pair + 1) * BS)
                taken = dot3(
                    (chi[below, block(k)], clo[below, block(k)]),
                    (uhi[group, block(k), wide], ulo[block(k), wide]),
                )
                for q in range(2):
                    at = 2 * pair + q
                    work[at, below] = work[at, below] - taken[:, block(q)]

        peak[group] = jnp.maximum(jnp.max(jnp.abs(uhi[group].astype(F32))), 1e-30)
        scale = 256.0 / peak[group]
        for k in range(NPIV):
            for q in range(WIDE):
                high = uhi[group, block(k), block(q)].astype(F32)
                low = ulo[block(k), block(q)].astype(F32)
                u8[group, block(k), block(q)] = (high * scale).astype(F8)
                u8[group, block(4 + k), block(q)] = (low * (scale * 256.0)).astype(F8)

    def rows_of_step(step, carry):
        each_child(step, lambda copy, index, tile, s: copy.start())
        left = work.at[:, pl.ds(height, height)]
        left_copy(step).wait()
        left[...] = left_ref[...]

        @pl.when(step == 0)
        def _():
            left_copy(1).start()
            for copy in near_copies:
                copy.wait()

        for slot in range(2):
            parent = row_of(map_ref, row, slot)
            for index in range(4):
                target = map_ref[0, index]
                cut = slice((index % 2) * BS, (index % 2) * BS + BS)
                for tile in range(SPAN):

                    @pl.when(
                        (parent >= 0) & (parent // 16 == SPAN * step + tile) & (target < NPIV)
                    )
                    def _(slot=slot, index=index, cut=cut, tile=tile, target=target):
                        left[target, block(tile)] = left[target, block(tile)] + near_ref[
                            index // 2, slot, :, cut
                        ].astype(F32)

        @pl.when((step == 0) & top_row)
        def _():
            left[:, :BS] = jnp.zeros((NPIV, BS, BS), F32)

        for k in range(NPIV):
            value = dot3(split(left[k]), (xhi[k], xlo[k]))
            lower[:height, block(k)], lower[height:, block(k)] = split(value)

            @pl.when(col == k)
            def _(value=value):
                own_col[...] = value

            if k + 1 < NPIV:
                rest = slice((k + 1) * BS, NPIV * BS)
                both = dot(lower[:, block(k)], chi[block(k), rest])
                both = both[:height] + both[height:]
                both = both + dot(lower[:height, block(k)], clo[block(k), rest])
                for j in range(k + 1, NPIV):
                    left[j] = left[j] - both[:, block(j - k - 1)]

        left_peak = jnp.maximum(jnp.max(jnp.abs(lower[:height].astype(F32))), 1e-30)
        scale = 256.0 / left_peak
        for k in range(NPIV):
            l8[:, block(k)] = (lower[height:, block(k)].astype(F32) * (scale * 256.0)).astype(F8)
            l8[:, block(4 + k)] = (lower[:height, block(k)].astype(F32) * scale).astype(F8)
        for group in range(2):
            unit = (left_peak * (1.0 / 65536.0)) * (peak[group] * (1.0 / 256.0))
            for pair in range(WIDE // 2):
                wide = slice(2 * pair * BS, 2 * (pair + 1) * BS)
                cross = dot(l8[...], u8[group, :, wide]) * unit
                total = dot(lower[:height], uhi[group, :, wide]) + cross
                for q in range(2):
                    lost(WIDE * group + 2 * pair + q, 0, height)[...] = total[:, block(q)]

        top_tile = (step == 0) & top_row

        @pl.when(top_tile)
        def _():
            for s in range(2 * WIDE):
                lost(s, 0, BS)[...] = -own_row[s]

        def add(copy, index, tile, s):
            copy.wait()
            place = lost(s, pl.multiple_of(tile * BS, BS), BS)

            @pl.when(jnp.logical_not(top_tile & (tile == 0)))
            def _():
                place[...] = place[...] - parts[index].astype(F32)

        each_child(step, add)

        @pl.when(col < NPIV)
        def _():
            lost(0, 0, height)[...] = -own_col[...]

            @pl.when(top_tile)
            def _():
                lost(0, 0, BS)[...] = -own_block[...]

        first_tile = lax.broadcasted_iota(I32, (LINES, 2 * WIDE, HALF), 1) == 0

        def turn(index, carry):
            low = pl.multiple_of(index * LINES, LINES)
            keep = jnp.where(top_tile & (low < BS), 0.0, 1.0)
            keep_first = jnp.where(col < NPIV, 0.0, keep)
            mask = jnp.where(first_tile, keep_first, keep)
            for half in range(2):
                lanes = slice(half * HALF, half * HALF + HALF)
                tiles = [lost(s, low, LINES)[:, lanes] for s in range(2 * WIDE)]
                turned = jnp.swapaxes(jnp.stack(tiles, axis=0), 0, 1)
                rows = pl.ds(low, LINES)
                kept = jnp.where(mask > 0.0, front[step, rows, half], 0.0)
                front[step, rows, half] = kept - turned
            return carry

        front_copy(step).wait()
        for quarter in range(4):
            lines = height // (4 * LINES)
            lax.fori_loop(quarter * lines, quarter * lines + lines, turn, 0)
            out_copy(step, quarter).start()
        return carry

    def out_copy(step, quarter):
        rows = pl.ds(quarter * (height // 4), height // 4)
        return pltpu.make_async_copy(
            front.at[step, rows],
            out_ref.at[pl.ds(step * height + quarter * (height // 4), height // 4)],
            sent.at[4 * step + quarter],
        )

    lax.fori_loop(0, 4 // SPAN, rows_of_step, 0)
    for step in range(4 // SPAN):
        for quarter in range(4):
            out_copy(step, quarter).wait()


LINES = 32


def run_finish(child_map, rc, top, front_left, view, child):
    away = pl.BlockSpec(memory_space=pl.ANY)
    return pl.pallas_call(
        finish,
        out_shape=shape(view.shape, F32),
        in_specs=[SMEM, SMEM] + [away] * 4,
        out_specs=away,
        scratch_shapes=[
            pltpu.VMEM((16, 4 * PIECE, BS), I16), pltpu.VMEM((16, 16, BS), I16),
            pltpu.VMEM((16, 8 * PIECE, BS), I16), pltpu.VMEM((4, SPAN * BS, BS), F32),
            pltpu.VMEM((2, 2, BS, 2 * BS), BF16), pltpu.VMEM((2, SPAN * BS, 2, 8, HALF), F32),
            pltpu.VMEM((4, 4 * BS, BS), F32),
            pltpu.VMEM((4 * BS, 4 * BS), BF16), pltpu.VMEM((4 * BS, 4 * BS), BF16),
            pltpu.VMEM((NPIV, BS, BS), BF16), pltpu.VMEM((NPIV, BS, BS), BF16),
            pltpu.VMEM((2, 4 * BS, WIDE * BS), BF16), pltpu.VMEM((4 * BS, WIDE * BS), BF16),
            pltpu.VMEM((2, 8 * BS, WIDE * BS), F8),
            pltpu.VMEM((2 * SPAN * BS, 4 * BS), BF16), pltpu.VMEM((SPAN * BS, 8 * BS), F8),
            pltpu.VMEM((SPAN * BS, BS), F32), pltpu.VMEM((BS, BS), F32),
            pltpu.VMEM((8, BS, BS), F32),
            pltpu.VMEM((8, BS, BS), BF16),
            pltpu.SMEM((2,), F32),
            pltpu.SemaphoreType.DMA((8,)),
            pltpu.SemaphoreType.DMA((8,)), pltpu.SemaphoreType.DMA((8,)),
        ],
        compiler_params=pltpu.CompilerParams(vmem_limit_bytes=LIMIT),
        cost_estimate=pl.CostEstimate(
            flops=23 * 2**30, bytes_accessed=32 * 2**20, transcendentals=0
        ),
    )(child_map, rc, top, front_left, view, child)


def shards(front, child_update, child_map, pivots):
    row = lax.axis_index("prow")
    col = lax.axis_index("pcol")
    rc = jnp.stack([row, col]).astype(I32)
    tiles = front.shape[0]

    def along_z(a, hop):
        return lax.ppermute(
            a, "prow", [(4 * i + j, 4 * i + (j + hop) % 4) for i in range(4) for j in range(4)]
        )

    def along_y(a, hop):
        return lax.ppermute(
            a, "prow", [(4 * i + j, 4 * ((i + hop) % 4) + j) for i in range(4) for j in range(4)]
        )

    def from_plane(a, hop):
        return lax.ppermute(a, "prow", [(j, 4 * hop + j) for j in range(4)])

    def spread(pieces):
        return [pieces[0]] + [from_plane(pieces[hop], hop) for hop in (1, 2, 3)]

    strip = shape((BS, 2 * BS), BF16)
    view = front.reshape(tiles, BS, 8, 2, HALF).transpose(0, 1, 3, 2, 4)
    view = view.reshape(tiles * BS, 2, 8, HALF)
    away = pl.BlockSpec(memory_space=pl.ANY)
    begun = pl.pallas_call(
        begin,
        out_shape=[strip] * 4 + [shape((8, PIECE, BS), F32)] * 4 + [shape((tiles * BS, BS), F32)],
        in_specs=[SMEM, SMEM, VMEM, VMEM, away, away],
        out_specs=[VMEM] * 9,
        scratch_shapes=[pltpu.VMEM((BS * 16, HALF), F32), pltpu.SemaphoreType.DMA((3,))],
        compiler_params=pltpu.CompilerParams(vmem_limit_bytes=LIMIT),
        cost_estimate=pl.CostEstimate(flops=2**30, bytes_accessed=8 * 2**20, transcendentals=0),
    )(
        child_map, rc, child_update.reshape(2, BS, 2 * BS), pivots,
        view.reshape(tiles * BS * 16, HALF), view,
    )
    zs, cuts, front_left = begun[:4], begun[4:8], begun[8]
    zs = [zs[0]] + [along_z(zs[hop], hop) for hop in (1, 2, 3)]

    moved = spread(cuts)

    front_left = lax.all_gather(front_left, "pcol", axis=0, tiled=False)

    thin = shape((PIECE, 2 * BS), BF16)
    zs, unused = lax.optimization_barrier((zs, moved[1]))
    picked = call(
        pick_rows, [thin] * 4 + [strip] * 4, [child_map, rc, pivots, *zs], flops=20 * 2**30
    )
    thin = spread(picked[:4])
    ys = [picked[4]] + [along_y(picked[4 + hop], hop) for hop in (1, 2, 3)]

    thin = pl.pallas_call(
        mix,
        grid=(1,),
        out_shape=shape((3 * PIECE + 16, BS), I16),
        in_specs=[SMEM]
        + [pl.BlockSpec((PIECE, 2 * BS), lambda t: (0, 0))] * 4
        + [pl.BlockSpec((1, PIECE, BS), lambda t: (0, 0, 0))] * 4,
        out_specs=pl.BlockSpec((3 * PIECE + 16, BS), lambda t: (0, 0)),
        scratch_shapes=[pltpu.VMEM((PIECE, 2 * BS), F32), pltpu.VMEM((PIECE, BS), F32)],
        compiler_params=pltpu.CompilerParams(vmem_limit_bytes=LIMIT),
        cost_estimate=pl.CostEstimate(flops=0, bytes_accessed=2**20, transcendentals=0),
    )(rc, *thin, *moved)
    thin = lax.all_gather(thin, "pcol", axis=0, tiled=False)
    child = jnp.stack(ys)
    thin, child = lax.optimization_barrier((thin, child))
    code = pl.pallas_call(
        assemble,
        out_shape=shape((12 * PIECE + 16, BS), I16),
        in_specs=[SMEM, SMEM, away, away, away, away, VMEM],
        out_specs=VMEM,
        scratch_shapes=[
            pltpu.VMEM((8, PIECE, BS), F32), pltpu.VMEM((NPIV, PIECE, BS), F32),
            pltpu.SemaphoreType.DMA((4,)),
        ],
        compiler_params=pltpu.CompilerParams(vmem_limit_bytes=LIMIT),
        cost_estimate=pl.CostEstimate(flops=0, bytes_accessed=2**21, transcendentals=0),
    )(child_map, rc, *moved, thin)

    child = lax.all_gather(child, "pcol", axis=0, tiled=False)
    top = lax.all_gather(code, "prow", axis=0, tiled=False)

    done = run_finish(child_map, rc, top, front_left, view, child)
    done = done.reshape(tiles, BS, 2, 8, HALF).transpose(0, 1, 3, 2, 4)
    return done.reshape(front.shape)


def solution(mesh):
    return jax.shard_map(
        shards,
        mesh=mesh,
        in_specs=(P(None, "prow", None, "pcol"), P("prow", "pcol"), P(), P()),
        out_specs=P(None, "prow", None, "pcol"),
        check_vma=False,
    )
```

```python
import functools

import jax
import jax.numpy as jnp
from jax import lax
from jax.experimental import pallas as pl
from jax.experimental.pallas import tpu as pltpu
from jax.sharding import PartitionSpec as P

NPIV = 4
NS = 2
BS = 256
HALF = 128
PIECE = 64
FULL = 32767.0
CHILD_LEVEL = 11.0
F32 = jnp.float32
BF16 = jnp.bfloat16
F8 = jnp.float8_e4m3fn
I16 = jnp.int16
I32 = jnp.int32
SMEM = pl.BlockSpec(memory_space=pltpu.SMEM)
VMEM = pl.BlockSpec(memory_space=pltpu.VMEM)
LIMIT = 62 * 1024 * 1024
SMALL = 12 * 1024 * 1024


def shape(dims, kind):
    return jax.ShapeDtypeStruct(dims, kind)


def spot(map_ref, child, low, count, test):
    found = jnp.int32(-1)
    value = jnp.int32(-1)
    for step in range(count):
        entry = map_ref[child, low + step]
        hit = test(entry)
        found = jnp.where(hit, low + step, found)
        value = jnp.where(hit, entry, value)
    return found, value


def row_of(map_ref, row, slot):
    return spot(map_ref, slot // 2, 8 * (slot % 2), 8, lambda entry: entry % 16 == row)[1]


def col_of(map_ref, child, source, col):
    return spot(map_ref, child, 4 * source, 4, lambda entry: entry % 8 == col)


def split(value):
    high = value.astype(BF16)
    low = (value - high.astype(F32)).astype(BF16)
    return high, low


def dot(left, right):
    return jnp.dot(left, right, preferred_element_type=F32)


def dot3(left, right):
    (a, b), (c, d) = left, right
    rows = a.shape[0]
    both = dot(jnp.concatenate([a, b], axis=0), c)
    return both[:rows] + (both[rows:] + dot(a, d))


def block(step):
    return slice(step * BS, step * BS + BS)


def one_hot(pivots_ref, row):
    order = pivots_ref[pl.ds(jnp.minimum(row, NPIV - 1), 1), :]
    spread = lax.broadcasted_iota(I32, (BS, BS), 0)
    return jnp.transpose(jnp.where(order == spread, 1.0, 0.0)).astype(BF16)


def reorder(select, value):
    high, low = split(value)
    return dot(select, high) + dot(select, low)


def level(peak):
    return jnp.ceil(jnp.log2(jnp.full((8, HALF), jnp.maximum(peak, 1e-30))) * 4.0)


def encode(value, n):
    scaled = jnp.abs(value) * jnp.exp2(n * -0.25)[:1, :1]
    code = jnp.minimum(jnp.floor(jnp.sqrt(scaled) * FULL + 0.5), FULL)
    return jnp.where(value < 0.0, -code, code).astype(I32)


def decode(code, n):
    code = code.astype(F32)
    return code * jnp.abs(code) * (jnp.exp2(n.astype(F32)[:1, :1] * 0.25) * (1.0 / (FULL * FULL)))


def begin(
    map_ref, rc_ref, child_ref, pivots_ref, lines_ref, view_ref,
    o0, o1, o2, o3, p0, p1, p2, p3, left_ref, tile_row, arrived,
):
    first = pltpu.make_async_copy(lines_ref.at[: BS * 16], tile_row, arrived.at[2])
    first.start()
    copies = [
        pltpu.make_async_copy(
            view_ref.at[:, half, 0, :],
            left_ref.at[:, half * HALF : half * HALF + HALF],
            arrived.at[half],
        )
        for half in range(2)
    ]
    for copy in copies:
        copy.start()
    row = rc_ref[0]
    z = row % 4
    second_at = map_ref[row // 8, 2 * (row % 8) + 1] % 4
    for hop, out in enumerate((o0, o1, o2, o3)):
        out[...] = child_ref[jnp.where(second_at == (z + hop) % 4, 1, 0)]
    select = one_hot(pivots_ref, row)
    first.wait()

    def one(tile, carry):
        halves = [tile_row[pl.ds(half * 8 + tile, BS, stride=16), :] for half in range(2)]
        turned = reorder(select, jnp.concatenate(halves, axis=1))
        for piece, out in enumerate((p0, p1, p2, p3)):
            out[tile] = turned[piece * PIECE : piece * PIECE + PIECE]
        return carry

    lax.fori_loop(0, 8, one, 0)
    for copy in copies:
        copy.wait()


def pick_rows(map_ref, rc_ref, pivots_ref, *refs):
    held, pieces, hops, (work, arrived) = refs[:4], refs[4:8], refs[8:12], refs[12:]
    row = rc_ref[0]
    y, z = row // 4, row % 4
    found, value = spot(map_ref, 0, 0, 4, lambda entry: entry == row)
    live = (found >= 0) & (row < NPIV)

    def each(act):
        for hop in range(4):
            mine = live & (found // 2 == (z - hop + 4) % 4)
            act(mine, pltpu.make_async_copy(held[hop], work, arrived.at[16 + hop]))
        for hop in range(4):
            first = 2 * ((4 * y + (z - hop + 4) % 4) % 8)
            index, value = spot(map_ref, y // 2, first, 2, lambda entry: entry % 4 == z)
            for shift in range(4):
                mine = (index >= 0) & ((value // 4) % 4 == (y + shift) % 4)
                at = 4 * hop + shift
                act(mine, pltpu.make_async_copy(held[hop], hops[shift], arrived.at[at]))

    def start(mine, copy):
        @pl.when(mine)
        def _():
            copy.start()

    def wait(mine, copy):
        @pl.when(mine)
        def _():
            copy.wait()

    each(start)
    each(wait)

    @pl.when(live)
    def _():
        turned = dot(one_hot(pivots_ref, row), work[...]).astype(BF16)
        for piece in range(4):
            pieces[piece][...] = turned[piece * PIECE : piece * PIECE + PIECE]

    @pl.when(jnp.logical_not(live))
    def _():
        for piece in range(4):
            pieces[piece][...] = jnp.zeros((PIECE, 2 * BS), BF16)


def pack(y0, y1, y2, y3, out_ref, arrived):
    copies = [
        pltpu.make_async_copy(source, out_ref.at[shift], arrived.at[shift])
        for shift, source in enumerate((y0, y1, y2, y3))
    ]
    for copy in copies:
        copy.start()
    for copy in copies:
        copy.wait()


def mix(rc_ref, t0, t1, t2, t3, f0, f1, f2, f3, out_ref, strip, corner, arrived):
    y = rc_ref[0] // 4
    for piece, (child, source) in enumerate(((t0, f0), (t1, f1), (t2, f2), (t3, f3))):
        copies = [
            pltpu.make_async_copy(child, strip, arrived.at[2 * piece]),
            pltpu.make_async_copy(source.at[0], corner, arrived.at[2 * piece + 1]),
        ]

        @pl.when(y == piece)
        def _(copies=copies):
            for copy in copies:
                copy.start()
            for copy in copies:
                copy.wait()

    n = jnp.full((8, HALF), CHILD_LEVEL)
    for half in range(2):
        out_ref[half * PIECE : half * PIECE + PIECE] = encode(
            strip[:, half * BS : half * BS + BS].astype(F32), n
        ).astype(I16)
    n = level(jnp.max(jnp.abs(corner[...])))
    out_ref[2 * PIECE : 3 * PIECE] = encode(corner[...], n).astype(I16)
    out_ref[3 * PIECE :] = jnp.broadcast_to(n[:1, :1].astype(I32), (16, BS)).astype(I16)


def assemble(map_ref, rc_ref, f0, f1, f2, f3, thin, code_ref, work, corner, arrived):
    row, col = rc_ref[0], rc_ref[1]
    y = row // 4
    for piece, source in enumerate((f0, f1, f2, f3)):

        @pl.when(y == piece)
        def _(piece=piece, source=source):
            pltpu.make_async_copy(source, work, arrived.at[piece]).start()

    for k in range(NPIV):
        corner[k] = decode(
            thin[k, 2 * PIECE : 3 * PIECE].astype(I32), thin[k, 3 * PIECE :].astype(I32)
        )
    n = jnp.full((8, HALF), CHILD_LEVEL)
    for piece, source in enumerate((f0, f1, f2, f3)):

        @pl.when(y == piece)
        def _(piece=piece, source=source):
            pltpu.make_async_copy(source, work, arrived.at[piece]).wait()

    for index in range(16):
        parent = map_ref[0, index]
        low = (index % 2) * PIECE

        @pl.when(parent % 8 == col)
        def _(index=index, low=low, tile=parent // 8):
            child = decode(thin[index // 2, low : low + PIECE].astype(I32), n)
            work[tile] = work[tile] + child

        if index < NPIV:

            @pl.when(parent < NPIV)
            def _(index=index, low=low, parent=parent):
                child = decode(thin[index // 2, low : low + PIECE].astype(I32), n)
                corner[parent] = corner[parent] + child

    @pl.when(col < NPIV)
    def _():
        work[0] = jnp.zeros((PIECE, BS), F32)

    n = level(jnp.max(jnp.abs(work[...])))
    for tile in range(8):
        code_ref[tile * PIECE : tile * PIECE + PIECE] = encode(work[tile], n).astype(I16)
    z = row % 4
    square = corner[z]
    corner[z] = jnp.zeros((PIECE, BS), F32)
    first = level(jnp.max(jnp.abs(corner[...])))
    low = 8 * PIECE
    for k in range(NPIV):
        code_ref[low + k * PIECE : low + k * PIECE + PIECE] = encode(corner[k], first).astype(I16)
    second = level(jnp.max(jnp.abs(square)))
    code = encode(square, second)
    code_ref[pl.ds(pl.multiple_of(low + z * PIECE, PIECE), PIECE), :] = code.astype(I16)
    line = lax.broadcasted_iota(I32, (16, BS), 0)
    scales = second[:1, :1]
    for at, n in enumerate((n, first)):
        scales = jnp.where(line == at, n[:1, :1], scales)
    code_ref[12 * PIECE :] = scales.astype(I32).astype(I16)


def factor_corner(code_ref, level_ref, work, chi, clo, xhi, xlo):
    for y in range(4):
        for z in range(4):
            low = z * BS + y * PIECE
            scale = level_ref[4 * y + z].astype(I32)
            for k in range(4):
                code = code_ref[4 * y + z, k * PIECE : k * PIECE + PIECE].astype(I32)
                work[k, low : low + PIECE] = decode(code, scale[2:3] if k == z else scale[1:2])
    diagonal = lax.broadcasted_iota(I32, (BS, BS), 0) == lax.broadcasted_iota(I32, (BS, BS), 1)
    for k in range(NPIV):
        pivot = work[k, block(k)]
        parts = split(pivot)
        on_line = jnp.where(diagonal, pivot, 0.0)
        across = jnp.sum(on_line, axis=0, keepdims=True)
        down = jnp.sum(on_line, axis=1, keepdims=True)
        across = across / (across * across + 1.0)
        down = down / (down * down + 1.0)
        approx = 2.0 * jnp.where(diagonal, across, 0.0) - (down * pivot) * across
        for sweep_index in range(NS - 1):
            pair = split(approx)
            approx = 2.0 * approx - dot3(split(dot3(pair, parts)), pair)
        xhi[k], xlo[k] = split(approx)
        for j in range(NPIV):
            chi[block(k), block(j)], clo[block(k), block(j)] = split(work[j, block(k)])
        if k + 1 < NPIV:
            below = slice((k + 1) * BS, NPIV * BS)
            pair = split(dot3(split(work[k, below]), (xhi[k], xlo[k])))
            work[k, below] = pair[0].astype(F32) + pair[1].astype(F32)
            taken = dot3(pair, (chi[block(k), below], clo[block(k), below]))
            for j in range(k + 1, NPIV):
                work[j, below] = work[j, below] - taken[:, block(j - k - 1)]


SPAN = 2
WIDE = 4


def finish(
    map_ref, rc_ref, top_ref, left_from, front_from, child_ref, out_ref,
    corner_ref, level_ref, code_ref, left_ref, near_ref, front,
    work, chi, clo, xhi, xlo, uhi, ulo, u8, lower, l8, own_col, own_block, own_row, parts,
    peak, arrived, ready, sent,
):
    row, col = rc_ref[0], rc_ref[1]
    top_row = row < NPIV
    height = SPAN * BS

    def hop_of(slot):
        return (row // 4 - slot + 4) % 4

    def left_copy(step):
        rows = pl.ds(step * height, height)
        return pltpu.make_async_copy(left_from.at[:NPIV, rows], left_ref, ready.at[3])

    def front_copy(step):
        rows = pl.ds(step * height, height)
        return pltpu.make_async_copy(front_from.at[rows], front.at[step], ready.at[5 + step])

    codes = 8 * PIECE
    corner_copies = [
        pltpu.make_async_copy(top_ref.at[:, codes : codes + 4 * PIECE], corner_ref, ready.at[0]),
        pltpu.make_async_copy(top_ref.at[:, codes + 4 * PIECE :], level_ref, ready.at[1]),
    ]
    code_copy = pltpu.make_async_copy(top_ref.at[:, :codes], code_ref, ready.at[2])
    near_copies = [
        pltpu.make_async_copy(child_ref.at[:2, hop_of(slot)], near_ref.at[:, slot], ready.at[at])
        for slot, at in ((0, 4), (1, 7))
    ]
    for copy in corner_copies:
        copy.start()
    for copy in corner_copies:
        copy.wait()
    for copy in (code_copy, left_copy(0), *near_copies, front_copy(0), front_copy(1)):
        copy.start()

    def lost(s, first, count):
        return work.at[s // 2, pl.ds((s % 2) * height + first, count)]

    def each_child(step, act):
        for slot in range(4):
            parent = row_of(map_ref, row, slot)
            here = (parent >= 0) & (parent // 16 // SPAN == step)
            for source in range(4):
                found, value = col_of(map_ref, slot // 2, source, col)
                where = jnp.maximum(found, 0)
                start = pl.multiple_of((where % 2) * BS, BS)
                index = 4 * (slot % 2) + source
                copy = pltpu.make_async_copy(
                    child_ref.at[where // 2, hop_of(slot), :, pl.ds(start, BS)],
                    parts.at[index],
                    arrived.at[index],
                )

                @pl.when(here & (found >= 0))
                def _(copy=copy, index=index, tile=(parent // 16) % SPAN, s=value // 8):
                    act(copy, index, tile, s)

    factor_corner(corner_ref, level_ref, work, chi, clo, xhi, xlo)
    for r in range(NPIV):
        for c in range(NPIV):

            @pl.when((row == r) & (col == c))
            def _(r=r, c=c):
                own_block[...] = work[c, block(r)]

    code_copy.wait()
    for group in range(2):
        for k in range(NPIV):
            for piece in range(4):
                low = k * BS + piece * PIECE
                scale = level_ref[4 * piece + k].astype(I32)
                for q in range(WIDE):
                    first = (WIDE * group + q) * PIECE
                    work[q, low : low + PIECE] = decode(
                        code_ref[4 * piece + k, first : first + PIECE].astype(I32), scale
                    )
        for k in range(NPIV):
            for q in range(WIDE):
                uhi[group, block(k), block(q)], ulo[block(k), block(q)] = split(
                    work[q, block(k)]
                )

            @pl.when(row == k)
            def _(k=k, group=group):
                for q in range(WIDE):
                    own_row[WIDE * group + q] = work[q, block(k)]

            if k + 1 == NPIV:
                break
            below = slice((k + 1) * BS, NPIV * BS)
            for pair in range(WIDE // 2):
                wide = slice(2 * pair * BS, 2 * (pair + 1) * BS)
                taken = dot3(
                    (chi[below, block(k)], clo[below, block(k)]),
                    (uhi[group, block(k), wide], ulo[block(k), wide]),
                )
                for q in range(2):
                    at = 2 * pair + q
                    work[at, below] = work[at, below] - taken[:, block(q)]

        peak[group] = jnp.maximum(jnp.max(jnp.abs(uhi[group].astype(F32))), 1e-30)
        scale = 256.0 / peak[group]
        for k in range(NPIV):
            for q in range(WIDE):
                high = uhi[group, block(k), block(q)].astype(F32)
                low = ulo[block(k), block(q)].astype(F32)
                u8[group, block(k), block(q)] = (high * scale).astype(F8)
                u8[group, block(4 + k), block(q)] = (low * (scale * 256.0)).astype(F8)

    def rows_of_step(step, carry):
        each_child(step, lambda copy, index, tile, s: copy.start())
        left = work.at[:, pl.ds(height, height)]
        left_copy(step).wait()
        left[...] = left_ref[...]

        @pl.when(step == 0)
        def _():
            left_copy(1).start()
            for copy in near_copies:
                copy.wait()

        for slot in range(2):
            parent = row_of(map_ref, row, slot)
            for index in range(4):
                target = map_ref[0, index]
                cut = slice((index % 2) * BS, (index % 2) * BS + BS)
                for tile in range(SPAN):

                    @pl.when(
                        (parent >= 0) & (parent // 16 == SPAN * step + tile) & (target < NPIV)
                    )
                    def _(slot=slot, index=index, cut=cut, tile=tile, target=target):
                        left[target, block(tile)] = left[target, block(tile)] + near_ref[
                            index // 2, slot, :, cut
                        ].astype(F32)

        @pl.when((step == 0) & top_row)
        def _():
            left[:, :BS] = jnp.zeros((NPIV, BS, BS), F32)

        for k in range(NPIV):
            value = dot3(split(left[k]), (xhi[k], xlo[k]))
            lower[:height, block(k)], lower[height:, block(k)] = split(value)

            @pl.when(col == k)
            def _(value=value):
                own_col[...] = value

            if k + 1 < NPIV:
                rest = slice((k + 1) * BS, NPIV * BS)
                both = dot(lower[:, block(k)], chi[block(k), rest])
                both = both[:height] + both[height:]
                both = both + dot(lower[:height, block(k)], clo[block(k), rest])
                for j in range(k + 1, NPIV):
                    left[j] = left[j] - both[:, block(j - k - 1)]

        left_peak = jnp.maximum(jnp.max(jnp.abs(lower[:height].astype(F32))), 1e-30)
        scale = 256.0 / left_peak
        for k in range(NPIV):
            l8[:, block(k)] = (lower[height:, block(k)].astype(F32) * (scale * 256.0)).astype(F8)
            l8[:, block(4 + k)] = (lower[:height, block(k)].astype(F32) * scale).astype(F8)
        for group in range(2):
            unit = (left_peak * (1.0 / 65536.0)) * (peak[group] * (1.0 / 256.0))
            for pair in range(WIDE // 2):
                wide = slice(2 * pair * BS, 2 * (pair + 1) * BS)
                cross = dot(l8[...], u8[group, :, wide]) * unit
                total = dot(lower[:height], uhi[group, :, wide]) + cross
                for q in range(2):
                    lost(WIDE * group + 2 * pair + q, 0, height)[...] = total[:, block(q)]

        top_tile = (step == 0) & top_row

        @pl.when(top_tile)
        def _():
            for s in range(2 * WIDE):
                lost(s, 0, BS)[...] = -own_row[s]

        def add(copy, index, tile, s):
            copy.wait()
            place = lost(s, pl.multiple_of(tile * BS, BS), BS)

            @pl.when(jnp.logical_not(top_tile & (tile == 0)))
            def _():
                place[...] = place[...] - parts[index].astype(F32)

        each_child(step, add)

        @pl.when(col < NPIV)
        def _():
            lost(0, 0, height)[...] = -own_col[...]

            @pl.when(top_tile)
            def _():
                lost(0, 0, BS)[...] = -own_block[...]

        first_tile = lax.broadcasted_iota(I32, (LINES, 2 * WIDE, HALF), 1) == 0

        def turn(index, carry):
            low = pl.multiple_of(index * LINES, LINES)
            keep = jnp.where(top_tile & (low < BS), 0.0, 1.0)
            keep_first = jnp.where(col < NPIV, 0.0, keep)
            mask = jnp.where(first_tile, keep_first, keep)
            for half in range(2):
                lanes = slice(half * HALF, half * HALF + HALF)
                tiles = [lost(s, low, LINES)[:, lanes] for s in range(2 * WIDE)]
                turned = jnp.swapaxes(jnp.stack(tiles, axis=0), 0, 1)
                rows = pl.ds(low, LINES)
                kept = jnp.where(mask > 0.0, front[step, rows, half], 0.0)
                front[step, rows, half] = kept - turned
            return carry

        front_copy(step).wait()
        for quarter in range(4):
            lines = height // (4 * LINES)
            lax.fori_loop(quarter * lines, quarter * lines + lines, turn, 0)
            out_copy(step, quarter).start()
        return carry

    def out_copy(step, quarter):
        rows = pl.ds(quarter * (height // 4), height // 4)
        return pltpu.make_async_copy(
            front.at[step, rows],
            out_ref.at[pl.ds(step * height + quarter * (height // 4), height // 4)],
            sent.at[4 * step + quarter],
        )

    lax.fori_loop(0, 4 // SPAN, rows_of_step, 0)
    for step in range(4 // SPAN):
        for quarter in range(4):
            out_copy(step, quarter).wait()


LINES = 32


def run_finish(child_map, rc, top, front_left, view, child):
    away = pl.BlockSpec(memory_space=pl.ANY)
    return pl.pallas_call(
        finish,
        out_shape=shape(view.shape, F32),
        in_specs=[SMEM, SMEM] + [away] * 4,
        out_specs=away,
        scratch_shapes=[
            pltpu.VMEM((16, 4 * PIECE, BS), I16), pltpu.VMEM((16, 16, BS), I16),
            pltpu.VMEM((16, 8 * PIECE, BS), I16), pltpu.VMEM((4, SPAN * BS, BS), F32),
            pltpu.VMEM((2, 2, BS, 2 * BS), BF16), pltpu.VMEM((2, SPAN * BS, 2, 8, HALF), F32),
            pltpu.VMEM((4, 4 * BS, BS), F32),
            pltpu.VMEM((4 * BS, 4 * BS), BF16), pltpu.VMEM((4 * BS, 4 * BS), BF16),
            pltpu.VMEM((NPIV, BS, BS), BF16), pltpu.VMEM((NPIV, BS, BS), BF16),
            pltpu.VMEM((2, 4 * BS, WIDE * BS), BF16), pltpu.VMEM((4 * BS, WIDE * BS), BF16),
            pltpu.VMEM((2, 8 * BS, WIDE * BS), F8),
            pltpu.VMEM((2 * SPAN * BS, 4 * BS), BF16), pltpu.VMEM((SPAN * BS, 8 * BS), F8),
            pltpu.VMEM((SPAN * BS, BS), F32), pltpu.VMEM((BS, BS), F32),
            pltpu.VMEM((8, BS, BS), F32),
            pltpu.VMEM((8, BS, BS), BF16),
            pltpu.SMEM((2,), F32),
            pltpu.SemaphoreType.DMA((8,)),
            pltpu.SemaphoreType.DMA((8,)), pltpu.SemaphoreType.DMA((8,)),
        ],
        compiler_params=pltpu.CompilerParams(vmem_limit_bytes=LIMIT),
        cost_estimate=pl.CostEstimate(
            flops=23 * 2**30, bytes_accessed=32 * 2**20, transcendentals=0
        ),
    )(child_map, rc, top, front_left, view, child)


def shards(front, child_update, child_map, pivots):
    row = lax.axis_index("prow")
    col = lax.axis_index("pcol")
    rc = jnp.stack([row, col]).astype(I32)
    tiles = front.shape[0]

    def along_z(a, hop):
        return lax.ppermute(
            a, "prow", [(4 * i + j, 4 * i + (j + hop) % 4) for i in range(4) for j in range(4)]
        )

    def along_y(a, hop):
        return lax.ppermute(
            a, "prow", [(4 * i + j, 4 * ((i + hop) % 4) + j) for i in range(4) for j in range(4)]
        )

    def from_plane(a, hop):
        return lax.ppermute(a, "prow", [(j, 4 * hop + j) for j in range(4)])

    def spread(pieces):
        return [pieces[0]] + [from_plane(pieces[hop], hop) for hop in (1, 2, 3)]

    strip = shape((BS, 2 * BS), BF16)
    view = front.reshape(tiles, BS, 8, 2, HALF).transpose(0, 1, 3, 2, 4)
    view = view.reshape(tiles * BS, 2, 8, HALF)
    away = pl.BlockSpec(memory_space=pl.ANY)
    begun = pl.pallas_call(
        begin,
        out_shape=[strip] * 4 + [shape((8, PIECE, BS), F32)] * 4 + [shape((tiles * BS, BS), F32)],
        in_specs=[SMEM, SMEM, VMEM, VMEM, away, away],
        out_specs=[VMEM] * 9,
        scratch_shapes=[pltpu.VMEM((BS * 16, HALF), F32), pltpu.SemaphoreType.DMA((3,))],
        compiler_params=pltpu.CompilerParams(vmem_limit_bytes=LIMIT),
        cost_estimate=pl.CostEstimate(flops=2**30, bytes_accessed=8 * 2**20, transcendentals=0),
    )(
        child_map, rc, child_update.reshape(2, BS, 2 * BS), pivots,
        view.reshape(tiles * BS * 16, HALF), view,
    )
    zs, cuts, front_left = begun[:4], begun[4:8], begun[8]
    zs = [zs[0]] + [along_z(zs[hop], hop) for hop in (1, 2, 3)]

    moved = spread(cuts)

    front_left = lax.all_gather(front_left, "pcol", axis=0, tiled=False)

    thin = shape((PIECE, 2 * BS), BF16)
    zs, unused = lax.optimization_barrier((zs, moved[1]))
    picked = pl.pallas_call(
        pick_rows,
        out_shape=[thin] * 4 + [strip] * 4,
        in_specs=[SMEM, SMEM, VMEM] + [away] * 4,
        out_specs=[VMEM] * 4 + [away] * 4,
        scratch_shapes=[pltpu.VMEM((BS, 2 * BS), BF16), pltpu.SemaphoreType.DMA((20,))],
        compiler_params=pltpu.CompilerParams(vmem_limit_bytes=SMALL),
        cost_estimate=pl.CostEstimate(
            flops=20 * 2**30, bytes_accessed=2 * 2**20, transcendentals=0
        ),
    )(child_map, rc, pivots, *zs)
    thin = spread(picked[:4])
    ys = [picked[4]] + [along_y(picked[4 + hop], hop) for hop in (1, 2, 3)]

    thin = pl.pallas_call(
        mix,
        out_shape=shape((3 * PIECE + 16, BS), I16),
        in_specs=[SMEM] + [away] * 8,
        out_specs=VMEM,
        scratch_shapes=[
            pltpu.VMEM((PIECE, 2 * BS), BF16), pltpu.VMEM((PIECE, BS), F32),
            pltpu.SemaphoreType.DMA((8,)),
        ],
        compiler_params=pltpu.CompilerParams(vmem_limit_bytes=SMALL),
        cost_estimate=pl.CostEstimate(flops=0, bytes_accessed=2**20, transcendentals=0),
    )(rc, *thin, *moved)
    thin = lax.all_gather(thin, "pcol", axis=0, tiled=False)
    child = pl.pallas_call(
        pack,
        out_shape=shape((4, BS, 2 * BS), BF16),
        in_specs=[away] * 4,
        out_specs=away,
        scratch_shapes=[pltpu.SemaphoreType.DMA((4,))],
        compiler_params=pltpu.CompilerParams(vmem_limit_bytes=SMALL),
        cost_estimate=pl.CostEstimate(flops=0, bytes_accessed=2**21, transcendentals=0),
    )(*ys)
    thin, child = lax.optimization_barrier((thin, child))
    code = pl.pallas_call(
        assemble,
        out_shape=shape((12 * PIECE + 16, BS), I16),
        in_specs=[SMEM, SMEM, away, away, away, away, VMEM],
        out_specs=VMEM,
        scratch_shapes=[
            pltpu.VMEM((8, PIECE, BS), F32), pltpu.VMEM((NPIV, PIECE, BS), F32),
            pltpu.SemaphoreType.DMA((4,)),
        ],
        compiler_params=pltpu.CompilerParams(vmem_limit_bytes=SMALL),
        cost_estimate=pl.CostEstimate(flops=0, bytes_accessed=2**21, transcendentals=0),
    )(child_map, rc, *moved, thin)

    child = lax.all_gather(child, "pcol", axis=0, tiled=False)
    top = lax.all_gather(code, "prow", axis=0, tiled=False)

    done = run_finish(child_map, rc, top, front_left, view, child)
    done = done.reshape(tiles, BS, 2, 8, HALF).transpose(0, 1, 3, 2, 4)
    return done.reshape(front.shape)


def solution(mesh):
    return jax.shard_map(
        shards,
        mesh=mesh,
        in_specs=(P(None, "prow", None, "pcol"), P("prow", "pcol"), P(), P()),
        out_specs=P(None, "prow", None, "pcol"),
        check_vma=False,
    )
```

```python
import functools

import jax
import jax.numpy as jnp
from jax import lax
from jax.experimental import pallas as pl
from jax.experimental.pallas import tpu as pltpu
from jax.sharding import PartitionSpec as P

NPIV = 4
NS = 2
BS = 256
HALF = 128
PIECE = 64
FULL = 32767.0
CHILD_LEVEL = 11.0
F32 = jnp.float32
BF16 = jnp.bfloat16
F8 = jnp.float8_e4m3fn
I16 = jnp.int16
I32 = jnp.int32
SMEM = pl.BlockSpec(memory_space=pltpu.SMEM)
VMEM = pl.BlockSpec(memory_space=pltpu.VMEM)
LIMIT = 62 * 1024 * 1024
SMALL = 12 * 1024 * 1024


def shape(dims, kind):
    return jax.ShapeDtypeStruct(dims, kind)


def spot(map_ref, child, low, count, test):
    found = jnp.int32(-1)
    value = jnp.int32(-1)
    for step in range(count):
        entry = map_ref[child, low + step]
        hit = test(entry)
        found = jnp.where(hit, low + step, found)
        value = jnp.where(hit, entry, value)
    return found, value


def row_of(map_ref, row, slot):
    return spot(map_ref, slot // 2, 8 * (slot % 2), 8, lambda entry: entry % 16 == row)[1]


def col_of(map_ref, child, source, col):
    return spot(map_ref, child, 4 * source, 4, lambda entry: entry % 8 == col)


def split(value):
    high = value.astype(BF16)
    low = (value - high.astype(F32)).astype(BF16)
    return high, low


def dot(left, right):
    return jnp.dot(left, right, preferred_element_type=F32)


def dot3(left, right):
    (a, b), (c, d) = left, right
    rows = a.shape[0]
    both = dot(jnp.concatenate([a, b], axis=0), c)
    return both[:rows] + (both[rows:] + dot(a, d))


def block(step):
    return slice(step * BS, step * BS + BS)


def one_hot(pivots_ref, row):
    order = pivots_ref[pl.ds(jnp.minimum(row, NPIV - 1), 1), :]
    spread = lax.broadcasted_iota(I32, (BS, BS), 0)
    return jnp.transpose(jnp.where(order == spread, 1.0, 0.0)).astype(BF16)


def reorder(select, value):
    high, low = split(value)
    return dot(select, high) + dot(select, low)


def level(peak):
    return jnp.ceil(jnp.log2(jnp.full((8, HALF), jnp.maximum(peak, 1e-30))) * 4.0)


def encode(value, n):
    scaled = jnp.abs(value) * jnp.exp2(n * -0.25)[:1, :1]
    code = jnp.minimum(jnp.floor(jnp.sqrt(scaled) * FULL + 0.5), FULL)
    return jnp.where(value < 0.0, -code, code).astype(I32)


def decode(code, n):
    code = code.astype(F32)
    return code * jnp.abs(code) * (jnp.exp2(n.astype(F32)[:1, :1] * 0.25) * (1.0 / (FULL * FULL)))


def begin(
    map_ref, rc_ref, child_ref, pivots_ref, lines_ref, view_ref,
    o0, o1, o2, o3, p0, p1, p2, p3, word_ref, tile_row, left_ref, arrived,
):
    first = pltpu.make_async_copy(lines_ref.at[: BS * 16], tile_row, arrived.at[2])
    first.start()
    copies = [
        pltpu.make_async_copy(
            view_ref.at[:, half, 0, :],
            left_ref.at[:, half * HALF : half * HALF + HALF],
            arrived.at[half],
        )
        for half in range(2)
    ]
    for copy in copies:
        copy.start()
    row = rc_ref[0]
    z = row % 4
    second_at = map_ref[row // 8, 2 * (row % 8) + 1] % 4
    for hop, out in enumerate((o0, o1, o2, o3)):
        out[...] = child_ref[jnp.where(second_at == (z + hop) % 4, 1, 0)]
    select = one_hot(pivots_ref, row)
    first.wait()

    def one(tile, carry):
        halves = [tile_row[pl.ds(half * 8 + tile, BS, stride=16), :] for half in range(2)]
        turned = reorder(select, jnp.concatenate(halves, axis=1))
        for piece, out in enumerate((p0, p1, p2, p3)):
            out[tile] = turned[piece * PIECE : piece * PIECE + PIECE]
        return carry

    lax.fori_loop(0, 8, one, 0)
    for copy in copies:
        copy.wait()

    @pl.when(row < NPIV)
    def _():
        left_ref[:BS] = jnp.zeros((BS, BS), F32)

    n = level(jnp.max(jnp.abs(left_ref[...])))
    height = SPAN * BS
    for tile in range(SPAN):
        upper = encode(left_ref[tile * BS : tile * BS + BS], n)
        lower = encode(left_ref[height + tile * BS : height + tile * BS + BS], n)
        word_ref[tile * BS : tile * BS + BS] = upper * 65536 + (lower & 65535)
    word_ref[height:] = jnp.broadcast_to(n[:1, :1].astype(I32), (8, BS))


def pick_rows(map_ref, rc_ref, pivots_ref, *refs):
    held, pieces, hops, (work, arrived) = refs[:4], refs[4:8], refs[8:12], refs[12:]
    row = rc_ref[0]
    y, z = row // 4, row % 4
    found, value = spot(map_ref, 0, 0, 4, lambda entry: entry == row)
    live = (found >= 0) & (row < NPIV)

    def each(act):
        for hop in range(4):
            mine = live & (found // 2 == (z - hop + 4) % 4)
            act(mine, pltpu.make_async_copy(held[hop], work, arrived.at[16 + hop]))
        for hop in range(4):
            first = 2 * ((4 * y + (z - hop + 4) % 4) % 8)
            index, value = spot(map_ref, y // 2, first, 2, lambda entry: entry % 4 == z)
            for shift in range(4):
                mine = (index >= 0) & ((value // 4) % 4 == (y + shift) % 4)
                at = 4 * hop + shift
                act(mine, pltpu.make_async_copy(held[hop], hops[shift], arrived.at[at]))

    def start(mine, copy):
        @pl.when(mine)
        def _():
            copy.start()

    def wait(mine, copy):
        @pl.when(mine)
        def _():
            copy.wait()

    each(start)
    each(wait)

    @pl.when(live)
    def _():
        turned = dot(one_hot(pivots_ref, row), work[...]).astype(BF16)
        for piece in range(4):
            pieces[piece][...] = turned[piece * PIECE : piece * PIECE + PIECE]

    @pl.when(jnp.logical_not(live))
    def _():
        for piece in range(4):
            pieces[piece][...] = jnp.zeros((PIECE, 2 * BS), BF16)


def pack(y0, y1, y2, y3, out_ref, arrived):
    copies = [
        pltpu.make_async_copy(source, out_ref.at[shift], arrived.at[shift])
        for shift, source in enumerate((y0, y1, y2, y3))
    ]
    for copy in copies:
        copy.start()
    for copy in copies:
        copy.wait()


def mix(rc_ref, t0, t1, t2, t3, f0, f1, f2, f3, out_ref, strip, corner, arrived):
    y = rc_ref[0] // 4
    for piece, (child, source) in enumerate(((t0, f0), (t1, f1), (t2, f2), (t3, f3))):
        copies = [
            pltpu.make_async_copy(child, strip, arrived.at[2 * piece]),
            pltpu.make_async_copy(source.at[0], corner, arrived.at[2 * piece + 1]),
        ]

        @pl.when(y == piece)
        def _(copies=copies):
            for copy in copies:
                copy.start()
            for copy in copies:
                copy.wait()

    n = jnp.full((8, HALF), CHILD_LEVEL)
    for half in range(2):
        out_ref[half * PIECE : half * PIECE + PIECE] = encode(
            strip[:, half * BS : half * BS + BS].astype(F32), n
        ).astype(I16)
    n = level(jnp.max(jnp.abs(corner[...])))
    out_ref[2 * PIECE : 3 * PIECE] = encode(corner[...], n).astype(I16)
    out_ref[3 * PIECE :] = jnp.broadcast_to(n[:1, :1].astype(I32), (16, BS)).astype(I16)


def assemble(map_ref, rc_ref, f0, f1, f2, f3, thin, code_ref, work, corner, arrived):
    row, col = rc_ref[0], rc_ref[1]
    y = row // 4
    for piece, source in enumerate((f0, f1, f2, f3)):

        @pl.when(y == piece)
        def _(piece=piece, source=source):
            pltpu.make_async_copy(source, work, arrived.at[piece]).start()

    for k in range(NPIV):
        corner[k] = decode(
            thin[k, 2 * PIECE : 3 * PIECE].astype(I32), thin[k, 3 * PIECE :].astype(I32)
        )
    n = jnp.full((8, HALF), CHILD_LEVEL)
    for piece, source in enumerate((f0, f1, f2, f3)):

        @pl.when(y == piece)
        def _(piece=piece, source=source):
            pltpu.make_async_copy(source, work, arrived.at[piece]).wait()

    for index in range(16):
        parent = map_ref[0, index]
        low = (index % 2) * PIECE

        @pl.when(parent % 8 == col)
        def _(index=index, low=low, tile=parent // 8):
            child = decode(thin[index // 2, low : low + PIECE].astype(I32), n)
            work[tile] = work[tile] + child

        if index < NPIV:

            @pl.when(parent < NPIV)
            def _(index=index, low=low, parent=parent):
                child = decode(thin[index // 2, low : low + PIECE].astype(I32), n)
                corner[parent] = corner[parent] + child

    @pl.when(col < NPIV)
    def _():
        work[0] = jnp.zeros((PIECE, BS), F32)

    n = level(jnp.max(jnp.abs(work[...])))
    for tile in range(8):
        code_ref[tile * PIECE : tile * PIECE + PIECE] = encode(work[tile], n).astype(I16)
    z = row % 4
    square = corner[z]
    corner[z] = jnp.zeros((PIECE, BS), F32)
    first = level(jnp.max(jnp.abs(corner[...])))
    low = 8 * PIECE
    for k in range(NPIV):
        code_ref[low + k * PIECE : low + k * PIECE + PIECE] = encode(corner[k], first).astype(I16)
    second = level(jnp.max(jnp.abs(square)))
    code = encode(square, second)
    code_ref[pl.ds(pl.multiple_of(low + z * PIECE, PIECE), PIECE), :] = code.astype(I16)
    line = lax.broadcasted_iota(I32, (16, BS), 0)
    scales = second[:1, :1]
    for at, n in enumerate((n, first)):
        scales = jnp.where(line == at, n[:1, :1], scales)
    code_ref[12 * PIECE :] = scales.astype(I32).astype(I16)


def factor_corner(code_ref, level_ref, work, chi, clo, xhi, xlo):
    for y in range(4):
        for z in range(4):
            low = z * BS + y * PIECE
            scale = level_ref[4 * y + z].astype(I32)
            for k in range(4):
                code = code_ref[4 * y + z, k * PIECE : k * PIECE + PIECE].astype(I32)
                work[k, low : low + PIECE] = decode(code, scale[2:3] if k == z else scale[1:2])
    diagonal = lax.broadcasted_iota(I32, (BS, BS), 0) == lax.broadcasted_iota(I32, (BS, BS), 1)
    for k in range(NPIV):
        pivot = work[k, block(k)]
        parts = split(pivot)
        on_line = jnp.where(diagonal, pivot, 0.0)
        across = jnp.sum(on_line, axis=0, keepdims=True)
        down = jnp.sum(on_line, axis=1, keepdims=True)
        across = across / (across * across + 1.0)
        down = down / (down * down + 1.0)
        approx = 2.0 * jnp.where(diagonal, across, 0.0) - (down * pivot) * across
        for sweep_index in range(NS - 1):
            pair = split(approx)
            approx = 2.0 * approx - dot3(split(dot3(pair, parts)), pair)
        xhi[k], xlo[k] = split(approx)
        for j in range(NPIV):
            chi[block(k), block(j)], clo[block(k), block(j)] = split(work[j, block(k)])
        if k + 1 < NPIV:
            below = slice((k + 1) * BS, NPIV * BS)
            pair = split(dot3(split(work[k, below]), (xhi[k], xlo[k])))
            work[k, below] = pair[0].astype(F32) + pair[1].astype(F32)
            taken = dot3(pair, (chi[block(k), below], clo[block(k), below]))
            for j in range(k + 1, NPIV):
                work[j, below] = work[j, below] - taken[:, block(j - k - 1)]


SPAN = 2
WIDE = 4


def finish(
    map_ref, rc_ref, top_ref, left_from, front_from, child_ref, out_ref,
    corner_ref, level_ref, code_ref, left_ref, near_ref, front,
    work, chi, clo, xhi, xlo, uhi, ulo, u8, lower, l8, own_col, own_block, own_row, parts,
    peak, arrived, ready, sent,
):
    row, col = rc_ref[0], rc_ref[1]
    top_row = row < NPIV
    height = SPAN * BS

    def hop_of(slot):
        return (row // 4 - slot + 4) % 4

    left_copy = pltpu.make_async_copy(left_from.at[:NPIV], left_ref, ready.at[3])

    def front_copy(step):
        rows = pl.ds(step * height, height)
        return pltpu.make_async_copy(front_from.at[rows], front.at[step], ready.at[5 + step])

    codes = 8 * PIECE
    corner_copies = [
        pltpu.make_async_copy(top_ref.at[:, codes : codes + 4 * PIECE], corner_ref, ready.at[0]),
        pltpu.make_async_copy(top_ref.at[:, codes + 4 * PIECE :], level_ref, ready.at[1]),
    ]
    code_copy = pltpu.make_async_copy(top_ref.at[:, :codes], code_ref, ready.at[2])
    near_copies = [
        pltpu.make_async_copy(child_ref.at[:2, hop_of(slot)], near_ref.at[:, slot], ready.at[at])
        for slot, at in ((0, 4), (1, 7))
    ]
    for copy in corner_copies:
        copy.start()
    for copy in corner_copies:
        copy.wait()
    for copy in (code_copy, left_copy, *near_copies, front_copy(0), front_copy(1)):
        copy.start()

    def lost(s, first, count):
        return work.at[s // 2, pl.ds((s % 2) * height + first, count)]

    def each_child(step, act):
        for slot in range(4):
            parent = row_of(map_ref, row, slot)
            here = (parent >= 0) & (parent // 16 // SPAN == step)
            for source in range(4):
                found, value = col_of(map_ref, slot // 2, source, col)
                where = jnp.maximum(found, 0)
                start = pl.multiple_of((where % 2) * BS, BS)
                index = 4 * (slot % 2) + source
                copy = pltpu.make_async_copy(
                    child_ref.at[where // 2, hop_of(slot), :, pl.ds(start, BS)],
                    parts.at[index],
                    arrived.at[index],
                )

                @pl.when(here & (found >= 0))
                def _(copy=copy, index=index, tile=(parent // 16) % SPAN, s=value // 8):
                    act(copy, index, tile, s)

    factor_corner(corner_ref, level_ref, work, chi, clo, xhi, xlo)
    for r in range(NPIV):
        for c in range(NPIV):

            @pl.when((row == r) & (col == c))
            def _(r=r, c=c):
                own_block[...] = work[c, block(r)]

    code_copy.wait()
    for group in range(2):
        for k in range(NPIV):
            for piece in range(4):
                low = k * BS + piece * PIECE
                scale = level_ref[4 * piece + k].astype(I32)
                for q in range(WIDE):
                    first = (WIDE * group + q) * PIECE
                    work[q, low : low + PIECE] = decode(
                        code_ref[4 * piece + k, first : first + PIECE].astype(I32), scale
                    )
        for k in range(NPIV):
            for q in range(WIDE):
                uhi[group, block(k), block(q)], ulo[block(k), block(q)] = split(
                    work[q, block(k)]
                )

            @pl.when(row == k)
            def _(k=k, group=group):
                for q in range(WIDE):
                    own_row[WIDE * group + q] = work[q, block(k)]

            if k + 1 == NPIV:
                break
            below = slice((k + 1) * BS, NPIV * BS)
            for pair in range(WIDE // 2):
                wide = slice(2 * pair * BS, 2 * (pair + 1) * BS)
                taken = dot3(
                    (chi[below, block(k)], clo[below, block(k)]),
                    (uhi[group, block(k), wide], ulo[block(k), wide]),
                )
                for q in range(2):
                    at = 2 * pair + q
                    work[at, below] = work[at, below] - taken[:, block(q)]

        peak[group] = jnp.maximum(jnp.max(jnp.abs(uhi[group].astype(F32))), 1e-30)
        scale = 256.0 / peak[group]
        for k in range(NPIV):
            for q in range(WIDE):
                high = uhi[group, block(k), block(q)].astype(F32)
                low = ulo[block(k), block(q)].astype(F32)
                u8[group, block(k), block(q)] = (high * scale).astype(F8)
                u8[group, block(4 + k), block(q)] = (low * (scale * 256.0)).astype(F8)

    def rows_of_step(step, carry):
        each_child(step, lambda copy, index, tile, s: copy.start())
        left = work.at[:, pl.ds(height, height)]

        @pl.when(step == 0)
        def _():
            left_copy.wait()
            for copy in near_copies:
                copy.wait()

        for k in range(NPIV):
            word = left_ref[k, :height]
            word = jnp.where(step == 0, word, lax.shift_left(word, 16))
            left[k] = decode(lax.shift_right_arithmetic(word, 16), left_ref[k, height:])

        for slot in range(2):
            parent = row_of(map_ref, row, slot)
            for index in range(4):
                target = map_ref[0, index]
                cut = slice((index % 2) * BS, (index % 2) * BS + BS)
                for tile in range(SPAN):

                    @pl.when(
                        (parent >= 0) & (parent // 16 == SPAN * step + tile) & (target < NPIV)
                    )
                    def _(slot=slot, index=index, cut=cut, tile=tile, target=target):
                        left[target, block(tile)] = left[target, block(tile)] + near_ref[
                            index // 2, slot, :, cut
                        ].astype(F32)

        @pl.when((step == 0) & top_row)
        def _():
            left[:, :BS] = jnp.zeros((NPIV, BS, BS), F32)

        for k in range(NPIV):
            value = dot3(split(left[k]), (xhi[k], xlo[k]))
            lower[:height, block(k)], lower[height:, block(k)] = split(value)

            @pl.when(col == k)
            def _(value=value):
                own_col[...] = value

            if k + 1 < NPIV:
                rest = slice((k + 1) * BS, NPIV * BS)
                both = dot(lower[:, block(k)], chi[block(k), rest])
                both = both[:height] + both[height:]
                both = both + dot(lower[:height, block(k)], clo[block(k), rest])
                for j in range(k + 1, NPIV):
                    left[j] = left[j] - both[:, block(j - k - 1)]

        left_peak = jnp.maximum(jnp.max(jnp.abs(lower[:height].astype(F32))), 1e-30)
        scale = 256.0 / left_peak
        for k in range(NPIV):
            l8[:, block(k)] = (lower[height:, block(k)].astype(F32) * (scale * 256.0)).astype(F8)
            l8[:, block(4 + k)] = (lower[:height, block(k)].astype(F32) * scale).astype(F8)
        for group in range(2):
            unit = (left_peak * (1.0 / 65536.0)) * (peak[group] * (1.0 / 256.0))
            for pair in range(WIDE // 2):
                wide = slice(2 * pair * BS, 2 * (pair + 1) * BS)
                cross = dot(l8[...], u8[group, :, wide]) * unit
                total = dot(lower[:height], uhi[group, :, wide]) + cross
                for q in range(2):
                    lost(WIDE * group + 2 * pair + q, 0, height)[...] = total[:, block(q)]

        top_tile = (step == 0) & top_row

        @pl.when(top_tile)
        def _():
            for s in range(2 * WIDE):
                lost(s, 0, BS)[...] = -own_row[s]

        def add(copy, index, tile, s):
            copy.wait()
            place = lost(s, pl.multiple_of(tile * BS, BS), BS)

            @pl.when(jnp.logical_not(top_tile & (tile == 0)))
            def _():
                place[...] = place[...] - parts[index].astype(F32)

        each_child(step, add)

        @pl.when(col < NPIV)
        def _():
            lost(0, 0, height)[...] = -own_col[...]

            @pl.when(top_tile)
            def _():
                lost(0, 0, BS)[...] = -own_block[...]

        first_tile = lax.broadcasted_iota(I32, (LINES, 2 * WIDE, HALF), 1) == 0

        def turn(index, carry):
            low = pl.multiple_of(index * LINES, LINES)
            keep = jnp.where(top_tile & (low < BS), 0.0, 1.0)
            keep_first = jnp.where(col < NPIV, 0.0, keep)
            mask = jnp.where(first_tile, keep_first, keep)
            for half in range(2):
                lanes = slice(half * HALF, half * HALF + HALF)
                tiles = [lost(s, low, LINES)[:, lanes] for s in range(2 * WIDE)]
                turned = jnp.swapaxes(jnp.stack(tiles, axis=0), 0, 1)
                rows = pl.ds(low, LINES)
                kept = jnp.where(mask > 0.0, front[step, rows, half], 0.0)
                front[step, rows, half] = kept - turned
            return carry

        front_copy(step).wait()
        for quarter in range(4):
            lines = height // (4 * LINES)
            lax.fori_loop(quarter * lines, quarter * lines + lines, turn, 0)
            out_copy(step, quarter).start()
        return carry

    def out_copy(step, quarter):
        rows = pl.ds(quarter * (height // 4), height // 4)
        return pltpu.make_async_copy(
            front.at[step, rows],
            out_ref.at[pl.ds(step * height + quarter * (height // 4), height // 4)],
            sent.at[4 * step + quarter],
        )

    lax.fori_loop(0, 4 // SPAN, rows_of_step, 0)
    for step in range(4 // SPAN):
        for quarter in range(4):
            out_copy(step, quarter).wait()


LINES = 32


def run_finish(child_map, rc, top, front_left, view, child):
    away = pl.BlockSpec(memory_space=pl.ANY)
    return pl.pallas_call(
        finish,
        out_shape=shape(view.shape, F32),
        in_specs=[SMEM, SMEM] + [away] * 4,
        out_specs=away,
        scratch_shapes=[
            pltpu.VMEM((16, 4 * PIECE, BS), I16), pltpu.VMEM((16, 16, BS), I16),
            pltpu.VMEM((16, 8 * PIECE, BS), I16), pltpu.VMEM((4, SPAN * BS + 8, BS), I32),
            pltpu.VMEM((2, 2, BS, 2 * BS), BF16), pltpu.VMEM((2, SPAN * BS, 2, 8, HALF), F32),
            pltpu.VMEM((4, 4 * BS, BS), F32),
            pltpu.VMEM((4 * BS, 4 * BS), BF16), pltpu.VMEM((4 * BS, 4 * BS), BF16),
            pltpu.VMEM((NPIV, BS, BS), BF16), pltpu.VMEM((NPIV, BS, BS), BF16),
            pltpu.VMEM((2, 4 * BS, WIDE * BS), BF16), pltpu.VMEM((4 * BS, WIDE * BS), BF16),
            pltpu.VMEM((2, 8 * BS, WIDE * BS), F8),
            pltpu.VMEM((2 * SPAN * BS, 4 * BS), BF16), pltpu.VMEM((SPAN * BS, 8 * BS), F8),
            pltpu.VMEM((SPAN * BS, BS), F32), pltpu.VMEM((BS, BS), F32),
            pltpu.VMEM((8, BS, BS), F32),
            pltpu.VMEM((8, BS, BS), BF16),
            pltpu.SMEM((2,), F32),
            pltpu.SemaphoreType.DMA((8,)),
            pltpu.SemaphoreType.DMA((8,)), pltpu.SemaphoreType.DMA((8,)),
        ],
        compiler_params=pltpu.CompilerParams(vmem_limit_bytes=LIMIT),
        cost_estimate=pl.CostEstimate(
            flops=23 * 2**30, bytes_accessed=32 * 2**20, transcendentals=0
        ),
    )(child_map, rc, top, front_left, view, child)


def shards(front, child_update, child_map, pivots):
    row = lax.axis_index("prow")
    col = lax.axis_index("pcol")
    rc = jnp.stack([row, col]).astype(I32)
    tiles = front.shape[0]

    def along_z(a, hop):
        return lax.ppermute(
            a, "prow", [(4 * i + j, 4 * i + (j + hop) % 4) for i in range(4) for j in range(4)]
        )

    def along_y(a, hop):
        return lax.ppermute(
            a, "prow", [(4 * i + j, 4 * ((i + hop) % 4) + j) for i in range(4) for j in range(4)]
        )

    def from_plane(a, hop):
        return lax.ppermute(a, "prow", [(j, 4 * hop + j) for j in range(4)])

    def spread(pieces):
        return [pieces[0]] + [from_plane(pieces[hop], hop) for hop in (1, 2, 3)]

    strip = shape((BS, 2 * BS), BF16)
    view = front.reshape(tiles, BS, 8, 2, HALF).transpose(0, 1, 3, 2, 4)
    view = view.reshape(tiles * BS, 2, 8, HALF)
    away = pl.BlockSpec(memory_space=pl.ANY)
    begun = pl.pallas_call(
        begin,
        out_shape=[strip] * 4 + [shape((8, PIECE, BS), F32)] * 4 + [shape((SPAN * BS + 8, BS), I32)],
        in_specs=[SMEM, SMEM, VMEM, VMEM, away, away],
        out_specs=[VMEM] * 9,
        scratch_shapes=[
            pltpu.VMEM((BS * 16, HALF), F32), pltpu.VMEM((tiles * BS, BS), F32),
            pltpu.SemaphoreType.DMA((3,)),
        ],
        compiler_params=pltpu.CompilerParams(vmem_limit_bytes=LIMIT),
        cost_estimate=pl.CostEstimate(flops=2**30, bytes_accessed=8 * 2**20, transcendentals=0),
    )(
        child_map, rc, child_update.reshape(2, BS, 2 * BS), pivots,
        view.reshape(tiles * BS * 16, HALF), view,
    )
    zs, cuts, front_left = begun[:4], begun[4:8], begun[8]
    zs = [zs[0]] + [along_z(zs[hop], hop) for hop in (1, 2, 3)]

    moved = spread(cuts)

    front_left = lax.all_gather(front_left, "pcol", axis=0, tiled=False)

    thin = shape((PIECE, 2 * BS), BF16)
    zs, unused = lax.optimization_barrier((zs, moved[1]))
    picked = pl.pallas_call(
        pick_rows,
        out_shape=[thin] * 4 + [strip] * 4,
        in_specs=[SMEM, SMEM, VMEM] + [away] * 4,
        out_specs=[VMEM] * 4 + [away] * 4,
        scratch_shapes=[pltpu.VMEM((BS, 2 * BS), BF16), pltpu.SemaphoreType.DMA((20,))],
        compiler_params=pltpu.CompilerParams(vmem_limit_bytes=SMALL),
        cost_estimate=pl.CostEstimate(
            flops=20 * 2**30, bytes_accessed=2 * 2**20, transcendentals=0
        ),
    )(child_map, rc, pivots, *zs)
    thin = spread(picked[:4])
    ys = [picked[4]] + [along_y(picked[4 + hop], hop) for hop in (1, 2, 3)]

    thin = pl.pallas_call(
        mix,
        out_shape=shape((3 * PIECE + 16, BS), I16),
        in_specs=[SMEM] + [away] * 8,
        out_specs=VMEM,
        scratch_shapes=[
            pltpu.VMEM((PIECE, 2 * BS), BF16), pltpu.VMEM((PIECE, BS), F32),
            pltpu.SemaphoreType.DMA((8,)),
        ],
        compiler_params=pltpu.CompilerParams(vmem_limit_bytes=SMALL),
        cost_estimate=pl.CostEstimate(flops=0, bytes_accessed=2**20, transcendentals=0),
    )(rc, *thin, *moved)
    thin = lax.all_gather(thin, "pcol", axis=0, tiled=False)
    child = pl.pallas_call(
        pack,
        out_shape=shape((4, BS, 2 * BS), BF16),
        in_specs=[away] * 4,
        out_specs=away,
        scratch_shapes=[pltpu.SemaphoreType.DMA((4,))],
        compiler_params=pltpu.CompilerParams(vmem_limit_bytes=SMALL),
        cost_estimate=pl.CostEstimate(flops=0, bytes_accessed=2**21, transcendentals=0),
    )(*ys)
    thin, child = lax.optimization_barrier((thin, child))
    code = pl.pallas_call(
        assemble,
        out_shape=shape((12 * PIECE + 16, BS), I16),
        in_specs=[SMEM, SMEM, away, away, away, away, VMEM],
        out_specs=VMEM,
        scratch_shapes=[
            pltpu.VMEM((8, PIECE, BS), F32), pltpu.VMEM((NPIV, PIECE, BS), F32),
            pltpu.SemaphoreType.DMA((4,)),
        ],
        compiler_params=pltpu.CompilerParams(vmem_limit_bytes=SMALL),
        cost_estimate=pl.CostEstimate(flops=0, bytes_accessed=2**21, transcendentals=0),
    )(child_map, rc, *moved, thin)

    child = lax.all_gather(child, "pcol", axis=0, tiled=False)
    top = lax.all_gather(code, "prow", axis=0, tiled=False)

    done = run_finish(child_map, rc, top, front_left, view, child)
    done = done.reshape(tiles, BS, 2, 8, HALF).transpose(0, 1, 3, 2, 4)
    return done.reshape(front.shape)


def solution(mesh):
    return jax.shard_map(
        shards,
        mesh=mesh,
        in_specs=(P(None, "prow", None, "pcol"), P("prow", "pcol"), P(), P()),
        out_specs=P(None, "prow", None, "pcol"),
        check_vma=False,
    )
```

```python
import functools

import jax
import jax.numpy as jnp
from jax import lax
from jax.experimental import pallas as pl
from jax.experimental.pallas import tpu as pltpu
from jax.sharding import PartitionSpec as P

NPIV = 4
NS = 2
BS = 256
HALF = 128
PIECE = 64
FULL = 32767.0
CHILD_LEVEL = 11.0
F32 = jnp.float32
BF16 = jnp.bfloat16
F8 = jnp.float8_e4m3fn
I16 = jnp.int16
I32 = jnp.int32
SMEM = pl.BlockSpec(memory_space=pltpu.SMEM)
VMEM = pl.BlockSpec(memory_space=pltpu.VMEM)
LIMIT = 62 * 1024 * 1024
SMALL = 12 * 1024 * 1024


def shape(dims, kind):
    return jax.ShapeDtypeStruct(dims, kind)


def spot(map_ref, child, low, count, test):
    found = jnp.int32(-1)
    value = jnp.int32(-1)
    for step in range(count):
        entry = map_ref[child, low + step]
        hit = test(entry)
        found = jnp.where(hit, low + step, found)
        value = jnp.where(hit, entry, value)
    return found, value


def row_of(map_ref, row, slot):
    return spot(map_ref, slot // 2, 8 * (slot % 2), 8, lambda entry: entry % 16 == row)[1]


def col_of(map_ref, child, source, col):
    return spot(map_ref, child, 4 * source, 4, lambda entry: entry % 8 == col)


def split(value):
    high = value.astype(BF16)
    low = (value - high.astype(F32)).astype(BF16)
    return high, low


def dot(left, right):
    return jnp.dot(left, right, preferred_element_type=F32)


def dot3(left, right):
    (a, b), (c, d) = left, right
    rows = a.shape[0]
    both = dot(jnp.concatenate([a, b], axis=0), c)
    return both[:rows] + (both[rows:] + dot(a, d))


def block(step):
    return slice(step * BS, step * BS + BS)


def one_hot(pivots_ref, row):
    order = pivots_ref[pl.ds(jnp.minimum(row, NPIV - 1), 1), :]
    spread = lax.broadcasted_iota(I32, (BS, BS), 0)
    return jnp.transpose(jnp.where(order == spread, 1.0, 0.0)).astype(BF16)


def reorder(select, value):
    high, low = split(value)
    return dot(select, high) + dot(select, low)


def level(peak):
    return jnp.ceil(jnp.log2(jnp.full((8, HALF), jnp.maximum(peak, 1e-30))) * 4.0)


def encode(value, n):
    scaled = jnp.abs(value) * jnp.exp2(n * -0.25)[:1, :1]
    code = jnp.minimum(jnp.floor(jnp.sqrt(scaled) * FULL + 0.5), FULL)
    return jnp.where(value < 0.0, -code, code).astype(I32)


def decode(code, n):
    code = code.astype(F32)
    return code * jnp.abs(code) * (jnp.exp2(n.astype(F32)[:1, :1] * 0.25) * (1.0 / (FULL * FULL)))


def begin(
    map_ref, rc_ref, child_ref, pivots_ref, lines_ref, view_ref,
    o0, o1, o2, o3, p0, p1, p2, p3, word_ref, tile_row, left_ref, arrived,
):
    first = pltpu.make_async_copy(lines_ref.at[: BS * 16], tile_row, arrived.at[2])
    first.start()
    copies = [
        pltpu.make_async_copy(
            view_ref.at[:, half, 0, :],
            left_ref.at[:, half * HALF : half * HALF + HALF],
            arrived.at[half],
        )
        for half in range(2)
    ]
    for copy in copies:
        copy.start()
    row = rc_ref[0]
    z = row % 4
    second_at = map_ref[row // 8, 2 * (row % 8) + 1] % 4
    for hop, out in enumerate((o0, o1, o2, o3)):
        out[...] = child_ref[jnp.where(second_at == (z + hop) % 4, 1, 0)]
    select = one_hot(pivots_ref, row)
    first.wait()

    def one(tile, carry):
        halves = [tile_row[pl.ds(half * 8 + tile, BS, stride=16), :] for half in range(2)]
        turned = reorder(select, jnp.concatenate(halves, axis=1))
        for piece, out in enumerate((p0, p1, p2, p3)):
            out[tile] = turned[piece * PIECE : piece * PIECE + PIECE]
        return carry

    lax.fori_loop(0, 8, one, 0)
    for copy in copies:
        copy.wait()

    @pl.when(row < NPIV)
    def _():
        left_ref[:BS] = jnp.zeros((BS, BS), F32)

    n = level(jnp.max(jnp.abs(left_ref[...])))
    height = SPAN * BS
    for tile in range(SPAN):
        upper = encode(left_ref[tile * BS : tile * BS + BS], n)
        lower = encode(left_ref[height + tile * BS : height + tile * BS + BS], n)
        word_ref[tile * BS : tile * BS + BS] = upper * 65536 + (lower & 65535)
    word_ref[height:] = jnp.broadcast_to(n[:1, :1].astype(I32), (8, BS))


def pick_rows(map_ref, rc_ref, pivots_ref, *refs):
    held, pieces, hops, (work, arrived) = refs[:4], refs[4:8], refs[8:12], refs[12:]
    row = rc_ref[0]
    y, z = row // 4, row % 4
    found, value = spot(map_ref, 0, 0, 4, lambda entry: entry == row)
    live = (found >= 0) & (row < NPIV)

    def each(act):
        for hop in range(4):
            mine = live & (found // 2 == (z - hop + 4) % 4)
            act(mine, pltpu.make_async_copy(held[hop], work, arrived.at[16 + hop]))
        for hop in range(4):
            first = 2 * ((4 * y + (z - hop + 4) % 4) % 8)
            index, value = spot(map_ref, y // 2, first, 2, lambda entry: entry % 4 == z)
            for shift in range(4):
                mine = (index >= 0) & ((value // 4) % 4 == (y + shift) % 4)
                at = 4 * hop + shift
                act(mine, pltpu.make_async_copy(held[hop], hops[shift], arrived.at[at]))

    def start(mine, copy):
        @pl.when(mine)
        def _():
            copy.start()

    def wait(mine, copy):
        @pl.when(mine)
        def _():
            copy.wait()

    each(start)
    each(wait)

    @pl.when(live)
    def _():
        turned = dot(one_hot(pivots_ref, row), work[...]).astype(BF16)
        for piece in range(4):
            pieces[piece][...] = turned[piece * PIECE : piece * PIECE + PIECE]

    @pl.when(jnp.logical_not(live))
    def _():
        for piece in range(4):
            pieces[piece][...] = jnp.zeros((PIECE, 2 * BS), BF16)


def pack(y0, y1, y2, y3, out_ref, arrived):
    copies = [
        pltpu.make_async_copy(source, out_ref.at[shift], arrived.at[shift])
        for shift, source in enumerate((y0, y1, y2, y3))
    ]
    for copy in copies:
        copy.start()
    for copy in copies:
        copy.wait()


def mix(rc_ref, t0, t1, t2, t3, f0, f1, f2, f3, out_ref, strip, corner, arrived):
    y = rc_ref[0] // 4
    for piece, (child, source) in enumerate(((t0, f0), (t1, f1), (t2, f2), (t3, f3))):
        copies = [
            pltpu.make_async_copy(child, strip, arrived.at[2 * piece]),
            pltpu.make_async_copy(source.at[0], corner, arrived.at[2 * piece + 1]),
        ]

        @pl.when(y == piece)
        def _(copies=copies):
            for copy in copies:
                copy.start()
            for copy in copies:
                copy.wait()

    n = jnp.full((8, HALF), CHILD_LEVEL)
    for half in range(2):
        out_ref[half * PIECE : half * PIECE + PIECE] = encode(
            strip[:, half * BS : half * BS + BS].astype(F32), n
        ).astype(I16)
    n = level(jnp.max(jnp.abs(corner[...])))
    out_ref[2 * PIECE : 3 * PIECE] = encode(corner[...], n).astype(I16)
    out_ref[3 * PIECE :] = jnp.broadcast_to(n[:1, :1].astype(I32), (16, BS)).astype(I16)


def assemble(map_ref, rc_ref, f0, f1, f2, f3, thin, code_ref, work, corner, arrived):
    row, col = rc_ref[0], rc_ref[1]
    y = row // 4
    for piece, source in enumerate((f0, f1, f2, f3)):

        @pl.when(y == piece)
        def _(piece=piece, source=source):
            pltpu.make_async_copy(source, work, arrived.at[piece]).start()

    for k in range(NPIV):
        corner[k] = decode(
            thin[k, 2 * PIECE : 3 * PIECE].astype(I32), thin[k, 3 * PIECE :].astype(I32)
        )
    n = jnp.full((8, HALF), CHILD_LEVEL)
    for piece, source in enumerate((f0, f1, f2, f3)):

        @pl.when(y == piece)
        def _(piece=piece, source=source):
            pltpu.make_async_copy(source, work, arrived.at[piece]).wait()

    for index in range(16):
        parent = map_ref[0, index]
        low = (index % 2) * PIECE

        @pl.when(parent % 8 == col)
        def _(index=index, low=low, tile=parent // 8):
            child = decode(thin[index // 2, low : low + PIECE].astype(I32), n)
            work[tile] = work[tile] + child

        if index < NPIV:

            @pl.when(parent < NPIV)
            def _(index=index, low=low, parent=parent):
                child = decode(thin[index // 2, low : low + PIECE].astype(I32), n)
                corner[parent] = corner[parent] + child

    @pl.when(col < NPIV)
    def _():
        work[0] = jnp.zeros((PIECE, BS), F32)

    n = level(jnp.max(jnp.abs(work[...])))
    for tile in range(8):
        code_ref[tile * PIECE : tile * PIECE + PIECE] = encode(work[tile], n).astype(I16)
    z = row % 4
    square = corner[z]
    corner[z] = jnp.zeros((PIECE, BS), F32)
    first = level(jnp.max(jnp.abs(corner[...])))
    low = 8 * PIECE
    for k in range(NPIV):
        code_ref[low + k * PIECE : low + k * PIECE + PIECE] = encode(corner[k], first).astype(I16)
    second = level(jnp.max(jnp.abs(square)))
    code = encode(square, second)
    code_ref[pl.ds(pl.multiple_of(low + z * PIECE, PIECE), PIECE), :] = code.astype(I16)
    line = lax.broadcasted_iota(I32, (16, BS), 0)
    scales = second[:1, :1]
    for at, n in enumerate((n, first)):
        scales = jnp.where(line == at, n[:1, :1], scales)
    code_ref[12 * PIECE :] = scales.astype(I32).astype(I16)


def factor_corner(code_ref, level_ref, work, chi, clo, xhi, xlo):
    for y in range(4):
        for z in range(4):
            low = z * BS + y * PIECE
            scale = level_ref[4 * y + z].astype(I32)
            for k in range(4):
                code = code_ref[4 * y + z, k * PIECE : k * PIECE + PIECE].astype(I32)
                work[k, low : low + PIECE] = decode(code, scale[2:3] if k == z else scale[1:2])
    diagonal = lax.broadcasted_iota(I32, (BS, BS), 0) == lax.broadcasted_iota(I32, (BS, BS), 1)
    for k in range(NPIV):
        pivot = work[k, block(k)]
        parts = split(pivot)
        on_line = jnp.where(diagonal, pivot, 0.0)
        across = jnp.sum(on_line, axis=0, keepdims=True)
        down = jnp.sum(on_line, axis=1, keepdims=True)
        across = across / (across * across + 1.0)
        down = down / (down * down + 1.0)
        approx = 2.0 * jnp.where(diagonal, across, 0.0) - (down * pivot) * across
        for sweep_index in range(NS - 1):
            pair = split(approx)
            approx = 2.0 * approx - dot3(split(dot3(pair, parts)), pair)
        xhi[k], xlo[k] = split(approx)
        for j in range(NPIV):
            chi[block(k), block(j)], clo[block(k), block(j)] = split(work[j, block(k)])
        if k + 1 < NPIV:
            below = slice((k + 1) * BS, NPIV * BS)
            pair = split(dot3(split(work[k, below]), (xhi[k], xlo[k])))
            work[k, below] = pair[0].astype(F32) + pair[1].astype(F32)
            taken = dot3(pair, (chi[block(k), below], clo[block(k), below]))
            for j in range(k + 1, NPIV):
                work[j, below] = work[j, below] - taken[:, block(j - k - 1)]


SPAN = 2
WIDE = 4


def finish(
    map_ref, rc_ref, top_ref, left_from, front_from, child_ref, out_ref,
    corner_ref, level_ref, code_ref, left_ref, near_ref, front,
    work, chi, clo, xhi, xlo, uhi, ulo, u8, lower, l8, own_col, own_block, own_row, parts,
    peak, arrived, ready, sent,
):
    row, col = rc_ref[0], rc_ref[1]
    top_row = row < NPIV
    height = SPAN * BS

    def hop_of(slot):
        return (row // 4 - slot + 4) % 4

    left_copy = pltpu.make_async_copy(left_from.at[:NPIV], left_ref, ready.at[3])

    def front_copy(step):
        rows = pl.ds(step * height, height)
        return pltpu.make_async_copy(front_from.at[rows], front.at[step], ready.at[5 + step])

    codes = 8 * PIECE
    corner_copies = [
        pltpu.make_async_copy(top_ref.at[:, codes : codes + 4 * PIECE], corner_ref, ready.at[0]),
        pltpu.make_async_copy(top_ref.at[:, codes + 4 * PIECE :], level_ref, ready.at[1]),
    ]
    code_copy = pltpu.make_async_copy(top_ref.at[:, :codes], code_ref, ready.at[2])
    near_copies = [
        pltpu.make_async_copy(child_ref.at[:2, hop_of(slot)], near_ref.at[:, slot], ready.at[at])
        for slot, at in ((0, 4), (1, 7))
    ]
    for copy in corner_copies:
        copy.start()
    for copy in corner_copies:
        copy.wait()
    for copy in (code_copy, left_copy, *near_copies, front_copy(0), front_copy(1)):
        copy.start()

    def lost(s, first, count):
        return work.at[s // 2, pl.ds((s % 2) * height + first, count)]

    def each_child(step, act):
        for slot in range(4):
            parent = row_of(map_ref, row, slot)
            here = (parent >= 0) & (parent // 16 // SPAN == step)
            for source in range(4):
                found, value = col_of(map_ref, slot // 2, source, col)
                where = jnp.maximum(found, 0)
                start = pl.multiple_of((where % 2) * BS, BS)
                index = 4 * (slot % 2) + source
                copy = pltpu.make_async_copy(
                    child_ref.at[where // 2, hop_of(slot), :, pl.ds(start, BS)],
                    parts.at[index],
                    arrived.at[index],
                )

                @pl.when(here & (found >= 0))
                def _(copy=copy, index=index, tile=(parent // 16) % SPAN, s=value // 8):
                    act(copy, index, tile, s)

    factor_corner(corner_ref, level_ref, work, chi, clo, xhi, xlo)
    for r in range(NPIV):
        for c in range(NPIV):

            @pl.when((row == r) & (col == c))
            def _(r=r, c=c):
                own_block[...] = work[c, block(r)]

    code_copy.wait()
    for group in range(2):
        for k in range(NPIV):
            for piece in range(4):
                low = k * BS + piece * PIECE
                scale = level_ref[4 * piece + k].astype(I32)
                for q in range(WIDE):
                    first = (WIDE * group + q) * PIECE
                    work[q, low : low + PIECE] = decode(
                        code_ref[4 * piece + k, first : first + PIECE].astype(I32), scale
                    )
        for k in range(NPIV):
            for q in range(WIDE):
                uhi[group, block(k), block(q)], ulo[block(k), block(q)] = split(
                    work[q, block(k)]
                )

            @pl.when(row == k)
            def _(k=k, group=group):
                for q in range(WIDE):
                    own_row[WIDE * group + q] = work[q, block(k)]

            if k + 1 == NPIV:
                break
            below = slice((k + 1) * BS, NPIV * BS)
            for pair in range(WIDE // 2):
                wide = slice(2 * pair * BS, 2 * (pair + 1) * BS)
                taken = dot3(
                    (chi[below, block(k)], clo[below, block(k)]),
                    (uhi[group, block(k), wide], ulo[block(k), wide]),
                )
                for q in range(2):
                    at = 2 * pair + q
                    work[at, below] = work[at, below] - taken[:, block(q)]

        peak[group] = jnp.maximum(jnp.max(jnp.abs(uhi[group].astype(F32))), 1e-30)
        scale = 256.0 / peak[group]
        for k in range(NPIV):
            for q in range(WIDE):
                high = uhi[group, block(k), block(q)].astype(F32)
                low = ulo[block(k), block(q)].astype(F32)
                u8[group, block(k), block(q)] = (high * scale).astype(F8)
                u8[group, block(4 + k), block(q)] = (low * (scale * 256.0)).astype(F8)

    def rows_of_step(step, carry):
        each_child(step, lambda copy, index, tile, s: copy.start())
        left = work.at[:, pl.ds(height, height)]

        @pl.when(step == 0)
        def _():
            left_copy.wait()
            for copy in near_copies:
                copy.wait()

        for k in range(NPIV):
            word = left_ref[k, :height]
            word = jnp.where(step == 0, word, lax.shift_left(word, 16))
            left[k] = decode(lax.shift_right_arithmetic(word, 16), left_ref[k, height:])

        for slot in range(2):
            parent = row_of(map_ref, row, slot)
            for index in range(4):
                target = map_ref[0, index]
                cut = slice((index % 2) * BS, (index % 2) * BS + BS)
                for tile in range(SPAN):

                    @pl.when(
                        (parent >= 0) & (parent // 16 == SPAN * step + tile) & (target < NPIV)
                    )
                    def _(slot=slot, index=index, cut=cut, tile=tile, target=target):
                        left[target, block(tile)] = left[target, block(tile)] + near_ref[
                            index // 2, slot, :, cut
                        ].astype(F32)

        @pl.when((step == 0) & top_row)
        def _():
            left[:, :BS] = jnp.zeros((NPIV, BS, BS), F32)

        for k in range(NPIV):
            value = dot3(split(left[k]), (xhi[k], xlo[k]))
            lower[:height, block(k)], lower[height:, block(k)] = split(value)

            @pl.when(col == k)
            def _(value=value):
                own_col[...] = value

            if k + 1 < NPIV:
                rest = slice((k + 1) * BS, NPIV * BS)
                both = dot(lower[:, block(k)], chi[block(k), rest])
                both = both[:height] + both[height:]
                both = both + dot(lower[:height, block(k)], clo[block(k), rest])
                for j in range(k + 1, NPIV):
                    left[j] = left[j] - both[:, block(j - k - 1)]

        left_peak = jnp.maximum(jnp.max(jnp.abs(lower[:height].astype(F32))), 1e-30)
        scale = 256.0 / left_peak
        for k in range(NPIV):
            l8[:, block(k)] = (lower[height:, block(k)].astype(F32) * (scale * 256.0)).astype(F8)
            l8[:, block(4 + k)] = (lower[:height, block(k)].astype(F32) * scale).astype(F8)
        for group in range(2):
            unit = (left_peak * (1.0 / 65536.0)) * (peak[group] * (1.0 / 256.0))
            for pair in range(WIDE // 2):
                wide = slice(2 * pair * BS, 2 * (pair + 1) * BS)
                cross = dot(l8[...], u8[group, :, wide]) * unit
                total = dot(lower[:height], uhi[group, :, wide]) + cross
                for q in range(2):
                    lost(WIDE * group + 2 * pair + q, 0, height)[...] = total[:, block(q)]

        top_tile = (step == 0) & top_row

        @pl.when(top_tile)
        def _():
            for s in range(2 * WIDE):
                lost(s, 0, BS)[...] = -own_row[s]

        def add(copy, index, tile, s):
            copy.wait()
            place = lost(s, pl.multiple_of(tile * BS, BS), BS)

            @pl.when(jnp.logical_not(top_tile & (tile == 0)))
            def _():
                place[...] = place[...] - parts[index].astype(F32)

        each_child(step, add)

        @pl.when(col < NPIV)
        def _():
            lost(0, 0, height)[...] = -own_col[...]

            @pl.when(top_tile)
            def _():
                lost(0, 0, BS)[...] = -own_block[...]

        first_tile = lax.broadcasted_iota(I32, (LINES, 2 * WIDE, HALF), 1) == 0

        def turn(index, carry):
            low = pl.multiple_of(index * LINES, LINES)
            keep = jnp.where(top_tile & (low < BS), 0.0, 1.0)
            keep_first = jnp.where(col < NPIV, 0.0, keep)
            mask = jnp.where(first_tile, keep_first, keep)
            for half in range(2):
                lanes = slice(half * HALF, half * HALF + HALF)
                tiles = [lost(s, low, LINES)[:, lanes] for s in range(2 * WIDE)]
                turned = jnp.swapaxes(jnp.stack(tiles, axis=0), 0, 1)
                rows = pl.ds(low, LINES)
                kept = jnp.where(mask > 0.0, front[step, rows, half], 0.0)
                front[step, rows, half] = kept - turned
            return carry

        front_copy(step).wait()
        for quarter in range(4):
            lines = height // (4 * LINES)
            lax.fori_loop(quarter * lines, quarter * lines + lines, turn, 0)
            out_copy(step, quarter).start()
        return carry

    def out_copy(step, quarter):
        rows = pl.ds(quarter * (height // 4), height // 4)
        return pltpu.make_async_copy(
            front.at[step, rows],
            out_ref.at[pl.ds(step * height + quarter * (height // 4), height // 4)],
            sent.at[4 * step + quarter],
        )

    lax.fori_loop(0, 4 // SPAN, rows_of_step, 0)
    for step in range(4 // SPAN):
        for quarter in range(4):
            out_copy(step, quarter).wait()


LINES = 16


def run_finish(child_map, rc, top, front_left, view, child):
    away = pl.BlockSpec(memory_space=pl.ANY)
    return pl.pallas_call(
        finish,
        out_shape=shape(view.shape, F32),
        in_specs=[SMEM, SMEM] + [away] * 4,
        out_specs=away,
        scratch_shapes=[
            pltpu.VMEM((16, 4 * PIECE, BS), I16), pltpu.VMEM((16, 16, BS), I16),
            pltpu.VMEM((16, 8 * PIECE, BS), I16), pltpu.VMEM((4, SPAN * BS + 8, BS), I32),
            pltpu.VMEM((2, 2, BS, 2 * BS), BF16), pltpu.VMEM((2, SPAN * BS, 2, 8, HALF), F32),
            pltpu.VMEM((4, 4 * BS, BS), F32),
            pltpu.VMEM((4 * BS, 4 * BS), BF16), pltpu.VMEM((4 * BS, 4 * BS), BF16),
            pltpu.VMEM((NPIV, BS, BS), BF16), pltpu.VMEM((NPIV, BS, BS), BF16),
            pltpu.VMEM((2, 4 * BS, WIDE * BS), BF16), pltpu.VMEM((4 * BS, WIDE * BS), BF16),
            pltpu.VMEM((2, 8 * BS, WIDE * BS), F8),
            pltpu.VMEM((2 * SPAN * BS, 4 * BS), BF16), pltpu.VMEM((SPAN * BS, 8 * BS), F8),
            pltpu.VMEM((SPAN * BS, BS), F32), pltpu.VMEM((BS, BS), F32),
            pltpu.VMEM((8, BS, BS), F32),
            pltpu.VMEM((8, BS, BS), BF16),
            pltpu.SMEM((2,), F32),
            pltpu.SemaphoreType.DMA((8,)),
            pltpu.SemaphoreType.DMA((8,)), pltpu.SemaphoreType.DMA((8,)),
        ],
        compiler_params=pltpu.CompilerParams(vmem_limit_bytes=LIMIT),
        cost_estimate=pl.CostEstimate(
            flops=23 * 2**30, bytes_accessed=32 * 2**20, transcendentals=0
        ),
    )(child_map, rc, top, front_left, view, child)


def shards(front, child_update, child_map, pivots):
    row = lax.axis_index("prow")
    col = lax.axis_index("pcol")
    rc = jnp.stack([row, col]).astype(I32)
    tiles = front.shape[0]

    def along_z(a, hop):
        return lax.ppermute(
            a, "prow", [(4 * i + j, 4 * i + (j + hop) % 4) for i in range(4) for j in range(4)]
        )

    def along_y(a, hop):
        return lax.ppermute(
            a, "prow", [(4 * i + j, 4 * ((i + hop) % 4) + j) for i in range(4) for j in range(4)]
        )

    def from_plane(a, hop):
        return lax.ppermute(a, "prow", [(j, 4 * hop + j) for j in range(4)])

    def spread(pieces):
        return [pieces[0]] + [from_plane(pieces[hop], hop) for hop in (1, 2, 3)]

    strip = shape((BS, 2 * BS), BF16)
    view = front.reshape(tiles, BS, 8, 2, HALF).transpose(0, 1, 3, 2, 4)
    view = view.reshape(tiles * BS, 2, 8, HALF)
    away = pl.BlockSpec(memory_space=pl.ANY)
    begun = pl.pallas_call(
        begin,
        out_shape=[strip] * 4 + [shape((8, PIECE, BS), F32)] * 4 + [shape((SPAN * BS + 8, BS), I32)],
        in_specs=[SMEM, SMEM, VMEM, VMEM, away, away],
        out_specs=[VMEM] * 9,
        scratch_shapes=[
            pltpu.VMEM((BS * 16, HALF), F32), pltpu.VMEM((tiles * BS, BS), F32),
            pltpu.SemaphoreType.DMA((3,)),
        ],
        compiler_params=pltpu.CompilerParams(vmem_limit_bytes=LIMIT),
        cost_estimate=pl.CostEstimate(flops=2**30, bytes_accessed=8 * 2**20, transcendentals=0),
    )(
        child_map, rc, child_update.reshape(2, BS, 2 * BS), pivots,
        view.reshape(tiles * BS * 16, HALF), view,
    )
    zs, cuts, front_left = begun[:4], begun[4:8], begun[8]
    zs = [zs[0]] + [along_z(zs[hop], hop) for hop in (1, 2, 3)]

    moved = spread(cuts)

    front_left = lax.all_gather(front_left, "pcol", axis=0, tiled=False)

    thin = shape((PIECE, 2 * BS), BF16)
    zs, unused = lax.optimization_barrier((zs, moved[1]))
    picked = pl.pallas_call(
        pick_rows,
        out_shape=[thin] * 4 + [strip] * 4,
        in_specs=[SMEM, SMEM, VMEM] + [away] * 4,
        out_specs=[VMEM] * 4 + [away] * 4,
        scratch_shapes=[pltpu.VMEM((BS, 2 * BS), BF16), pltpu.SemaphoreType.DMA((20,))],
        compiler_params=pltpu.CompilerParams(vmem_limit_bytes=SMALL),
        cost_estimate=pl.CostEstimate(
            flops=20 * 2**30, bytes_accessed=2 * 2**20, transcendentals=0
        ),
    )(child_map, rc, pivots, *zs)
    thin = spread(picked[:4])
    ys = [picked[4]] + [along_y(picked[4 + hop], hop) for hop in (1, 2, 3)]

    thin = pl.pallas_call(
        mix,
        out_shape=shape((3 * PIECE + 16, BS), I16),
        in_specs=[SMEM] + [away] * 8,
        out_specs=VMEM,
        scratch_shapes=[
            pltpu.VMEM((PIECE, 2 * BS), BF16), pltpu.VMEM((PIECE, BS), F32),
            pltpu.SemaphoreType.DMA((8,)),
        ],
        compiler_params=pltpu.CompilerParams(vmem_limit_bytes=SMALL),
        cost_estimate=pl.CostEstimate(flops=0, bytes_accessed=2**20, transcendentals=0),
    )(rc, *thin, *moved)
    thin = lax.all_gather(thin, "pcol", axis=0, tiled=False)
    child = pl.pallas_call(
        pack,
        out_shape=shape((4, BS, 2 * BS), BF16),
        in_specs=[away] * 4,
        out_specs=away,
        scratch_shapes=[pltpu.SemaphoreType.DMA((4,))],
        compiler_params=pltpu.CompilerParams(vmem_limit_bytes=SMALL),
        cost_estimate=pl.CostEstimate(flops=0, bytes_accessed=2**21, transcendentals=0),
    )(*ys)
    thin, child = lax.optimization_barrier((thin, child))
    code = pl.pallas_call(
        assemble,
        out_shape=shape((12 * PIECE + 16, BS), I16),
        in_specs=[SMEM, SMEM, away, away, away, away, VMEM],
        out_specs=VMEM,
        scratch_shapes=[
            pltpu.VMEM((8, PIECE, BS), F32), pltpu.VMEM((NPIV, PIECE, BS), F32),
            pltpu.SemaphoreType.DMA((4,)),
        ],
        compiler_params=pltpu.CompilerParams(vmem_limit_bytes=SMALL),
        cost_estimate=pl.CostEstimate(flops=0, bytes_accessed=2**21, transcendentals=0),
    )(child_map, rc, *moved, thin)

    child = lax.all_gather(child, "pcol", axis=0, tiled=False)
    top = lax.all_gather(code, "prow", axis=0, tiled=False)

    done = run_finish(child_map, rc, top, front_left, view, child)
    done = done.reshape(tiles, BS, 2, 8, HALF).transpose(0, 1, 3, 2, 4)
    return done.reshape(front.shape)


def solution(mesh):
    return jax.shard_map(
        shards,
        mesh=mesh,
        in_specs=(P(None, "prow", None, "pcol"), P("prow", "pcol"), P(), P()),
        out_specs=P(None, "prow", None, "pcol"),
        check_vma=False,
    )
```

```python
import functools

import jax
import jax.numpy as jnp
from jax import lax
from jax.experimental import pallas as pl
from jax.experimental.pallas import tpu as pltpu
from jax.sharding import PartitionSpec as P

NPIV = 4
NS = 2
BS = 256
HALF = 128
PIECE = 64
FULL = 32767.0
CHILD_LEVEL = 11.0
F32 = jnp.float32
BF16 = jnp.bfloat16
F8 = jnp.float8_e4m3fn
I16 = jnp.int16
I32 = jnp.int32
SMEM = pl.BlockSpec(memory_space=pltpu.SMEM)
VMEM = pl.BlockSpec(memory_space=pltpu.VMEM)
LIMIT = 62 * 1024 * 1024
SMALL = 12 * 1024 * 1024


def shape(dims, kind):
    return jax.ShapeDtypeStruct(dims, kind)


def spot(map_ref, child, low, count, test):
    found = jnp.int32(-1)
    value = jnp.int32(-1)
    for step in range(count):
        entry = map_ref[child, low + step]
        hit = test(entry)
        found = jnp.where(hit, low + step, found)
        value = jnp.where(hit, entry, value)
    return found, value


def row_of(map_ref, row, slot):
    return spot(map_ref, slot // 2, 8 * (slot % 2), 8, lambda entry: entry % 16 == row)[1]


def col_of(map_ref, child, source, col):
    return spot(map_ref, child, 4 * source, 4, lambda entry: entry % 8 == col)


def split(value):
    high = value.astype(BF16)
    low = (value - high.astype(F32)).astype(BF16)
    return high, low


def dot(left, right):
    return jnp.dot(left, right, preferred_element_type=F32)


def dot3(left, right):
    (a, b), (c, d) = left, right
    rows = a.shape[0]
    both = dot(jnp.concatenate([a, b], axis=0), c)
    return both[:rows] + (both[rows:] + dot(a, d))


def block(step):
    return slice(step * BS, step * BS + BS)


def one_hot(pivots_ref, row):
    order = pivots_ref[pl.ds(jnp.minimum(row, NPIV - 1), 1), :]
    spread = lax.broadcasted_iota(I32, (BS, BS), 0)
    return jnp.transpose(jnp.where(order == spread, 1.0, 0.0)).astype(BF16)


def reorder(select, value):
    high, low = split(value)
    return dot(select, high) + dot(select, low)


def level(peak):
    return jnp.ceil(jnp.log2(jnp.full((8, HALF), jnp.maximum(peak, 1e-30))) * 4.0)


def encode(value, n):
    scaled = jnp.abs(value) * jnp.exp2(n * -0.25)[:1, :1]
    code = jnp.minimum(jnp.floor(jnp.sqrt(scaled) * FULL + 0.5), FULL)
    return jnp.where(value < 0.0, -code, code).astype(I32)


def decode(code, n):
    code = code.astype(F32)
    return code * jnp.abs(code) * (jnp.exp2(n.astype(F32)[:1, :1] * 0.25) * (1.0 / (FULL * FULL)))


def begin(
    map_ref, rc_ref, child_ref, pivots_ref, lines_ref, view_ref,
    o0, o1, o2, o3, p0, p1, p2, p3, word_ref, tile_row, left_ref, arrived,
):
    first = pltpu.make_async_copy(lines_ref.at[: BS * 16], tile_row, arrived.at[2])
    first.start()
    copies = [
        pltpu.make_async_copy(
            view_ref.at[:, half, 0, :],
            left_ref.at[:, half * HALF : half * HALF + HALF],
            arrived.at[half],
        )
        for half in range(2)
    ]
    for copy in copies:
        copy.start()
    row = rc_ref[0]
    z = row % 4
    second_at = map_ref[row // 8, 2 * (row % 8) + 1] % 4
    for hop, out in enumerate((o0, o1, o2, o3)):
        out[...] = child_ref[jnp.where(second_at == (z + hop) % 4, 1, 0)]
    select = one_hot(pivots_ref, row)
    first.wait()

    def one(tile, carry):
        halves = [tile_row[pl.ds(half * 8 + tile, BS, stride=16), :] for half in range(2)]
        turned = reorder(select, jnp.concatenate(halves, axis=1))
        for piece, out in enumerate((p0, p1, p2, p3)):
            out[tile] = turned[piece * PIECE : piece * PIECE + PIECE]
        return carry

    lax.fori_loop(0, 8, one, 0)
    for copy in copies:
        copy.wait()

    @pl.when(row < NPIV)
    def _():
        left_ref[:BS] = jnp.zeros((BS, BS), F32)

    n = level(jnp.max(jnp.abs(left_ref[...])))
    height = SPAN * BS
    for tile in range(SPAN):
        upper = encode(left_ref[tile * BS : tile * BS + BS], n)
        lower = encode(left_ref[height + tile * BS : height + tile * BS + BS], n)
        word_ref[tile * BS : tile * BS + BS] = upper * 65536 + (lower & 65535)
    word_ref[height:] = jnp.broadcast_to(n[:1, :1].astype(I32), (8, BS))


def pick_rows(map_ref, rc_ref, pivots_ref, *refs):
    held, pieces, hops, (work, arrived) = refs[:4], refs[4:8], refs[8:12], refs[12:]
    row = rc_ref[0]
    y, z = row // 4, row % 4
    found, value = spot(map_ref, 0, 0, 4, lambda entry: entry == row)
    live = (found >= 0) & (row < NPIV)

    def each(act):
        for hop in range(4):
            mine = live & (found // 2 == (z - hop + 4) % 4)
            act(mine, pltpu.make_async_copy(held[hop], work, arrived.at[16 + hop]))
        for hop in range(4):
            first = 2 * ((4 * y + (z - hop + 4) % 4) % 8)
            index, value = spot(map_ref, y // 2, first, 2, lambda entry: entry % 4 == z)
            for shift in range(4):
                mine = (index >= 0) & ((value // 4) % 4 == (y + shift) % 4)
                at = 4 * hop + shift
                act(mine, pltpu.make_async_copy(held[hop], hops[shift], arrived.at[at]))

    def start(mine, copy):
        @pl.when(mine)
        def _():
            copy.start()

    def wait(mine, copy):
        @pl.when(mine)
        def _():
            copy.wait()

    each(start)
    each(wait)

    @pl.when(live)
    def _():
        turned = dot(one_hot(pivots_ref, row), work[...]).astype(BF16)
        for piece in range(4):
            pieces[piece][...] = turned[piece * PIECE : piece * PIECE + PIECE]

    @pl.when(jnp.logical_not(live))
    def _():
        for piece in range(4):
            pieces[piece][...] = jnp.zeros((PIECE, 2 * BS), BF16)


def pack(y0, y1, y2, y3, out_ref, arrived):
    copies = [
        pltpu.make_async_copy(source, out_ref.at[shift], arrived.at[shift])
        for shift, source in enumerate((y0, y1, y2, y3))
    ]
    for copy in copies:
        copy.start()
    for copy in copies:
        copy.wait()


def mix(rc_ref, t0, t1, t2, t3, f0, f1, f2, f3, out_ref, strip, corner, arrived):
    y = rc_ref[0] // 4
    for piece, (child, source) in enumerate(((t0, f0), (t1, f1), (t2, f2), (t3, f3))):
        copies = [
            pltpu.make_async_copy(child, strip, arrived.at[2 * piece]),
            pltpu.make_async_copy(source.at[0], corner, arrived.at[2 * piece + 1]),
        ]

        @pl.when(y == piece)
        def _(copies=copies):
            for copy in copies:
                copy.start()
            for copy in copies:
                copy.wait()

    n = jnp.full((8, HALF), CHILD_LEVEL)
    for half in range(2):
        out_ref[half * PIECE : half * PIECE + PIECE] = encode(
            strip[:, half * BS : half * BS + BS].astype(F32), n
        ).astype(I16)
    n = level(jnp.max(jnp.abs(corner[...])))
    out_ref[2 * PIECE : 3 * PIECE] = encode(corner[...], n).astype(I16)
    out_ref[3 * PIECE :] = jnp.broadcast_to(n[:1, :1].astype(I32), (16, BS)).astype(I16)


def assemble(map_ref, rc_ref, f0, f1, f2, f3, thin, code_ref, work, corner, arrived):
    row, col = rc_ref[0], rc_ref[1]
    y = row // 4
    for piece, source in enumerate((f0, f1, f2, f3)):

        @pl.when(y == piece)
        def _(piece=piece, source=source):
            pltpu.make_async_copy(source, work, arrived.at[piece]).start()

    for k in range(NPIV):
        corner[k] = decode(
            thin[k, 2 * PIECE : 3 * PIECE].astype(I32), thin[k, 3 * PIECE :].astype(I32)
        )
    n = jnp.full((8, HALF), CHILD_LEVEL)
    for piece, source in enumerate((f0, f1, f2, f3)):

        @pl.when(y == piece)
        def _(piece=piece, source=source):
            pltpu.make_async_copy(source, work, arrived.at[piece]).wait()

    for index in range(16):
        parent = map_ref[0, index]
        low = (index % 2) * PIECE

        @pl.when(parent % 8 == col)
        def _(index=index, low=low, tile=parent // 8):
            child = decode(thin[index // 2, low : low + PIECE].astype(I32), n)
            work[tile] = work[tile] + child

        if index < NPIV:

            @pl.when(parent < NPIV)
            def _(index=index, low=low, parent=parent):
                child = decode(thin[index // 2, low : low + PIECE].astype(I32), n)
                corner[parent] = corner[parent] + child

    @pl.when(col < NPIV)
    def _():
        work[0] = jnp.zeros((PIECE, BS), F32)

    n = level(jnp.max(jnp.abs(work[...])))
    for tile in range(8):
        code_ref[tile * PIECE : tile * PIECE + PIECE] = encode(work[tile], n).astype(I16)
    z = row % 4
    square = corner[z]
    corner[z] = jnp.zeros((PIECE, BS), F32)
    first = level(jnp.max(jnp.abs(corner[...])))
    low = 8 * PIECE
    for k in range(NPIV):
        code_ref[low + k * PIECE : low + k * PIECE + PIECE] = encode(corner[k], first).astype(I16)
    second = level(jnp.max(jnp.abs(square)))
    code = encode(square, second)
    code_ref[pl.ds(pl.multiple_of(low + z * PIECE, PIECE), PIECE), :] = code.astype(I16)
    line = lax.broadcasted_iota(I32, (16, BS), 0)
    scales = second[:1, :1]
    for at, n in enumerate((n, first)):
        scales = jnp.where(line == at, n[:1, :1], scales)
    code_ref[12 * PIECE :] = scales.astype(I32).astype(I16)


def factor_corner(code_ref, level_ref, work, chi, clo, xhi, xlo):
    for y in range(4):
        for z in range(4):
            low = z * BS + y * PIECE
            scale = level_ref[4 * y + z].astype(I32)
            for k in range(4):
                code = code_ref[4 * y + z, k * PIECE : k * PIECE + PIECE].astype(I32)
                work[k, low : low + PIECE] = decode(code, scale[2:3] if k == z else scale[1:2])
    diagonal = lax.broadcasted_iota(I32, (BS, BS), 0) == lax.broadcasted_iota(I32, (BS, BS), 1)
    for k in range(NPIV):
        pivot = work[k, block(k)]
        parts = split(pivot)
        on_line = jnp.where(diagonal, pivot, 0.0)
        across = jnp.sum(on_line, axis=0, keepdims=True)
        down = jnp.sum(on_line, axis=1, keepdims=True)
        across = across / (across * across + 1.0)
        down = down / (down * down + 1.0)
        approx = 2.0 * jnp.where(diagonal, across, 0.0) - (down * pivot) * across
        for sweep_index in range(NS - 1):
            pair = split(approx)
            approx = 2.0 * approx - dot3(split(dot3(pair, parts)), pair)
        xhi[k], xlo[k] = split(approx)
        for j in range(NPIV):
            chi[block(k), block(j)], clo[block(k), block(j)] = split(work[j, block(k)])
        if k + 1 < NPIV:
            below = slice((k + 1) * BS, NPIV * BS)
            pair = split(dot3(split(work[k, below]), (xhi[k], xlo[k])))
            work[k, below] = pair[0].astype(F32) + pair[1].astype(F32)
            taken = dot3(pair, (chi[block(k), below], clo[block(k), below]))
            for j in range(k + 1, NPIV):
                work[j, below] = work[j, below] - taken[:, block(j - k - 1)]


SPAN = 2
WIDE = 4


def finish(
    map_ref, rc_ref, top_ref, left_from, front_from, child_ref, out_ref,
    corner_ref, level_ref, code_ref, left_ref, near_ref, front,
    work, chi, clo, xhi, xlo, uhi, ulo, u8, lower, l8, own_col, own_block, own_row, parts,
    peak, arrived, ready, sent,
):
    row, col = rc_ref[0], rc_ref[1]
    top_row = row < NPIV
    height = SPAN * BS

    def hop_of(slot):
        return (row // 4 - slot + 4) % 4

    left_copy = pltpu.make_async_copy(left_from.at[:NPIV], left_ref, ready.at[3])

    def front_copy(step):
        rows = pl.ds(step * height, height)
        return pltpu.make_async_copy(front_from.at[rows], front.at[step], ready.at[5 + step])

    codes = 8 * PIECE
    corner_copies = [
        pltpu.make_async_copy(top_ref.at[:, codes : codes + 4 * PIECE], corner_ref, ready.at[0]),
        pltpu.make_async_copy(top_ref.at[:, codes + 4 * PIECE :], level_ref, ready.at[1]),
    ]
    code_copy = pltpu.make_async_copy(top_ref.at[:, :codes], code_ref, ready.at[2])
    near_copies = [
        pltpu.make_async_copy(child_ref.at[:2, hop_of(slot)], near_ref.at[:, slot], ready.at[at])
        for slot, at in ((0, 4), (1, 7))
    ]
    for copy in corner_copies:
        copy.start()
    for copy in corner_copies:
        copy.wait()
    for copy in (code_copy, left_copy, *near_copies, front_copy(0), front_copy(1)):
        copy.start()

    def lost(s, first, count):
        return work.at[s // 2, pl.ds((s % 2) * height + first, count)]

    def each_child(step, act):
        for slot in range(4):
            parent = row_of(map_ref, row, slot)
            here = (parent >= 0) & (parent // 16 // SPAN == step)
            for source in range(4):
                found, value = col_of(map_ref, slot // 2, source, col)
                where = jnp.maximum(found, 0)
                start = pl.multiple_of((where % 2) * BS, BS)
                index = 4 * (slot % 2) + source
                copy = pltpu.make_async_copy(
                    child_ref.at[where // 2, hop_of(slot), :, pl.ds(start, BS)],
                    parts.at[index],
                    arrived.at[index],
                )

                @pl.when(here & (found >= 0))
                def _(copy=copy, index=index, tile=(parent // 16) % SPAN, s=value // 8):
                    act(copy, index, tile, s)

    factor_corner(corner_ref, level_ref, work, chi, clo, xhi, xlo)
    for r in range(NPIV):
        for c in range(NPIV):

            @pl.when((row == r) & (col == c))
            def _(r=r, c=c):
                own_block[...] = work[c, block(r)]

    code_copy.wait()
    for group in range(2):
        for k in range(NPIV):
            for piece in range(4):
                low = k * BS + piece * PIECE
                scale = level_ref[4 * piece + k].astype(I32)
                for q in range(WIDE):
                    first = (WIDE * group + q) * PIECE
                    work[q, low : low + PIECE] = decode(
                        code_ref[4 * piece + k, first : first + PIECE].astype(I32), scale
                    )
        for k in range(NPIV):
            for q in range(WIDE):
                uhi[group, block(k), block(q)], ulo[block(k), block(q)] = split(
                    work[q, block(k)]
                )

            @pl.when(row == k)
            def _(k=k, group=group):
                for q in range(WIDE):
                    own_row[WIDE * group + q] = work[q, block(k)]

            if k + 1 == NPIV:
                break
            below = slice((k + 1) * BS, NPIV * BS)
            for pair in range(WIDE // 2):
                wide = slice(2 * pair * BS, 2 * (pair + 1) * BS)
                taken = dot3(
                    (chi[below, block(k)], clo[below, block(k)]),
                    (uhi[group, block(k), wide], ulo[block(k), wide]),
                )
                for q in range(2):
                    at = 2 * pair + q
                    work[at, below] = work[at, below] - taken[:, block(q)]

        peak[group] = jnp.maximum(jnp.max(jnp.abs(uhi[group].astype(F32))), 1e-30)
        scale = 256.0 / peak[group]
        for k in range(NPIV):
            for q in range(WIDE):
                high = uhi[group, block(k), block(q)].astype(F32)
                low = ulo[block(k), block(q)].astype(F32)
                u8[group, block(k), block(q)] = (high * scale).astype(F8)
                u8[group, block(4 + k), block(q)] = (low * (scale * 256.0)).astype(F8)

    def rows_of_step(step, carry):
        each_child(step, lambda copy, index, tile, s: copy.start())
        left = work.at[:, pl.ds(height, height)]

        @pl.when(step == 0)
        def _():
            left_copy.wait()
            for copy in near_copies:
                copy.wait()

        for k in range(NPIV):
            word = left_ref[k, :height]
            word = jnp.where(step == 0, word, lax.shift_left(word, 16))
            left[k] = decode(lax.shift_right_arithmetic(word, 16), left_ref[k, height:])

        for slot in range(2):
            parent = row_of(map_ref, row, slot)
            for index in range(4):
                target = map_ref[0, index]
                cut = slice((index % 2) * BS, (index % 2) * BS + BS)
                for tile in range(SPAN):

                    @pl.when(
                        (parent >= 0) & (parent // 16 == SPAN * step + tile) & (target < NPIV)
                    )
                    def _(slot=slot, index=index, cut=cut, tile=tile, target=target):
                        left[target, block(tile)] = left[target, block(tile)] + near_ref[
                            index // 2, slot, :, cut
                        ].astype(F32)

        @pl.when((step == 0) & top_row)
        def _():
            left[:, :BS] = jnp.zeros((NPIV, BS, BS), F32)

        for k in range(NPIV):
            value = dot3(split(left[k]), (xhi[k], xlo[k]))
            lower[:height, block(k)], lower[height:, block(k)] = split(value)

            @pl.when(col == k)
            def _(value=value):
                own_col[...] = value

            if k + 1 < NPIV:
                rest = slice((k + 1) * BS, NPIV * BS)
                both = dot(lower[:, block(k)], chi[block(k), rest])
                both = both[:height] + both[height:]
                both = both + dot(lower[:height, block(k)], clo[block(k), rest])
                for j in range(k + 1, NPIV):
                    left[j] = left[j] - both[:, block(j - k - 1)]

        left_peak = jnp.maximum(jnp.max(jnp.abs(lower[:height].astype(F32))), 1e-30)
        scale = 256.0 / left_peak
        for k in range(NPIV):
            l8[:, block(k)] = (lower[height:, block(k)].astype(F32) * (scale * 256.0)).astype(F8)
            l8[:, block(4 + k)] = (lower[:height, block(k)].astype(F32) * scale).astype(F8)
        for group in range(2):
            unit = (left_peak * (1.0 / 65536.0)) * (peak[group] * (1.0 / 256.0))
            for pair in range(WIDE // 2):
                wide = slice(2 * pair * BS, 2 * (pair + 1) * BS)
                cross = dot(l8[...], u8[group, :, wide]) * unit
                total = dot(lower[:height], uhi[group, :, wide]) + cross
                for q in range(2):
                    lost(WIDE * group + 2 * pair + q, 0, height)[...] = total[:, block(q)]

        top_tile = (step == 0) & top_row

        @pl.when(top_tile)
        def _():
            for s in range(2 * WIDE):
                lost(s, 0, BS)[...] = -own_row[s]

        def add(copy, index, tile, s):
            copy.wait()
            place = lost(s, pl.multiple_of(tile * BS, BS), BS)

            @pl.when(jnp.logical_not(top_tile & (tile == 0)))
            def _():
                place[...] = place[...] - parts[index].astype(F32)

        each_child(step, add)

        @pl.when(col < NPIV)
        def _():
            lost(0, 0, height)[...] = -own_col[...]

            @pl.when(top_tile)
            def _():
                lost(0, 0, BS)[...] = -own_block[...]

        first_tile = lax.broadcasted_iota(I32, (LINES, 2 * WIDE, HALF), 1) == 0

        def turn(index, carry):
            low = pl.multiple_of(index * LINES, LINES)
            keep = jnp.where(top_tile & (low < BS), 0.0, 1.0)
            keep_first = jnp.where(col < NPIV, 0.0, keep)
            mask = jnp.where(first_tile, keep_first, keep)
            for half in range(2):
                lanes = slice(half * HALF, half * HALF + HALF)
                tiles = [lost(s, low, LINES)[:, lanes] for s in range(2 * WIDE)]
                turned = jnp.swapaxes(jnp.stack(tiles, axis=0), 0, 1)
                rows = pl.ds(low, LINES)
                kept = jnp.where(mask > 0.0, front[step, rows, half], 0.0)
                front[step, rows, half] = kept - turned
            return carry

        front_copy(step).wait()
        for quarter in range(4):
            lines = height // (4 * LINES)
            lax.fori_loop(quarter * lines, quarter * lines + lines, turn, 0)
            out_copy(step, quarter).start()
        return carry

    def out_copy(step, quarter):
        rows = pl.ds(quarter * (height // 4), height // 4)
        return pltpu.make_async_copy(
            front.at[step, rows],
            out_ref.at[pl.ds(step * height + quarter * (height // 4), height // 4)],
            sent.at[4 * step + quarter],
        )

    lax.fori_loop(0, 4 // SPAN, rows_of_step, 0)
    for step in range(4 // SPAN):
        for quarter in range(4):
            out_copy(step, quarter).wait()


LINES = 32


def run_finish(child_map, rc, top, front_left, view, child):
    away = pl.BlockSpec(memory_space=pl.ANY)
    return pl.pallas_call(
        finish,
        out_shape=shape(view.shape, F32),
        in_specs=[SMEM, SMEM] + [away] * 4,
        out_specs=away,
        scratch_shapes=[
            pltpu.VMEM((16, 4 * PIECE, BS), I16), pltpu.VMEM((16, 16, BS), I16),
            pltpu.VMEM((16, 8 * PIECE, BS), I16), pltpu.VMEM((4, SPAN * BS + 8, BS), I32),
            pltpu.VMEM((2, 2, BS, 2 * BS), BF16), pltpu.VMEM((2, SPAN * BS, 2, 8, HALF), F32),
            pltpu.VMEM((4, 4 * BS, BS), F32),
            pltpu.VMEM((4 * BS, 4 * BS), BF16), pltpu.VMEM((4 * BS, 4 * BS), BF16),
            pltpu.VMEM((NPIV, BS, BS), BF16), pltpu.VMEM((NPIV, BS, BS), BF16),
            pltpu.VMEM((2, 4 * BS, WIDE * BS), BF16), pltpu.VMEM((4 * BS, WIDE * BS), BF16),
            pltpu.VMEM((2, 8 * BS, WIDE * BS), F8),
            pltpu.VMEM((2 * SPAN * BS, 4 * BS), BF16), pltpu.VMEM((SPAN * BS, 8 * BS), F8),
            pltpu.VMEM((SPAN * BS, BS), F32), pltpu.VMEM((BS, BS), F32),
            pltpu.VMEM((8, BS, BS), F32),
            pltpu.VMEM((8, BS, BS), BF16),
            pltpu.SMEM((2,), F32),
            pltpu.SemaphoreType.DMA((8,)),
            pltpu.SemaphoreType.DMA((8,)), pltpu.SemaphoreType.DMA((8,)),
        ],
        compiler_params=pltpu.CompilerParams(vmem_limit_bytes=LIMIT),
        cost_estimate=pl.CostEstimate(
            flops=23 * 2**30, bytes_accessed=32 * 2**20, transcendentals=0
        ),
    )(child_map, rc, top, front_left, view, child)


def shards(front, child_update, child_map, pivots):
    row = lax.axis_index("prow")
    col = lax.axis_index("pcol")
    rc = jnp.stack([row, col]).astype(I32)
    tiles = front.shape[0]

    def along_z(a, hop):
        return lax.ppermute(
            a, "prow", [(4 * i + j, 4 * i + (j + hop) % 4) for i in range(4) for j in range(4)]
        )

    def along_y(a, hop):
        return lax.ppermute(
            a, "prow", [(4 * i + j, 4 * ((i + hop) % 4) + j) for i in range(4) for j in range(4)]
        )

    def from_plane(a, hop):
        return lax.ppermute(a, "prow", [(j, 4 * hop + j) for j in range(4)])

    def spread(pieces):
        return [pieces[0]] + [from_plane(pieces[hop], hop) for hop in (1, 2, 3)]

    strip = shape((BS, 2 * BS), BF16)
    view = front.reshape(tiles, BS, 8, 2, HALF).transpose(0, 1, 3, 2, 4)
    view = view.reshape(tiles * BS, 2, 8, HALF)
    away = pl.BlockSpec(memory_space=pl.ANY)
    begun = pl.pallas_call(
        begin,
        out_shape=[strip] * 4 + [shape((8, PIECE, BS), F32)] * 4 + [shape((SPAN * BS + 8, BS), I32)],
        in_specs=[SMEM, SMEM, VMEM, VMEM, away, away],
        out_specs=[VMEM] * 9,
        scratch_shapes=[
            pltpu.VMEM((BS * 16, HALF), F32), pltpu.VMEM((tiles * BS, BS), F32),
            pltpu.SemaphoreType.DMA((3,)),
        ],
        compiler_params=pltpu.CompilerParams(vmem_limit_bytes=2 * SMALL),
        cost_estimate=pl.CostEstimate(flops=2**30, bytes_accessed=8 * 2**20, transcendentals=0),
    )(
        child_map, rc, child_update.reshape(2, BS, 2 * BS), pivots,
        view.reshape(tiles * BS * 16, HALF), view,
    )
    zs, cuts, front_left = begun[:4], begun[4:8], begun[8]
    zs = [zs[0]] + [along_z(zs[hop], hop) for hop in (1, 2, 3)]

    moved = spread(cuts)

    front_left = lax.all_gather(front_left, "pcol", axis=0, tiled=False)

    thin = shape((PIECE, 2 * BS), BF16)
    zs, unused = lax.optimization_barrier((zs, moved[1]))
    picked = pl.pallas_call(
        pick_rows,
        out_shape=[thin] * 4 + [strip] * 4,
        in_specs=[SMEM, SMEM, VMEM] + [away] * 4,
        out_specs=[VMEM] * 4 + [away] * 4,
        scratch_shapes=[pltpu.VMEM((BS, 2 * BS), BF16), pltpu.SemaphoreType.DMA((20,))],
        compiler_params=pltpu.CompilerParams(vmem_limit_bytes=SMALL),
        cost_estimate=pl.CostEstimate(
            flops=20 * 2**30, bytes_accessed=2 * 2**20, transcendentals=0
        ),
    )(child_map, rc, pivots, *zs)
    thin = spread(picked[:4])
    ys = [picked[4]] + [along_y(picked[4 + hop], hop) for hop in (1, 2, 3)]

    thin = pl.pallas_call(
        mix,
        out_shape=shape((3 * PIECE + 16, BS), I16),
        in_specs=[SMEM] + [away] * 8,
        out_specs=VMEM,
        scratch_shapes=[
            pltpu.VMEM((PIECE, 2 * BS), BF16), pltpu.VMEM((PIECE, BS), F32),
            pltpu.SemaphoreType.DMA((8,)),
        ],
        compiler_params=pltpu.CompilerParams(vmem_limit_bytes=SMALL),
        cost_estimate=pl.CostEstimate(flops=0, bytes_accessed=2**20, transcendentals=0),
    )(rc, *thin, *moved)
    thin = lax.all_gather(thin, "pcol", axis=0, tiled=False)
    child = pl.pallas_call(
        pack,
        out_shape=shape((4, BS, 2 * BS), BF16),
        in_specs=[away] * 4,
        out_specs=away,
        scratch_shapes=[pltpu.SemaphoreType.DMA((4,))],
        compiler_params=pltpu.CompilerParams(vmem_limit_bytes=SMALL),
        cost_estimate=pl.CostEstimate(flops=0, bytes_accessed=2**21, transcendentals=0),
    )(*ys)
    thin, child = lax.optimization_barrier((thin, child))
    code = pl.pallas_call(
        assemble,
        out_shape=shape((12 * PIECE + 16, BS), I16),
        in_specs=[SMEM, SMEM, away, away, away, away, VMEM],
        out_specs=VMEM,
        scratch_shapes=[
            pltpu.VMEM((8, PIECE, BS), F32), pltpu.VMEM((NPIV, PIECE, BS), F32),
            pltpu.SemaphoreType.DMA((4,)),
        ],
        compiler_params=pltpu.CompilerParams(vmem_limit_bytes=SMALL),
        cost_estimate=pl.CostEstimate(flops=0, bytes_accessed=2**21, transcendentals=0),
    )(child_map, rc, *moved, thin)

    child = lax.all_gather(child, "pcol", axis=0, tiled=False)
    top = lax.all_gather(code, "prow", axis=0, tiled=False)

    done = run_finish(child_map, rc, top, front_left, view, child)
    done = done.reshape(tiles, BS, 2, 8, HALF).transpose(0, 1, 3, 2, 4)
    return done.reshape(front.shape)


def solution(mesh):
    return jax.shard_map(
        shards,
        mesh=mesh,
        in_specs=(P(None, "prow", None, "pcol"), P("prow", "pcol"), P(), P()),
        out_specs=P(None, "prow", None, "pcol"),
        check_vma=False,
    )
```
